32 devices in a mesh: span: 4 (over x, core), seq: 8 (over z, y).
Axes of the slice: x: 2, y: 2, z: 4, core: 2. Of those that a mesh axis runs over, the one named last changes fastest.
Arguments:
- inputs: bfloat16 [2, 2048, 2560], P(None, ('span', 'seq')), may hold values from -6 to 6
- norm_one: bfloat16 [2560], P(('span', 'seq')), may hold values from 0.25 to 1.75
- rec_proj: bfloat16 [2560, 5120], P(('span', 'seq')), may hold values from -0.125 to 0.125
- conv_weight: bfloat16 [2560, 4], P(('span', 'seq')), may hold values from -3 to 3
- conv_bias: bfloat16 [2560], P(('span', 'seq')), may hold values from -3 to 3
- gate_weight: bfloat16 [2560, 512], P(('span', 'seq')), may hold values from -0.375 to 0.375
- gate_bias: bfloat16 [2560, 2], P(('span', 'seq')), may hold values from -4 to 4
- decay_param: bfloat16 [2560], P(('span', 'seq')), may hold values from -14 to -3.5
- out_proj: bfloat16 [2560, 2560], P(('span', 'seq')), may hold values from -0.5 to 0.5
- norm_two: bfloat16 [2560], P(('span', 'seq')), may hold values from 0.25 to 1.75
- mlp_wide: bfloat16 [2560, 2, 7680], P('span', None, 'seq'), may hold values from -0.125 to 0.125
- mlp_narrow: bfloat16 [2560, 7680], P('span', 'seq'), may hold values from -0.09375 to 0.09375
- cotangent: bfloat16 [2, 2048, 2560], P(None, ('span', 'seq')), may hold values from -6 to 6
Outputs:
- output: bfloat16 [2, 2048, 2560], P(None, ('span', 'seq'))
- input_grad: float32 [2, 2048, 2560], P(None, ('span', 'seq'))
- norm_one_grad: float32 [2560], P(('span', 'seq'))
- rec_proj_grad: float32 [2560, 5120], P(('span', 'seq'))
- conv_weight_grad: float32 [2560, 4], P(('span', 'seq'))
- conv_bias_grad: float32 [2560], P(('span', 'seq'))
- gate_weight_grad: float32 [2560, 512], P(('span', 'seq'))
- gate_bias_grad: float32 [2560, 2], P(('span', 'seq'))
- decay_param_grad: float32 [2560], P(('span', 'seq'))
- out_proj_grad: float32 [2560, 2560], P(('span', 'seq'))
- norm_two_grad: float32 [2560], P(('span', 'seq'))
- mlp_wide_grad: float32 [2560, 2, 7680], P('span', None, 'seq')
- mlp_narrow_grad: float32 [2560, 7680], P('span', 'seq')
The draws below stay inside these ranges and needn't reach their ends.
All inputs are finite; a program needn't handle non-finite values.
Results may differ from the reference program's by a relative error of at most 0.008.
The reference program's roundings to bfloat16 on the way (of `normal_one` and `x_branch`) count: a program that leaves them out, or rounds other values in their place, can miss the bound.
Values may be sent and summed in bfloat16 or wider, within the bound.
A program may use at most 384 MiB of HBM per device.

```python
import jax
import jax.numpy as jnp
from jax import lax

D = 2560
F = 7680
HEADS = 10
CONV = 4
MB = 2
BW = 256
SEQ_LEN = 2048


def draw_decay_param(key, part):
    key = jax.random.fold_in(key, 7)
    first, second = jax.random.split(key)
    spot = jax.random.uniform(first, (D,), jnp.float32)
    pick = jax.random.uniform(second, (D,), jnp.float32)
    share = 0.5
    slow_rate = jnp.exp(jnp.log(0.1 / SEQ_LEN) + spot * jnp.log(10.0))
    fast_rate = jnp.exp(jnp.log(0.02) + spot * jnp.log(5.0))
    rate = jnp.where(pick < share, slow_rate, fast_rate)
    return jnp.log(jnp.expm1(rate / 4.0)).astype(jnp.bfloat16)


def levels(key, extent, pieces, least, top_value):
    level, own = 1.0, jax.random.fold_in(key, 6)
    for position, parts in pieces:
        draws = jnp.exp(jax.random.uniform(jax.random.fold_in(own, position), (parts,), jnp.float32, least / len(pieces), top_value / len(pieces)))
        level = level * jnp.repeat(draws, extent[position] // parts).reshape([-1 if axis == position else 1 for axis in range(len(extent))])
    return level


def bell_draw(key, shape, spread, reach, pieces=(), held_as=jnp.bfloat16):
    array = jax.random.normal(key, shape, jnp.float32) * spread
    if len(pieces) > 0:
        array = levels(key, shape, pieces, -0.22, 0.18) * array
    return jnp.clip(array, min=-reach, max=reach).astype(held_as)


def setup_inputs(seed: int = 0) -> dict:
    arg_keys = jax.random.split(jax.random.key(seed), 14)
    inputs = bell_draw(arg_keys[0], (MB, SEQ_LEN, D), 1.0, 6.0, ((1, 32),))
    norm_one = jnp.clip(1.0 + 0.15 * jax.random.normal(arg_keys[1], (D,), jnp.float32), 0.25, 1.75).astype(jnp.bfloat16)
    rec_proj = bell_draw(arg_keys[2], (D, 2 * D), D ** -0.5, 0.125, ((0, 32),))
    conv_weight = bell_draw(arg_keys[3], (D, CONV), 0.5, 3.0, ((0, 32),))
    conv_bias = bell_draw(arg_keys[4], (D,), 0.5, 3.0, ((0, 32),))
    gate_weight = bell_draw(arg_keys[5], (D, 2 * BW), BW ** -0.5, 0.375, ((0, 32),))
    gate_bias = bell_draw(arg_keys[6], (D, 2), 1.0, 4.0, ((0, 32),))
    decay_param = draw_decay_param(jax.random.fold_in(arg_keys[13], 71), 0)
    out_proj = bell_draw(arg_keys[8], (D, D), (D // 16) ** -0.5, 0.5, ((0, 32),))
    norm_two = jnp.clip(1.0 + 0.15 * jax.random.normal(arg_keys[9], (D,), jnp.float32), 0.25, 1.75).astype(jnp.bfloat16)
    mlp_wide = bell_draw(arg_keys[10], (D, 2, F), D ** -0.5, 0.125, ((0, 4), (2, 8)))
    mlp_narrow = bell_draw(arg_keys[11], (D, F), (F // 2) ** -0.5, 0.09375, ((0, 4), (1, 8)))
    cotangent = bell_draw(arg_keys[12], (MB, SEQ_LEN, D), 1.0, 6.0, ((1, 32),))
    return {"inputs": inputs, "norm_one": norm_one, "rec_proj": rec_proj, "conv_weight": conv_weight, "conv_bias": conv_bias, "gate_weight": gate_weight, "gate_bias": gate_bias, "decay_param": decay_param, "out_proj": out_proj, "norm_two": norm_two, "mlp_wide": mlp_wide, "mlp_narrow": mlp_narrow, "cotangent": cotangent}


HIGH = lax.Precision.HIGHEST
EPS = 1e-06

@jax.custom_vjp
def low(v):
    return lax.optimization_barrier(v.astype(jnp.bfloat16)).astype(jnp.float32)

@jax.custom_vjp
def low_back(v):
    return v

def low_keep(v):
    return (low(v), None)

def low_pass(kept, grad):
    return (grad,)

def back_keep(v):
    return (v, None)

def back_low(kept, grad):
    return (low(grad),)
low.defvjp(low_keep, low_pass)
low_back.defvjp(back_keep, back_low)

def affine(left, right):
    return (left[0] * right[0], right[0] * left[1] + right[1])

def normed(v, gain):
    return v * lax.rsqrt(lax.optimization_barrier(jnp.mean(v * v, axis=-1, keepdims=True)) + EPS) * gain

def forward(x, gain_one, proj, conv_weight, conv_bias, gate_weight, gate_bias, decay_param, out_proj, gain_two, mlp_wide, mlp_narrow):
    batch, steps, width = x.shape
    head_w = width // HEADS
    normal_one = low(normed(x, gain_one))
    projected = low_back(jnp.einsum('mtd,de->mte', normal_one, proj, precision=HIGH))
    x_branch = low(projected[..., :width])
    y_branch = jax.nn.gelu(projected[..., width:])
    padded = jnp.pad(x_branch, ((0, 0), (CONV - 1, 0), (0, 0)))
    conv_out = conv_bias + jnp.zeros_like(x_branch)
    for k in range(CONV):
        conv_out = conv_out + conv_weight[:, k] * padded[:, CONV - 1 - k:CONV - 1 - k + steps]
    blocks = low(conv_out).reshape(batch, steps, HEADS, head_w)
    gate_pre = low_back(jnp.einsum('mthc,hcd->mthd', blocks, gate_weight.reshape(HEADS, head_w, 2 * head_w), precision=HIGH))
    recur = jax.nn.sigmoid(gate_pre[..., :head_w].reshape(batch, steps, width) + gate_bias[:, 0])
    inject = jax.nn.sigmoid(gate_pre[..., head_w:].reshape(batch, steps, width) + gate_bias[:, 1])
    log_decay = -8.0 * recur * jax.nn.softplus(decay_param)
    decay = jnp.exp(log_decay)
    driven = jnp.sqrt(-jnp.expm1(2.0 * log_decay)) * inject * conv_out
    states = lax.associative_scan(affine, (decay, driven), axis=1)[1]
    mixed = low(states * y_branch)
    resid = x + low_back(jnp.einsum('mtd,de->mte', mixed, out_proj, precision=HIGH))
    normal_two = low(normed(resid, gain_two))
    gate_up = low_back(jnp.einsum('mtd,dkf->mtkf', normal_two, mlp_wide, precision=HIGH))
    hidden = low(jax.nn.gelu(gate_up[..., 0, :]) * gate_up[..., 1, :])
    return resid + jnp.einsum('mtf,df->mtd', hidden, mlp_narrow, precision=HIGH)

def reference(inputs, norm_one, rec_proj, conv_weight, conv_bias, gate_weight, gate_bias, decay_param, out_proj, norm_two, mlp_wide, mlp_narrow, cotangent):
    floats = [v.astype(jnp.float32) for v in (inputs, norm_one, rec_proj, conv_weight, conv_bias, gate_weight, gate_bias, decay_param, out_proj, norm_two, mlp_wide, mlp_narrow)]
    final, pullback = jax.vjp(forward, *floats)
    grads = pullback(cotangent.astype(jnp.float32))
    return (final.astype(jnp.bfloat16), grads[0], grads[1], grads[2], grads[3], grads[4], grads[5], grads[6], grads[7], grads[8], grads[9], grads[10], grads[11])
```

```python
import functools

import jax
import jax.numpy as jnp
from jax import lax
from jax.experimental import pallas as pl
from jax.experimental.pallas import tpu as pltpu
from jax.sharding import PartitionSpec as P

CONV = 4
EPS = 1e-06
AXES = ("span", "seq")
F32 = jnp.float32
BF16 = jnp.bfloat16
SUBS = 8


def swap(value, mask):
    count = lax.axis_size("span") * lax.axis_size("seq")
    return lax.ppermute(value, AXES, [(i, i ^ mask) for i in range(count)])


def dot(a, b, dims, out=F32):
    return lax.dot_general(a, b, ((dims[0], dims[1]), ((), ())), preferred_element_type=F32).astype(out)


def nn(a, b, out=F32):
    return dot(a, b, ((1,), (0,)), out)


def nt(a, b, out=F32):
    return dot(a, b, ((1,), (1,)), out)


def tn(a, b, out=F32):
    return dot(a, b, ((0,), (0,)), out)


def normed(v, gain):
    return v * lax.rsqrt(jnp.mean(v * v, axis=-1, keepdims=True) + EPS) * gain


def norm_back(v, gain, grad):
    scale = lax.rsqrt(jnp.mean(v * v, axis=-1, keepdims=True) + EPS)
    z = v * scale
    e = grad * gain
    return scale * (e - z * jnp.mean(e * z, axis=-1, keepdims=True)), jnp.sum(grad * z, axis=0)


def one_less_exp(u):
    series = 1.0 + u / 7.0
    for n in (6.0, 5.0, 4.0, 3.0, 2.0):
        series = 1.0 + u / n * series
    return jnp.where(u > -0.25, -u * series, 1.0 - jnp.exp(u))


def roll(v, by):
    return pltpu.roll(v, by % SUBS, 0)


def quarter_of(shape, quarters):
    return lax.broadcasted_iota(jnp.int32, shape, 0) % quarters


def spread(v, quarters, at):
    q = quarter_of(v.shape, quarters)
    held = jnp.where(q == at, v, 0.0)
    total = held
    for k in range(1, quarters):
        total = total + roll(held, k if at == 0 else -k)
    return total


def scan_carries(prods, sums, quarters, backward):
    q = quarter_of(prods[0].shape, quarters)
    sign = -1 if backward else 1
    order = (1, 0) if backward else (0, 1)
    place = quarters - 1 - q if backward else q
    whole = None
    enter = [None, None]
    for b in order:
        p, s = prods[b], sums[b]
        d = 1
        while d < quarters:
            pp, ss = roll(p, sign * d), roll(s, sign * d)
            ok = place >= d
            s = jnp.where(ok, p * ss + s, s)
            p = jnp.where(ok, p * pp, p)
            d *= 2
        first = place == 0
        ep = jnp.where(first, 1.0, roll(p, sign))
        es = jnp.where(first, 0.0, roll(s, sign))
        last = 0 if backward else quarters - 1
        tp, ts = spread(p, quarters, last), spread(s, quarters, last)
        if whole is None:
            enter[b] = (ep, es)
            whole = (tp, ts)
        else:
            enter[b] = (ep * whole[0], ep * whole[1] + es)
            whole = (tp * whole[0], tp * whole[1] + ts)
    return enter, whole


def earlier_rows(groups, halo, quarters, steps):
    q = quarter_of(groups[0].shape[1:], quarters)
    edge = CONV - 1
    out = []
    for b in (0, 1):
        ahead = []
        for k in range(edge, 0, -1):
            same = roll(groups[b][steps - k], 1)
            before = halo[k - 1] if b == 0 else roll(groups[0][steps - k], 1 - quarters)
            ahead.append(jnp.where(q == 0, before, same)[None])
        out.append(jnp.concatenate([*ahead, groups[b]], axis=0))
    return out


def forward_kernel(steps, quarters, xb, chan, gate, conv_o, recur_o, inject_o, decay_o, local_o, prod_o, enter_o, carry_o):
    rows = 2 * steps * SUBS
    width = xb.shape[1]
    head = xb[...].astype(F32)
    groups = [head[b * steps * SUBS : (b + 1) * steps * SUBS].reshape(steps, SUBS, width) for b in (0, 1)]
    halo = [head[rows + k * SUBS : rows + (k + 1) * SUBS] for k in range(CONV - 1)]
    edge = CONV - 1
    convs = []
    for ext in earlier_rows(groups, halo, quarters, steps):
        total = jnp.broadcast_to(chan[4:5][None], (steps, SUBS, width))
        for k in range(CONV):
            total = total + chan[k : k + 1][None] * ext[edge - k : edge - k + steps]
        convs.append(total.reshape(steps * SUBS, width))
    conv = jnp.concatenate(convs, axis=0)
    pre = jnp.dot(conv.astype(BF16), gate[...], preferred_element_type=F32)
    recur = jax.nn.sigmoid(pre[:, :width] + chan[5:6])
    inject = jax.nn.sigmoid(pre[:, width:] + chan[6:7])
    log_decay = -8.0 * recur * chan[7:8]
    decay = jnp.exp(log_decay)
    driven = jnp.sqrt(one_less_exp(2.0 * log_decay)) * inject * conv
    conv_o[...] = conv
    recur_o[...] = recur
    inject_o[...] = inject
    decay_o[...] = decay
    prods, sums = [], []
    for b in (0, 1):
        h = p = None
        for t in range(steps):
            at = (b * steps + t) * SUBS
            d, u = decay[at : at + SUBS], driven[at : at + SUBS]
            h = u if h is None else d * h + u
            p = d if p is None else d * p
            local_o[at : at + SUBS] = h
            prod_o[at : at + SUBS] = p
        prods.append(p)
        sums.append(h)
    enter, whole = scan_carries(prods, sums, quarters, False)
    for b in (0, 1):
        enter_o[b * SUBS : (b + 1) * SUBS] = enter[b][0]
        enter_o[(2 + b) * SUBS : (3 + b) * SUBS] = enter[b][1]
    q = quarter_of(whole[0].shape, quarters)
    carry_o[...] = jnp.where(q == 0, whole[0], whole[1])


def adjoint_kernel(steps, quarters, grad, decay, prod, local_o, after_o, enter_o, carry_o):
    prods, sums = [], []
    for b in (0, 1):
        g = r = None
        for t in range(steps - 1, -1, -1):
            at = (b * steps + t) * SUBS
            rows = slice(at, at + SUBS)
            a = grad[rows] if g is None else grad[rows] + g
            r = jnp.ones_like(a) if r is None else r * decay[at + SUBS : at + 2 * SUBS]
            local_o[rows] = a
            after_o[rows] = r
            g = decay[rows] * a
        last = ((b + 1) * steps - 1) * SUBS
        prods.append(prod[last : last + SUBS])
        sums.append(g)
    enter, whole = scan_carries(prods, sums, quarters, True)
    for b in (0, 1):
        enter_o[b * SUBS : (b + 1) * SUBS] = enter[b][0]
        enter_o[(2 + b) * SUBS : (3 + b) * SUBS] = enter[b][1]
    carry_o[...] = whole[1]


def backward_kernel(
    steps, quarters, local, after, states, came, entered, conv_r, recur_r, inject_r, decay_r, xb, chan, gate,
    dx_o, spill_o, gate_o, small_o,
):
    rows = 2 * steps * SUBS
    width = xb.shape[1]
    edge = CONV - 1
    block = steps * SUBS

    def by_step(v):
        return [v[b * block : (b + 1) * block].reshape(steps, SUBS, width) for b in (0, 1)]

    adjoint = jnp.concatenate(
        [
            (l + a * came[b * SUBS : (b + 1) * SUBS][None]).reshape(block, width)
            for b, (l, a) in enumerate(zip(by_step(local[...]), by_step(after[...])))
        ],
        axis=0,
    )
    earlier = jnp.concatenate(
        [
            jnp.concatenate([entered[b * SUBS : (b + 1) * SUBS], states[b * block : (b + 1) * block - SUBS]], axis=0)
            for b in (0, 1)
        ],
        axis=0,
    )
    conv, recur, inject, decay = conv_r[...], recur_r[...], inject_r[...], decay_r[...]
    rate = chan[7:8]
    mult = jnp.sqrt(one_less_exp(-16.0 * recur * rate))
    d_decay = adjoint * earlier
    d_log = d_decay * decay - adjoint * inject * conv * (decay * decay / mult)
    d_inject = adjoint * mult * conv
    d_conv = adjoint * mult * inject
    d_rate = jnp.sum(d_log * (-8.0 * recur), axis=0, keepdims=True)
    d_recur = d_log * (-8.0 * rate) * recur * (1.0 - recur)
    d_inject = d_inject * inject * (1.0 - inject)
    low = jnp.concatenate([d_recur.astype(BF16), d_inject.astype(BF16)], axis=1)
    d_conv = d_conv + lax.dot_general(low, gate[...], (((1,), (1,)), ((), ())), preferred_element_type=F32)
    gate_o[...] = lax.dot_general(conv.astype(BF16), low, (((0,), (0,)), ((), ())), preferred_element_type=F32)
    head = xb[...].astype(F32)
    halo = [head[rows + k * SUBS : rows + (k + 1) * SUBS] for k in range(edge)]
    exts = earlier_rows(by_step(head), halo, quarters, steps)
    groups = by_step(d_conv)
    for k in range(CONV):
        taps = sum(
            jnp.sum(groups[b] * exts[b][edge - k : edge - k + steps], axis=(0, 1), keepdims=True)[0] for b in (0, 1)
        )
        small_o[k : k + 1] = taps
    small_o[4:5] = jnp.sum(d_conv, axis=0, keepdims=True)
    small_o[5:6] = jnp.sum(d_recur, axis=0, keepdims=True)
    small_o[6:7] = jnp.sum(d_inject, axis=0, keepdims=True)
    small_o[7:8] = d_rate
    q = quarter_of((SUBS, width), quarters)
    for b in (0, 1):
        beyond = []
        for j in range(edge):
            same = roll(groups[b][j], -1)
            later = roll(groups[1][j], quarters - 1) if b == 0 else jnp.zeros_like(same)
            beyond.append(jnp.where(q == quarters - 1, later, same)[None])
        ext = jnp.concatenate([groups[b], *beyond], axis=0)
        total = chan[0:1][None] * ext[:steps]
        for k in range(1, CONV):
            total = total + chan[k : k + 1][None] * ext[k : k + steps]
        dx_o[b * block : (b + 1) * block] = total.reshape(block, width)
    for j in range(1, CONV):
        total = jnp.zeros((SUBS, width), F32)
        for k in range(j, CONV):
            total = total + chan[k : k + 1] * groups[0][k - j]
        spill_o[(j - 1) * SUBS : j * SUBS] = total


def by_heads(kernel, heads, head_w, arrays, outs):
    def spec(shape, tall):
        if tall:
            return pl.BlockSpec((head_w, shape[1]), lambda h: (h, 0))
        return pl.BlockSpec((shape[0], head_w), lambda h: (0, h))

    return pl.pallas_call(
        kernel,
        grid=(heads,),
        in_specs=[spec(a.shape, tall) for a, tall in arrays],
        out_specs=[spec(s, tall) for s, tall in outs],
        out_shape=[jax.ShapeDtypeStruct(s, F32) for s, _ in outs],
        compiler_params=pltpu.CompilerParams(vmem_limit_bytes=48 * 1024 * 1024),
    )(*[a for a, _ in arrays])


def on_device(
    inputs, norm_one, rec_proj, conv_weight, conv_bias, gate_weight, gate_bias, decay_param, out_proj, norm_two,
    mlp_wide, mlp_narrow, cotangent,
):
    spans, seqs = lax.axis_size("span"), lax.axis_size("seq")
    count = spans * seqs
    span, seq = lax.axis_index("span"), lax.axis_index("seq")
    me = span * seqs + seq
    side = me % 2
    pair = me // 2
    pairs = count // 2
    batch, tokens, width = inputs.shape
    half = width // 2
    quarters = SUBS // batch
    steps = tokens // quarters
    own = batch * tokens
    rows = 2 * own
    head_w = gate_weight.shape[1] // 2
    heads = half // head_w
    edge = CONV - 1
    share = width // count
    units = mlp_narrow.shape[1]
    inner = [2 * k for k in range(1, seqs // 2)]
    core = seqs
    xs = [2 * seqs * k for k in range(1, spans // 2)]
    top = count // 2
    upper = me // top

    def to_rows(v):
        return v.reshape(batch, quarters, steps, width).transpose(2, 0, 1, 3).reshape(own, width)

    def from_rows(v):
        return v.reshape(steps, batch, quarters, width).transpose(1, 2, 0, 3).reshape(batch, tokens, width)

    def in_order(mine, other, axis):
        return jnp.concatenate([jnp.where(side == 0, mine, other), jnp.where(side == 0, other, mine)], axis=axis)

    def cut(v, index, size, axis):
        return lax.dynamic_slice_in_dim(v, index * size, size, axis)

    small = jnp.concatenate(
        [norm_one[:, None], norm_two[:, None], conv_weight, conv_bias[:, None], gate_bias, decay_param[:, None]], axis=1
    )
    small = lax.all_gather(small, AXES, axis=0, tiled=True).astype(F32).T
    gain_one, gain_two = small[0], small[1]
    rate_pre = cut(small[9:10], side, half, 1)
    chan = cut(jnp.concatenate([small[2:9], jax.nn.softplus(small[9:10])], axis=0), side, half, 1)

    def gathered_rows(block, buffer, place):
        pieces = {0: block}
        for m in inner:
            pieces[m] = swap(block, m)
        for m in xs:
            for n in (0, *inner):
                pieces[m ^ n] = swap(pieces[n], m)
        for n in list(pieces):
            pieces[core ^ n] = swap(pieces[n], core)
        for m, piece in pieces.items():
            buffer = lax.dynamic_update_slice_in_dim(buffer, piece, place(me ^ m), 0)
        return buffer

    def columns_half(block):
        mine, theirs = cut(block, side, half, 1), cut(block, 1 - side, half, 1)
        block = in_order(mine, swap(theirs, 1), 0)
        return gathered_rows(block, jnp.zeros((width, half), BF16), lambda d: d // 2 * 2 * share)

    def rows_half(block):
        full = lax.all_gather(block, AXES, axis=0, tiled=True)
        return cut(full, side, half, 0)

    proj_x = columns_half(rec_proj[:, :width])
    proj_y = columns_half(rec_proj[:, width:])
    gates = rows_half(gate_weight)
    out_half = rows_half(out_proj)

    mine = to_rows(inputs)
    x = mine.astype(F32)
    tail = inputs[:, tokens - edge :]
    halo = lax.ppermute(tail, AXES, [(i, i + 1) for i in range(1, count - 1, 2)]) + lax.ppermute(
        tail, AXES, [(i, i + 2) for i in range(1, count - 2, 2)]
    )
    halo = jnp.zeros((edge, batch, quarters, width), BF16).at[:, :, 0].set(halo[:, ::-1].transpose(1, 0, 2))
    both = in_order(mine, swap(mine, 1), 0)
    lead = jnp.concatenate([both, halo.reshape(edge * SUBS, width), jnp.zeros((8, width), BF16)], axis=0)
    normal_one = normed(lead.astype(F32), gain_one).astype(BF16)
    x_branch = nn(normal_one, proj_x, BF16)
    normal_one = normal_one[:rows]
    y_pre = nn(normal_one, proj_y)
    y_branch, gelu_back = jax.vjp(jax.nn.gelu, y_pre)

    kernel = functools.partial(forward_kernel, steps, quarters)
    full = ((rows, half), False)
    ends = ((4 * SUBS, half), False)
    conv, recur, inject, decay, local, prod, enter, carry = by_heads(
        kernel, heads, head_w, [(x_branch, False), (chan, False), (gates, True)],
        [full] * 6 + [ends, ((SUBS, half), False)],
    )

    def exchanged(carry):
        every = lax.all_gather(carry, AXES, axis=0).reshape(pairs, 2, *carry.shape)
        return lax.dynamic_index_in_dim(every, side, 1, keepdims=False)

    carries = exchanged(carry).reshape(pairs, batch, quarters, half)
    totals = carries[:, :, 0]
    h = jnp.zeros((batch, half), F32)
    for j in range(pairs - 1):
        h = jnp.where(j < pair, totals[j] * h + carries[j, :, 1], h)

    def at_subs(v):
        return jnp.repeat(v, quarters, axis=0)

    def entering(enter, h):
        enter = enter.reshape(2, 2, SUBS, half)
        return enter[0] * at_subs(h)[None] + enter[1]

    def by_steps(v):
        return v.reshape(2, steps, SUBS, half)

    entered = entering(enter, h)
    states = (by_steps(local) + by_steps(prod) * entered[:, None]).reshape(rows, half)
    mixed = (states * y_branch).astype(BF16)

    def over_sides(partial):
        partial = partial.reshape(2, own, width)
        other = lax.dynamic_index_in_dim(partial, 1 - side, 0, keepdims=False).astype(BF16)
        return lax.dynamic_index_in_dim(partial, side, 0, keepdims=False) + swap(other, 1).astype(F32)

    resid = x + over_sides(nn(mixed, out_half))

    def by_span(v):
        size = width // spans
        return jnp.concatenate([cut(v, span ^ j, size, 1) for j in range(spans)], axis=1)

    def span_gather(block):
        pieces = {0: block}
        for m in xs:
            pieces[m] = swap(block, m)
        for n in list(pieces):
            pieces[n ^ core] = swap(pieces[n], core)
        return jnp.concatenate([pieces[m * seqs] for m in range(spans)], axis=1)

    wide = span_gather(mlp_wide.transpose(1, 2, 0).reshape(2 * units, width // spans))
    narrow = span_gather(mlp_narrow.T)

    def token_gather(v):
        blocks = [v] + [swap(v, m) for m in inner]
        others = [swap(b, 1) for b in blocks]
        return jnp.concatenate(blocks, axis=0), jnp.concatenate(others, axis=0)

    c = to_rows(cotangent)
    grads = token_gather(by_span(c))
    c = c.astype(F32)
    normal_two = token_gather(by_span(normed(resid, gain_two).astype(BF16)))

    def activate(values):
        return jax.nn.gelu(values[:, :units]) * values[:, units:]

    hidden, wide_back = [], []
    for part in (0, 1):
        value, back = jax.vjp(activate, nt(normal_two[part], wide))
        hidden.append(value.astype(BF16))
        wide_back.append(back(nt(grads[part], narrow))[0].astype(BF16))

    def token_scatter(far, near):
        near = near.reshape(len(inner) + 1, own, width)
        far = far.reshape(len(inner) + 1, own, width)
        blocks = [near[k] + swap(far[k], 1).astype(F32) for k in range(len(inner) + 1)]
        total = blocks[0]
        for k, m in enumerate(inner):
            total = total + swap(blocks[k + 1].astype(BF16), m).astype(F32)
        return by_span(total)

    normal_two_grad = token_scatter(nn(wide_back[1], wide, BF16), nn(wide_back[0], wide))
    down = token_scatter(nn(hidden[1], narrow, BF16), nn(hidden[0], narrow))
    output = from_rows((resid + down).astype(BF16))

    def span_scatter(left, right):
        size = width // spans
        kept = [j for j in range(spans) if j % 2 == 0]
        given = [j for j in range(spans) if j % 2 == 1]

        def columns(js):
            return jnp.concatenate([right[:, j * size : (j + 1) * size] for j in js], axis=1)

        recv = swap(tn(left, columns(given), BF16), core)
        total = tn(left, columns(kept)) + recv.astype(F32)
        out = total[:, :size]
        for k, m in enumerate(xs):
            out = out + swap(total[:, (k + 1) * size : (k + 2) * size].astype(BF16), m).astype(F32)
        return out

    all_normal = jnp.concatenate(normal_two, axis=0)
    all_grads = jnp.concatenate(grads, axis=0)
    wide_owned = span_scatter(jnp.concatenate(wide_back, axis=0), all_normal)
    wide_owned = wide_owned.reshape(2, units, width // spans).transpose(2, 0, 1)
    narrow_owned = span_scatter(jnp.concatenate(hidden, axis=0), all_grads).T

    resid_part, gain_two_grad = norm_back(resid, gain_two, normal_two_grad)
    resid_grad = c + resid_part
    branch_low = resid_grad.astype(BF16)
    branch_low = in_order(branch_low, swap(branch_low, 1), 0)
    mixed_grad = nt(branch_low, out_half)
    states_grad = mixed_grad * y_branch
    y_grad = gelu_back(mixed_grad * states)[0].astype(BF16)

    kernel = functools.partial(adjoint_kernel, steps, quarters)
    local_adj, after, back_enter, back_carry = by_heads(
        kernel, heads, head_w, [(states_grad, False), (decay, False), (prod, False)],
        [full, full, ends, ((SUBS, half), False)],
    )
    back_carries = exchanged(back_carry).reshape(pairs, batch, quarters, half)[:, :, 0]
    h = jnp.zeros((batch, half), F32)
    for j in range(pairs - 1, 0, -1):
        h = jnp.where(j > pair, totals[j] * h + back_carries[j], h)
    came = entering(back_enter, h)
    kernel = functools.partial(backward_kernel, steps, quarters)
    flat = (2 * SUBS, half)
    dx, spill, gate_grad, small_grad = by_heads(
        kernel, heads, head_w,
        [
            (local_adj, False), (after, False), (states, False), (came.reshape(flat), False),
            (entered.reshape(flat), False), (conv, False), (recur, False), (inject, False), (decay, False),
            (x_branch, False), (chan, False), (gates, True),
        ],
        [full, ((edge * SUBS, half), False), ((half, 2 * head_w), True), ((SUBS, half), False)],
    )
    spill = lax.ppermute(
        spill.reshape(edge, batch, quarters, half)[::-1, :, 0], AXES, [(i, i - 2) for i in range(2, count)]
    )
    spill = jnp.pad(
        spill[:, :, None], ((0, 0), (0, 0), (quarters - 1, 0), (0, 0))
    ).reshape(edge * SUBS, half)
    x_grad = jnp.concatenate([dx[: rows - edge * SUBS], dx[rows - edge * SUBS :] + spill], axis=0).astype(BF16)

    normal_one_grad = over_sides(nt(y_grad, proj_y) + nt(x_grad, proj_x))
    input_part, gain_one_grad = norm_back(x, gain_one, normal_one_grad)
    input_grad = from_rows(resid_grad + input_part)

    def blocks_of(v, masks, wrap):
        size = 2 * share
        return [lax.dynamic_slice_in_dim(v, (me ^ m) // 2 % wrap * size, size, 0) for m in masks]

    def to_columns_owner(v_kept, v_given):
        recv = swap(v_given, core)
        n = len(inner) + 1
        total = (v_kept + recv.astype(F32)).reshape(len(xs) + 1, n, 2 * share, v_kept.shape[1])
        near = total[0]
        for k, m in enumerate(xs):
            near = near + swap(total[k + 1].astype(BF16), m).astype(F32)
        out = near[0]
        for k, m in enumerate(inner):
            out = out + swap(near[k + 1].astype(BF16), m).astype(F32)
        out = out.reshape(2, share, out.shape[1])
        other = lax.dynamic_index_in_dim(out, 1 - side, 0, keepdims=False).astype(BF16)
        return lax.dynamic_index_in_dim(out, side, 0, keepdims=False), swap(other, 1).astype(F32)

    order = [m ^ n for m in (0, *xs) for n in (0, *inner)]
    turned = normal_one.T
    kept = jnp.concatenate(blocks_of(turned, order, pairs), axis=0)
    given = jnp.concatenate(blocks_of(turned, [m ^ core for m in order], pairs), axis=0)
    proj_owned = jnp.concatenate(
        [in_order(*to_columns_owner(nn(kept, g), nn(given, g, BF16)), 1) for g in (x_grad, y_grad)], axis=1
    )

    def to_rows_owner(v_kept, v_given):
        cols = v_kept.shape[1]
        total = (v_kept + swap(v_given, core).astype(F32)).reshape(len(low_order), 2 * share, cols)
        away = cut(total, 1 - upper, cols // 2, 2).astype(BF16)
        near = cut(total, upper, cols // 2, 2) + swap(away, top).astype(F32)
        out = near[0]
        for k, m in enumerate(low_order[1:]):
            out = out + swap(near[k + 1].astype(BF16), m).astype(F32)
        other = swap(out.astype(BF16), top).astype(F32)
        out = in_order(out, other, 1).reshape(2, share, cols)
        gone = lax.dynamic_index_in_dim(out, 1 - side, 0, keepdims=False).astype(BF16)
        here = lax.dynamic_index_in_dim(out, side, 0, keepdims=False)
        return jnp.where(upper == side, here, swap(gone, 1).astype(F32))

    low_order = [m ^ n for m in (0, *[v for v in xs if v < top]) for n in (0, *inner)]
    turned = mixed.T
    kept = jnp.concatenate(blocks_of(turned, low_order, pairs // 2), axis=0)
    given = jnp.concatenate(blocks_of(turned, [m ^ core for m in low_order], pairs // 2), axis=0)
    out_owned = to_rows_owner(nn(kept, branch_low), nn(given, branch_low, BF16))
    by_row = jnp.concatenate([gate_grad, small_grad.T, jnp.zeros((half, head_w - SUBS), F32)], axis=1)
    kept = jnp.concatenate(blocks_of(by_row, low_order, pairs // 2), axis=0)
    given = jnp.concatenate(blocks_of(by_row, [m ^ core for m in low_order], pairs // 2), axis=0).astype(BF16)
    rest = to_rows_owner(kept, given)
    gate_owned, small_owned = rest[:, : 2 * head_w], rest[:, 2 * head_w : 2 * head_w + SUBS]

    gains = jnp.pad(jnp.stack([gain_one_grad, gain_two_grad], axis=1), ((0, 0), (0, 126)))
    kept = jnp.concatenate(blocks_of(gains, order, pairs), axis=0)
    given = jnp.concatenate(blocks_of(gains, [m ^ core for m in order], pairs), axis=0)
    gains = sum(to_columns_owner(kept, given))

    return (
        output,
        input_grad,
        gains[:, 0],
        proj_owned,
        small_owned[:, :CONV],
        small_owned[:, 4],
        gate_owned,
        small_owned[:, 5:7],
        small_owned[:, 7] * jax.nn.sigmoid(decay_param.astype(F32)),
        out_owned,
        gains[:, 1],
        wide_owned,
        narrow_owned,
    )


def solution(mesh):
    both = ("span", "seq")
    tokens = P(None, both, None)
    placed = (
        tokens, P(both), P(both, None), P(both, None), P(both), P(both, None), P(both, None), P(both), P(both, None),
        P(both), P("span", None, "seq"), P("span", "seq"), tokens,
    )
    given = (
        tokens, tokens, P(both), P(both, None), P(both, None), P(both), P(both, None), P(both, None), P(both),
        P(both, None), P(both), P("span", None, "seq"), P("span", "seq"),
    )
    return jax.shard_map(on_device, mesh=mesh, in_specs=placed, out_specs=given, check_vma=False)
```

```python
import functools

import jax
import jax.numpy as jnp
from jax import lax
from jax.experimental import pallas as pl
from jax.experimental.pallas import tpu as pltpu
from jax.sharding import PartitionSpec as P

CONV = 4
EPS = 1e-06
AXES = ("span", "seq")
F32 = jnp.float32
BF16 = jnp.bfloat16
SUBS = 8


def swap(value, mask):
    count = lax.axis_size("span") * lax.axis_size("seq")
    return lax.ppermute(value, AXES, [(i, i ^ mask) for i in range(count)])


def dot(a, b, dims, out=F32):
    return lax.dot_general(a, b, ((dims[0], dims[1]), ((), ())), preferred_element_type=F32).astype(out)


def nn(a, b, out=F32):
    return dot(a, b, ((1,), (0,)), out)


def nt(a, b, out=F32):
    return dot(a, b, ((1,), (1,)), out)


def tn(a, b, out=F32):
    return dot(a, b, ((0,), (0,)), out)


def normed(v, gain):
    return v * lax.rsqrt(jnp.mean(v * v, axis=-1, keepdims=True) + EPS) * gain


def norm_back(v, gain, grad):
    scale = lax.rsqrt(jnp.mean(v * v, axis=-1, keepdims=True) + EPS)
    z = v * scale
    e = grad * gain
    return scale * (e - z * jnp.mean(e * z, axis=-1, keepdims=True)), jnp.sum(grad * z, axis=0)


def one_less_exp(u):
    series = 1.0 + u / 7.0
    for n in (6.0, 5.0, 4.0, 3.0, 2.0):
        series = 1.0 + u / n * series
    return jnp.where(u > -0.25, -u * series, 1.0 - jnp.exp(u))


def roll(v, by):
    return pltpu.roll(v, by % SUBS, 0)


def quarter_of(shape, quarters):
    return lax.broadcasted_iota(jnp.int32, shape, 0) % quarters


def spread(v, quarters, at):
    q = quarter_of(v.shape, quarters)
    held = jnp.where(q == at, v, 0.0)
    total = held
    for k in range(1, quarters):
        total = total + roll(held, k if at == 0 else -k)
    return total


def scan_carries(prods, sums, quarters, backward):
    q = quarter_of(prods[0].shape, quarters)
    sign = -1 if backward else 1
    order = (1, 0) if backward else (0, 1)
    place = quarters - 1 - q if backward else q
    whole = None
    enter = [None, None]
    for b in order:
        p, s = prods[b], sums[b]
        d = 1
        while d < quarters:
            pp, ss = roll(p, sign * d), roll(s, sign * d)
            ok = place >= d
            s = jnp.where(ok, p * ss + s, s)
            p = jnp.where(ok, p * pp, p)
            d *= 2
        first = place == 0
        ep = jnp.where(first, 1.0, roll(p, sign))
        es = jnp.where(first, 0.0, roll(s, sign))
        last = 0 if backward else quarters - 1
        tp, ts = spread(p, quarters, last), spread(s, quarters, last)
        if whole is None:
            enter[b] = (ep, es)
            whole = (tp, ts)
        else:
            enter[b] = (ep * whole[0], ep * whole[1] + es)
            whole = (tp * whole[0], tp * whole[1] + ts)
    return enter, whole


def earlier_rows(groups, halo, quarters, steps):
    q = quarter_of(groups[0].shape[1:], quarters)
    edge = CONV - 1
    out = []
    for b in (0, 1):
        ahead = []
        for k in range(edge, 0, -1):
            same = roll(groups[b][steps - k], 1)
            before = halo[k - 1] if b == 0 else roll(groups[0][steps - k], 1 - quarters)
            ahead.append(jnp.where(q == 0, before, same)[None])
        out.append(jnp.concatenate([*ahead, groups[b]], axis=0))
    return out


def forward_kernel(steps, quarters, xb, chan, gate, conv_o, recur_o, inject_o, decay_o, local_o, prod_o, enter_o, carry_o):
    rows = 2 * steps * SUBS
    width = xb.shape[1]
    head = xb[...].astype(F32)
    groups = [head[b * steps * SUBS : (b + 1) * steps * SUBS].reshape(steps, SUBS, width) for b in (0, 1)]
    halo = [head[rows + k * SUBS : rows + (k + 1) * SUBS] for k in range(CONV - 1)]
    edge = CONV - 1
    convs = []
    for ext in earlier_rows(groups, halo, quarters, steps):
        total = jnp.broadcast_to(chan[4:5][None], (steps, SUBS, width))
        for k in range(CONV):
            total = total + chan[k : k + 1][None] * ext[edge - k : edge - k + steps]
        convs.append(total.reshape(steps * SUBS, width))
    conv = jnp.concatenate(convs, axis=0)
    pre = jnp.dot(conv.astype(BF16), gate[...], preferred_element_type=F32)
    recur = jax.nn.sigmoid(pre[:, :width] + chan[5:6])
    inject = jax.nn.sigmoid(pre[:, width:] + chan[6:7])
    log_decay = -8.0 * recur * chan[7:8]
    decay = jnp.exp(log_decay)
    driven = jnp.sqrt(one_less_exp(2.0 * log_decay)) * inject * conv
    conv_o[...] = conv
    recur_o[...] = recur
    inject_o[...] = inject
    decay_o[...] = decay
    prods, sums = [], []
    for b in (0, 1):
        h = p = None
        for t in range(steps):
            at = (b * steps + t) * SUBS
            d, u = decay[at : at + SUBS], driven[at : at + SUBS]
            h = u if h is None else d * h + u
            p = d if p is None else d * p
            local_o[at : at + SUBS] = h
            prod_o[at : at + SUBS] = p
        prods.append(p)
        sums.append(h)
    enter, whole = scan_carries(prods, sums, quarters, False)
    for b in (0, 1):
        enter_o[b * SUBS : (b + 1) * SUBS] = enter[b][0]
        enter_o[(2 + b) * SUBS : (3 + b) * SUBS] = enter[b][1]
    q = quarter_of(whole[0].shape, quarters)
    carry_o[...] = jnp.where(q == 0, whole[0], whole[1])


def adjoint_kernel(steps, quarters, grad, decay, prod, local_o, after_o, enter_o, carry_o):
    prods, sums = [], []
    for b in (0, 1):
        g = r = None
        for t in range(steps - 1, -1, -1):
            at = (b * steps + t) * SUBS
            rows = slice(at, at + SUBS)
            a = grad[rows] if g is None else grad[rows] + g
            r = jnp.ones_like(a) if r is None else r * decay[at + SUBS : at + 2 * SUBS]
            local_o[rows] = a
            after_o[rows] = r
            g = decay[rows] * a
        last = ((b + 1) * steps - 1) * SUBS
        prods.append(prod[last : last + SUBS])
        sums.append(g)
    enter, whole = scan_carries(prods, sums, quarters, True)
    for b in (0, 1):
        enter_o[b * SUBS : (b + 1) * SUBS] = enter[b][0]
        enter_o[(2 + b) * SUBS : (3 + b) * SUBS] = enter[b][1]
    carry_o[...] = whole[1]


def backward_kernel(
    steps, quarters, local, after, states, came, entered, conv_r, recur_r, inject_r, decay_r, xb, chan, gate,
    dx_o, spill_o, gate_o, small_o,
):
    rows = 2 * steps * SUBS
    width = xb.shape[1]
    edge = CONV - 1
    block = steps * SUBS

    def by_step(v):
        return [v[b * block : (b + 1) * block].reshape(steps, SUBS, width) for b in (0, 1)]

    adjoint = jnp.concatenate(
        [
            (l + a * came[b * SUBS : (b + 1) * SUBS][None]).reshape(block, width)
            for b, (l, a) in enumerate(zip(by_step(local[...]), by_step(after[...])))
        ],
        axis=0,
    )
    earlier = jnp.concatenate(
        [
            jnp.concatenate([entered[b * SUBS : (b + 1) * SUBS], states[b * block : (b + 1) * block - SUBS]], axis=0)
            for b in (0, 1)
        ],
        axis=0,
    )
    conv, recur, inject, decay = conv_r[...], recur_r[...], inject_r[...], decay_r[...]
    rate = chan[7:8]
    mult = jnp.sqrt(one_less_exp(-16.0 * recur * rate))
    d_decay = adjoint * earlier
    d_log = d_decay * decay - adjoint * inject * conv * (decay * decay / mult)
    d_inject = adjoint * mult * conv
    d_conv = adjoint * mult * inject
    d_rate = jnp.sum(d_log * (-8.0 * recur), axis=0, keepdims=True)
    d_recur = d_log * (-8.0 * rate) * recur * (1.0 - recur)
    d_inject = d_inject * inject * (1.0 - inject)
    low = jnp.concatenate([d_recur.astype(BF16), d_inject.astype(BF16)], axis=1)
    d_conv = d_conv + lax.dot_general(low, gate[...], (((1,), (1,)), ((), ())), preferred_element_type=F32)
    gate_o[...] = lax.dot_general(conv.astype(BF16), low, (((0,), (0,)), ((), ())), preferred_element_type=F32)
    head = xb[...].astype(F32)
    halo = [head[rows + k * SUBS : rows + (k + 1) * SUBS] for k in range(edge)]
    exts = earlier_rows(by_step(head), halo, quarters, steps)
    groups = by_step(d_conv)
    for k in range(CONV):
        taps = sum(
            jnp.sum(groups[b] * exts[b][edge - k : edge - k + steps], axis=(0, 1), keepdims=True)[0] for b in (0, 1)
        )
        small_o[k : k + 1] = taps
    small_o[4:5] = jnp.sum(d_conv, axis=0, keepdims=True)
    small_o[5:6] = jnp.sum(d_recur, axis=0, keepdims=True)
    small_o[6:7] = jnp.sum(d_inject, axis=0, keepdims=True)
    small_o[7:8] = d_rate
    q = quarter_of((SUBS, width), quarters)
    for b in (0, 1):
        beyond = []
        for j in range(edge):
            same = roll(groups[b][j], -1)
            later = roll(groups[1][j], quarters - 1) if b == 0 else jnp.zeros_like(same)
            beyond.append(jnp.where(q == quarters - 1, later, same)[None])
        ext = jnp.concatenate([groups[b], *beyond], axis=0)
        total = chan[0:1][None] * ext[:steps]
        for k in range(1, CONV):
            total = total + chan[k : k + 1][None] * ext[k : k + steps]
        dx_o[b * block : (b + 1) * block] = total.reshape(block, width)
    for j in range(1, CONV):
        total = jnp.zeros((SUBS, width), F32)
        for k in range(j, CONV):
            total = total + chan[k : k + 1] * groups[0][k - j]
        spill_o[(j - 1) * SUBS : j * SUBS] = total


def by_heads(kernel, heads, head_w, arrays, outs):
    def spec(shape, tall):
        if tall:
            return pl.BlockSpec((head_w, shape[1]), lambda h: (h, 0))
        return pl.BlockSpec((shape[0], head_w), lambda h: (0, h))

    return pl.pallas_call(
        kernel,
        grid=(heads,),
        in_specs=[spec(a.shape, tall) for a, tall in arrays],
        out_specs=[spec(s, tall) for s, tall in outs],
        out_shape=[jax.ShapeDtypeStruct(s, F32) for s, _ in outs],
        compiler_params=pltpu.CompilerParams(vmem_limit_bytes=48 * 1024 * 1024),
    )(*[a for a, _ in arrays])


MESH = pl.DeviceIdType.MESH
VMEM_LIMIT = 60 * 1024 * 1024


class Links:
    def __init__(self, sizes, sends, recvs):
        self.spans, self.seqs = sizes
        self.span, self.seq = lax.axis_index("span"), lax.axis_index("seq")
        self.sends, self.recvs = sends, recvs
        self.used = 0
        self.open = []

    def flipped(self, index, mask):
        bit = 1
        while bit <= mask:
            if mask & bit:
                index = index + (1 - 2 * (index // bit % 2)) * bit
            bit *= 2
        return index

    def peer(self, mask):
        low, high = mask % self.seqs, mask // self.seqs
        return (self.flipped(self.span, high), self.flipped(self.seq, low))

    def other(self, mask):
        span, seq = self.peer(mask)
        return span * self.seqs + seq

    def greet(self, masks):
        barrier = pltpu.get_barrier_semaphore()
        for mask in masks:
            pl.semaphore_signal(barrier, inc=1, device_id=self.peer(mask), device_id_type=MESH)
        pl.semaphore_wait(barrier, len(masks))

    def send(self, source, target, mask, only=None):
        slot = self.used
        self.used += 1
        copy = pltpu.make_async_remote_copy(
            source, target, self.sends.at[slot], self.recvs.at[slot], device_id=self.peer(mask), device_id_type=MESH
        )
        if only is None:
            copy.start()
        else:
            pl.when(only)(copy.start)
        self.open.append((copy, only))
        return copy

    def close(self):
        for copy, only in self.open:
            if only is None:
                copy.wait_send()
            else:
                pl.when(only)(copy.wait_send)


def in_turn(parts, order):
    for name in order:
        next(parts[name], None)
    for part in parts.values():
        for _ in part:
            pass


def gather_kernel(
    sizes, share, half, rec_proj, out_proj, gate_weight, small, tokens, wide, narrow,
    proj_x, proj_y, out_half, gates, every, tokens_o, wide_o, narrow_o, sends, recvs, locals_,
):
    links = Links(sizes, sends, recvs)
    spans, seqs = sizes
    count = spans * seqs
    me = links.span * seqs + links.seq
    side = me % 2
    upper = me // (count // 2)
    inner = [2 * k for k in range(1, seqs // 2)]
    core, top = seqs, count // 2
    double = 2 * share
    links.greet([1, *inner, core, top])
    kept = [0]

    def local(source, target, only=None):
        copy = pltpu.make_async_copy(source, target, locals_.at[kept[0]])
        kept[0] += 1
        if only is None:
            copy.start()
        else:
            pl.when(only)(copy.start)
        return copy

    def pieces_out(place, piece):
        over_inner = {m: links.send(piece(place(me)), piece(place(me)), m) for m in inner}
        over_top = {0: links.send(piece(place(me)), piece(place(me)), top)}
        over_core = [links.send(piece(place(me)), piece(place(me)), core)]
        yield
        for m in inner:
            over_inner[m].wait_recv()
            there = piece(place(links.other(m)))
            over_top[m] = links.send(there, there, top)
            over_core.append(links.send(there, there, core))
        yield
        for m in (0, *inner):
            over_top[m].wait_recv()
            there = piece(place(links.other(top + m)))
            over_core.append(links.send(there, there, core))
        yield
        for copy in over_core:
            copy.wait_recv()

    def columns_part(source, first, target):
        def piece(start):
            return target.at[pl.ds(pl.multiple_of(start, 16), double)]

        def columns(which):
            return source.at[:, pl.ds(pl.multiple_of(first + which * half, 128), half)]

        row = target.at[pl.ds(pl.multiple_of(me * share, 16), share)]
        mine = local(columns(side), row)
        theirs = links.send(columns(1 - side), row, 1)
        yield
        mine.wait()
        theirs.wait_recv()
        yield from pieces_out(lambda d: d // 2 * double, piece)

    def whole_part(source, target):
        height = source.shape[0]

        def piece(start):
            return target.at[pl.ds(pl.multiple_of(start, 16), 2 * height)]

        row = target.at[pl.ds(pl.multiple_of(me * height, 16), height)]
        mine = local(source, row)
        theirs = links.send(source, row, 1)
        yield
        mine.wait()
        theirs.wait_recv()
        yield from pieces_out(lambda d: d // 2 * 2 * height, piece)

    def rows_part(source, target):
        width = source.shape[1]
        pairs_half = count // 4

        def place(d):
            return d // 2 % pairs_half * double

        def rows(start, size):
            return target.at[pl.ds(pl.multiple_of(start, 16), size)]

        def piece(start, which):
            return target.at[pl.ds(pl.multiple_of(start, 16), double), pl.ds(pl.multiple_of(which * (width // 2), 128), width // 2)]

        holds = side == upper
        row = rows(place(me) + side * share, share)
        mine = local(source, row, holds)
        gift = links.send(source, row, 1, side != upper)
        yield

        @pl.when(holds)
        def _():
            mine.wait()
            gift.wait_recv()

        across = links.send(rows(place(me), double), rows(place(me), double), top, holds)
        pl.when(side != upper)(across.wait_recv)
        over_inner = {m: links.send(piece(place(me), upper), piece(place(me), upper), m) for m in inner}
        over_core = [links.send(rows(place(me), double), rows(place(me), double), core)]
        over_top = {}
        yield
        for m in inner:
            over_inner[m].wait_recv()
            there = piece(place(links.other(m)), upper)
            over_top[m] = links.send(there, there, top)
            over_core.append(links.send(there, there, core))
        yield
        for m in inner:
            over_top[m].wait_recv()
            there = piece(place(links.other(m)), 1 - upper)
            over_core.append(links.send(there, there, core))
        yield
        for copy in over_core:
            copy.wait_recv()

    parts = {
        "x": columns_part(rec_proj, 0, proj_x),
        "s": whole_part(small, every),
        "g": rows_part(gate_weight, gates),
        "y": columns_part(rec_proj, 2 * half, proj_y),
        "o": rows_part(out_proj, out_half),
    }
    in_turn(parts, "xsgxsgyoxyxogsygsygoyo")
    links.close()


def gather_weights(sizes, rec_proj, out_proj, gate_weight, small, tokens, wide, narrow):
    share = rec_proj.shape[0]
    half = rec_proj.shape[1] // 4
    count = sizes[0] * sizes[1]
    held = [
        (count * share, half), (count * share, half), (count // 2 * share, out_proj.shape[1]),
        (count // 2 * share, gate_weight.shape[1]), (count * small.shape[0], small.shape[1]),
        tokens.shape, wide.shape, narrow.shape,
    ]
    anywhere = pl.BlockSpec(memory_space=pl.ANY)
    copies = 5 * 16
    return pl.pallas_call(
        functools.partial(gather_kernel, sizes, share, half),
        in_specs=[anywhere] * 7,
        out_specs=[anywhere] * 8,
        out_shape=[jax.ShapeDtypeStruct(s, BF16) for s in held],
        scratch_shapes=[
            pltpu.SemaphoreType.DMA((copies,)), pltpu.SemaphoreType.DMA((copies,)), pltpu.SemaphoreType.DMA((8,))
        ],
        input_output_aliases={4: 5, 5: 6, 6: 7},
        compiler_params=pltpu.CompilerParams(collective_id=0, has_side_effects=True, vmem_limit_bytes=VMEM_LIMIT),
    )(rec_proj, out_proj, gate_weight, small, tokens, wide, narrow)


def scatter_kernel(
    sizes, share, kept_d, given_d, kept_m, given_m, grad_x, grad_y, branch, kept_g, given_g, kept_n, given_n,
    proj_o, out_o, gate_o, gain_o, sends, recvs, *bufs,
):
    links = Links(sizes, sends, recvs)
    spans, seqs = sizes
    count = spans * seqs
    me = links.span * seqs + links.seq
    side = me % 2
    upper = me // (count // 2)
    inner = [2 * k for k in range(1, seqs // 2)]
    core, top = seqs, count // 2
    double = 2 * share
    n = len(inner) + 1
    links.greet([1, *inner, core, top])

    def part(kept, given, cols, scratch, finish):
        to_core, from_core, to_top, from_top, to_inner, from_inner, to_side, from_side = scratch
        crossing = []
        for i in range(2):
            for j in range(n):
                to_core[i * n + j] = given((1 - i) * n + j).astype(BF16)
            crossing.append(links.send(to_core.at[pl.ds(i * n, n)], from_core.at[pl.ds(i * n, n)], core))
        yield
        crossing[0].wait_recv()
        over_top = {}
        for j in (*range(1, n), 0):
            to_top[j] = (kept(n + j) + from_core[j].astype(F32)).astype(BF16)
            over_top[j] = links.send(to_top.at[j], from_top.at[j], top)
        crossing[1].wait_recv()
        yield
        over_inner = []
        for j in range(1, n):
            over_top[j].wait_recv()
            to_inner[j - 1] = (kept(j) + from_core[n + j].astype(F32) + from_top[j].astype(F32)).astype(BF16)
            over_inner.append(links.send(to_inner.at[j - 1], from_inner.at[j - 1], inner[j - 1]))
        over_top[0].wait_recv()
        yield
        total = kept(0) + from_core[n].astype(F32) + from_top[0].astype(F32)
        for j in range(1, n):
            over_inner[j - 1].wait_recv()
            total = total + from_inner[j - 1].astype(F32)
        yield from finish(total, to_side, from_side)

    def sided(total):
        low, high = total[:share], total[share:]
        first = side == 0
        return jnp.where(first, low, high), jnp.where(first, high, low)

    def by_columns(put):
        def finish(total, to_side, from_side):
            mine, theirs = sided(total)
            to_side[...] = theirs.astype(BF16)
            copy = links.send(to_side, from_side, 1)
            yield
            copy.wait_recv()
            put(mine, from_side[...].astype(F32))

        return finish

    def into(first, cols):
        def put(mine, recv):
            proj_o[:, first : first + cols] = jnp.where(side == 0, mine, recv)
            proj_o[:, first + cols : first + 2 * cols] = jnp.where(side == 0, recv, mine)

        return put

    def put_gain(mine, recv):
        gain_o[...] = mine + recv

    def by_rows(target, to_last, from_last):
        cols = target.shape[1] // 2

        def finish(total, to_side, from_side):
            to_side[...] = total.astype(BF16)
            copy = links.send(to_side, from_side, top)
            yield
            copy.wait_recv()
            other = from_side[...].astype(F32)
            first = side == 0
            (low, low_far), (high, high_far) = sided(jnp.where(first, total, other)), sided(jnp.where(first, other, total))
            to_last[:, :cols] = low_far.astype(BF16)
            to_last[:, cols:] = high_far.astype(BF16)
            copy = links.send(to_last, from_last, 1)
            yield
            copy.wait_recv()
            holds = side == upper
            target[:, :cols] = jnp.where(holds, low, from_last[:, :cols].astype(F32))
            target[:, cols:] = jnp.where(holds, high, from_last[:, cols:].astype(F32))

        return finish

    def product(lhs, rhs, wrap, columns=None):
        def block(j):
            rows = lhs[j % wrap * double : (j % wrap + 1) * double]
            if columns is None:
                return jnp.dot(rows, rhs[...], preferred_element_type=F32)
            which = upper if j < n else 1 - upper
            right = rhs[:, pl.ds(pl.multiple_of(which * columns, 128), columns)]
            return jnp.dot(rows, right, preferred_element_type=F32)

        return block

    def stored(blocks, columns=None):
        def block(j):
            if columns is None:
                return blocks[j * double : (j + 1) * double].astype(F32)
            which = upper if j < n else 1 - upper
            return blocks[j % n * double : (j % n + 1) * double, pl.ds(pl.multiple_of(which * columns, 128), columns)].astype(F32)

        return block

    half = grad_x.shape[1]
    wide = branch.shape[1] // 2
    thin = kept_g.shape[1] // 2
    parts = {
        "y": part(product(kept_d, grad_y, 2 * n), product(given_d, grad_y, 2 * n), half, bufs[0:8], by_columns(into(2 * half, half))),
        "o": part(product(kept_m, branch, n, wide), product(given_m, branch, n, wide), wide, bufs[8:16], by_rows(out_o, *bufs[16:18])),
        "x": part(product(kept_d, grad_x, 2 * n), product(given_d, grad_x, 2 * n), half, bufs[18:26], by_columns(into(0, half))),
        "g": part(stored(kept_g, thin), stored(given_g, thin), thin, bufs[26:34], by_rows(gate_o, *bufs[34:36])),
        "n": part(stored(kept_n), stored(given_n), kept_n.shape[1], bufs[36:44], by_columns(put_gain)),
    }
    in_turn(parts, "yxoyxoyxgnoyxgnoygnoxoygnoxgngg")
    links.close()


def scatter_grads(sizes, kept_d, given_d, kept_m, given_m, grad_x, grad_y, branch, kept_g, given_g, kept_n, given_n):
    n = sizes[1] // 2
    share = kept_d.shape[0] // (4 * n)
    half, wide, thin, gain = grad_x.shape[1], branch.shape[1], kept_g.shape[1], kept_n.shape[1]

    def scratch(cols, last):
        double = 2 * share
        side = share if last is None else double
        shapes = [(2 * n, double, cols)] * 2 + [(n, double, cols)] * 2 + [(n - 1, double, cols)] * 2 + [(side, cols)] * 2
        if last is not None:
            shapes += [(share, last)] * 2
        return [pltpu.VMEM(s, BF16) for s in shapes]

    bufs = [*scratch(half, None), *scratch(wide // 2, wide), *scratch(half, None), *scratch(thin // 2, thin), *scratch(gain, None)]
    copies = 5 * (2 + n + (n - 1) + 2)
    inside = pl.BlockSpec(memory_space=pltpu.VMEM)
    return pl.pallas_call(
        functools.partial(scatter_kernel, sizes, share),
        in_specs=[inside] * 11,
        out_specs=[inside] * 4,
        out_shape=[jax.ShapeDtypeStruct((share, cols), F32) for cols in (4 * half, wide, thin, gain)],
        scratch_shapes=[pltpu.SemaphoreType.DMA((copies,)), pltpu.SemaphoreType.DMA((copies,)), *bufs],
        compiler_params=pltpu.CompilerParams(collective_id=1, has_side_effects=True, vmem_limit_bytes=VMEM_LIMIT),
    )(kept_d, given_d, kept_m, given_m, grad_x, grad_y, branch, kept_g, given_g, kept_n, given_n)


def on_device(
    inputs, norm_one, rec_proj, conv_weight, conv_bias, gate_weight, gate_bias, decay_param, out_proj, norm_two,
    mlp_wide, mlp_narrow, cotangent,
):
    spans, seqs = lax.axis_size("span"), lax.axis_size("seq")
    count = spans * seqs
    span, seq = lax.axis_index("span"), lax.axis_index("seq")
    me = span * seqs + seq
    side = me % 2
    pair = me // 2
    pairs = count // 2
    batch, tokens, width = inputs.shape
    half = width // 2
    quarters = SUBS // batch
    steps = tokens // quarters
    own = batch * tokens
    rows = 2 * own
    head_w = gate_weight.shape[1] // 2
    heads = half // head_w
    edge = CONV - 1
    share = width // count
    units = mlp_narrow.shape[1]
    inner = [2 * k for k in range(1, seqs // 2)]
    core = seqs
    xs = [2 * seqs * k for k in range(1, spans // 2)]
    top = count // 2
    upper = me // top

    def to_rows(v):
        return v.reshape(batch, quarters, steps, width).transpose(2, 0, 1, 3).reshape(own, width)

    def from_rows(v):
        return v.reshape(steps, batch, quarters, width).transpose(1, 2, 0, 3).reshape(batch, tokens, width)

    def in_order(mine, other, axis):
        return jnp.concatenate([jnp.where(side == 0, mine, other), jnp.where(side == 0, other, mine)], axis=axis)

    def cut(v, index, size, axis):
        return lax.dynamic_slice_in_dim(v, index * size, size, axis)

    direct = share % 16 == 0 and spans == 4

    def gathered_rows(block, buffer, place):
        pieces = {0: block}
        for m in inner:
            pieces[m] = swap(block, m)
        for m in xs:
            for n in (0, *inner):
                pieces[m ^ n] = swap(pieces[n], m)
        for n in list(pieces):
            pieces[core ^ n] = swap(pieces[n], core)
        for m, piece in pieces.items():
            buffer = lax.dynamic_update_slice_in_dim(buffer, piece, place(me ^ m), 0)
        return buffer

    def columns_half(block):
        mine, theirs = cut(block, side, half, 1), cut(block, 1 - side, half, 1)
        block = in_order(mine, swap(theirs, 1), 0)
        return gathered_rows(block, jnp.zeros((width, half), BF16), lambda d: d // 2 * 2 * share)

    def rows_half(block):
        full = lax.all_gather(block, AXES, axis=0, tiled=True)
        return cut(full, side, half, 0)

    def by_span(v):
        size = width // spans
        return jnp.concatenate([cut(v, span ^ j, size, 1) for j in range(spans)], axis=1)

    small = jnp.stack([norm_one, norm_two, *conv_weight.T, conv_bias, *gate_bias.T, decay_param])
    wide_own = mlp_wide.transpose(1, 2, 0).reshape(2 * units, width // spans)
    narrow_own = mlp_narrow.T
    grads_own = by_span(to_rows(cotangent))
    if direct:
        packed = jnp.pad(small, ((0, 6), (0, -share % 128)))
        proj_x, proj_y, out_half, gates, small, grads_own, wide_own, narrow_own = gather_weights(
            (spans, seqs), rec_proj, out_proj, gate_weight, packed, grads_own, wide_own, narrow_own
        )
        small = small.reshape(count, 16, -1)[:, :10, :share].transpose(1, 0, 2).reshape(10, width)
    else:
        proj_x = columns_half(rec_proj[:, :width])
        proj_y = columns_half(rec_proj[:, width:])
        gates = rows_half(gate_weight)
        out_half = rows_half(out_proj)
        small = lax.all_gather(small, AXES, axis=1, tiled=True)
    small = small.astype(F32)
    gain_one, gain_two = small[0], small[1]
    chan = cut(jnp.concatenate([small[2:9], jax.nn.softplus(small[9:10])], axis=0), side, half, 1)

    mine = to_rows(inputs)
    x = mine.astype(F32)
    tail = inputs[:, tokens - edge :]
    halo = lax.ppermute(tail, AXES, [(i, i + 1) for i in range(1, count - 1, 2)]) + lax.ppermute(
        tail, AXES, [(i, i + 2) for i in range(1, count - 2, 2)]
    )
    halo = jnp.zeros((edge, batch, quarters, width), BF16).at[:, :, 0].set(halo[:, ::-1].transpose(1, 0, 2))
    both = in_order(mine, swap(mine, 1), 0)
    lead = jnp.concatenate([both, halo.reshape(edge * SUBS, width), jnp.zeros((8, width), BF16)], axis=0)
    normal_one = normed(lead.astype(F32), gain_one).astype(BF16)
    x_branch = nn(normal_one, proj_x, BF16)
    normal_one = normal_one[:rows]
    y_pre = nn(normal_one, proj_y)
    y_branch, gelu_back = jax.vjp(jax.nn.gelu, y_pre)

    kernel = functools.partial(forward_kernel, steps, quarters)
    full = ((rows, half), False)
    ends = ((4 * SUBS, half), False)
    conv, recur, inject, decay, local, prod, enter, carry = by_heads(
        kernel, heads, head_w, [(x_branch, False), (chan, False), (gates, True)],
        [full] * 6 + [ends, ((SUBS, half), False)],
    )

    def exchanged(carry):
        every = lax.all_gather(carry, AXES, axis=0).reshape(pairs, 2, *carry.shape)
        return lax.dynamic_index_in_dim(every, side, 1, keepdims=False)

    carries = exchanged(carry).reshape(pairs, batch, quarters, half)
    totals = carries[:, :, 0]
    h = jnp.zeros((batch, half), F32)
    for j in range(pairs - 1):
        h = jnp.where(j < pair, totals[j] * h + carries[j, :, 1], h)

    def at_subs(v):
        return jnp.repeat(v, quarters, axis=0)

    def entering(enter, h):
        enter = enter.reshape(2, 2, SUBS, half)
        return enter[0] * at_subs(h)[None] + enter[1]

    def by_steps(v):
        return v.reshape(2, steps, SUBS, half)

    entered = entering(enter, h)
    states = (by_steps(local) + by_steps(prod) * entered[:, None]).reshape(rows, half)
    mixed = (states * y_branch).astype(BF16)

    def over_sides(partial):
        partial = partial.reshape(2, own, width)
        other = lax.dynamic_index_in_dim(partial, 1 - side, 0, keepdims=False).astype(BF16)
        return lax.dynamic_index_in_dim(partial, side, 0, keepdims=False) + swap(other, 1).astype(F32)

    resid = x + over_sides(nn(mixed, out_half))

    def span_gather(block):
        pieces = {0: block}
        for m in xs:
            pieces[m] = swap(block, m)
        for n in list(pieces):
            pieces[n ^ core] = swap(pieces[n], core)
        return jnp.concatenate([pieces[m * seqs] for m in range(spans)], axis=1)

    wide = span_gather(wide_own)
    narrow = span_gather(narrow_own)

    def token_gather(v):
        blocks = [v] + [swap(v, m) for m in inner]
        others = [swap(b, 1) for b in blocks]
        return jnp.concatenate(blocks, axis=0), jnp.concatenate(others, axis=0)

    grads = token_gather(grads_own)
    c = to_rows(cotangent).astype(F32)
    normal_two = token_gather(by_span(normed(resid, gain_two).astype(BF16)))

    def activate(values):
        return jax.nn.gelu(values[:, :units]) * values[:, units:]

    hidden, wide_back = [], []
    for part in (0, 1):
        value, back = jax.vjp(activate, nt(normal_two[part], wide))
        hidden.append(value.astype(BF16))
        wide_back.append(back(nt(grads[part], narrow))[0].astype(BF16))

    def token_scatter(far, near):
        near = near.reshape(len(inner) + 1, own, width)
        far = far.reshape(len(inner) + 1, own, width)
        blocks = [near[k] + swap(far[k], 1).astype(F32) for k in range(len(inner) + 1)]
        total = blocks[0]
        for k, m in enumerate(inner):
            total = total + swap(blocks[k + 1].astype(BF16), m).astype(F32)
        return by_span(total)

    normal_two_grad = token_scatter(nn(wide_back[1], wide, BF16), nn(wide_back[0], wide))
    down = token_scatter(nn(hidden[1], narrow, BF16), nn(hidden[0], narrow))
    output = from_rows((resid + down).astype(BF16))

    def span_scatter(left, right):
        size = width // spans
        kept = [j for j in range(spans) if j % 2 == 0]
        given = [j for j in range(spans) if j % 2 == 1]

        def columns(js):
            return jnp.concatenate([right[:, j * size : (j + 1) * size] for j in js], axis=1)

        recv = swap(tn(left, columns(given), BF16), core)
        total = tn(left, columns(kept)) + recv.astype(F32)
        out = total[:, :size]
        for k, m in enumerate(xs):
            out = out + swap(total[:, (k + 1) * size : (k + 2) * size].astype(BF16), m).astype(F32)
        return out

    all_normal = jnp.concatenate(normal_two, axis=0)
    all_grads = jnp.concatenate(grads, axis=0)
    wide_owned = span_scatter(jnp.concatenate(wide_back, axis=0), all_normal)
    wide_owned = wide_owned.reshape(2, units, width // spans).transpose(2, 0, 1)
    narrow_owned = span_scatter(jnp.concatenate(hidden, axis=0), all_grads).T

    resid_part, gain_two_grad = norm_back(resid, gain_two, normal_two_grad)
    resid_grad = c + resid_part
    branch_low = resid_grad.astype(BF16)
    branch_low = in_order(branch_low, swap(branch_low, 1), 0)
    mixed_grad = nt(branch_low, out_half)
    states_grad = mixed_grad * y_branch
    y_grad = gelu_back(mixed_grad * states)[0].astype(BF16)

    kernel = functools.partial(adjoint_kernel, steps, quarters)
    local_adj, after, back_enter, back_carry = by_heads(
        kernel, heads, head_w, [(states_grad, False), (decay, False), (prod, False)],
        [full, full, ends, ((SUBS, half), False)],
    )
    back_carries = exchanged(back_carry).reshape(pairs, batch, quarters, half)[:, :, 0]
    h = jnp.zeros((batch, half), F32)
    for j in range(pairs - 1, 0, -1):
        h = jnp.where(j > pair, totals[j] * h + back_carries[j], h)
    came = entering(back_enter, h)
    kernel = functools.partial(backward_kernel, steps, quarters)
    flat = (2 * SUBS, half)
    dx, spill, gate_grad, small_grad = by_heads(
        kernel, heads, head_w,
        [
            (local_adj, False), (after, False), (states, False), (came.reshape(flat), False),
            (entered.reshape(flat), False), (conv, False), (recur, False), (inject, False), (decay, False),
            (x_branch, False), (chan, False), (gates, True),
        ],
        [full, ((edge * SUBS, half), False), ((half, 2 * head_w), True), ((SUBS, half), False)],
    )
    spill = lax.ppermute(
        spill.reshape(edge, batch, quarters, half)[::-1, :, 0], AXES, [(i, i - 2) for i in range(2, count)]
    )
    spill = jnp.pad(
        spill[:, :, None], ((0, 0), (0, 0), (quarters - 1, 0), (0, 0))
    ).reshape(edge * SUBS, half)
    x_grad = jnp.concatenate([dx[: rows - edge * SUBS], dx[rows - edge * SUBS :] + spill], axis=0).astype(BF16)

    normal_one_grad = over_sides(nt(y_grad, proj_y) + nt(x_grad, proj_x))
    input_part, gain_one_grad = norm_back(x, gain_one, normal_one_grad)
    input_grad = from_rows(resid_grad + input_part)

    def blocks_of(v, masks, wrap):
        size = 2 * share
        return [lax.dynamic_slice_in_dim(v, (me ^ m) // 2 % wrap * size, size, 0) for m in masks]

    def to_columns_owner(v_kept, v_given):
        recv = swap(v_given, core)
        n = len(inner) + 1
        total = (v_kept + recv.astype(F32)).reshape(len(xs) + 1, n, 2 * share, v_kept.shape[1])
        near = total[0]
        for k, m in enumerate(xs):
            near = near + swap(total[k + 1].astype(BF16), m).astype(F32)
        out = near[0]
        for k, m in enumerate(inner):
            out = out + swap(near[k + 1].astype(BF16), m).astype(F32)
        out = out.reshape(2, share, out.shape[1])
        other = lax.dynamic_index_in_dim(out, 1 - side, 0, keepdims=False).astype(BF16)
        return lax.dynamic_index_in_dim(out, side, 0, keepdims=False), swap(other, 1).astype(F32)

    def to_rows_owner(v_kept, v_given):
        cols = v_kept.shape[1]
        total = (v_kept + swap(v_given, core).astype(F32)).reshape(len(low_order), 2 * share, cols)
        away = cut(total, 1 - upper, cols // 2, 2).astype(BF16)
        near = cut(total, upper, cols // 2, 2) + swap(away, top).astype(F32)
        out = near[0]
        for k, m in enumerate(low_order[1:]):
            out = out + swap(near[k + 1].astype(BF16), m).astype(F32)
        other = swap(out.astype(BF16), top).astype(F32)
        out = in_order(out, other, 1).reshape(2, share, cols)
        gone = lax.dynamic_index_in_dim(out, 1 - side, 0, keepdims=False).astype(BF16)
        here = lax.dynamic_index_in_dim(out, side, 0, keepdims=False)
        return jnp.where(upper == side, here, swap(gone, 1).astype(F32))

    order = [m ^ n for m in (0, *xs) for n in (0, *inner)]
    low_order = [m ^ n for m in (0, *[v for v in xs if v < top]) for n in (0, *inner)]

    def ordered(v, masks, wrap):
        return [jnp.concatenate(blocks_of(v, [m ^ c for m in masks], wrap), axis=0) for c in (0, core)]

    kept_d, given_d = ordered(normal_one.T, order, pairs)
    kept_m, given_m = ordered(mixed.T, low_order, pairs // 2)
    by_row = jnp.concatenate([gate_grad, small_grad.T, jnp.zeros((half, head_w - SUBS), F32)], axis=1)
    kept_g, given_g = ordered(by_row, low_order, pairs // 2)
    gains = jnp.pad(jnp.stack([gain_one_grad, gain_two_grad], axis=1), ((0, 0), (0, 126)))
    kept_n, given_n = ordered(gains, order, pairs)
    if direct:
        proj_owned, out_owned, rest, gains = scatter_grads(
            (spans, seqs), kept_d, given_d, kept_m, given_m, x_grad, y_grad, branch_low, kept_g, given_g, kept_n, given_n
        )
    else:
        proj_owned = jnp.concatenate(
            [in_order(*to_columns_owner(nn(kept_d, g), nn(given_d, g, BF16)), 1) for g in (x_grad, y_grad)], axis=1
        )
        out_owned = to_rows_owner(nn(kept_m, branch_low), nn(given_m, branch_low, BF16))
        rest = to_rows_owner(kept_g, given_g.astype(BF16))
        gains = sum(to_columns_owner(kept_n, given_n.astype(BF16)))
    gate_owned, small_owned = rest[:, : 2 * head_w], rest[:, 2 * head_w : 2 * head_w + SUBS]

    return (
        output,
        input_grad,
        gains[:, 0],
        proj_owned,
        small_owned[:, :CONV],
        small_owned[:, 4],
        gate_owned,
        small_owned[:, 5:7],
        small_owned[:, 7] * jax.nn.sigmoid(decay_param.astype(F32)),
        out_owned,
        gains[:, 1],
        wide_owned,
        narrow_owned,
    )


def solution(mesh):
    both = ("span", "seq")
    tokens = P(None, both, None)
    placed = (
        tokens, P(both), P(both, None), P(both, None), P(both), P(both, None), P(both, None), P(both), P(both, None),
        P(both), P("span", None, "seq"), P("span", "seq"), tokens,
    )
    given = (
        tokens, tokens, P(both), P(both, None), P(both, None), P(both), P(both, None), P(both, None), P(both),
        P(both, None), P(both), P("span", None, "seq"), P("span", "seq"),
    )
    return jax.shard_map(on_device, mesh=mesh, in_specs=placed, out_specs=given, check_vma=False)
```

```python
import functools

import jax
import jax.numpy as jnp
from jax import lax
from jax.experimental import pallas as pl
from jax.experimental.pallas import tpu as pltpu
from jax.sharding import PartitionSpec as P

CONV = 4
EPS = 1e-06
AXES = ("span", "seq")
F32 = jnp.float32
BF16 = jnp.bfloat16
SUBS = 8


def swap(value, mask):
    count = lax.axis_size("span") * lax.axis_size("seq")
    return lax.ppermute(value, AXES, [(i, i ^ mask) for i in range(count)])


def dot(a, b, dims, out=F32):
    return lax.dot_general(a, b, ((dims[0], dims[1]), ((), ())), preferred_element_type=F32).astype(out)


def nn(a, b, out=F32):
    return dot(a, b, ((1,), (0,)), out)


def nt(a, b, out=F32):
    return dot(a, b, ((1,), (1,)), out)


def tn(a, b, out=F32):
    return dot(a, b, ((0,), (0,)), out)


def normed(v, gain):
    return v * lax.rsqrt(jnp.mean(v * v, axis=-1, keepdims=True) + EPS) * gain


def norm_back(v, gain, grad):
    scale = lax.rsqrt(jnp.mean(v * v, axis=-1, keepdims=True) + EPS)
    z = v * scale
    e = grad * gain
    return scale * (e - z * jnp.mean(e * z, axis=-1, keepdims=True)), jnp.sum(grad * z, axis=0)


def one_less_exp(u):
    series = 1.0 + u / 7.0
    for n in (6.0, 5.0, 4.0, 3.0, 2.0):
        series = 1.0 + u / n * series
    return jnp.where(u > -0.25, -u * series, 1.0 - jnp.exp(u))


def roll(v, by):
    return pltpu.roll(v, by % SUBS, 0)


def quarter_of(shape, quarters):
    return lax.broadcasted_iota(jnp.int32, shape, 0) % quarters


def spread(v, quarters, at):
    q = quarter_of(v.shape, quarters)
    held = jnp.where(q == at, v, 0.0)
    total = held
    for k in range(1, quarters):
        total = total + roll(held, k if at == 0 else -k)
    return total


def scan_carries(prods, sums, quarters, backward):
    q = quarter_of(prods[0].shape, quarters)
    sign = -1 if backward else 1
    order = (1, 0) if backward else (0, 1)
    place = quarters - 1 - q if backward else q
    whole = None
    enter = [None, None]
    for b in order:
        p, s = prods[b], sums[b]
        d = 1
        while d < quarters:
            pp, ss = roll(p, sign * d), roll(s, sign * d)
            ok = place >= d
            s = jnp.where(ok, p * ss + s, s)
            p = jnp.where(ok, p * pp, p)
            d *= 2
        first = place == 0
        ep = jnp.where(first, 1.0, roll(p, sign))
        es = jnp.where(first, 0.0, roll(s, sign))
        last = 0 if backward else quarters - 1
        tp, ts = spread(p, quarters, last), spread(s, quarters, last)
        if whole is None:
            enter[b] = (ep, es)
            whole = (tp, ts)
        else:
            enter[b] = (ep * whole[0], ep * whole[1] + es)
            whole = (tp * whole[0], tp * whole[1] + ts)
    return enter, whole


def earlier_rows(groups, halo, quarters, steps):
    q = quarter_of(groups[0].shape[1:], quarters)
    edge = CONV - 1
    out = []
    for b in (0, 1):
        ahead = []
        for k in range(edge, 0, -1):
            same = roll(groups[b][steps - k], 1)
            before = halo[k - 1] if b == 0 else roll(groups[0][steps - k], 1 - quarters)
            ahead.append(jnp.where(q == 0, before, same)[None])
        out.append(jnp.concatenate([*ahead, groups[b]], axis=0))
    return out


def forward_kernel(steps, quarters, xb, chan, gate, conv_o, recur_o, inject_o, decay_o, local_o, prod_o, enter_o, carry_o):
    rows = 2 * steps * SUBS
    width = xb.shape[1]
    head = xb[...].astype(F32)
    groups = [head[b * steps * SUBS : (b + 1) * steps * SUBS].reshape(steps, SUBS, width) for b in (0, 1)]
    halo = [head[rows + k * SUBS : rows + (k + 1) * SUBS] for k in range(CONV - 1)]
    edge = CONV - 1
    convs = []
    for ext in earlier_rows(groups, halo, quarters, steps):
        total = jnp.broadcast_to(chan[4:5][None], (steps, SUBS, width))
        for k in range(CONV):
            total = total + chan[k : k + 1][None] * ext[edge - k : edge - k + steps]
        convs.append(total.reshape(steps * SUBS, width))
    conv = jnp.concatenate(convs, axis=0)
    pre = jnp.dot(conv.astype(BF16), gate[...], preferred_element_type=F32)
    recur = jax.nn.sigmoid(pre[:, :width] + chan[5:6])
    inject = jax.nn.sigmoid(pre[:, width:] + chan[6:7])
    log_decay = -8.0 * recur * chan[7:8]
    decay = jnp.exp(log_decay)
    driven = jnp.sqrt(one_less_exp(2.0 * log_decay)) * inject * conv
    conv_o[...] = conv
    recur_o[...] = recur
    inject_o[...] = inject
    decay_o[...] = decay
    prods, sums = [], []
    for b in (0, 1):
        h = p = None
        for t in range(steps):
            at = (b * steps + t) * SUBS
            d, u = decay[at : at + SUBS], driven[at : at + SUBS]
            h = u if h is None else d * h + u
            p = d if p is None else d * p
            local_o[at : at + SUBS] = h
            prod_o[at : at + SUBS] = p
        prods.append(p)
        sums.append(h)
    enter, whole = scan_carries(prods, sums, quarters, False)
    for b in (0, 1):
        enter_o[b * SUBS : (b + 1) * SUBS] = enter[b][0]
        enter_o[(2 + b) * SUBS : (3 + b) * SUBS] = enter[b][1]
    q = quarter_of(whole[0].shape, quarters)
    carry_o[...] = jnp.where(q == 0, whole[0], whole[1])


def adjoint_kernel(steps, quarters, grad, decay, flow, local_o, after_o, enter_o, carry_o):
    prods, sums = [], []
    for b in (0, 1):
        g = r = None
        for t in range(steps - 1, -1, -1):
            at = (b * steps + t) * SUBS
            rows = slice(at, at + SUBS)
            a = grad[rows] if g is None else grad[rows] + g
            r = jnp.ones_like(a) if r is None else r * decay[at + SUBS : at + 2 * SUBS]
            local_o[rows] = a
            after_o[rows] = r
            g = decay[rows] * a
        prods.append(flow[(2 + b) * SUBS : (3 + b) * SUBS])
        sums.append(g)
    enter, whole = scan_carries(prods, sums, quarters, True)
    for b in (0, 1):
        enter_o[b * SUBS : (b + 1) * SUBS] = enter[b][0]
        enter_o[(2 + b) * SUBS : (3 + b) * SUBS] = enter[b][1]
    q = quarter_of(whole[0].shape, quarters)
    carry_o[...] = jnp.where(q == 0, whole[0], whole[1])


def backward_kernel(
    steps, quarters, local, after, states, came, entered, conv_r, recur_r, inject_r, decay_r, xb, chan, gate,
    dx_o, spill_o, gate_o, small_o,
):
    rows = 2 * steps * SUBS
    width = xb.shape[1]
    edge = CONV - 1
    block = steps * SUBS

    def by_step(v):
        return [v[b * block : (b + 1) * block].reshape(steps, SUBS, width) for b in (0, 1)]

    adjoint = jnp.concatenate(
        [
            (l + a * came[b * SUBS : (b + 1) * SUBS][None]).reshape(block, width)
            for b, (l, a) in enumerate(zip(by_step(local[...]), by_step(after[...])))
        ],
        axis=0,
    )
    earlier = jnp.concatenate(
        [
            jnp.concatenate([entered[b * SUBS : (b + 1) * SUBS], states[b * block : (b + 1) * block - SUBS]], axis=0)
            for b in (0, 1)
        ],
        axis=0,
    )
    conv, recur, inject, decay = conv_r[...], recur_r[...], inject_r[...], decay_r[...]
    rate = chan[7:8]
    mult = jnp.sqrt(one_less_exp(-16.0 * recur * rate))
    d_decay = adjoint * earlier
    d_log = d_decay * decay - adjoint * inject * conv * (decay * decay / mult)
    d_inject = adjoint * mult * conv
    d_conv = adjoint * mult * inject
    d_rate = jnp.sum(d_log * (-8.0 * recur), axis=0, keepdims=True)
    d_recur = d_log * (-8.0 * rate) * recur * (1.0 - recur)
    d_inject = d_inject * inject * (1.0 - inject)
    low = jnp.concatenate([d_recur.astype(BF16), d_inject.astype(BF16)], axis=1)
    d_conv = d_conv + lax.dot_general(low, gate[...], (((1,), (1,)), ((), ())), preferred_element_type=F32)
    gate_o[...] = lax.dot_general(conv.astype(BF16), low, (((0,), (0,)), ((), ())), preferred_element_type=F32)
    head = xb[...].astype(F32)
    halo = [head[rows + k * SUBS : rows + (k + 1) * SUBS] for k in range(edge)]
    exts = earlier_rows(by_step(head), halo, quarters, steps)
    groups = by_step(d_conv)
    for k in range(CONV):
        taps = sum(
            jnp.sum(groups[b] * exts[b][edge - k : edge - k + steps], axis=(0, 1), keepdims=True)[0] for b in (0, 1)
        )
        small_o[k : k + 1] = taps
    small_o[4:5] = jnp.sum(d_conv, axis=0, keepdims=True)
    small_o[5:6] = jnp.sum(d_recur, axis=0, keepdims=True)
    small_o[6:7] = jnp.sum(d_inject, axis=0, keepdims=True)
    small_o[7:8] = d_rate
    q = quarter_of((SUBS, width), quarters)
    for b in (0, 1):
        beyond = []
        for j in range(edge):
            same = roll(groups[b][j], -1)
            later = roll(groups[1][j], quarters - 1) if b == 0 else jnp.zeros_like(same)
            beyond.append(jnp.where(q == quarters - 1, later, same)[None])
        ext = jnp.concatenate([groups[b], *beyond], axis=0)
        total = chan[0:1][None] * ext[:steps]
        for k in range(1, CONV):
            total = total + chan[k : k + 1][None] * ext[k : k + steps]
        dx_o[b * block : (b + 1) * block] = total.reshape(block, width)
    for j in range(1, CONV):
        total = jnp.zeros((SUBS, width), F32)
        for k in range(j, CONV):
            total = total + chan[k : k + 1] * groups[0][k - j]
        spill_o[(j - 1) * SUBS : j * SUBS] = total


def by_heads(kernel, heads, head_w, arrays, outs):
    def spec(shape, tall):
        if tall:
            return pl.BlockSpec((head_w, shape[1]), lambda h: (h, 0))
        return pl.BlockSpec((shape[0], head_w), lambda h: (0, h))

    return pl.pallas_call(
        kernel,
        grid=(heads,),
        in_specs=[spec(a.shape, tall) for a, tall in arrays],
        out_specs=[spec(s, tall) for s, tall in outs],
        out_shape=[jax.ShapeDtypeStruct(s, F32) for s, _ in outs],
        compiler_params=pltpu.CompilerParams(vmem_limit_bytes=48 * 1024 * 1024),
    )(*[a for a, _ in arrays])


MESH = pl.DeviceIdType.MESH
VMEM_LIMIT = 60 * 1024 * 1024


class Links:
    def __init__(self, sizes, sends, recvs):
        self.spans, self.seqs = sizes
        self.span, self.seq = lax.axis_index("span"), lax.axis_index("seq")
        self.sends, self.recvs = sends, recvs
        self.used = 0
        self.open = []

    def flipped(self, index, mask):
        bit = 1
        while bit <= mask:
            if mask & bit:
                index = index + (1 - 2 * (index // bit % 2)) * bit
            bit *= 2
        return index

    def peer(self, mask):
        low, high = mask % self.seqs, mask // self.seqs
        return (self.flipped(self.span, high), self.flipped(self.seq, low))

    def other(self, mask):
        span, seq = self.peer(mask)
        return span * self.seqs + seq

    def greet(self, masks):
        barrier = pltpu.get_barrier_semaphore()
        for mask in masks:
            pl.semaphore_signal(barrier, inc=1, device_id=self.peer(mask), device_id_type=MESH)
        pl.semaphore_wait(barrier, len(masks))

    def plan(self, source, target, mask, only=None):
        slot = self.used
        self.used += 1
        copy = pltpu.make_async_remote_copy(
            source, target, self.sends.at[slot], self.recvs.at[slot], device_id=self.peer(mask), device_id_type=MESH
        )
        self.open.append((copy, only))
        return copy

    def send(self, source, target, mask, only=None):
        copy = self.plan(source, target, mask, only)
        if only is None:
            copy.start()
        else:
            pl.when(only)(copy.start)
        return copy

    def close(self):
        for copy, only in self.open:
            if only is None:
                copy.wait_send()
            else:
                pl.when(only)(copy.wait_send)


def in_turn(parts, order):
    for name in order:
        next(parts[name], None)
    for part in parts.values():
        for _ in part:
            pass


def gather_kernel(
    sizes, share, half, rec_proj, out_proj, gate_weight, small, tokens, wide, narrow,
    proj_x, proj_y, out_half, gates, every, tokens_o, wide_o, narrow_o, sends, recvs, locals_,
):
    links = Links(sizes, sends, recvs)
    spans, seqs = sizes
    count = spans * seqs
    me = links.span * seqs + links.seq
    side = me % 2
    upper = me // (count // 2)
    inner = [2 * k for k in range(1, seqs // 2)]
    core, top = seqs, count // 2
    double = 2 * share
    links.greet([1, *inner, core, top])
    kept = [0]

    def local(source, target, only=None):
        copy = pltpu.make_async_copy(source, target, locals_.at[kept[0]])
        kept[0] += 1
        if only is None:
            copy.start()
        else:
            pl.when(only)(copy.start)
        return copy

    def pieces_out(place, piece):
        over_inner = {m: links.send(piece(place(me)), piece(place(me)), m) for m in inner}
        over_top = {0: links.send(piece(place(me)), piece(place(me)), top)}
        over_core = [links.send(piece(place(me)), piece(place(me)), core)]
        yield
        for m in inner:
            over_inner[m].wait_recv()
            there = piece(place(links.other(m)))
            over_top[m] = links.send(there, there, top)
            over_core.append(links.send(there, there, core))
        yield
        for m in (0, *inner):
            over_top[m].wait_recv()
            there = piece(place(links.other(top + m)))
            over_core.append(links.send(there, there, core))
        yield
        for copy in over_core:
            copy.wait_recv()

    def columns_part(source, first, target):
        def piece(start):
            return target.at[pl.ds(pl.multiple_of(start, 16), double)]

        def columns(which):
            return source.at[:, pl.ds(pl.multiple_of(first + which * half, 128), half)]

        row = target.at[pl.ds(pl.multiple_of(me * share, 16), share)]
        mine = local(columns(side), row)
        theirs = links.send(columns(1 - side), row, 1)
        yield
        mine.wait()
        theirs.wait_recv()
        yield from pieces_out(lambda d: d // 2 * double, piece)

    def whole_part(source, target):
        height = source.shape[0]

        def piece(start):
            return target.at[pl.ds(pl.multiple_of(start, 16), 2 * height)]

        row = target.at[pl.ds(pl.multiple_of(me * height, 16), height)]
        mine = local(source, row)
        theirs = links.send(source, row, 1)
        yield
        mine.wait()
        theirs.wait_recv()
        yield from pieces_out(lambda d: d // 2 * 2 * height, piece)

    def rows_part(source, target):
        width = source.shape[1]
        pairs_half = count // 4

        def place(d):
            return d // 2 % pairs_half * double

        def rows(start, size):
            return target.at[pl.ds(pl.multiple_of(start, 16), size)]

        def piece(start, which):
            return target.at[pl.ds(pl.multiple_of(start, 16), double), pl.ds(pl.multiple_of(which * (width // 2), 128), width // 2)]

        holds = side == upper
        row = rows(place(me) + side * share, share)
        mine = local(source, row, holds)
        gift = links.send(source, row, 1, side != upper)
        yield

        @pl.when(holds)
        def _():
            mine.wait()
            gift.wait_recv()

        across = links.send(rows(place(me), double), rows(place(me), double), top, holds)
        pl.when(side != upper)(across.wait_recv)
        over_inner = {m: links.send(piece(place(me), upper), piece(place(me), upper), m) for m in inner}
        over_core = [links.send(rows(place(me), double), rows(place(me), double), core)]
        over_top = {}
        yield
        for m in inner:
            over_inner[m].wait_recv()
            there = piece(place(links.other(m)), upper)
            over_top[m] = links.send(there, there, top)
            over_core.append(links.send(there, there, core))
        yield
        for m in inner:
            over_top[m].wait_recv()
            there = piece(place(links.other(m)), 1 - upper)
            over_core.append(links.send(there, there, core))
        yield
        for copy in over_core:
            copy.wait_recv()

    parts = {
        "x": columns_part(rec_proj, 0, proj_x),
        "s": whole_part(small, every),
        "g": rows_part(gate_weight, gates),
        "y": columns_part(rec_proj, 2 * half, proj_y),
        "o": rows_part(out_proj, out_half),
    }
    in_turn(parts, "xsgxsgyoxyxogsygsygoyo")
    links.close()


def gather_weights(sizes, rec_proj, out_proj, gate_weight, small, tokens, wide, narrow):
    share = rec_proj.shape[0]
    half = rec_proj.shape[1] // 4
    count = sizes[0] * sizes[1]
    held = [
        (count * share, half), (count * share, half), (count // 2 * share, out_proj.shape[1]),
        (count // 2 * share, gate_weight.shape[1]), (count * small.shape[0], small.shape[1]),
        tokens.shape, wide.shape, narrow.shape,
    ]
    anywhere = pl.BlockSpec(memory_space=pl.ANY)
    copies = 5 * 16
    return pl.pallas_call(
        functools.partial(gather_kernel, sizes, share, half),
        in_specs=[anywhere] * 7,
        out_specs=[anywhere] * 8,
        out_shape=[jax.ShapeDtypeStruct(s, BF16) for s in held],
        scratch_shapes=[
            pltpu.SemaphoreType.DMA((copies,)), pltpu.SemaphoreType.DMA((copies,)), pltpu.SemaphoreType.DMA((8,))
        ],
        input_output_aliases={4: 5, 5: 6, 6: 7},
        compiler_params=pltpu.CompilerParams(collective_id=0, has_side_effects=True, vmem_limit_bytes=VMEM_LIMIT),
    )(rec_proj, out_proj, gate_weight, small, tokens, wide, narrow)


def scatter_kernel(
    sizes, share, kept_d, given_d, kept_m, given_m, grad_x, grad_y, branch, kept_g, given_g, kept_n, given_n,
    proj_o, out_o, gate_o, gain_o, sends, recvs, *bufs,
):
    links = Links(sizes, sends, recvs)
    spans, seqs = sizes
    count = spans * seqs
    me = links.span * seqs + links.seq
    side = me % 2
    upper = me // (count // 2)
    inner = [2 * k for k in range(1, seqs // 2)]
    core, top = seqs, count // 2
    double = 2 * share
    n = len(inner) + 1
    links.greet([1, *inner, core, top])

    def part(kept, given, cols, scratch, finish):
        to_core, from_core, to_top, from_top, to_inner, from_inner, to_side, from_side = scratch
        crossing = []
        for i in range(2):
            for j in range(n):
                to_core[i * n + j] = given((1 - i) * n + j).astype(BF16)
            crossing.append(links.send(to_core.at[pl.ds(i * n, n)], from_core.at[pl.ds(i * n, n)], core))
        yield
        crossing[0].wait_recv()
        over_top = {}
        for j in (*range(1, n), 0):
            to_top[j] = (kept(n + j) + from_core[j].astype(F32)).astype(BF16)
            over_top[j] = links.send(to_top.at[j], from_top.at[j], top)
        crossing[1].wait_recv()
        yield
        over_inner = []
        for j in range(1, n):
            over_top[j].wait_recv()
            to_inner[j - 1] = (kept(j) + from_core[n + j].astype(F32) + from_top[j].astype(F32)).astype(BF16)
            over_inner.append(links.send(to_inner.at[j - 1], from_inner.at[j - 1], inner[j - 1]))
        over_top[0].wait_recv()
        yield
        total = kept(0) + from_core[n].astype(F32) + from_top[0].astype(F32)
        for j in range(1, n):
            over_inner[j - 1].wait_recv()
            total = total + from_inner[j - 1].astype(F32)
        yield from finish(total, to_side, from_side)

    def sided(total):
        low, high = total[:share], total[share:]
        first = side == 0
        return jnp.where(first, low, high), jnp.where(first, high, low)

    def by_columns(put):
        def finish(total, to_side, from_side):
            mine, theirs = sided(total)
            to_side[...] = theirs.astype(BF16)
            copy = links.send(to_side, from_side, 1)
            yield
            copy.wait_recv()
            put(mine, from_side[...].astype(F32))

        return finish

    def into(first, cols):
        def put(mine, recv):
            proj_o[:, first : first + cols] = jnp.where(side == 0, mine, recv)
            proj_o[:, first + cols : first + 2 * cols] = jnp.where(side == 0, recv, mine)

        return put

    def put_gain(mine, recv):
        gain_o[...] = mine + recv

    def by_rows(target, to_last, from_last):
        cols = target.shape[1] // 2

        def finish(total, to_side, from_side):
            to_side[...] = total.astype(BF16)
            copy = links.send(to_side, from_side, top)
            yield
            copy.wait_recv()
            other = from_side[...].astype(F32)
            first = side == 0
            (low, low_far), (high, high_far) = sided(jnp.where(first, total, other)), sided(jnp.where(first, other, total))
            to_last[:, :cols] = low_far.astype(BF16)
            to_last[:, cols:] = high_far.astype(BF16)
            copy = links.send(to_last, from_last, 1)
            yield
            copy.wait_recv()
            holds = side == upper
            target[:, :cols] = jnp.where(holds, low, from_last[:, :cols].astype(F32))
            target[:, cols:] = jnp.where(holds, high, from_last[:, cols:].astype(F32))

        return finish

    def product(lhs, rhs, wrap, columns=None):
        def block(j):
            rows = lhs[j % wrap * double : (j % wrap + 1) * double]
            if columns is None:
                return jnp.dot(rows, rhs[...], preferred_element_type=F32)
            which = upper if j < n else 1 - upper
            right = rhs[:, pl.ds(pl.multiple_of(which * columns, 128), columns)]
            return jnp.dot(rows, right, preferred_element_type=F32)

        return block

    def stored(blocks, columns=None):
        def block(j):
            if columns is None:
                return blocks[j * double : (j + 1) * double].astype(F32)
            which = upper if j < n else 1 - upper
            return blocks[j % n * double : (j % n + 1) * double, pl.ds(pl.multiple_of(which * columns, 128), columns)].astype(F32)

        return block

    half = grad_x.shape[1]
    wide = branch.shape[1] // 2
    thin = kept_g.shape[1] // 2
    parts = {
        "y": part(product(kept_d, grad_y, 2 * n), product(given_d, grad_y, 2 * n), half, bufs[0:8], by_columns(into(2 * half, half))),
        "o": part(product(kept_m, branch, n, wide), product(given_m, branch, n, wide), wide, bufs[8:16], by_rows(out_o, *bufs[16:18])),
        "x": part(product(kept_d, grad_x, 2 * n), product(given_d, grad_x, 2 * n), half, bufs[18:26], by_columns(into(0, half))),
        "g": part(stored(kept_g, thin), stored(given_g, thin), thin, bufs[26:34], by_rows(gate_o, *bufs[34:36])),
        "n": part(stored(kept_n), stored(given_n), kept_n.shape[1], bufs[36:44], by_columns(put_gain)),
    }
    in_turn(parts, "yxoyxoyxgnoyxgnoygnoxoygnoxgngg")
    links.close()


def scatter_grads(sizes, kept_d, given_d, kept_m, given_m, grad_x, grad_y, branch, kept_g, given_g, kept_n, given_n):
    n = sizes[1] // 2
    share = kept_d.shape[0] // (4 * n)
    half, wide, thin, gain = grad_x.shape[1], branch.shape[1], kept_g.shape[1], kept_n.shape[1]

    def scratch(cols, last):
        double = 2 * share
        side = share if last is None else double
        shapes = [(2 * n, double, cols)] * 2 + [(n, double, cols)] * 2 + [(n - 1, double, cols)] * 2 + [(side, cols)] * 2
        if last is not None:
            shapes += [(share, last)] * 2
        return [pltpu.VMEM(s, BF16) for s in shapes]

    bufs = [*scratch(half, None), *scratch(wide // 2, wide), *scratch(half, None), *scratch(thin // 2, thin), *scratch(gain, None)]
    copies = 5 * (2 + n + (n - 1) + 2)
    inside = pl.BlockSpec(memory_space=pltpu.VMEM)
    return pl.pallas_call(
        functools.partial(scatter_kernel, sizes, share),
        in_specs=[inside] * 11,
        out_specs=[inside] * 4,
        out_shape=[jax.ShapeDtypeStruct((share, cols), F32) for cols in (4 * half, wide, thin, gain)],
        scratch_shapes=[pltpu.SemaphoreType.DMA((copies,)), pltpu.SemaphoreType.DMA((copies,)), *bufs],
        compiler_params=pltpu.CompilerParams(collective_id=1, has_side_effects=True, vmem_limit_bytes=VMEM_LIMIT),
    )(kept_d, given_d, kept_m, given_m, grad_x, grad_y, branch, kept_g, given_g, kept_n, given_n)


def gelu_parts(v):
    root = 0.7978845608028654
    t = jnp.tanh(root * (v + 0.044715 * (v * v * v)))
    slope = 0.5 * (1.0 + t) + 0.5 * v * (1.0 - t * t) * root * (1.0 + 3.0 * 0.044715 * (v * v))
    return 0.5 * v * (1.0 + t), slope


def feed_kernel(sizes, masks, own, *refs):
    chunks = len(masks)
    spans = sizes[0]
    own_rows, refs = refs[0], refs[1:]
    cots, refs = refs[: 2 * chunks], refs[2 * chunks :]
    wides, refs = refs[:spans], refs[spans:]
    narrows, refs = refs[:spans], refs[spans:]
    grad_o, near_o, far_o, rows_o, cots_o, act_o, hidden_o, refs = *refs[:7], refs[7:]
    (rows, cot, wide, narrow, act, hidden, near, down_near, down_far, to_side, from_side, to_inner, from_inner,
     sends, recvs, loads, stores) = refs
    units = narrow.shape[0]
    width = narrow.shape[1]
    size = width // spans
    pair = 2 * own
    links = Links(sizes, sends, recvs)

    def load(source, target, slot):
        copy = pltpu.make_async_copy(source, target, loads.at[slot])
        copy.start()
        return copy

    first = load(own_rows, rows.at[pl.ds(0, own)], 0)
    late = [load(cots[b], cot.at[pl.ds(b * own, own)], 1 + b) for b in range(2 * chunks)]
    for j in range(spans):
        columns = pl.ds(j * size, size)
        late.append(load(wides[j], wide.at[:, columns], 1 + 2 * chunks + j))
        late.append(load(narrows[j], narrow.at[:, columns], 1 + 2 * chunks + spans + j))
    links.greet([1, *masks[1:]])
    first.wait()

    def block(b):
        return rows.at[pl.ds(b * own, own)]

    each = range(chunks)
    over_side = [links.plan(block(2 * i), block(2 * i + 1), 1) for i in each]
    over_inner = [None] + [links.plan(block(0), block(2 * i), masks[i]) for i in each[1:]]
    back_side = [links.plan(to_side.at[i], from_side.at[i], 1) for i in each]
    back_inner = [links.plan(to_inner.at[i - 1], from_inner.at[i - 1], masks[i]) for i in each[1:]]
    over_side[0].start()
    over_inner[1].start()
    for copy in late:
        copy.wait()

    def onward(i):
        over_inner[i].wait_recv()
        over_side[i].start()
        if i + 1 < chunks:
            over_inner[i + 1].start()

    def give_on(i):
        back_side[i].wait_recv()
        to_inner[i - 1] = (near[i].astype(F32) + from_side[i].astype(F32)).astype(BF16)
        back_inner[i - 1].start()

    def ahead(i):
        over_side[i].wait_recv()
        if i == 0:
            onward(1)
        else:
            back_side[i - 1].start()

    def behind(i):
        if 0 < i < chunks - 1:
            onward(i + 1)
        if i == chunks - 1:
            back_side[i].start()
        if i > 1:
            give_on(i - 1)

    def compute(i):
        here = pl.ds(pl.multiple_of(i * pair, 16), pair)
        mine = rows[here]
        given = cot[here]
        start = 0
        while start < units:
            n = min(384, units - start)
            gate = lax.dot_general(mine, wide[start : start + n], (((1,), (1,)), ((), ())), preferred_element_type=F32)
            up = lax.dot_general(
                mine, wide[units + start : units + start + n], (((1,), (1,)), ((), ())), preferred_element_type=F32
            )
            back = lax.dot_general(given, narrow[start : start + n], (((1,), (1,)), ((), ())), preferred_element_type=F32)
            value, slope = gelu_parts(gate)
            hidden[here, start : start + n] = (value * up).astype(BF16)
            act[here, start : start + n] = (back * up * slope).astype(BF16)
            act[here, units + start : units + start + n] = (back * value).astype(BF16)
            start += n
        step = 512

        @pl.loop(0, width // step)
        def _(k):
            columns = pl.ds(pl.multiple_of(k * step, 128), step)
            total = jnp.dot(act[here], wide[:, columns], preferred_element_type=F32)
            near[i, :, columns] = total[:own].astype(BF16)
            to_side[i, :, columns] = total[own:].astype(BF16)
            total = jnp.dot(hidden[here], narrow[:, columns], preferred_element_type=F32)
            down_near[i, :, columns] = total[:own].astype(BF16)
            down_far[i, :, columns] = total[own:].astype(BF16)

    @pl.loop(0, chunks)
    def _(i):
        for k in range(chunks):
            pl.when(i == k)(functools.partial(ahead, k))
        compute(i)
        for k in range(chunks):
            pl.when(i == k)(functools.partial(behind, k))

    pairs = [(rows, rows_o), (cot, cots_o), (act, act_o), (hidden, hidden_o), (down_near, near_o), (down_far, far_o)]
    out = []
    for k, (source, target) in enumerate(pairs):
        out.append(pltpu.make_async_copy(source, target, stores.at[k]))
        out[-1].start()
    give_on(chunks - 1)
    back_side[0].wait_recv()
    total = near[0].astype(F32) + from_side[0].astype(F32)
    for k in range(chunks - 1):
        back_inner[k].wait_recv()
        total = total + from_inner[k].astype(F32)
    grad_o[...] = total
    for copy in out:
        copy.wait()
    links.close()


def feed_forward(sizes, masks, own_rows, cots, wides, narrows):
    own, width = own_rows.shape
    units = narrows[0].shape[0]
    chunks = len(masks)
    total = 2 * chunks * own
    anywhere = pl.BlockSpec(memory_space=pl.ANY)
    copies = 4 * chunks
    blocks = (chunks, own, width)
    shapes = [blocks, blocks, (total, width), (total, width), (total, 2 * units), (total, units)]
    held = [
        (total, width), (total, width), (2 * units, width), (units, width), (total, 2 * units), (total, units), blocks, blocks,
        blocks, blocks, blocks, (chunks - 1, own, width), (chunks - 1, own, width),
    ]
    return pl.pallas_call(
        functools.partial(feed_kernel, sizes, masks, own),
        in_specs=[anywhere] * (1 + 2 * chunks + 2 * len(wides)),
        out_specs=[pl.BlockSpec(memory_space=pltpu.VMEM)] + [anywhere] * 6,
        out_shape=[jax.ShapeDtypeStruct((own, width), F32)] + [jax.ShapeDtypeStruct(s, BF16) for s in shapes],
        scratch_shapes=[pltpu.VMEM(s, BF16) for s in held]
        + [pltpu.SemaphoreType.DMA((k,)) for k in (copies, copies, 1 + 2 * chunks + 2 * len(wides), 6)],
        compiler_params=pltpu.CompilerParams(collective_id=2, has_side_effects=True, vmem_limit_bytes=VMEM_LIMIT),
    )(own_rows, *cots, *wides, *narrows)


def expanded(v, quarters):
    return spread(v, quarters, 0), spread(roll(v, -1), quarters, 0)


def chunk_inflow(links, line, blocks, quarters, backward, between):
    n, spans = line.shape[0], blocks.shape[0]
    place = links.seq // 2
    copies = [links.send(line.at[0], line.at[k], 2 * k) for k in range(1, n)]
    for copy in copies:
        copy.wait_recv()
    between()
    one, nought = jnp.ones(line.shape[1:], F32), jnp.zeros(line.shape[1:], F32)
    prod, total = one, nought
    all_prod, all_total = one, nought

    def ordered(count):
        return range(count - 1, -1, -1) if backward else range(count)

    def ahead(j, at):
        return at < j if backward else at > j

    for j in ordered(n):
        p, s = expanded(line[links.flipped(place, j)], quarters)
        inside = ahead(j, place)
        total = jnp.where(inside, p * total + s, total)
        prod = jnp.where(inside, p * prod, prod)
        all_total = p * all_total + s
        all_prod = p * all_prod
    q = quarter_of(line.shape[1:], quarters)
    blocks[0] = jnp.where(q == 0, all_prod, all_total)
    copies = [links.send(blocks.at[0], blocks.at[m], m * links.seqs) for m in range(1, spans)]
    for copy in copies:
        copy.wait_recv()
    h = nought
    for j in ordered(spans):
        p, s = expanded(blocks[links.flipped(links.span, j)], quarters)
        h = jnp.where(ahead(j, links.span), p * h + s, h)
    return prod * h + total


def by_head(heads, head_w, body):
    @pl.loop(0, heads)
    def _(h):
        start = pl.multiple_of(h * head_w, 128)
        columns = pl.ds(start, head_w)
        body(lambda ref: ref.at[:, columns], lambda ref: ref.at[pl.ds(start, head_w)])


def recur_kernel(
    sizes, steps, quarters, heads, inner, xb, chan, gate, y_pre, out_w, x_own, gain, cot, wide, narrow, *refs
):
    spans, seqs = sizes
    core, tops = seqs, [2 * seqs * k for k in range(1, spans // 2)]
    n = len(inner) + 1
    outs, refs = refs[: 8 + 2 * (spans - 1) + 2 * n], refs[8 + 2 * (spans - 1) + 2 * n :]
    conv, recur, inject, decay, states, flow_o, mixed, resid = outs[:8]
    wides, narrows = outs[8 : 7 + spans], outs[7 + spans : 6 + 2 * spans]
    cots, normal = outs[6 + 2 * spans : -1], outs[-1]
    prod, enter, line, blocks, inflow, to_side, from_side, low, sends, recvs = refs
    links = Links(sizes, sends, recvs)
    side = links.seq % 2
    own, width = x_own.shape
    rows = 2 * own
    masks = [1, *inner, *[m * seqs for m in range(1, spans)]]
    links.greet(masks)
    early = pl.ds(0, wide.shape[0] // 4)
    later = pl.ds(wide.shape[0] // 4, wide.shape[0] - wide.shape[0] // 4)
    across_wide = [links.send(wide.at[early], wides[m // seqs - 1].at[early], m) for m in tops]
    beside = [links.send(wide, wides[0], core), links.send(narrow, narrows[0], core)]
    over_inner = {m: links.plan(cot, cots[2 * k], m) for k, m in enumerate(inner)}
    over_side = [links.send(cot, cots[2 * len(inner)], 1)]
    head_w = gate.shape[1] // 2

    def gates(cols, tall):
        forward_kernel(
            steps, quarters, cols(xb), cols(chan), tall(gate), cols(conv), cols(recur), cols(inject), cols(decay),
            cols(states), cols(prod), cols(enter), cols(line.at[0]),
        )

    by_head(heads, head_w, gates)
    inflow[...] = chunk_inflow(
        links, line, blocks, quarters, False, lambda: [over_inner[m].start() for m in inner]
    )
    across_wide += [links.send(wide.at[later], wides[m // seqs - 1].at[later], m) for m in tops]
    across_narrow = {m: links.send(narrow, narrows[m // seqs - 1], m) for m in tops}
    block = steps * SUBS

    def mix(cols, tall):
        ins, flow, hold, gain_y = cols(inflow), cols(flow_o), cols(states), cols(y_pre)
        for b in (0, 1):
            entered = cols(enter)[b * SUBS : (b + 1) * SUBS] * ins[...] + cols(enter)[(2 + b) * SUBS : (3 + b) * SUBS]
            flow[b * SUBS : (b + 1) * SUBS] = entered
            flow[(2 + b) * SUBS : (3 + b) * SUBS] = cols(prod)[(b + 1) * block - SUBS : (b + 1) * block]
            here = slice(b * block, (b + 1) * block)
            total = hold[here].reshape(steps, SUBS, head_w) + cols(prod)[here].reshape(steps, SUBS, head_w) * entered[None]
            total = total.reshape(block, head_w)
            hold[here] = total
            cols(mixed)[here] = (total * gelu_parts(gain_y[here])[0]).astype(BF16)

    by_head(heads, head_w, mix)
    step = 512

    @pl.loop(0, width // step)
    def _(k):
        columns = pl.ds(pl.multiple_of(k * step, 128), step)
        total = jnp.dot(mixed[...], out_w[:, columns], preferred_element_type=F32)
        first = side == 0
        resid[:, columns] = x_own[:, columns].astype(F32) + jnp.where(first, total[:own], total[own:])
        to_side[:, columns] = jnp.where(first, total[own:], total[:own]).astype(BF16)

    partial = links.send(to_side, from_side, 1)
    partial.wait_recv()
    few = 16
    size = width // spans

    @pl.loop(0, own // few)
    def _(k):
        here = pl.ds(pl.multiple_of(k * few, few), few)
        total = resid[here] + from_side[here].astype(F32)
        resid[here] = total
        low[here] = normed(total, gain[...]).astype(BF16)

    for j in range(spans):
        start = pl.multiple_of(links.flipped(links.span, j) * size, 128)
        normal[:, j * size : (j + 1) * size] = low[:, pl.ds(start, size)]

    for k, m in enumerate(inner):
        over_inner[m].wait_recv()
        over_side.append(links.send(cots[2 * k], cots[2 * k + 1], 1))
    for copy in across_wide:
        copy.wait_recv()
    for m in tops:
        beside.append(links.send(wides[m // seqs - 1], wides[m // seqs], core))
    for m in tops:
        across_narrow[m].wait_recv()
        beside.append(links.send(narrows[m // seqs - 1], narrows[m // seqs], core))
    for copy in (*beside, *over_side):
        copy.wait_recv()
    links.close()


def recurrent(sizes, steps, quarters, heads, inner, xb, chan, gate, y_pre, out_w, x_own, gain, cot, wide, narrow):
    spans, seqs = sizes
    half = xb.shape[1]
    own, width = x_own.shape
    rows = 2 * own
    n = len(inner) + 1
    inside, anywhere = pl.BlockSpec(memory_space=pltpu.VMEM), pl.BlockSpec(memory_space=pl.ANY)
    full = jax.ShapeDtypeStruct((rows, half), F32)

    def low(shape):
        return jax.ShapeDtypeStruct(shape, BF16)

    shapes = [
        *[full] * 5, jax.ShapeDtypeStruct((4 * SUBS, half), F32), low((rows, half)), jax.ShapeDtypeStruct((own, width), F32),
        *[low(wide.shape)] * (spans - 1), *[low(narrow.shape)] * (spans - 1), *[low(cot.shape)] * (2 * n - 1), low((own, width)),
    ]
    copies = 3 * (spans // 2) * 2 + 2 * n + 2 + (n - 1) + spans
    end = (SUBS, half)
    outs = pl.pallas_call(
        functools.partial(recur_kernel, sizes, steps, quarters, heads, inner),
        in_specs=[inside] * 7 + [anywhere] * 3,
        out_specs=[inside] * 8 + [anywhere] * (len(shapes) - 9) + [inside],
        out_shape=shapes,
        scratch_shapes=[
            pltpu.VMEM((rows, half), F32), pltpu.VMEM((4 * SUBS, half), F32), pltpu.VMEM((n, *end), F32),
            pltpu.VMEM((spans, *end), F32), pltpu.VMEM(end, F32), *[pltpu.VMEM((own, width), BF16)] * 3,
            pltpu.SemaphoreType.DMA((copies,)), pltpu.SemaphoreType.DMA((copies,)),
        ],
        compiler_params=pltpu.CompilerParams(collective_id=3, has_side_effects=True, vmem_limit_bytes=VMEM_LIMIT),
    )(xb, chan, gate, y_pre, out_w, x_own, gain, cot, wide, narrow)
    wides, narrows = outs[8 : 7 + spans], outs[7 + spans : 6 + 2 * spans]
    received = outs[6 + 2 * spans : -1]
    near, far = [cot] + [received[2 * k] for k in range(n - 1)], [received[2 * (n - 1)]] + [received[2 * k + 1] for k in range(n - 1)]
    cots = [b for pair in zip(near, far) for b in pair]
    return outs[:8], [wide, *wides], [narrow, *narrows], cots, outs[-1]


def return_kernel(
    sizes, steps, quarters, heads, inner, branch, out_w, y_pre, states, decay, flow, conv, recur, inject, xb, chan, gate,
    near, far, wide, narrow, branch_o, y_grad, dx, spill, gate_o, small, down, wides, narrows,
    grad, local, after, enter, carry, line, blocks, inflow, dmix, from_side, to_inner, from_inner, sends, recvs,
):
    spans, seqs = sizes
    tops = [2 * seqs * k for k in range(1, spans // 2)]
    n = len(inner) + 1
    links = Links(sizes, sends, recvs)
    side = links.seq % 2
    own, width = branch.shape
    links.greet([1, *inner, *[m * seqs for m in range(1, spans)]])
    place = pl.ds(pl.multiple_of(side * own, 16), own)
    whole = links.send(branch, branch_o.at[place], 1)
    tall = wide.shape[1] // 2
    across = [links.send(wide.at[k, pl.ds(0, tall)], wides.at[k, pl.ds(0, tall)], m) for k, m in enumerate(tops)]
    branch_o[place] = branch[...]
    whole.wait_recv()
    sums = [*range(1, n), 0]
    over_side = {}

    def side_sum(i):
        over_side[sums[i]] = links.send(far.at[sums[i]], from_side.at[sums[i]], 1)

    over_inner = []

    def inner_sum(i):
        k = sums[i]
        over_side[k].wait_recv()
        if k:
            to_inner[k - 1] = (near[k].astype(F32) + from_side[k].astype(F32)).astype(BF16)
            over_inner.append(links.send(to_inner.at[k - 1], from_inner.at[k - 1], inner[k - 1]))

    side_sum(0)
    head_w = gate.shape[1] // 2

    def first(cols, tall):
        mixed_grad = lax.dot_general(branch_o[...], tall(out_w)[...], (((1,), (1,)), ((), ())), preferred_element_type=F32)
        value, slope = gelu_parts(cols(y_pre)[...])
        cols(grad)[...] = mixed_grad * value
        cols(y_grad)[...] = (mixed_grad * cols(states)[...] * slope).astype(BF16)
        adjoint_kernel(
            steps, quarters, cols(grad), cols(decay), cols(flow), cols(local), cols(after), cols(enter), cols(line.at[0])
        )

    by_head(heads, head_w, first)

    def between():
        inner_sum(0)
        side_sum(1)

    inflow[...] = chunk_inflow(links, line, blocks, quarters, True, between)
    for k, m in enumerate(tops):
        across.append(links.send(wide.at[k, pl.ds(tall, tall)], wides.at[k, pl.ds(tall, tall)], m))
        across.append(links.send(narrow.at[k], narrows.at[k], m))
    inner_sum(1)
    side_sum(2)

    def second(cols, tall):
        came = jnp.concatenate(
            [
                cols(enter)[b * SUBS : (b + 1) * SUBS] * cols(inflow)[...] + cols(enter)[(2 + b) * SUBS : (3 + b) * SUBS]
                for b in (0, 1)
            ],
            axis=0,
        )
        backward_kernel(
            steps, quarters, cols(local), cols(after), cols(states), came, cols(flow), cols(conv), cols(recur),
            cols(inject), cols(decay), cols(xb), cols(chan), tall(gate), cols(dx), cols(spill), tall(gate_o), cols(small),
        )

    by_head(heads, head_w, second)
    for i in range(2, n):
        inner_sum(i)
        if i + 1 < n:
            side_sum(i + 1)
    few = 16
    for copy in over_inner:
        copy.wait_recv()

    @pl.loop(0, own // few)
    def _(k):
        here = pl.ds(pl.multiple_of(k * few, few), few)
        total = near[0, here].astype(F32) + from_side[0, here].astype(F32)
        for j in range(n - 1):
            total = total + from_inner[j, here].astype(F32)
        down[here] = total

    for copy in across:
        copy.wait_recv()
    links.close()


def returned(sizes, steps, quarters, heads, inner, branch, out_w, y_pre, states, decay, flow, conv, recur, inject, xb, chan, gate,
             near, far, wide, narrow):
    spans, _ = sizes
    own, width = branch.shape
    rows, half = y_pre.shape
    n = len(inner) + 1
    inside, anywhere = pl.BlockSpec(memory_space=pltpu.VMEM), pl.BlockSpec(memory_space=pl.ANY)

    def high(*shape):
        return jax.ShapeDtypeStruct(shape, F32)

    def low(*shape):
        return jax.ShapeDtypeStruct(shape, BF16)

    shapes = [
        low(rows, width), low(rows, half), high(rows, half), high((CONV - 1) * SUBS, half), high(*gate.shape), high(SUBS, half),
        high(own, width), low(*wide.shape), low(*narrow.shape),
    ]
    end = (SUBS, half)
    copies = 3 * (spans // 2) + 2 * n + 2 * n + spans + 1
    return pl.pallas_call(
        functools.partial(return_kernel, sizes, steps, quarters, heads, inner),
        in_specs=[inside] * 14 + [anywhere] * 2,
        out_specs=[inside] * 7 + [anywhere] * 2,
        out_shape=shapes,
        scratch_shapes=[
            *[pltpu.VMEM((rows, half), F32)] * 3, pltpu.VMEM((4 * SUBS, half), F32), pltpu.VMEM(end, F32),
            pltpu.VMEM((n, *end), F32), pltpu.VMEM((spans, *end), F32), pltpu.VMEM(end, F32), pltpu.VMEM(end, F32),
            pltpu.VMEM((n, own, width), BF16), pltpu.VMEM((n - 1, own, width), BF16), pltpu.VMEM((n - 1, own, width), BF16),
            pltpu.SemaphoreType.DMA((copies,)), pltpu.SemaphoreType.DMA((copies,)),
        ],
        compiler_params=pltpu.CompilerParams(collective_id=4, has_side_effects=True, vmem_limit_bytes=VMEM_LIMIT),
    )(branch, out_w, y_pre, states, decay, flow, conv, recur, inject, xb, chan, gate, near, far, wide, narrow)


def on_device(
    inputs, norm_one, rec_proj, conv_weight, conv_bias, gate_weight, gate_bias, decay_param, out_proj, norm_two,
    mlp_wide, mlp_narrow, cotangent,
):
    spans, seqs = lax.axis_size("span"), lax.axis_size("seq")
    count = spans * seqs
    span, seq = lax.axis_index("span"), lax.axis_index("seq")
    me = span * seqs + seq
    side = me % 2
    pair = me // 2
    pairs = count // 2
    batch, tokens, width = inputs.shape
    half = width // 2
    quarters = SUBS // batch
    steps = tokens // quarters
    own = batch * tokens
    rows = 2 * own
    head_w = gate_weight.shape[1] // 2
    heads = half // head_w
    edge = CONV - 1
    share = width // count
    units = mlp_narrow.shape[1]
    inner = [2 * k for k in range(1, seqs // 2)]
    core = seqs
    xs = [2 * seqs * k for k in range(1, spans // 2)]
    top = count // 2
    upper = me // top

    def to_rows(v):
        return v.reshape(batch, quarters, steps, width).transpose(2, 0, 1, 3).reshape(own, width)

    def from_rows(v):
        return v.reshape(steps, batch, quarters, width).transpose(1, 2, 0, 3).reshape(batch, tokens, width)

    def in_order(mine, other, axis):
        return jnp.concatenate([jnp.where(side == 0, mine, other), jnp.where(side == 0, other, mine)], axis=axis)

    def cut(v, index, size, axis):
        return lax.dynamic_slice_in_dim(v, index * size, size, axis)

    direct = share % 16 == 0 and spans == 4

    def gathered_rows(block, buffer, place):
        pieces = {0: block}
        for m in inner:
            pieces[m] = swap(block, m)
        for m in xs:
            for n in (0, *inner):
                pieces[m ^ n] = swap(pieces[n], m)
        for n in list(pieces):
            pieces[core ^ n] = swap(pieces[n], core)
        for m, piece in pieces.items():
            buffer = lax.dynamic_update_slice_in_dim(buffer, piece, place(me ^ m), 0)
        return buffer

    def columns_half(block):
        mine, theirs = cut(block, side, half, 1), cut(block, 1 - side, half, 1)
        block = in_order(mine, swap(theirs, 1), 0)
        return gathered_rows(block, jnp.zeros((width, half), BF16), lambda d: d // 2 * 2 * share)

    def rows_half(block):
        full = lax.all_gather(block, AXES, axis=0, tiled=True)
        return cut(full, side, half, 0)

    def by_span(v):
        size = width // spans
        return jnp.concatenate([cut(v, span ^ j, size, 1) for j in range(spans)], axis=1)

    small = jnp.stack([norm_one, norm_two, *conv_weight.T, conv_bias, *gate_bias.T, decay_param])
    wide_own = mlp_wide.transpose(1, 2, 0).reshape(2 * units, width // spans)
    narrow_own = mlp_narrow.T
    grads_own = by_span(to_rows(cotangent))
    if direct:
        packed = jnp.pad(small, ((0, 6), (0, -share % 128)))
        proj_x, proj_y, out_half, gates, small, grads_own, wide_own, narrow_own = gather_weights(
            (spans, seqs), rec_proj, out_proj, gate_weight, packed, grads_own, wide_own, narrow_own
        )
        small = small.reshape(count, 16, -1)[:, :10, :share].transpose(1, 0, 2).reshape(10, width)
    else:
        proj_x = columns_half(rec_proj[:, :width])
        proj_y = columns_half(rec_proj[:, width:])
        gates = rows_half(gate_weight)
        out_half = rows_half(out_proj)
        small = lax.all_gather(small, AXES, axis=1, tiled=True)
    small = small.astype(F32)
    gain_one, gain_two = small[0], small[1]
    chan = cut(jnp.concatenate([small[2:9], jax.nn.softplus(small[9:10])], axis=0), side, half, 1)

    mine = to_rows(inputs)
    x = mine.astype(F32)
    tail = inputs[:, tokens - edge :]
    halo = lax.ppermute(tail, AXES, [(i, i + 1) for i in range(1, count - 1, 2)]) + lax.ppermute(
        tail, AXES, [(i, i + 2) for i in range(1, count - 2, 2)]
    )
    halo = jnp.zeros((edge, batch, quarters, width), BF16).at[:, :, 0].set(halo[:, ::-1].transpose(1, 0, 2))
    both = in_order(mine, swap(mine, 1), 0)
    lead = jnp.concatenate([both, halo.reshape(edge * SUBS, width), jnp.zeros((8, width), BF16)], axis=0)
    normal_one = normed(lead.astype(F32), gain_one).astype(BF16)
    x_branch = nn(normal_one, proj_x, BF16)
    normal_one = normal_one[:rows]
    y_pre = nn(normal_one, proj_y)
    def over_sides(partial):
        partial = partial.reshape(2, own, width)
        other = lax.dynamic_index_in_dim(partial, 1 - side, 0, keepdims=False).astype(BF16)
        return lax.dynamic_index_in_dim(partial, side, 0, keepdims=False) + swap(other, 1).astype(F32)

    def exchanged(carry):
        every = lax.all_gather(carry, AXES, axis=0).reshape(pairs, 2, batch, quarters, half)
        every = lax.dynamic_index_in_dim(every, side, 1, keepdims=False)
        return every[:, :, 0], every[:, :, 1]

    def entering(enter, h):
        enter = enter.reshape(2, 2, SUBS, half)
        return enter[0] * jnp.repeat(h, quarters, axis=0)[None] + enter[1]

    def by_steps(v):
        return v.reshape(2, steps, SUBS, half)

    def span_gather(block):
        pieces = {0: block}
        for m in xs:
            pieces[m] = swap(block, m)
        for n in list(pieces):
            pieces[n ^ core] = swap(pieces[n], core)
        return [pieces[m * seqs] for m in range(spans)]

    def token_gather(v):
        blocks = [v] + [swap(v, m) for m in inner]
        return [b for block in blocks for b in (block, swap(block, 1))]

    c = to_rows(cotangent).astype(F32)
    if direct:
        (conv, recur, inject, decay, states, flow, mixed, resid), wides, narrows, cots, normal_two = recurrent(
            (spans, seqs), steps, quarters, heads, inner, x_branch, chan, gates, y_pre, out_half, mine, gain_two[None],
            grads_own, wide_own, narrow_own,
        )
    else:
        y_branch, gelu_back = jax.vjp(jax.nn.gelu, y_pre)
        kernel = functools.partial(forward_kernel, steps, quarters)
        full = ((rows, half), False)
        ends = ((4 * SUBS, half), False)
        conv, recur, inject, decay, local, prod, enter, carry = by_heads(
            kernel, heads, head_w, [(x_branch, False), (chan, False), (gates, True)],
            [full] * 6 + [ends, ((SUBS, half), False)],
        )
        prods, sums = exchanged(carry)
        h = jnp.zeros((batch, half), F32)
        for j in range(pairs - 1):
            h = jnp.where(j < pair, prods[j] * h + sums[j], h)
        entered = entering(enter, h)
        states = (by_steps(local) + by_steps(prod) * entered[:, None]).reshape(rows, half)
        flow = jnp.concatenate([entered, by_steps(prod)[:, -1]], axis=0).reshape(4 * SUBS, half)
        mixed = (states * y_branch).astype(BF16)
        resid = x + over_sides(nn(mixed, out_half))
        normal_two = by_span(normed(resid, gain_two).astype(BF16))
        wides, narrows = span_gather(wide_own), span_gather(narrow_own)
        cots = token_gather(grads_own)

    def token_scatter(near, far):
        total = None
        for k, m in enumerate((0, *inner)):
            block = near[k].astype(F32) + swap(far[k], 1).astype(F32)
            total = block if m == 0 else total + swap(block.astype(BF16), m).astype(F32)
        return by_span(total)

    if direct:
        normal_two_grad, near, far, all_normal, all_grads, all_act, all_hidden = feed_forward(
            (spans, seqs), [0, *inner], normal_two, cots, wides, narrows
        )
        normal_two_grad = by_span(normal_two_grad)
    else:
        wide, narrow = jnp.concatenate(wides, axis=1), jnp.concatenate(narrows, axis=1)
        all_normal = jnp.concatenate(token_gather(normal_two), axis=0)
        all_grads = jnp.concatenate(cots, axis=0)

        def activate(values):
            return jax.nn.gelu(values[:, :units]) * values[:, units:]

        value, back = jax.vjp(activate, nt(all_normal, wide))
        all_hidden = value.astype(BF16)
        all_act = back(nt(all_grads, narrow))[0].astype(BF16)

        def sided(v):
            v = v.reshape(len(inner) + 1, 2, own, width)
            return v[:, 0], v[:, 1]

        normal_two_grad = token_scatter(*sided(nn(all_act, wide, BF16)))
        near, far = sided(nn(all_hidden, narrow, BF16))
    size = width // spans

    def core_sum(left, right):
        def columns(odd):
            return jnp.concatenate([right[:, j * size : (j + 1) * size] for j in range(odd, spans, 2)], axis=1)

        recv = swap(tn(left, columns(1), BF16), core)
        total = tn(left, columns(0)) + recv.astype(F32)
        away = [total[:, k * size : (k + 1) * size].astype(BF16) for k in range(1, spans // 2)]
        return total[:, :size], jnp.stack(away)

    wide_kept, wide_away = core_sum(all_act, all_normal)
    narrow_kept, narrow_away = core_sum(all_hidden, all_grads)
    resid_part, gain_two_grad = norm_back(resid, gain_two, normal_two_grad)
    resid_grad = c + resid_part
    branch_low = resid_grad.astype(BF16)
    if direct:
        branch_low, y_grad, dx, spill, gate_grad, small_grad, down, wide_came, narrow_came = returned(
            (spans, seqs), steps, quarters, heads, inner, branch_low, out_half, y_pre, states, decay, flow, conv, recur, inject,
            x_branch, chan, gates, near, far, wide_away, narrow_away,
        )
        down = by_span(down)
    else:
        down = token_scatter(near, far)
        wide_came = jnp.stack([swap(wide_away[k], m) for k, m in enumerate(xs)])
        narrow_came = jnp.stack([swap(narrow_away[k], m) for k, m in enumerate(xs)])
        branch_low = in_order(branch_low, swap(branch_low, 1), 0)
        mixed_grad = nt(branch_low, out_half)
        y_grad = gelu_back(mixed_grad * states)[0].astype(BF16)
        kernel = functools.partial(adjoint_kernel, steps, quarters)
        local_adj, after, enter, carry = by_heads(
            kernel, heads, head_w, [(mixed_grad * y_branch, False), (decay, False), (flow, False)],
            [full, full, ends, ((SUBS, half), False)],
        )
        prods, sums = exchanged(carry)
        h = jnp.zeros((batch, half), F32)
        for j in range(pairs - 1, 0, -1):
            h = jnp.where(j > pair, prods[j] * h + sums[j], h)
        came = entering(enter, h).reshape(2 * SUBS, half)
        kernel = functools.partial(backward_kernel, steps, quarters)
        dx, spill, gate_grad, small_grad = by_heads(
            kernel, heads, head_w,
            [(v, False) for v in (local_adj, after, states, came, flow, conv, recur, inject, decay, x_branch, chan)]
            + [(gates, True)],
            [full, ((edge * SUBS, half), False), ((half, 2 * head_w), True), ((SUBS, half), False)],
        )
    output = from_rows((resid + down).astype(BF16))
    wide_owned = wide_kept + jnp.sum(wide_came.astype(F32), axis=0)
    wide_owned = wide_owned.reshape(2, units, size).transpose(2, 0, 1)
    narrow_owned = (narrow_kept + jnp.sum(narrow_came.astype(F32), axis=0)).T
    spill = lax.ppermute(
        spill.reshape(edge, batch, quarters, half)[::-1, :, 0], AXES, [(i, i - 2) for i in range(2, count)]
    )
    spill = jnp.pad(
        spill[:, :, None], ((0, 0), (0, 0), (quarters - 1, 0), (0, 0))
    ).reshape(edge * SUBS, half)
    x_grad = jnp.concatenate([dx[: rows - edge * SUBS], dx[rows - edge * SUBS :] + spill], axis=0).astype(BF16)

    normal_one_grad = over_sides(nt(y_grad, proj_y) + nt(x_grad, proj_x))
    input_part, gain_one_grad = norm_back(x, gain_one, normal_one_grad)
    input_grad = from_rows(resid_grad + input_part)

    def blocks_of(v, masks, wrap):
        size = 2 * share
        return [lax.dynamic_slice_in_dim(v, (me ^ m) // 2 % wrap * size, size, 0) for m in masks]

    def to_columns_owner(v_kept, v_given):
        recv = swap(v_given, core)
        n = len(inner) + 1
        total = (v_kept + recv.astype(F32)).reshape(len(xs) + 1, n, 2 * share, v_kept.shape[1])
        near = total[0]
        for k, m in enumerate(xs):
            near = near + swap(total[k + 1].astype(BF16), m).astype(F32)
        out = near[0]
        for k, m in enumerate(inner):
            out = out + swap(near[k + 1].astype(BF16), m).astype(F32)
        out = out.reshape(2, share, out.shape[1])
        other = lax.dynamic_index_in_dim(out, 1 - side, 0, keepdims=False).astype(BF16)
        return lax.dynamic_index_in_dim(out, side, 0, keepdims=False), swap(other, 1).astype(F32)

    def to_rows_owner(v_kept, v_given):
        cols = v_kept.shape[1]
        total = (v_kept + swap(v_given, core).astype(F32)).reshape(len(low_order), 2 * share, cols)
        away = cut(total, 1 - upper, cols // 2, 2).astype(BF16)
        near = cut(total, upper, cols // 2, 2) + swap(away, top).astype(F32)
        out = near[0]
        for k, m in enumerate(low_order[1:]):
            out = out + swap(near[k + 1].astype(BF16), m).astype(F32)
        other = swap(out.astype(BF16), top).astype(F32)
        out = in_order(out, other, 1).reshape(2, share, cols)
        gone = lax.dynamic_index_in_dim(out, 1 - side, 0, keepdims=False).astype(BF16)
        here = lax.dynamic_index_in_dim(out, side, 0, keepdims=False)
        return jnp.where(upper == side, here, swap(gone, 1).astype(F32))

    order = [m ^ n for m in (0, *xs) for n in (0, *inner)]
    low_order = [m ^ n for m in (0, *[v for v in xs if v < top]) for n in (0, *inner)]

    def ordered(v, masks, wrap):
        return [jnp.concatenate(blocks_of(v, [m ^ c for m in masks], wrap), axis=0) for c in (0, core)]

    kept_d, given_d = ordered(normal_one.T, order, pairs)
    kept_m, given_m = ordered(mixed.T, low_order, pairs // 2)
    by_row = jnp.concatenate([gate_grad, small_grad.T, jnp.zeros((half, head_w - SUBS), F32)], axis=1)
    kept_g, given_g = ordered(by_row, low_order, pairs // 2)
    gains = jnp.pad(jnp.stack([gain_one_grad, gain_two_grad], axis=1), ((0, 0), (0, 126)))
    kept_n, given_n = ordered(gains, order, pairs)
    if direct:
        proj_owned, out_owned, rest, gains = scatter_grads(
            (spans, seqs), kept_d, given_d, kept_m, given_m, x_grad, y_grad, branch_low, kept_g, given_g, kept_n, given_n
        )
    else:
        proj_owned = jnp.concatenate(
            [in_order(*to_columns_owner(nn(kept_d, g), nn(given_d, g, BF16)), 1) for g in (x_grad, y_grad)], axis=1
        )
        out_owned = to_rows_owner(nn(kept_m, branch_low), nn(given_m, branch_low, BF16))
        rest = to_rows_owner(kept_g, given_g.astype(BF16))
        gains = sum(to_columns_owner(kept_n, given_n.astype(BF16)))
    gate_owned, small_owned = rest[:, : 2 * head_w], rest[:, 2 * head_w : 2 * head_w + SUBS]

    return (
        output,
        input_grad,
        gains[:, 0],
        proj_owned,
        small_owned[:, :CONV],
        small_owned[:, 4],
        gate_owned,
        small_owned[:, 5:7],
        small_owned[:, 7] * jax.nn.sigmoid(decay_param.astype(F32)),
        out_owned,
        gains[:, 1],
        wide_owned,
        narrow_owned,
    )


def solution(mesh):
    both = ("span", "seq")
    tokens = P(None, both, None)
    placed = (
        tokens, P(both), P(both, None), P(both, None), P(both), P(both, None), P(both, None), P(both), P(both, None),
        P(both), P("span", None, "seq"), P("span", "seq"), tokens,
    )
    given = (
        tokens, tokens, P(both), P(both, None), P(both, None), P(both), P(both, None), P(both, None), P(both),
        P(both, None), P(both), P("span", None, "seq"), P("span", "seq"),
    )
    return jax.shard_map(on_device, mesh=mesh, in_specs=placed, out_specs=given, check_vma=False)
```

```python
import functools

import jax
import jax.numpy as jnp
from jax import lax
from jax.experimental import pallas as pl
from jax.experimental.pallas import tpu as pltpu
from jax.sharding import PartitionSpec as P

CONV = 4
EPS = 1e-06
AXES = ("span", "seq")
F32 = jnp.float32
BF16 = jnp.bfloat16
SUBS = 8


def swap(value, mask):
    count = lax.axis_size("span") * lax.axis_size("seq")
    return lax.ppermute(value, AXES, [(i, i ^ mask) for i in range(count)])


def dot(a, b, dims, out=F32):
    return lax.dot_general(a, b, ((dims[0], dims[1]), ((), ())), preferred_element_type=F32).astype(out)


def nn(a, b, out=F32):
    return dot(a, b, ((1,), (0,)), out)


def nt(a, b, out=F32):
    return dot(a, b, ((1,), (1,)), out)


def tn(a, b, out=F32):
    return dot(a, b, ((0,), (0,)), out)


def normed(v, gain):
    return v * lax.rsqrt(jnp.mean(v * v, axis=-1, keepdims=True) + EPS) * gain


def norm_back(v, gain, grad):
    scale = lax.rsqrt(jnp.mean(v * v, axis=-1, keepdims=True) + EPS)
    z = v * scale
    e = grad * gain
    return scale * (e - z * jnp.mean(e * z, axis=-1, keepdims=True)), jnp.sum(grad * z, axis=0)


def one_less_exp(u):
    series = 1.0 + u / 7.0
    for n in (6.0, 5.0, 4.0, 3.0, 2.0):
        series = 1.0 + u / n * series
    return jnp.where(u > -0.25, -u * series, 1.0 - jnp.exp(u))


def roll(v, by):
    return pltpu.roll(v, by % SUBS, 0)


def quarter_of(shape, quarters):
    return lax.broadcasted_iota(jnp.int32, shape, 0) % quarters


def spread(v, quarters, at):
    q = quarter_of(v.shape, quarters)
    held = jnp.where(q == at, v, 0.0)
    total = held
    for k in range(1, quarters):
        total = total + roll(held, k if at == 0 else -k)
    return total


def scan_carries(prods, sums, quarters, backward):
    q = quarter_of(prods[0].shape, quarters)
    sign = -1 if backward else 1
    order = (1, 0) if backward else (0, 1)
    place = quarters - 1 - q if backward else q
    whole = None
    enter = [None, None]
    for b in order:
        p, s = prods[b], sums[b]
        d = 1
        while d < quarters:
            pp, ss = roll(p, sign * d), roll(s, sign * d)
            ok = place >= d
            s = jnp.where(ok, p * ss + s, s)
            p = jnp.where(ok, p * pp, p)
            d *= 2
        first = place == 0
        ep = jnp.where(first, 1.0, roll(p, sign))
        es = jnp.where(first, 0.0, roll(s, sign))
        last = 0 if backward else quarters - 1
        tp, ts = spread(p, quarters, last), spread(s, quarters, last)
        if whole is None:
            enter[b] = (ep, es)
            whole = (tp, ts)
        else:
            enter[b] = (ep * whole[0], ep * whole[1] + es)
            whole = (tp * whole[0], tp * whole[1] + ts)
    return enter, whole


def earlier_rows(groups, halo, quarters, steps):
    q = quarter_of(groups[0].shape[1:], quarters)
    edge = CONV - 1
    out = []
    for b in (0, 1):
        ahead = []
        for k in range(edge, 0, -1):
            same = roll(groups[b][steps - k], 1)
            before = halo[k - 1] if b == 0 else roll(groups[0][steps - k], 1 - quarters)
            ahead.append(jnp.where(q == 0, before, same)[None])
        out.append(jnp.concatenate([*ahead, groups[b]], axis=0))
    return out


def forward_kernel(steps, quarters, xb, chan, gate, conv_o, recur_o, inject_o, decay_o, local_o, prod_o, enter_o, carry_o):
    rows = 2 * steps * SUBS
    width = xb.shape[1]
    head = xb[...].astype(F32)
    groups = [head[b * steps * SUBS : (b + 1) * steps * SUBS].reshape(steps, SUBS, width) for b in (0, 1)]
    halo = [head[rows + k * SUBS : rows + (k + 1) * SUBS] for k in range(CONV - 1)]
    edge = CONV - 1
    convs = []
    for ext in earlier_rows(groups, halo, quarters, steps):
        total = jnp.broadcast_to(chan[4:5][None], (steps, SUBS, width))
        for k in range(CONV):
            total = total + chan[k : k + 1][None] * ext[edge - k : edge - k + steps]
        convs.append(total.reshape(steps * SUBS, width))
    conv = jnp.concatenate(convs, axis=0)
    pre = jnp.dot(conv.astype(BF16), gate[...], preferred_element_type=F32)
    recur = jax.nn.sigmoid(pre[:, :width] + chan[5:6])
    inject = jax.nn.sigmoid(pre[:, width:] + chan[6:7])
    log_decay = -8.0 * recur * chan[7:8]
    decay = jnp.exp(log_decay)
    driven = jnp.sqrt(one_less_exp(2.0 * log_decay)) * inject * conv
    conv_o[...] = conv
    recur_o[...] = recur
    inject_o[...] = inject
    decay_o[...] = decay
    prods, sums = [], []
    for b in (0, 1):
        h = p = None
        for t in range(steps):
            at = (b * steps + t) * SUBS
            d, u = decay[at : at + SUBS], driven[at : at + SUBS]
            h = u if h is None else d * h + u
            p = d if p is None else d * p
            local_o[at : at + SUBS] = h
            prod_o[at : at + SUBS] = p
        prods.append(p)
        sums.append(h)
    enter, whole = scan_carries(prods, sums, quarters, False)
    for b in (0, 1):
        enter_o[b * SUBS : (b + 1) * SUBS] = enter[b][0]
        enter_o[(2 + b) * SUBS : (3 + b) * SUBS] = enter[b][1]
    q = quarter_of(whole[0].shape, quarters)
    carry_o[...] = jnp.where(q == 0, whole[0], whole[1])


def adjoint_kernel(steps, quarters, grad, decay, flow, local_o, after_o, enter_o, carry_o):
    prods, sums = [], []
    for b in (0, 1):
        g = r = None
        for t in range(steps - 1, -1, -1):
            at = (b * steps + t) * SUBS
            rows = slice(at, at + SUBS)
            a = grad[rows] if g is None else grad[rows] + g
            r = jnp.ones_like(a) if r is None else r * decay[at + SUBS : at + 2 * SUBS]
            local_o[rows] = a
            after_o[rows] = r
            g = decay[rows] * a
        prods.append(flow[(2 + b) * SUBS : (3 + b) * SUBS])
        sums.append(g)
    enter, whole = scan_carries(prods, sums, quarters, True)
    for b in (0, 1):
        enter_o[b * SUBS : (b + 1) * SUBS] = enter[b][0]
        enter_o[(2 + b) * SUBS : (3 + b) * SUBS] = enter[b][1]
    q = quarter_of(whole[0].shape, quarters)
    carry_o[...] = jnp.where(q == 0, whole[0], whole[1])


def backward_kernel(
    steps, quarters, local, after, states, came, entered, conv_r, recur_r, inject_r, decay_r, xb, chan, gate,
    dx_o, spill_o, gate_o, small_o,
):
    rows = 2 * steps * SUBS
    width = xb.shape[1]
    edge = CONV - 1
    block = steps * SUBS

    def by_step(v):
        return [v[b * block : (b + 1) * block].reshape(steps, SUBS, width) for b in (0, 1)]

    adjoint = jnp.concatenate(
        [
            (l + a * came[b * SUBS : (b + 1) * SUBS][None]).reshape(block, width)
            for b, (l, a) in enumerate(zip(by_step(local[...]), by_step(after[...])))
        ],
        axis=0,
    )
    earlier = jnp.concatenate(
        [
            jnp.concatenate([entered[b * SUBS : (b + 1) * SUBS], states[b * block : (b + 1) * block - SUBS]], axis=0)
            for b in (0, 1)
        ],
        axis=0,
    )
    conv, recur, inject, decay = conv_r[...], recur_r[...], inject_r[...], decay_r[...]
    rate = chan[7:8]
    mult = jnp.sqrt(one_less_exp(-16.0 * recur * rate))
    d_decay = adjoint * earlier
    d_log = d_decay * decay - adjoint * inject * conv * (decay * decay / mult)
    d_inject = adjoint * mult * conv
    d_conv = adjoint * mult * inject
    d_rate = jnp.sum(d_log * (-8.0 * recur), axis=0, keepdims=True)
    d_recur = d_log * (-8.0 * rate) * recur * (1.0 - recur)
    d_inject = d_inject * inject * (1.0 - inject)
    low = jnp.concatenate([d_recur.astype(BF16), d_inject.astype(BF16)], axis=1)
    d_conv = d_conv + lax.dot_general(low, gate[...], (((1,), (1,)), ((), ())), preferred_element_type=F32)
    gate_o[...] = lax.dot_general(conv.astype(BF16), low, (((0,), (0,)), ((), ())), preferred_element_type=F32)
    head = xb[...].astype(F32)
    halo = [head[rows + k * SUBS : rows + (k + 1) * SUBS] for k in range(edge)]
    exts = earlier_rows(by_step(head), halo, quarters, steps)
    groups = by_step(d_conv)
    for k in range(CONV):
        taps = sum(
            jnp.sum(groups[b] * exts[b][edge - k : edge - k + steps], axis=(0, 1), keepdims=True)[0] for b in (0, 1)
        )
        small_o[k : k + 1] = taps
    small_o[4:5] = jnp.sum(d_conv, axis=0, keepdims=True)
    small_o[5:6] = jnp.sum(d_recur, axis=0, keepdims=True)
    small_o[6:7] = jnp.sum(d_inject, axis=0, keepdims=True)
    small_o[7:8] = d_rate
    q = quarter_of((SUBS, width), quarters)
    for b in (0, 1):
        beyond = []
        for j in range(edge):
            same = roll(groups[b][j], -1)
            later = roll(groups[1][j], quarters - 1) if b == 0 else jnp.zeros_like(same)
            beyond.append(jnp.where(q == quarters - 1, later, same)[None])
        ext = jnp.concatenate([groups[b], *beyond], axis=0)
        total = chan[0:1][None] * ext[:steps]
        for k in range(1, CONV):
            total = total + chan[k : k + 1][None] * ext[k : k + steps]
        dx_o[b * block : (b + 1) * block] = total.reshape(block, width)
    for j in range(1, CONV):
        total = jnp.zeros((SUBS, width), F32)
        for k in range(j, CONV):
            total = total + chan[k : k + 1] * groups[0][k - j]
        spill_o[(j - 1) * SUBS : j * SUBS] = total


def by_heads(kernel, heads, head_w, arrays, outs):
    def spec(shape, tall):
        if tall:
            return pl.BlockSpec((head_w, shape[1]), lambda h: (h, 0))
        return pl.BlockSpec((shape[0], head_w), lambda h: (0, h))

    return pl.pallas_call(
        kernel,
        grid=(heads,),
        in_specs=[spec(a.shape, tall) for a, tall in arrays],
        out_specs=[spec(s, tall) for s, tall in outs],
        out_shape=[jax.ShapeDtypeStruct(s, F32) for s, _ in outs],
        compiler_params=pltpu.CompilerParams(vmem_limit_bytes=48 * 1024 * 1024),
    )(*[a for a, _ in arrays])


MESH = pl.DeviceIdType.MESH
VMEM_LIMIT = 60 * 1024 * 1024


class Links:
    def __init__(self, sizes, sends, recvs):
        self.spans, self.seqs = sizes
        self.span, self.seq = lax.axis_index("span"), lax.axis_index("seq")
        self.sends, self.recvs = sends, recvs
        self.used = 0
        self.open = []

    def flipped(self, index, mask):
        bit = 1
        while bit <= mask:
            if mask & bit:
                index = index + (1 - 2 * (index // bit % 2)) * bit
            bit *= 2
        return index

    def peer(self, mask):
        low, high = mask % self.seqs, mask // self.seqs
        return (self.flipped(self.span, high), self.flipped(self.seq, low))

    def other(self, mask):
        span, seq = self.peer(mask)
        return span * self.seqs + seq

    def greet(self, masks, others=()):
        barrier = pltpu.get_barrier_semaphore()
        for device in (*[self.peer(mask) for mask in masks], *others):
            pl.semaphore_signal(barrier, inc=1, device_id=device, device_id_type=MESH)
        pl.semaphore_wait(barrier, len(masks) + len(others))

    def plan(self, source, target, mask, only=None):
        slot = self.used
        self.used += 1
        copy = pltpu.make_async_remote_copy(
            source, target, self.sends.at[slot], self.recvs.at[slot], device_id=self.peer(mask), device_id_type=MESH
        )
        self.open.append((copy, only))
        return copy

    def send(self, source, target, mask, only=None):
        copy = self.plan(source, target, mask, only)
        if only is None:
            copy.start()
        else:
            pl.when(only)(copy.start)
        return copy

    def sent(self, copy):
        copy.wait_send()
        self.open = [(c, only) for c, only in self.open if c is not copy]

    def close(self):
        for copy, only in self.open:
            if only is None:
                copy.wait_send()
            else:
                pl.when(only)(copy.wait_send)


def in_turn(parts, order):
    for name in order:
        next(parts[name], None)
    for part in parts.values():
        for _ in part:
            pass


def gather_kernel(
    sizes, share, half, rec_proj, out_proj, gate_weight, small, tokens, wide, narrow,
    proj_x, proj_y, out_half, gates, every, tokens_o, wide_o, narrow_o, sends, recvs, locals_,
):
    links = Links(sizes, sends, recvs)
    spans, seqs = sizes
    count = spans * seqs
    me = links.span * seqs + links.seq
    side = me % 2
    upper = me // (count // 2)
    inner = [2 * k for k in range(1, seqs // 2)]
    core, top = seqs, count // 2
    double = 2 * share
    links.greet([1, *inner, core, top])
    kept = [0]

    def local(source, target, only=None):
        copy = pltpu.make_async_copy(source, target, locals_.at[kept[0]])
        kept[0] += 1
        if only is None:
            copy.start()
        else:
            pl.when(only)(copy.start)
        return copy

    def pieces_out(place, piece):
        over_inner = {m: links.send(piece(place(me)), piece(place(me)), m) for m in inner}
        over_top = {0: links.send(piece(place(me)), piece(place(me)), top)}
        over_core = [links.send(piece(place(me)), piece(place(me)), core)]
        yield
        for m in inner:
            over_inner[m].wait_recv()
            there = piece(place(links.other(m)))
            over_top[m] = links.send(there, there, top)
            over_core.append(links.send(there, there, core))
        yield
        for m in (0, *inner):
            over_top[m].wait_recv()
            there = piece(place(links.other(top + m)))
            over_core.append(links.send(there, there, core))
        yield
        for copy in over_core:
            copy.wait_recv()

    def columns_part(source, first, target):
        def piece(start):
            return target.at[pl.ds(pl.multiple_of(start, 16), double)]

        def columns(which):
            return source.at[:, pl.ds(pl.multiple_of(first + which * half, 128), half)]

        row = target.at[pl.ds(pl.multiple_of(me * share, 16), share)]
        mine = local(columns(side), row)
        theirs = links.send(columns(1 - side), row, 1)
        yield
        mine.wait()
        theirs.wait_recv()
        yield from pieces_out(lambda d: d // 2 * double, piece)

    def whole_part(source, target):
        height = source.shape[0]

        def piece(start):
            return target.at[pl.ds(pl.multiple_of(start, 16), 2 * height)]

        row = target.at[pl.ds(pl.multiple_of(me * height, 16), height)]
        mine = local(source, row)
        theirs = links.send(source, row, 1)
        yield
        mine.wait()
        theirs.wait_recv()
        yield from pieces_out(lambda d: d // 2 * 2 * height, piece)

    def rows_part(source, target):
        width = source.shape[1]
        pairs_half = count // 4

        def place(d):
            return d // 2 % pairs_half * double

        def rows(start, size):
            return target.at[pl.ds(pl.multiple_of(start, 16), size)]

        def piece(start, which):
            return target.at[pl.ds(pl.multiple_of(start, 16), double), pl.ds(pl.multiple_of(which * (width // 2), 128), width // 2)]

        holds = side == upper
        row = rows(place(me) + side * share, share)
        mine = local(source, row, holds)
        gift = links.send(source, row, 1, side != upper)
        yield

        @pl.when(holds)
        def _():
            mine.wait()
            gift.wait_recv()

        across = links.send(rows(place(me), double), rows(place(me), double), top, holds)
        pl.when(side != upper)(across.wait_recv)
        over_inner = {m: links.send(piece(place(me), upper), piece(place(me), upper), m) for m in inner}
        over_core = [links.send(rows(place(me), double), rows(place(me), double), core)]
        over_top = {}
        yield
        for m in inner:
            over_inner[m].wait_recv()
            there = piece(place(links.other(m)), upper)
            over_top[m] = links.send(there, there, top)
            over_core.append(links.send(there, there, core))
        yield
        for m in inner:
            over_top[m].wait_recv()
            there = piece(place(links.other(m)), 1 - upper)
            over_core.append(links.send(there, there, core))
        yield
        for copy in over_core:
            copy.wait_recv()

    parts = {
        "x": columns_part(rec_proj, 0, proj_x),
        "s": whole_part(small, every),
        "g": rows_part(gate_weight, gates),
        "y": columns_part(rec_proj, 2 * half, proj_y),
        "o": rows_part(out_proj, out_half),
    }
    in_turn(parts, "xsgxsgyoxyxogsygsygoyo")
    links.close()


def gather_weights(sizes, rec_proj, out_proj, gate_weight, small, tokens, wide, narrow):
    share = rec_proj.shape[0]
    half = rec_proj.shape[1] // 4
    count = sizes[0] * sizes[1]
    held = [
        (count * share, half), (count * share, half), (count // 2 * share, out_proj.shape[1]),
        (count // 2 * share, gate_weight.shape[1]), (count * small.shape[0], small.shape[1]),
        tokens.shape, wide.shape, narrow.shape,
    ]
    anywhere = pl.BlockSpec(memory_space=pl.ANY)
    copies = 5 * 16
    return pl.pallas_call(
        functools.partial(gather_kernel, sizes, share, half),
        in_specs=[anywhere] * 7,
        out_specs=[anywhere] * 8,
        out_shape=[jax.ShapeDtypeStruct(s, BF16) for s in held],
        scratch_shapes=[
            pltpu.SemaphoreType.DMA((copies,)), pltpu.SemaphoreType.DMA((copies,)), pltpu.SemaphoreType.DMA((8,))
        ],
        input_output_aliases={4: 5, 5: 6, 6: 7},
        compiler_params=pltpu.CompilerParams(collective_id=0, has_side_effects=True, vmem_limit_bytes=VMEM_LIMIT),
    )(rec_proj, out_proj, gate_weight, small, tokens, wide, narrow)


def scatter_kernel(
    sizes, share, turned, mixed, grad_x, grad_y, branch, gates, small, gain, x_own, gain_one, keep, part_own, part_other,
    proj_o, out_o, gate_o, input_o, sum_o, sends, recvs, from_part, vector, *bufs,
):
    links = Links(sizes, sends, recvs)
    spans, seqs = sizes
    count = spans * seqs
    me = links.span * seqs + links.seq
    side = me % 2
    upper = me // (count // 2)
    inner = [2 * k for k in range(1, seqs // 2)]
    core, top = seqs, count // 2
    double = 2 * share
    n = len(inner) + 1
    links.greet([1, *inner, core, top])
    whole = links.send(part_other, from_part, 1)

    def part(block, scratch, finish, shared=None):
        to_core, from_core, to_top, from_top, to_inner, from_inner, to_side, from_side = scratch
        if shared is not None:
            for copy in shared:
                links.sent(copy)
        crossing = [] if shared is None else shared
        crossing.clear()
        for i in range(2):
            for j in range(n):
                to_core[i * n + j] = block(1, (1 - i) * n + j).astype(BF16)
            crossing.append(links.send(to_core.at[pl.ds(i * n, n)], from_core.at[pl.ds(i * n, n)], core))
        mine = list(crossing)
        yield
        mine[0].wait_recv()
        over_top = {}
        for j in (*range(1, n), 0):
            to_top[j] = (block(0, n + j) + from_core[j].astype(F32)).astype(BF16)
            over_top[j] = links.send(to_top.at[j], from_top.at[j], top)
        mine[1].wait_recv()
        yield
        over_inner = []
        for j in range(1, n):
            over_top[j].wait_recv()
            to_inner[j - 1] = (block(0, j) + from_core[n + j].astype(F32) + from_top[j].astype(F32)).astype(BF16)
            over_inner.append(links.send(to_inner.at[j - 1], from_inner.at[j - 1], inner[j - 1]))
        over_top[0].wait_recv()
        yield
        total = block(0, 0) + from_core[n].astype(F32) + from_top[0].astype(F32)
        for j in range(1, n):
            over_inner[j - 1].wait_recv()
            total = total + from_inner[j - 1].astype(F32)
        yield from finish(total, to_side, from_side)

    def sided(total):
        low, high = total[:share], total[share:]
        first = side == 0
        return jnp.where(first, low, high), jnp.where(first, high, low)

    def by_columns(first, cols):
        def finish(total, to_side, from_side):
            mine, theirs = sided(total)
            to_side[...] = theirs.astype(BF16)
            copy = links.send(to_side, from_side, 1)
            yield
            copy.wait_recv()
            recv = from_side[...].astype(F32)
            proj_o[:, first : first + cols] = jnp.where(side == 0, mine, recv)
            proj_o[:, first + cols : first + 2 * cols] = jnp.where(side == 0, recv, mine)

        return finish

    def by_rows(target, to_last, from_last):
        cols = target.shape[1] // 2

        def finish(total, to_side, from_side):
            to_side[...] = total.astype(BF16)
            copy = links.send(to_side, from_side, top)
            yield
            copy.wait_recv()
            other = from_side[...].astype(F32)
            first = side == 0
            (low, low_far), (high, high_far) = sided(jnp.where(first, total, other)), sided(jnp.where(first, other, total))
            to_last[:, :cols] = low_far.astype(BF16)
            to_last[:, cols:] = high_far.astype(BF16)
            copy = links.send(to_last, from_last, 1)
            yield
            copy.wait_recv()
            holds = side == upper
            target[:, :cols] = jnp.where(holds, low, from_last[:, :cols].astype(F32))
            target[:, cols:] = jnp.where(holds, high, from_last[:, cols:].astype(F32))

        return finish

    def rows_of(c, j, whole):
        pairs = count // 2 if whole else count // 4
        owner = links.other(c * core + (j // n * top if whole else 0) + (0, *inner)[j % n])
        return pl.ds(pl.multiple_of(owner // 2 % pairs * double, 16), double)

    def columns_of(j, columns):
        return pl.ds(pl.multiple_of((upper if j < n else 1 - upper) * columns, 128), columns)

    def product(lhs, rhs):
        return lambda c, j: jnp.dot(lhs[rows_of(c, j, True)], rhs[...], preferred_element_type=F32)

    def product_half(lhs, rhs, columns):
        return lambda c, j: jnp.dot(lhs[rows_of(c, j, False)], rhs[:, columns_of(j, columns)], preferred_element_type=F32)

    def stored(blocks, columns):
        return lambda c, j: blocks[rows_of(c, j, False), columns_of(j, columns)]

    def sums():
        whole.wait_recv()
        few = 16
        own, width = x_own.shape
        vector[0] = jnp.zeros(vector.shape[1:], F32)
        vector[0, 1:2, :width] = gain[...]
        vector[0, :, width:] = small[...]

        @pl.loop(0, own // few)
        def _(k):
            here = pl.ds(pl.multiple_of(k * few, few), few)
            v = x_own[here].astype(F32)
            scale = lax.rsqrt(jnp.mean(v * v, axis=-1, keepdims=True) + EPS)
            z = v * scale
            d = part_own[here] + from_part[here].astype(F32)
            e = d * gain_one[...]
            input_o[here] = keep[here] + scale * (e - z * jnp.mean(e * z, axis=-1, keepdims=True))
            vector[0, 0:1, :width] += jnp.sum(d * z, axis=0, keepdims=True)

        slot = 1
        for masks in ([core], [top], inner):
            copies = [links.send(vector.at[0], vector.at[slot + k], m) for k, m in enumerate(masks)]
            yield
            for copy in copies:
                copy.wait_recv()
                links.sent(copy)
            total = vector[0]
            for k in range(len(masks)):
                total = total + vector[slot + k]
            vector[0] = total
            slot += len(masks)
        copy = links.send(vector.at[0], vector.at[slot], 1)
        yield
        copy.wait_recv()
        sum_o[:, :width] = vector[0, :, :width] + vector[slot, :, :width]
        sum_o[:, width:] = jnp.where(side == upper, vector[0, :, width:], vector[slot, :, width:])

    half = grad_x.shape[1]
    wide = branch.shape[1] // 2
    thin = gates.shape[1] // 2
    shared = []
    first = bufs[0]
    parts = {
        "y": part(product(turned, grad_y), [first, *bufs[1:8]], by_columns(2 * half, half), shared),
        "o": part(product_half(mixed, branch, wide), [first, *bufs[8:15]], by_rows(out_o, *bufs[15:17]), shared),
        "x": part(product(turned, grad_x), [first, *bufs[17:24]], by_columns(0, half), shared),
        "g": part(stored(gates, thin), bufs[24:32], by_rows(gate_o, *bufs[32:34])),
        "n": sums(),
    }
    in_turn(parts, "yoyxoyxgnoyxgnoygnoxoygnoxgnngg")
    links.close()


def scatter_grads(sizes, share, turned, mixed, grad_x, grad_y, branch, gates, small, gain, x_own, gain_one, keep, part_own, part_other):
    n = sizes[1] // 2
    half, wide, thin = grad_x.shape[1], branch.shape[1], gates.shape[1]
    own, width = x_own.shape
    double = 2 * share

    def scratch(cols, last, core=True):
        side = share if last is None else double
        shapes = [(2 * n, double, cols)] * (2 if core else 1) + [(n, double, cols)] * 2 + [(n - 1, double, cols)] * 2 + [(side, cols)] * 2
        if last is not None:
            shapes += [(share, last)] * 2
        return [pltpu.VMEM(s, BF16) for s in shapes]

    bufs = [*scratch(half, None), *scratch(wide // 2, wide, False), *scratch(half, None, False), *scratch(thin // 2, thin)]
    copies = 4 * (2 + n + (n - 1) + 2) + n + 4
    inside = pl.BlockSpec(memory_space=pltpu.VMEM)
    shapes = [(share, 4 * half), (share, wide), (share, thin), (own, width), (SUBS, width + half)]
    return pl.pallas_call(
        functools.partial(scatter_kernel, sizes, share),
        in_specs=[inside] * 13,
        out_specs=[inside] * 5,
        out_shape=[jax.ShapeDtypeStruct(s, F32) for s in shapes],
        scratch_shapes=[
            pltpu.SemaphoreType.DMA((copies,)), pltpu.SemaphoreType.DMA((copies,)), pltpu.VMEM((own, width), BF16),
            pltpu.VMEM((n + 3, SUBS, width + half), F32), *bufs,
        ],
        compiler_params=pltpu.CompilerParams(collective_id=1, has_side_effects=True, vmem_limit_bytes=VMEM_LIMIT),
    )(turned, mixed, grad_x, grad_y, branch, gates, small, gain, x_own, gain_one, keep, part_own, part_other)


def gelu_parts(v):
    root = 0.7978845608028654
    t = jnp.tanh(root * (v + 0.044715 * (v * v * v)))
    slope = 0.5 * (1.0 + t) + 0.5 * v * (1.0 - t * t) * root * (1.0 + 3.0 * 0.044715 * (v * v))
    return 0.5 * v * (1.0 + t), slope


def feed_kernel(sizes, masks, own, *refs):
    chunks = len(masks)
    spans = sizes[0]
    own_rows, refs = refs[0], refs[1:]
    cots, refs = refs[: 2 * chunks], refs[2 * chunks :]
    wides, refs = refs[:spans], refs[spans:]
    narrows, refs = refs[:spans], refs[spans:]
    grad_o, near_o, far_o, act_o, hidden_o, refs = *refs[:5], refs[5:]
    parts_o, refs = refs[: 2 + spans], refs[2 + spans :]
    (rows, cot, wide, narrow, act, hidden, near, down_near, down_far, to_side, from_side, to_inner, from_inner,
     sends, recvs, loads, stores) = refs
    units = narrow.shape[0]
    width = narrow.shape[1]
    size = width // spans
    pair = 2 * own
    links = Links(sizes, sends, recvs)

    def load(source, target, slot):
        copy = pltpu.make_async_copy(source, target, loads.at[slot])
        copy.start()
        return copy

    first = load(own_rows, rows.at[pl.ds(0, own)], 0)
    late = [load(cots[b], cot.at[pl.ds(b * own, own)], 1 + b) for b in range(2 * chunks)]
    for j in range(spans):
        columns = pl.ds(j * size, size)
        late.append(load(wides[j], wide.at[:, columns], 1 + 2 * chunks + j))
        late.append(load(narrows[j], narrow.at[:, columns], 1 + 2 * chunks + spans + j))
    links.greet([1, *masks[1:]])
    first.wait()

    def block(b):
        return rows.at[pl.ds(b * own, own)]

    each = range(chunks)
    over_side = [links.plan(block(2 * i), block(2 * i + 1), 1) for i in each]
    over_inner = [None] + [links.plan(block(0), block(2 * i), masks[i]) for i in each[1:]]
    back_side = [links.plan(to_side.at[i], from_side.at[i], 1) for i in each]
    back_inner = [links.plan(to_inner.at[i - 1], from_inner.at[i - 1], masks[i]) for i in each[1:]]
    over_side[0].start()
    over_inner[1].start()
    for copy in late:
        copy.wait()

    def onward(i):
        over_inner[i].wait_recv()
        over_side[i].start()
        if i + 1 < chunks:
            over_inner[i + 1].start()

    def give_on(i):
        back_side[i].wait_recv()
        to_inner[i - 1] = (near[i].astype(F32) + from_side[i].astype(F32)).astype(BF16)
        back_inner[i - 1].start()

    def ahead(i):
        over_side[i].wait_recv()
        if i == 0:
            onward(1)
        else:
            back_side[i - 1].start()

    def behind(i):
        if 0 < i < chunks - 1:
            onward(i + 1)
        if i == chunks - 1:
            back_side[i].start()
        if i > 1:
            give_on(i - 1)

    def compute(i):
        here = pl.ds(pl.multiple_of(i * pair, 16), pair)
        mine = rows[here]
        given = cot[here]
        start = 0
        while start < units:
            n = min(384, units - start)
            gate = lax.dot_general(mine, wide[start : start + n], (((1,), (1,)), ((), ())), preferred_element_type=F32)
            up = lax.dot_general(
                mine, wide[units + start : units + start + n], (((1,), (1,)), ((), ())), preferred_element_type=F32
            )
            back = lax.dot_general(given, narrow[start : start + n], (((1,), (1,)), ((), ())), preferred_element_type=F32)
            value, slope = gelu_parts(gate)
            hidden[here, start : start + n] = (value * up).astype(BF16)
            act[here, start : start + n] = (back * up * slope).astype(BF16)
            act[here, units + start : units + start + n] = (back * value).astype(BF16)
            start += n
        step = 512

        @pl.loop(0, width // step)
        def _(k):
            columns = pl.ds(pl.multiple_of(k * step, 128), step)
            total = jnp.dot(act[here], wide[:, columns], preferred_element_type=F32)
            near[i, :, columns] = total[:own].astype(BF16)
            to_side[i, :, columns] = total[own:].astype(BF16)
            total = jnp.dot(hidden[here], narrow[:, columns], preferred_element_type=F32)
            down_near[i, :, columns] = total[:own].astype(BF16)
            down_far[i, :, columns] = total[own:].astype(BF16)

    @pl.loop(0, chunks)
    def _(i):
        for k in range(chunks):
            pl.when(i == k)(functools.partial(ahead, k))
        compute(i)
        for k in range(chunks):
            pl.when(i == k)(functools.partial(behind, k))

    pairs = [(act, act_o), (hidden, hidden_o), (down_near, near_o), (down_far, far_o)]
    for k, source in enumerate((rows, cot)):
        for j in range(spans):
            target = parts_o[k * (1 + spans // 2) + (j // 2 if j % 2 == 0 else spans // 2)]
            if j % 2:
                target = target.at[:, pl.ds(j // 2 * size, size)]
            pairs.append((source.at[:, pl.ds(j * size, size)], target))
    out = []
    for k, (source, target) in enumerate(pairs):
        out.append(pltpu.make_async_copy(source, target, stores.at[k]))
        out[-1].start()
    give_on(chunks - 1)
    back_side[0].wait_recv()
    for k in range(chunks - 1):
        back_inner[k].wait_recv()
    for j in range(spans):
        columns = slice(j * size, (j + 1) * size)
        total = near[0, :, columns].astype(F32) + from_side[0, :, columns].astype(F32)
        for k in range(chunks - 1):
            total = total + from_inner[k, :, columns].astype(F32)
        grad_o[:, pl.ds(pl.multiple_of(links.flipped(links.span, j) * size, 128), size)] = total
    for copy in out:
        copy.wait()
    links.close()


def feed_forward(sizes, masks, own_rows, cots, wides, narrows):
    own, width = own_rows.shape
    units = narrows[0].shape[0]
    chunks = len(masks)
    total = 2 * chunks * own
    anywhere = pl.BlockSpec(memory_space=pl.ANY)
    copies = 4 * chunks
    blocks = (chunks, own, width)
    spans = sizes[0]
    features = [(total, width // spans)] * (spans // 2) + [(total, width // 2)]
    shapes = [blocks, blocks, (total, 2 * units), (total, units), *features, *features]
    held = [
        (total, width), (total, width), (2 * units, width), (units, width), (total, 2 * units), (total, units), blocks, blocks,
        blocks, blocks, blocks, (chunks - 1, own, width), (chunks - 1, own, width),
    ]
    return pl.pallas_call(
        functools.partial(feed_kernel, sizes, masks, own),
        in_specs=[anywhere] * (1 + 2 * chunks + 2 * len(wides)),
        out_specs=[pl.BlockSpec(memory_space=pltpu.VMEM)] + [anywhere] * len(shapes),
        out_shape=[jax.ShapeDtypeStruct((own, width), F32)] + [jax.ShapeDtypeStruct(s, BF16) for s in shapes],
        scratch_shapes=[pltpu.VMEM(s, BF16) for s in held]
        + [pltpu.SemaphoreType.DMA((k,)) for k in (copies, copies, 1 + 2 * chunks + 2 * len(wides), 4 + 2 * spans)],
        compiler_params=pltpu.CompilerParams(collective_id=2, has_side_effects=True, vmem_limit_bytes=VMEM_LIMIT),
    )(own_rows, *cots, *wides, *narrows)


def expanded(v, quarters):
    return spread(v, quarters, 0), spread(roll(v, -1), quarters, 0)


def chunk_inflow(links, line, blocks, quarters, backward, between):
    n, spans = line.shape[0], blocks.shape[0]
    place = links.seq // 2
    copies = [links.send(line.at[0], line.at[k], 2 * k) for k in range(1, n)]
    for copy in copies:
        copy.wait_recv()
    between()
    one, nought = jnp.ones(line.shape[1:], F32), jnp.zeros(line.shape[1:], F32)
    prod, total = one, nought
    all_prod, all_total = one, nought

    def ordered(count):
        return range(count - 1, -1, -1) if backward else range(count)

    def ahead(j, at):
        return at < j if backward else at > j

    for j in ordered(n):
        p, s = expanded(line[links.flipped(place, j)], quarters)
        inside = ahead(j, place)
        total = jnp.where(inside, p * total + s, total)
        prod = jnp.where(inside, p * prod, prod)
        all_total = p * all_total + s
        all_prod = p * all_prod
    q = quarter_of(line.shape[1:], quarters)
    blocks[0] = jnp.where(q == 0, all_prod, all_total)
    copies = [links.send(blocks.at[0], blocks.at[m], m * links.seqs) for m in range(1, spans)]
    for copy in copies:
        copy.wait_recv()
    h = nought
    for j in ordered(spans):
        p, s = expanded(blocks[links.flipped(links.span, j)], quarters)
        h = jnp.where(ahead(j, links.span), p * h + s, h)
    return prod * h + total


def by_head(heads, head_w, body):
    @pl.loop(0, heads)
    def _(h):
        start = pl.multiple_of(h * head_w, 128)
        columns = pl.ds(start, head_w)
        body(lambda ref: ref.at[:, columns], lambda ref: ref.at[pl.ds(start, head_w)])


def recur_kernel(
    sizes, steps, quarters, heads, inner, xb, chan, gate, y_pre, out_w, x_own, gain, cot, wide, narrow, *refs
):
    spans, seqs = sizes
    core, tops = seqs, [2 * seqs * k for k in range(1, spans // 2)]
    n = len(inner) + 1
    outs, refs = refs[: 8 + 2 * (spans - 1) + 2 * n], refs[8 + 2 * (spans - 1) + 2 * n :]
    conv, recur, inject, decay, states, flow_o, mixed, resid = outs[:8]
    wides, narrows = outs[8 : 7 + spans], outs[7 + spans : 6 + 2 * spans]
    cots, normal = outs[6 + 2 * spans : -1], outs[-1]
    prod, enter, line, blocks, inflow, to_side, from_side, low, sends, recvs = refs
    links = Links(sizes, sends, recvs)
    side = links.seq % 2
    own, width = x_own.shape
    rows = 2 * own
    masks = [1, *inner, *[m * seqs for m in range(1, spans)]]
    links.greet(masks)
    early = pl.ds(0, wide.shape[0] // 4)
    later = pl.ds(wide.shape[0] // 4, wide.shape[0] - wide.shape[0] // 4)
    across_wide = [links.send(wide.at[early], wides[m // seqs - 1].at[early], m) for m in tops]
    beside = [links.send(wide, wides[0], core), links.send(narrow, narrows[0], core)]
    over_inner = {m: links.plan(cot, cots[2 * k], m) for k, m in enumerate(inner)}
    over_side = [links.send(cot, cots[2 * len(inner)], 1)]
    head_w = gate.shape[1] // 2

    def gates(cols, tall):
        forward_kernel(
            steps, quarters, cols(xb), cols(chan), tall(gate), cols(conv), cols(recur), cols(inject), cols(decay),
            cols(states), cols(prod), cols(enter), cols(line.at[0]),
        )

    by_head(heads, head_w, gates)
    inflow[...] = chunk_inflow(
        links, line, blocks, quarters, False, lambda: [over_inner[m].start() for m in inner]
    )
    across_wide += [links.send(wide.at[later], wides[m // seqs - 1].at[later], m) for m in tops]
    across_narrow = {m: links.send(narrow, narrows[m // seqs - 1], m) for m in tops}
    block = steps * SUBS

    def mix(cols, tall):
        ins, flow, hold, gain_y = cols(inflow), cols(flow_o), cols(states), cols(y_pre)
        for b in (0, 1):
            entered = cols(enter)[b * SUBS : (b + 1) * SUBS] * ins[...] + cols(enter)[(2 + b) * SUBS : (3 + b) * SUBS]
            flow[b * SUBS : (b + 1) * SUBS] = entered
            flow[(2 + b) * SUBS : (3 + b) * SUBS] = cols(prod)[(b + 1) * block - SUBS : (b + 1) * block]
            here = slice(b * block, (b + 1) * block)
            total = hold[here].reshape(steps, SUBS, head_w) + cols(prod)[here].reshape(steps, SUBS, head_w) * entered[None]
            total = total.reshape(block, head_w)
            hold[here] = total
            cols(mixed)[here] = (total * gelu_parts(gain_y[here])[0]).astype(BF16)

    by_head(heads, head_w, mix)
    step = 512

    @pl.loop(0, width // step)
    def _(k):
        columns = pl.ds(pl.multiple_of(k * step, 128), step)
        total = jnp.dot(mixed[...], out_w[:, columns], preferred_element_type=F32)
        first = side == 0
        resid[:, columns] = x_own[:, columns].astype(F32) + jnp.where(first, total[:own], total[own:])
        to_side[:, columns] = jnp.where(first, total[own:], total[:own]).astype(BF16)

    partial = links.send(to_side, from_side, 1)
    partial.wait_recv()
    few = 16
    size = width // spans

    @pl.loop(0, own // few)
    def _(k):
        here = pl.ds(pl.multiple_of(k * few, few), few)
        total = resid[here] + from_side[here].astype(F32)
        resid[here] = total
        low[here] = normed(total, gain[...]).astype(BF16)

    for j in range(spans):
        start = pl.multiple_of(links.flipped(links.span, j) * size, 128)
        normal[:, j * size : (j + 1) * size] = low[:, pl.ds(start, size)]

    for k, m in enumerate(inner):
        over_inner[m].wait_recv()
        over_side.append(links.send(cots[2 * k], cots[2 * k + 1], 1))
    for copy in across_wide:
        copy.wait_recv()
    for m in tops:
        beside.append(links.send(wides[m // seqs - 1], wides[m // seqs], core))
    for m in tops:
        across_narrow[m].wait_recv()
        beside.append(links.send(narrows[m // seqs - 1], narrows[m // seqs], core))
    for copy in (*beside, *over_side):
        copy.wait_recv()
    links.close()


def recurrent(sizes, steps, quarters, heads, inner, xb, chan, gate, y_pre, out_w, x_own, gain, cot, wide, narrow):
    spans, seqs = sizes
    half = xb.shape[1]
    own, width = x_own.shape
    rows = 2 * own
    n = len(inner) + 1
    inside, anywhere = pl.BlockSpec(memory_space=pltpu.VMEM), pl.BlockSpec(memory_space=pl.ANY)
    full = jax.ShapeDtypeStruct((rows, half), F32)

    def low(shape):
        return jax.ShapeDtypeStruct(shape, BF16)

    shapes = [
        *[full] * 5, jax.ShapeDtypeStruct((4 * SUBS, half), F32), low((rows, half)), jax.ShapeDtypeStruct((own, width), F32),
        *[low(wide.shape)] * (spans - 1), *[low(narrow.shape)] * (spans - 1), *[low(cot.shape)] * (2 * n - 1), low((own, width)),
    ]
    copies = 3 * (spans // 2) * 2 + 2 * n + 2 + (n - 1) + spans
    end = (SUBS, half)
    outs = pl.pallas_call(
        functools.partial(recur_kernel, sizes, steps, quarters, heads, inner),
        in_specs=[inside] * 7 + [anywhere] * 3,
        out_specs=[inside] * 8 + [anywhere] * (len(shapes) - 9) + [inside],
        out_shape=shapes,
        scratch_shapes=[
            pltpu.VMEM((rows, half), F32), pltpu.VMEM((4 * SUBS, half), F32), pltpu.VMEM((n, *end), F32),
            pltpu.VMEM((spans, *end), F32), pltpu.VMEM(end, F32), *[pltpu.VMEM((own, width), BF16)] * 3,
            pltpu.SemaphoreType.DMA((copies,)), pltpu.SemaphoreType.DMA((copies,)),
        ],
        compiler_params=pltpu.CompilerParams(collective_id=3, has_side_effects=True, vmem_limit_bytes=VMEM_LIMIT),
    )(xb, chan, gate, y_pre, out_w, x_own, gain, cot, wide, narrow)
    wides, narrows = outs[8 : 7 + spans], outs[7 + spans : 6 + 2 * spans]
    received = outs[6 + 2 * spans : -1]
    near, far = [cot] + [received[2 * k] for k in range(n - 1)], [received[2 * (n - 1)]] + [received[2 * k + 1] for k in range(n - 1)]
    cots = [b for pair in zip(near, far) for b in pair]
    return outs[:8], [wide, *wides], [narrow, *narrows], cots, outs[-1]


def return_kernel(
    sizes, steps, quarters, heads, inner, branch, out_w, y_pre, states, decay, flow, conv, recur, inject, xb, chan, gate,
    resid, near, far, wide, narrow, branch_o, y_grad, x_grad, gate_o, small, output, wides, narrows, dx, spill, came_back, grad, local, after, enter, carry, line, blocks, inflow, dmix, from_side, to_inner, from_inner, sends, recvs,
):
    spans, seqs = sizes
    tops = [2 * seqs * k for k in range(1, spans // 2)]
    n = len(inner) + 1
    links = Links(sizes, sends, recvs)
    side = links.seq % 2
    own, width = branch.shape
    me, count = links.span * seqs + links.seq, spans * seqs

    def device(index):
        return (index // seqs, index % seqs)

    links.greet([1, *inner, *[m * seqs for m in range(1, spans)]], [device((me + 2) % count)])
    place = pl.ds(pl.multiple_of(side * own, 16), own)
    whole = links.send(branch, branch_o.at[place], 1)
    tall = wide.shape[1] // 2
    across = [links.send(wide.at[k, pl.ds(0, tall)], wides.at[k, pl.ds(0, tall)], m) for k, m in enumerate(tops)]
    branch_o[place] = branch[...]
    whole.wait_recv()
    sums = [*range(1, n), 0]
    over_side = {}

    def side_sum(i):
        over_side[sums[i]] = links.send(far.at[sums[i]], from_side.at[sums[i]], 1)

    over_inner = []

    def inner_sum(i):
        k = sums[i]
        over_side[k].wait_recv()
        if k:
            to_inner[k - 1] = (near[k].astype(F32) + from_side[k].astype(F32)).astype(BF16)
            over_inner.append(links.send(to_inner.at[k - 1], from_inner.at[k - 1], inner[k - 1]))

    side_sum(0)
    head_w = gate.shape[1] // 2

    def first(cols, tall):
        mixed_grad = lax.dot_general(branch_o[...], tall(out_w)[...], (((1,), (1,)), ((), ())), preferred_element_type=F32)
        value, slope = gelu_parts(cols(y_pre)[...])
        cols(grad)[...] = mixed_grad * value
        cols(y_grad)[...] = (mixed_grad * cols(states)[...] * slope).astype(BF16)
        adjoint_kernel(
            steps, quarters, cols(grad), cols(decay), cols(flow), cols(local), cols(after), cols(enter), cols(line.at[0])
        )

    by_head(heads, head_w, first)

    def between():
        inner_sum(0)
        side_sum(1)

    inflow[...] = chunk_inflow(links, line, blocks, quarters, True, between)
    for k, m in enumerate(tops):
        across.append(links.send(wide.at[k, pl.ds(tall, tall)], wides.at[k, pl.ds(tall, tall)], m))
        across.append(links.send(narrow.at[k], narrows.at[k], m))
    inner_sum(1)
    side_sum(2)

    def second(cols, tall):
        came = jnp.concatenate(
            [
                cols(enter)[b * SUBS : (b + 1) * SUBS] * cols(inflow)[...] + cols(enter)[(2 + b) * SUBS : (3 + b) * SUBS]
                for b in (0, 1)
            ],
            axis=0,
        )
        backward_kernel(
            steps, quarters, cols(local), cols(after), cols(states), came, cols(flow), cols(conv), cols(recur),
            cols(inject), cols(decay), cols(xb), cols(chan), tall(gate), cols(dx), cols(spill), tall(gate_o), cols(small),
        )

    by_head(heads, head_w, second)
    edge = (CONV - 1) * SUBS
    slot = links.used
    links.used += 1
    handed = pltpu.make_async_remote_copy(
        spill, came_back, links.sends.at[slot], links.recvs.at[slot], device_id=device(jnp.maximum(me - 2, 0)), device_id_type=MESH
    )
    pl.when(me >= 2)(handed.start)
    links.open.append((handed, me >= 2))
    rows = 2 * own
    x_grad[: rows - 2 * edge] = dx[: rows - 2 * edge].astype(BF16)
    for i in range(2, n):
        inner_sum(i)
        if i + 1 < n:
            side_sum(i + 1)
    pl.when(me + 2 < count)(handed.wait_recv)

    @pl.when(me + 2 >= count)
    def _():
        came_back[...] = jnp.zeros_like(came_back)

    last = quarter_of((SUBS, came_back.shape[1]), quarters) == quarters - 1
    total = [dx[rows - 2 * edge : rows - edge]]
    for k in range(CONV - 1, 0, -1):
        added = roll(came_back[(k - 1) * SUBS : k * SUBS], quarters - 1)
        total.append(dx[rows - k * SUBS : rows - (k - 1) * SUBS] + jnp.where(last, added, 0.0))
    x_grad[rows - 2 * edge :] = jnp.concatenate(total, axis=0).astype(BF16)
    few = 16
    size = width // spans
    for copy in over_inner:
        copy.wait_recv()

    for j in range(spans):
        columns = slice(j * size, (j + 1) * size)
        there = pl.ds(pl.multiple_of(links.flipped(links.span, j) * size, 128), size)
        total = resid[:, there] + near[0, :, columns].astype(F32) + from_side[0, :, columns].astype(F32)
        for k in range(n - 1):
            total = total + from_inner[k, :, columns].astype(F32)
        output[:, there] = total.astype(BF16)

    for copy in across:
        copy.wait_recv()
    links.close()


def returned(sizes, steps, quarters, heads, inner, branch, out_w, y_pre, states, decay, flow, conv, recur, inject, xb, chan, gate,
             resid, near, far, wide, narrow):
    spans, _ = sizes
    own, width = branch.shape
    rows, half = y_pre.shape
    n = len(inner) + 1
    inside, anywhere = pl.BlockSpec(memory_space=pltpu.VMEM), pl.BlockSpec(memory_space=pl.ANY)

    def high(*shape):
        return jax.ShapeDtypeStruct(shape, F32)

    def low(*shape):
        return jax.ShapeDtypeStruct(shape, BF16)

    shapes = [
        low(rows, width), low(rows, half), low(rows, half), high(*gate.shape), high(SUBS, half), low(own, width),
        low(*wide.shape), low(*narrow.shape),
    ]
    end = (SUBS, half)
    copies = 3 * (spans // 2) + 2 * n + 2 * n + spans + 2
    tail = ((CONV - 1) * SUBS, half)
    return pl.pallas_call(
        functools.partial(return_kernel, sizes, steps, quarters, heads, inner),
        in_specs=[inside] * 15 + [anywhere] * 2,
        out_specs=[inside] * 6 + [anywhere] * 2,
        out_shape=shapes,
        scratch_shapes=[
            pltpu.VMEM((rows, half), F32), pltpu.VMEM(tail, F32), pltpu.VMEM(tail, F32), *[pltpu.VMEM((rows, half), F32)] * 3, pltpu.VMEM((4 * SUBS, half), F32), pltpu.VMEM(end, F32),
            pltpu.VMEM((n, *end), F32), pltpu.VMEM((spans, *end), F32), pltpu.VMEM(end, F32), pltpu.VMEM(end, F32),
            pltpu.VMEM((n, own, width), BF16), pltpu.VMEM((n - 1, own, width), BF16), pltpu.VMEM((n - 1, own, width), BF16),
            pltpu.SemaphoreType.DMA((copies,)), pltpu.SemaphoreType.DMA((copies,)),
        ],
        compiler_params=pltpu.CompilerParams(collective_id=4, has_side_effects=True, vmem_limit_bytes=VMEM_LIMIT),
    )(branch, out_w, y_pre, states, decay, flow, conv, recur, inject, xb, chan, gate, resid, near, far, wide, narrow)


def on_device(
    inputs, norm_one, rec_proj, conv_weight, conv_bias, gate_weight, gate_bias, decay_param, out_proj, norm_two,
    mlp_wide, mlp_narrow, cotangent,
):
    spans, seqs = lax.axis_size("span"), lax.axis_size("seq")
    count = spans * seqs
    span, seq = lax.axis_index("span"), lax.axis_index("seq")
    me = span * seqs + seq
    side = me % 2
    pair = me // 2
    pairs = count // 2
    batch, tokens, width = inputs.shape
    half = width // 2
    quarters = SUBS // batch
    steps = tokens // quarters
    own = batch * tokens
    rows = 2 * own
    head_w = gate_weight.shape[1] // 2
    heads = half // head_w
    edge = CONV - 1
    share = width // count
    units = mlp_narrow.shape[1]
    inner = [2 * k for k in range(1, seqs // 2)]
    core = seqs
    xs = [2 * seqs * k for k in range(1, spans // 2)]
    top = count // 2
    upper = me // top

    def to_rows(v):
        return v.reshape(batch, quarters, steps, width).transpose(2, 0, 1, 3).reshape(own, width)

    def from_rows(v):
        return v.reshape(steps, batch, quarters, width).transpose(1, 2, 0, 3).reshape(batch, tokens, width)

    def in_order(mine, other, axis):
        return jnp.concatenate([jnp.where(side == 0, mine, other), jnp.where(side == 0, other, mine)], axis=axis)

    def cut(v, index, size, axis):
        return lax.dynamic_slice_in_dim(v, index * size, size, axis)

    direct = share % 16 == 0 and spans == 4

    def gathered_rows(block, buffer, place):
        pieces = {0: block}
        for m in inner:
            pieces[m] = swap(block, m)
        for m in xs:
            for n in (0, *inner):
                pieces[m ^ n] = swap(pieces[n], m)
        for n in list(pieces):
            pieces[core ^ n] = swap(pieces[n], core)
        for m, piece in pieces.items():
            buffer = lax.dynamic_update_slice_in_dim(buffer, piece, place(me ^ m), 0)
        return buffer

    def columns_half(block):
        mine, theirs = cut(block, side, half, 1), cut(block, 1 - side, half, 1)
        block = in_order(mine, swap(theirs, 1), 0)
        return gathered_rows(block, jnp.zeros((width, half), BF16), lambda d: d // 2 * 2 * share)

    def rows_half(block):
        full = lax.all_gather(block, AXES, axis=0, tiled=True)
        return cut(full, side, half, 0)

    def by_span(v):
        size = width // spans
        return jnp.concatenate([cut(v, span ^ j, size, 1) for j in range(spans)], axis=1)

    small = jnp.stack([norm_one, norm_two, *conv_weight.T, conv_bias, *gate_bias.T, decay_param])
    wide_own = mlp_wide.transpose(1, 2, 0).reshape(2 * units, width // spans)
    narrow_own = mlp_narrow.T
    grads_own = by_span(to_rows(cotangent))
    if direct:
        packed = jnp.pad(small, ((0, 6), (0, -share % 128)))
        proj_x, proj_y, out_half, gates, small, grads_own, wide_own, narrow_own = gather_weights(
            (spans, seqs), rec_proj, out_proj, gate_weight, packed, grads_own, wide_own, narrow_own
        )
        small = small.reshape(count, 16, -1)[:, :10, :share].transpose(1, 0, 2).reshape(10, width)
    else:
        proj_x = columns_half(rec_proj[:, :width])
        proj_y = columns_half(rec_proj[:, width:])
        gates = rows_half(gate_weight)
        out_half = rows_half(out_proj)
        small = lax.all_gather(small, AXES, axis=1, tiled=True)
    small = small.astype(F32)
    gain_one, gain_two = small[0], small[1]
    chan = cut(jnp.concatenate([small[2:9], jax.nn.softplus(small[9:10])], axis=0), side, half, 1)

    mine = to_rows(inputs)
    x = mine.astype(F32)
    tail = inputs[:, tokens - edge :]
    halo = lax.ppermute(tail, AXES, [(i, i + 1) for i in range(1, count - 1, 2)]) + lax.ppermute(
        tail, AXES, [(i, i + 2) for i in range(1, count - 2, 2)]
    )
    halo = jnp.zeros((edge, batch, quarters, width), BF16).at[:, :, 0].set(halo[:, ::-1].transpose(1, 0, 2))
    both = in_order(mine, swap(mine, 1), 0)
    lead = jnp.concatenate([both, halo.reshape(edge * SUBS, width), jnp.zeros((8, width), BF16)], axis=0)
    normal_one = normed(lead.astype(F32), gain_one).astype(BF16)
    x_branch = nn(normal_one, proj_x, BF16)
    normal_one = normal_one[:rows]
    y_pre = nn(normal_one, proj_y)
    def over_sides(partial):
        partial = partial.reshape(2, own, width)
        other = lax.dynamic_index_in_dim(partial, 1 - side, 0, keepdims=False).astype(BF16)
        return lax.dynamic_index_in_dim(partial, side, 0, keepdims=False) + swap(other, 1).astype(F32)

    def exchanged(carry):
        every = lax.all_gather(carry, AXES, axis=0).reshape(pairs, 2, batch, quarters, half)
        every = lax.dynamic_index_in_dim(every, side, 1, keepdims=False)
        return every[:, :, 0], every[:, :, 1]

    def entering(enter, h):
        enter = enter.reshape(2, 2, SUBS, half)
        return enter[0] * jnp.repeat(h, quarters, axis=0)[None] + enter[1]

    def by_steps(v):
        return v.reshape(2, steps, SUBS, half)

    def span_gather(block):
        pieces = {0: block}
        for m in xs:
            pieces[m] = swap(block, m)
        for n in list(pieces):
            pieces[n ^ core] = swap(pieces[n], core)
        return [pieces[m * seqs] for m in range(spans)]

    def token_gather(v):
        blocks = [v] + [swap(v, m) for m in inner]
        return [b for block in blocks for b in (block, swap(block, 1))]

    c = to_rows(cotangent).astype(F32)
    if direct:
        (conv, recur, inject, decay, states, flow, mixed, resid), wides, narrows, cots, normal_two = recurrent(
            (spans, seqs), steps, quarters, heads, inner, x_branch, chan, gates, y_pre, out_half, mine, gain_two[None],
            grads_own, wide_own, narrow_own,
        )
    else:
        y_branch, gelu_back = jax.vjp(jax.nn.gelu, y_pre)
        kernel = functools.partial(forward_kernel, steps, quarters)
        full = ((rows, half), False)
        ends = ((4 * SUBS, half), False)
        conv, recur, inject, decay, local, prod, enter, carry = by_heads(
            kernel, heads, head_w, [(x_branch, False), (chan, False), (gates, True)],
            [full] * 6 + [ends, ((SUBS, half), False)],
        )
        prods, sums = exchanged(carry)
        h = jnp.zeros((batch, half), F32)
        for j in range(pairs - 1):
            h = jnp.where(j < pair, prods[j] * h + sums[j], h)
        entered = entering(enter, h)
        states = (by_steps(local) + by_steps(prod) * entered[:, None]).reshape(rows, half)
        flow = jnp.concatenate([entered, by_steps(prod)[:, -1]], axis=0).reshape(4 * SUBS, half)
        mixed = (states * y_branch).astype(BF16)
        resid = x + over_sides(nn(mixed, out_half))
        normal_two = by_span(normed(resid, gain_two).astype(BF16))
        wides, narrows = span_gather(wide_own), span_gather(narrow_own)
        cots = token_gather(grads_own)

    def token_scatter(near, far):
        total = None
        for k, m in enumerate((0, *inner)):
            block = near[k].astype(F32) + swap(far[k], 1).astype(F32)
            total = block if m == 0 else total + swap(block.astype(BF16), m).astype(F32)
        return by_span(total)

    size = width // spans

    def by_core(v):
        blocks = [v[:, j * size : (j + 1) * size] for j in range(spans)]
        return [*blocks[::2], jnp.concatenate(blocks[1::2], axis=1)]

    if direct:
        normal_two_grad, near, far, all_act, all_hidden, *features = feed_forward(
            (spans, seqs), [0, *inner], normal_two, cots, wides, narrows
        )
        all_normal, all_grads = features[: 1 + spans // 2], features[1 + spans // 2 :]
    else:
        wide, narrow = jnp.concatenate(wides, axis=1), jnp.concatenate(narrows, axis=1)
        all_normal = jnp.concatenate(token_gather(normal_two), axis=0)
        all_grads = jnp.concatenate(cots, axis=0)

        def activate(values):
            return jax.nn.gelu(values[:, :units]) * values[:, units:]

        value, back = jax.vjp(activate, nt(all_normal, wide))
        all_hidden = value.astype(BF16)
        all_act = back(nt(all_grads, narrow))[0].astype(BF16)

        def sided(v):
            v = v.reshape(len(inner) + 1, 2, own, width)
            return v[:, 0], v[:, 1]

        all_normal, all_grads = by_core(all_normal), by_core(all_grads)
        normal_two_grad = token_scatter(*sided(nn(all_act, wide, BF16)))
        near, far = sided(nn(all_hidden, narrow, BF16))
    def core_sum(left, right):
        recv = swap(tn(left, right[-1], BF16), core).astype(F32)
        total = [tn(left, v) + recv[:, k * size : (k + 1) * size] for k, v in enumerate(right[:-1])]
        return total[0], jnp.stack([v.astype(BF16) for v in total[1:]])

    wide_kept, wide_away = core_sum(all_act, all_normal)
    narrow_kept, narrow_away = core_sum(all_hidden, all_grads)
    resid_part, gain_two_grad = norm_back(resid, gain_two, normal_two_grad)
    resid_grad = c + resid_part
    branch_low = resid_grad.astype(BF16)
    if direct:
        branch_low, y_grad, x_grad, gate_grad, small_grad, output, wide_came, narrow_came = returned(
            (spans, seqs), steps, quarters, heads, inner, branch_low, out_half, y_pre, states, decay, flow, conv, recur, inject,
            x_branch, chan, gates, resid, near, far, wide_away, narrow_away,
        )
    else:
        output = (resid + token_scatter(near, far)).astype(BF16)
        wide_came = jnp.stack([swap(wide_away[k], m) for k, m in enumerate(xs)])
        narrow_came = jnp.stack([swap(narrow_away[k], m) for k, m in enumerate(xs)])
        branch_low = in_order(branch_low, swap(branch_low, 1), 0)
        mixed_grad = nt(branch_low, out_half)
        y_grad = gelu_back(mixed_grad * states)[0].astype(BF16)
        kernel = functools.partial(adjoint_kernel, steps, quarters)
        local_adj, after, enter, carry = by_heads(
            kernel, heads, head_w, [(mixed_grad * y_branch, False), (decay, False), (flow, False)],
            [full, full, ends, ((SUBS, half), False)],
        )
        prods, sums = exchanged(carry)
        h = jnp.zeros((batch, half), F32)
        for j in range(pairs - 1, 0, -1):
            h = jnp.where(j > pair, prods[j] * h + sums[j], h)
        came = entering(enter, h).reshape(2 * SUBS, half)
        kernel = functools.partial(backward_kernel, steps, quarters)
        dx, spill, gate_grad, small_grad = by_heads(
            kernel, heads, head_w,
            [(v, False) for v in (local_adj, after, states, came, flow, conv, recur, inject, decay, x_branch, chan)]
            + [(gates, True)],
            [full, ((edge * SUBS, half), False), ((half, 2 * head_w), True), ((SUBS, half), False)],
        )
        spill = lax.ppermute(
            spill.reshape(edge, batch, quarters, half)[::-1, :, 0], AXES, [(i, i - 2) for i in range(2, count)]
        )
        spill = jnp.pad(
            spill[:, :, None], ((0, 0), (0, 0), (quarters - 1, 0), (0, 0))
        ).reshape(edge * SUBS, half)
        x_grad = jnp.concatenate([dx[: rows - edge * SUBS], dx[rows - edge * SUBS :] + spill], axis=0).astype(BF16)
    output = from_rows(output)
    wide_owned = wide_kept + jnp.sum(wide_came.astype(F32), axis=0)
    wide_owned = wide_owned.reshape(2, units, size).transpose(2, 0, 1)
    narrow_owned = (narrow_kept + jnp.sum(narrow_came.astype(F32), axis=0)).T
    normal_one_part = nt(y_grad, proj_y) + nt(x_grad, proj_x)

    def blocks_of(v, masks, wrap):
        size = 2 * share
        return [lax.dynamic_slice_in_dim(v, (me ^ m) // 2 % wrap * size, size, 0) for m in masks]

    def to_columns_owner(v_kept, v_given):
        recv = swap(v_given, core)
        n = len(inner) + 1
        total = (v_kept + recv.astype(F32)).reshape(len(xs) + 1, n, 2 * share, v_kept.shape[1])
        near = total[0]
        for k, m in enumerate(xs):
            near = near + swap(total[k + 1].astype(BF16), m).astype(F32)
        out = near[0]
        for k, m in enumerate(inner):
            out = out + swap(near[k + 1].astype(BF16), m).astype(F32)
        out = out.reshape(2, share, out.shape[1])
        other = lax.dynamic_index_in_dim(out, 1 - side, 0, keepdims=False).astype(BF16)
        return lax.dynamic_index_in_dim(out, side, 0, keepdims=False), swap(other, 1).astype(F32)

    def to_rows_owner(v_kept, v_given):
        cols = v_kept.shape[1]
        total = (v_kept + swap(v_given, core).astype(F32)).reshape(len(low_order), 2 * share, cols)
        away = cut(total, 1 - upper, cols // 2, 2).astype(BF16)
        near = cut(total, upper, cols // 2, 2) + swap(away, top).astype(F32)
        out = near[0]
        for k, m in enumerate(low_order[1:]):
            out = out + swap(near[k + 1].astype(BF16), m).astype(F32)
        other = swap(out.astype(BF16), top).astype(F32)
        out = in_order(out, other, 1).reshape(2, share, cols)
        gone = lax.dynamic_index_in_dim(out, 1 - side, 0, keepdims=False).astype(BF16)
        here = lax.dynamic_index_in_dim(out, side, 0, keepdims=False)
        return jnp.where(upper == side, here, swap(gone, 1).astype(F32))

    order = [m ^ n for m in (0, *xs) for n in (0, *inner)]
    low_order = [m ^ n for m in (0, *[v for v in xs if v < top]) for n in (0, *inner)]

    def ordered(v, masks, wrap):
        return [jnp.concatenate(blocks_of(v, [m ^ c for m in masks], wrap), axis=0) for c in (0, core)]

    if direct:
        part = normal_one_part.reshape(2, own, width)
        proj_owned, out_owned, gate_owned, input_grad, sums = scatter_grads(
            (spans, seqs), share, normal_one.T, mixed.T, x_grad, y_grad, branch_low, gate_grad, small_grad, gain_two_grad[None],
            mine, gain_one[None], resid_grad, lax.dynamic_index_in_dim(part, side, 0, keepdims=False),
            lax.dynamic_index_in_dim(part, 1 - side, 0, keepdims=False).astype(BF16),
        )
        gains = cut(sums[:2, :width], me, share, 1).T
        small_owned = cut(sums[:, width:], me % (count // 2), share, 1).T
    else:
        input_part, gain_one_grad = norm_back(x, gain_one, over_sides(normal_one_part))
        input_grad = resid_grad + input_part
        kept_d, given_d = ordered(normal_one.T, order, pairs)
        kept_m, given_m = ordered(mixed.T, low_order, pairs // 2)
        by_row = jnp.concatenate([gate_grad, small_grad.T, jnp.zeros((half, head_w - SUBS), F32)], axis=1)
        kept_g, given_g = ordered(by_row, low_order, pairs // 2)
        gains = jnp.pad(jnp.stack([gain_one_grad, gain_two_grad], axis=1), ((0, 0), (0, 126)))
        kept_n, given_n = ordered(gains, order, pairs)
        proj_owned = jnp.concatenate(
            [in_order(*to_columns_owner(nn(kept_d, g), nn(given_d, g, BF16)), 1) for g in (x_grad, y_grad)], axis=1
        )
        out_owned = to_rows_owner(nn(kept_m, branch_low), nn(given_m, branch_low, BF16))
        rest = to_rows_owner(kept_g, given_g.astype(BF16))
        gate_owned, small_owned = rest[:, : 2 * head_w], rest[:, 2 * head_w : 2 * head_w + SUBS]
        gains = sum(to_columns_owner(kept_n, given_n.astype(BF16)))
    input_grad = from_rows(input_grad)

    return (
        output,
        input_grad,
        gains[:, 0],
        proj_owned,
        small_owned[:, :CONV],
        small_owned[:, 4],
        gate_owned,
        small_owned[:, 5:7],
        small_owned[:, 7] * jax.nn.sigmoid(decay_param.astype(F32)),
        out_owned,
        gains[:, 1],
        wide_owned,
        narrow_owned,
    )


def solution(mesh):
    both = ("span", "seq")
    tokens = P(None, both, None)
    placed = (
        tokens, P(both), P(both, None), P(both, None), P(both), P(both, None), P(both, None), P(both), P(both, None),
        P(both), P("span", None, "seq"), P("span", "seq"), tokens,
    )
    given = (
        tokens, tokens, P(both), P(both, None), P(both, None), P(both), P(both, None), P(both, None), P(both),
        P(both, None), P(both), P("span", None, "seq"), P("span", "seq"),
    )
    return jax.shard_map(on_device, mesh=mesh, in_specs=placed, out_specs=given, check_vma=False)
```

```python
import functools

import jax
import jax.numpy as jnp
from jax import lax
from jax.experimental import pallas as pl
from jax.experimental.pallas import tpu as pltpu
from jax.sharding import PartitionSpec as P

CONV = 4
EPS = 1e-06
AXES = ("span", "seq")
F32 = jnp.float32
BF16 = jnp.bfloat16
SUBS = 8


def swap(value, mask):
    count = lax.axis_size("span") * lax.axis_size("seq")
    return lax.ppermute(value, AXES, [(i, i ^ mask) for i in range(count)])


def dot(a, b, dims, out=F32):
    return lax.dot_general(a, b, ((dims[0], dims[1]), ((), ())), preferred_element_type=F32).astype(out)


def nn(a, b, out=F32):
    return dot(a, b, ((1,), (0,)), out)


def nt(a, b, out=F32):
    return dot(a, b, ((1,), (1,)), out)


def tn(a, b, out=F32):
    return dot(a, b, ((0,), (0,)), out)


def normed(v, gain):
    return v * lax.rsqrt(jnp.mean(v * v, axis=-1, keepdims=True) + EPS) * gain


def norm_back(v, gain, grad):
    scale = lax.rsqrt(jnp.mean(v * v, axis=-1, keepdims=True) + EPS)
    z = v * scale
    e = grad * gain
    return scale * (e - z * jnp.mean(e * z, axis=-1, keepdims=True)), jnp.sum(grad * z, axis=0)


def one_less_exp(u):
    series = 1.0 + u / 7.0
    for n in (6.0, 5.0, 4.0, 3.0, 2.0):
        series = 1.0 + u / n * series
    return jnp.where(u > -0.25, -u * series, 1.0 - jnp.exp(u))


def roll(v, by):
    return pltpu.roll(v, by % SUBS, 0)


def quarter_of(shape, quarters):
    return lax.broadcasted_iota(jnp.int32, shape, 0) % quarters


def spread(v, quarters, at):
    q = quarter_of(v.shape, quarters)
    held = jnp.where(q == at, v, 0.0)
    total = held
    for k in range(1, quarters):
        total = total + roll(held, k if at == 0 else -k)
    return total


def scan_carries(prods, sums, quarters, backward):
    q = quarter_of(prods[0].shape, quarters)
    sign = -1 if backward else 1
    order = (1, 0) if backward else (0, 1)
    place = quarters - 1 - q if backward else q
    whole = None
    enter = [None, None]
    for b in order:
        p, s = prods[b], sums[b]
        d = 1
        while d < quarters:
            pp, ss = roll(p, sign * d), roll(s, sign * d)
            ok = place >= d
            s = jnp.where(ok, p * ss + s, s)
            p = jnp.where(ok, p * pp, p)
            d *= 2
        first = place == 0
        ep = jnp.where(first, 1.0, roll(p, sign))
        es = jnp.where(first, 0.0, roll(s, sign))
        last = 0 if backward else quarters - 1
        tp, ts = spread(p, quarters, last), spread(s, quarters, last)
        if whole is None:
            enter[b] = (ep, es)
            whole = (tp, ts)
        else:
            enter[b] = (ep * whole[0], ep * whole[1] + es)
            whole = (tp * whole[0], tp * whole[1] + ts)
    return enter, whole


def earlier_rows(groups, halo, quarters, steps):
    q = quarter_of(groups[0].shape[1:], quarters)
    edge = CONV - 1
    out = []
    for b in (0, 1):
        ahead = []
        for k in range(edge, 0, -1):
            same = roll(groups[b][steps - k], 1)
            before = halo[k - 1] if b == 0 else roll(groups[0][steps - k], 1 - quarters)
            ahead.append(jnp.where(q == 0, before, same)[None])
        out.append(jnp.concatenate([*ahead, groups[b]], axis=0))
    return out


def forward_kernel(steps, quarters, xb, chan, gate, conv_o, recur_o, inject_o, decay_o, local_o, prod_o, enter_o, carry_o):
    rows = 2 * steps * SUBS
    width = xb.shape[1]
    head = xb[...].astype(F32)
    groups = [head[b * steps * SUBS : (b + 1) * steps * SUBS].reshape(steps, SUBS, width) for b in (0, 1)]
    halo = [head[rows + k * SUBS : rows + (k + 1) * SUBS] for k in range(CONV - 1)]
    edge = CONV - 1
    convs = []
    for ext in earlier_rows(groups, halo, quarters, steps):
        total = jnp.broadcast_to(chan[4:5][None], (steps, SUBS, width))
        for k in range(CONV):
            total = total + chan[k : k + 1][None] * ext[edge - k : edge - k + steps]
        convs.append(total.reshape(steps * SUBS, width))
    conv = jnp.concatenate(convs, axis=0)
    pre = jnp.dot(conv.astype(BF16), gate[...], preferred_element_type=F32)
    recur = jax.nn.sigmoid(pre[:, :width] + chan[5:6])
    inject = jax.nn.sigmoid(pre[:, width:] + chan[6:7])
    log_decay = -8.0 * recur * chan[7:8]
    decay = jnp.exp(log_decay)
    driven = jnp.sqrt(one_less_exp(2.0 * log_decay)) * inject * conv
    conv_o[...] = conv
    recur_o[...] = recur
    inject_o[...] = inject
    decay_o[...] = decay
    prods, sums = [], []
    for b in (0, 1):
        h = p = None
        for t in range(steps):
            at = (b * steps + t) * SUBS
            d, u = decay[at : at + SUBS], driven[at : at + SUBS]
            h = u if h is None else d * h + u
            p = d if p is None else d * p
            local_o[at : at + SUBS] = h
            prod_o[at : at + SUBS] = p
        prods.append(p)
        sums.append(h)
    enter, whole = scan_carries(prods, sums, quarters, False)
    for b in (0, 1):
        enter_o[b * SUBS : (b + 1) * SUBS] = enter[b][0]
        enter_o[(2 + b) * SUBS : (3 + b) * SUBS] = enter[b][1]
    q = quarter_of(whole[0].shape, quarters)
    carry_o[...] = jnp.where(q == 0, whole[0], whole[1])


def adjoint_kernel(steps, quarters, grad, decay, flow, local_o, after_o, enter_o, carry_o):
    prods, sums = [], []
    for b in (0, 1):
        g = r = None
        for t in range(steps - 1, -1, -1):
            at = (b * steps + t) * SUBS
            rows = slice(at, at + SUBS)
            a = grad[rows] if g is None else grad[rows] + g
            r = jnp.ones_like(a) if r is None else r * decay[at + SUBS : at + 2 * SUBS]
            local_o[rows] = a
            after_o[rows] = r
            g = decay[rows] * a
        prods.append(flow[(2 + b) * SUBS : (3 + b) * SUBS])
        sums.append(g)
    enter, whole = scan_carries(prods, sums, quarters, True)
    for b in (0, 1):
        enter_o[b * SUBS : (b + 1) * SUBS] = enter[b][0]
        enter_o[(2 + b) * SUBS : (3 + b) * SUBS] = enter[b][1]
    q = quarter_of(whole[0].shape, quarters)
    carry_o[...] = jnp.where(q == 0, whole[0], whole[1])


def backward_kernel(
    steps, quarters, local, after, states, came, entered, conv_r, recur_r, inject_r, decay_r, xb, chan, gate,
    dx_o, spill_o, gate_o, small_o,
):
    rows = 2 * steps * SUBS
    width = xb.shape[1]
    edge = CONV - 1
    block = steps * SUBS

    def by_step(v):
        return [v[b * block : (b + 1) * block].reshape(steps, SUBS, width) for b in (0, 1)]

    adjoint = jnp.concatenate(
        [
            (l + a * came[b * SUBS : (b + 1) * SUBS][None]).reshape(block, width)
            for b, (l, a) in enumerate(zip(by_step(local[...]), by_step(after[...])))
        ],
        axis=0,
    )
    earlier = jnp.concatenate(
        [
            jnp.concatenate([entered[b * SUBS : (b + 1) * SUBS], states[b * block : (b + 1) * block - SUBS]], axis=0)
            for b in (0, 1)
        ],
        axis=0,
    )
    conv, recur, inject, decay = conv_r[...], recur_r[...], inject_r[...], decay_r[...]
    rate = chan[7:8]
    mult = jnp.sqrt(one_less_exp(-16.0 * recur * rate))
    d_decay = adjoint * earlier
    d_log = d_decay * decay - adjoint * inject * conv * (decay * decay / mult)
    d_inject = adjoint * mult * conv
    d_conv = adjoint * mult * inject
    d_rate = jnp.sum(d_log * (-8.0 * recur), axis=0, keepdims=True)
    d_recur = d_log * (-8.0 * rate) * recur * (1.0 - recur)
    d_inject = d_inject * inject * (1.0 - inject)
    low = jnp.concatenate([d_recur.astype(BF16), d_inject.astype(BF16)], axis=1)
    d_conv = d_conv + lax.dot_general(low, gate[...], (((1,), (1,)), ((), ())), preferred_element_type=F32)
    gate_o[...] = lax.dot_general(conv.astype(BF16), low, (((0,), (0,)), ((), ())), preferred_element_type=F32)
    head = xb[...].astype(F32)
    halo = [head[rows + k * SUBS : rows + (k + 1) * SUBS] for k in range(edge)]
    exts = earlier_rows(by_step(head), halo, quarters, steps)
    groups = by_step(d_conv)
    for k in range(CONV):
        taps = sum(
            jnp.sum(groups[b] * exts[b][edge - k : edge - k + steps], axis=(0, 1), keepdims=True)[0] for b in (0, 1)
        )
        small_o[k : k + 1] = taps
    small_o[4:5] = jnp.sum(d_conv, axis=0, keepdims=True)
    small_o[5:6] = jnp.sum(d_recur, axis=0, keepdims=True)
    small_o[6:7] = jnp.sum(d_inject, axis=0, keepdims=True)
    small_o[7:8] = d_rate
    q = quarter_of((SUBS, width), quarters)
    for b in (0, 1):
        beyond = []
        for j in range(edge):
            same = roll(groups[b][j], -1)
            later = roll(groups[1][j], quarters - 1) if b == 0 else jnp.zeros_like(same)
            beyond.append(jnp.where(q == quarters - 1, later, same)[None])
        ext = jnp.concatenate([groups[b], *beyond], axis=0)
        total = chan[0:1][None] * ext[:steps]
        for k in range(1, CONV):
            total = total + chan[k : k + 1][None] * ext[k : k + steps]
        dx_o[b * block : (b + 1) * block] = total.reshape(block, width)
    for j in range(1, CONV):
        total = jnp.zeros((SUBS, width), F32)
        for k in range(j, CONV):
            total = total + chan[k : k + 1] * groups[0][k - j]
        spill_o[(j - 1) * SUBS : j * SUBS] = total


def by_heads(kernel, heads, head_w, arrays, outs):
    def spec(shape, tall):
        if tall:
            return pl.BlockSpec((head_w, shape[1]), lambda h: (h, 0))
        return pl.BlockSpec((shape[0], head_w), lambda h: (0, h))

    return pl.pallas_call(
        kernel,
        grid=(heads,),
        in_specs=[spec(a.shape, tall) for a, tall in arrays],
        out_specs=[spec(s, tall) for s, tall in outs],
        out_shape=[jax.ShapeDtypeStruct(s, F32) for s, _ in outs],
        compiler_params=pltpu.CompilerParams(vmem_limit_bytes=48 * 1024 * 1024),
    )(*[a for a, _ in arrays])


MESH = pl.DeviceIdType.MESH
VMEM_LIMIT = 60 * 1024 * 1024


class Links:
    def __init__(self, sizes, sends, recvs):
        self.spans, self.seqs = sizes
        self.span, self.seq = lax.axis_index("span"), lax.axis_index("seq")
        self.sends, self.recvs = sends, recvs
        self.used = 0
        self.open = []

    def flipped(self, index, mask):
        bit = 1
        while bit <= mask:
            if mask & bit:
                index = index + (1 - 2 * (index // bit % 2)) * bit
            bit *= 2
        return index

    def flipped_index(self, index, mask):
        return self.flipped(index, mask)

    def peer(self, mask):
        low, high = mask % self.seqs, mask // self.seqs
        return (self.flipped(self.span, high), self.flipped(self.seq, low))

    def other(self, mask):
        span, seq = self.peer(mask)
        return span * self.seqs + seq

    def greet(self, masks, others=()):
        barrier = pltpu.get_barrier_semaphore()
        for device in (*[self.peer(mask) for mask in masks], *others):
            pl.semaphore_signal(barrier, inc=1, device_id=device, device_id_type=MESH)
        pl.semaphore_wait(barrier, len(masks) + len(others))

    def plan(self, source, target, mask, only=None, device=None):
        slot = self.used
        self.used += 1
        device = self.peer(mask) if device is None else device
        copy = pltpu.make_async_remote_copy(
            source, target, self.sends.at[slot], self.recvs.at[slot], device_id=device, device_id_type=MESH
        )
        self.open.append((copy, only))
        return copy

    def send(self, source, target, mask, only=None):
        copy = self.plan(source, target, mask, only)
        if only is None:
            copy.start()
        else:
            pl.when(only)(copy.start)
        return copy

    def sent(self, copy):
        copy.wait_send()
        self.open = [(c, only) for c, only in self.open if c is not copy]

    def close(self):
        for copy, only in self.open:
            if only is None:
                copy.wait_send()
            else:
                pl.when(only)(copy.wait_send)


def in_turn(parts, order):
    for name in order:
        next(parts[name], None)
    for part in parts.values():
        for _ in part:
            pass


def scatter_kernel(
    sizes, share, turned, mixed, grad_x, grad_y, branch, gates, small, gain, x_own, gain_one, keep, part_own, part_other,
    proj_o, out_o, gate_o, input_o, sum_o, sends, recvs, from_part, vector, *bufs,
):
    links = Links(sizes, sends, recvs)
    spans, seqs = sizes
    count = spans * seqs
    me = links.span * seqs + links.seq
    side = me % 2
    upper = me // (count // 2)
    inner = [2 * k for k in range(1, seqs // 2)]
    core, top = seqs, count // 2
    double = 2 * share
    n = len(inner) + 1
    links.greet([1, *inner, core, top])
    whole = links.send(part_other, from_part, 1)

    def part(block, scratch, finish, shared=None):
        to_core, from_core, to_top, from_top, to_inner, from_inner, to_side, from_side = scratch
        if shared is not None:
            for copy in shared:
                links.sent(copy)
        crossing = [] if shared is None else shared
        crossing.clear()
        for i in range(2):
            for j in range(n):
                to_core[i * n + j] = block(1, (1 - i) * n + j).astype(BF16)
            crossing.append(links.send(to_core.at[pl.ds(i * n, n)], from_core.at[pl.ds(i * n, n)], core))
        mine = list(crossing)
        yield
        mine[0].wait_recv()
        over_top = {}
        for j in (*range(1, n), 0):
            to_top[j] = (block(0, n + j) + from_core[j].astype(F32)).astype(BF16)
            over_top[j] = links.send(to_top.at[j], from_top.at[j], top)
        mine[1].wait_recv()
        yield
        over_inner = []
        for j in range(1, n):
            over_top[j].wait_recv()
            to_inner[j - 1] = (block(0, j) + from_core[n + j].astype(F32) + from_top[j].astype(F32)).astype(BF16)
            over_inner.append(links.send(to_inner.at[j - 1], from_inner.at[j - 1], inner[j - 1]))
        over_top[0].wait_recv()
        yield
        total = block(0, 0) + from_core[n].astype(F32) + from_top[0].astype(F32)
        for j in range(1, n):
            over_inner[j - 1].wait_recv()
            total = total + from_inner[j - 1].astype(F32)
        yield from finish(total, to_side, from_side)

    def sided(total):
        low, high = total[:share], total[share:]
        first = side == 0
        return jnp.where(first, low, high), jnp.where(first, high, low)

    def by_columns(first, cols):
        def finish(total, to_side, from_side):
            mine, theirs = sided(total)
            to_side[...] = theirs.astype(BF16)
            copy = links.send(to_side, from_side, 1)
            yield
            copy.wait_recv()
            recv = from_side[...].astype(F32)
            proj_o[:, first : first + cols] = jnp.where(side == 0, mine, recv)
            proj_o[:, first + cols : first + 2 * cols] = jnp.where(side == 0, recv, mine)

        return finish

    def by_rows(target, to_last, from_last):
        cols = target.shape[1] // 2

        def finish(total, to_side, from_side):
            to_side[...] = total.astype(BF16)
            copy = links.send(to_side, from_side, top)
            yield
            copy.wait_recv()
            other = from_side[...].astype(F32)
            first = side == 0
            (low, low_far), (high, high_far) = sided(jnp.where(first, total, other)), sided(jnp.where(first, other, total))
            to_last[:, :cols] = low_far.astype(BF16)
            to_last[:, cols:] = high_far.astype(BF16)
            copy = links.send(to_last, from_last, 1)
            yield
            copy.wait_recv()
            holds = side == upper
            target[:, :cols] = jnp.where(holds, low, from_last[:, :cols].astype(F32))
            target[:, cols:] = jnp.where(holds, high, from_last[:, cols:].astype(F32))

        return finish

    def rows_of(c, j, whole):
        pairs = count // 2 if whole else count // 4
        owner = links.other(c * core + (j // n * top if whole else 0) + (0, *inner)[j % n])
        return pl.ds(pl.multiple_of(owner // 2 % pairs * double, 16), double)

    def columns_of(j, columns):
        return pl.ds(pl.multiple_of((upper if j < n else 1 - upper) * columns, 128), columns)

    def product(lhs, rhs):
        return lambda c, j: jnp.dot(lhs[rows_of(c, j, True)], rhs[...], preferred_element_type=F32)

    def product_half(lhs, rhs, columns):
        return lambda c, j: jnp.dot(lhs[rows_of(c, j, False)], rhs[:, columns_of(j, columns)], preferred_element_type=F32)

    def stored(blocks, columns):
        return lambda c, j: blocks[rows_of(c, j, False), columns_of(j, columns)]

    def sums():
        whole.wait_recv()
        few = 16
        own, width = x_own.shape
        vector[0] = jnp.zeros(vector.shape[1:], F32)
        vector[0, 1:2, :width] = gain[...]
        vector[0, :, width:] = small[...]

        @pl.loop(0, own // few)
        def _(k):
            here = pl.ds(pl.multiple_of(k * few, few), few)
            v = x_own[here].astype(F32)
            scale = lax.rsqrt(jnp.mean(v * v, axis=-1, keepdims=True) + EPS)
            z = v * scale
            d = part_own[here] + from_part[here].astype(F32)
            e = d * gain_one[...]
            input_o[here] = keep[here] + scale * (e - z * jnp.mean(e * z, axis=-1, keepdims=True))
            vector[0, 0:1, :width] += jnp.sum(d * z, axis=0, keepdims=True)

        slot = 1
        for masks in ([core], [top], inner):
            copies = [links.send(vector.at[0], vector.at[slot + k], m) for k, m in enumerate(masks)]
            yield
            for copy in copies:
                copy.wait_recv()
                links.sent(copy)
            total = vector[0]
            for k in range(len(masks)):
                total = total + vector[slot + k]
            vector[0] = total
            slot += len(masks)
        copy = links.send(vector.at[0], vector.at[slot], 1)
        yield
        copy.wait_recv()
        sum_o[:, :width] = vector[0, :, :width] + vector[slot, :, :width]
        sum_o[:, width:] = jnp.where(side == upper, vector[0, :, width:], vector[slot, :, width:])

    half = grad_x.shape[1]
    wide = branch.shape[1] // 2
    thin = gates.shape[1] // 2
    shared = []
    first = bufs[0]
    parts = {
        "y": part(product(turned, grad_y), [first, *bufs[1:8]], by_columns(2 * half, half), shared),
        "o": part(product_half(mixed, branch, wide), [first, *bufs[8:15]], by_rows(out_o, *bufs[15:17]), shared),
        "x": part(product(turned, grad_x), [first, *bufs[17:24]], by_columns(0, half), shared),
        "g": part(stored(gates, thin), bufs[24:32], by_rows(gate_o, *bufs[32:34])),
        "n": sums(),
    }
    in_turn(parts, "yoyxoyxgnoyxgnoygnoxoygnoxgnngg")
    links.close()


def scatter_grads(sizes, share, turned, mixed, grad_x, grad_y, branch, gates, small, gain, x_own, gain_one, keep, part_own, part_other):
    n = sizes[1] // 2
    half, wide, thin = grad_x.shape[1], branch.shape[1], gates.shape[1]
    own, width = x_own.shape
    double = 2 * share

    def scratch(cols, last, core=True):
        side = share if last is None else double
        shapes = [(2 * n, double, cols)] * (2 if core else 1) + [(n, double, cols)] * 2 + [(n - 1, double, cols)] * 2 + [(side, cols)] * 2
        if last is not None:
            shapes += [(share, last)] * 2
        return [pltpu.VMEM(s, BF16) for s in shapes]

    bufs = [*scratch(half, None), *scratch(wide // 2, wide, False), *scratch(half, None, False), *scratch(thin // 2, thin)]
    copies = 4 * (2 + n + (n - 1) + 2) + n + 4
    inside = pl.BlockSpec(memory_space=pltpu.VMEM)
    shapes = [(share, 4 * half), (share, wide), (share, thin), (own, width), (SUBS, width + half)]
    return pl.pallas_call(
        functools.partial(scatter_kernel, sizes, share),
        in_specs=[inside] * 13,
        out_specs=[inside] * 5,
        out_shape=[jax.ShapeDtypeStruct(s, F32) for s in shapes],
        scratch_shapes=[
            pltpu.SemaphoreType.DMA((copies,)), pltpu.SemaphoreType.DMA((copies,)), pltpu.VMEM((own, width), BF16),
            pltpu.VMEM((n + 3, SUBS, width + half), F32), *bufs,
        ],
        compiler_params=pltpu.CompilerParams(collective_id=1, has_side_effects=True, vmem_limit_bytes=VMEM_LIMIT),
    )(turned, mixed, grad_x, grad_y, branch, gates, small, gain, x_own, gain_one, keep, part_own, part_other)


def gelu_parts(v):
    root = 0.7978845608028654
    t = jnp.tanh(root * (v + 0.044715 * (v * v * v)))
    slope = 0.5 * (1.0 + t) + 0.5 * v * (1.0 - t * t) * root * (1.0 + 3.0 * 0.044715 * (v * v))
    return 0.5 * v * (1.0 + t), slope


def feed_kernel(sizes, masks, own, *refs):
    chunks = len(masks)
    spans = sizes[0]
    own_rows, refs = refs[0], refs[1:]
    cots, refs = refs[0], refs[1:]
    wides, refs = refs[:spans], refs[spans:]
    narrows, refs = refs[:2], refs[2:]
    grad_o, near_o, far_o, act_o, hidden_o, refs = *refs[:5], refs[5:]
    parts_o, refs = refs[: 2 + spans], refs[2 + spans :]
    (rows, cot, wide, narrow, act, hidden, near, down_near, down_far, to_side, from_side, to_inner, from_inner,
     sends, recvs, loads, stores) = refs
    units = narrow.shape[0]
    width = narrow.shape[1]
    size = width // spans
    pair = 2 * own
    links = Links(sizes, sends, recvs)

    def load(source, target, slot):
        copy = pltpu.make_async_copy(source, target, loads.at[slot])
        copy.start()
        return copy

    first = load(own_rows, rows.at[pl.ds(0, own)], 0)
    late = [
        load(cots.at[links.flipped(links.seq // 2, masks[b // 2] // 2), b % 2], cot.at[pl.ds(b * own, own)], 1 + b)
        for b in range(2 * chunks)
    ]
    for j in range(spans):
        columns = pl.ds(j * size, size)
        late.append(load(wides[j], wide.at[:, columns], 1 + 2 * chunks + j))
        if j < 2:
            late.append(load(narrows[j], narrow.at[:, columns], 1 + 2 * chunks + spans + j))
    core, tops = sizes[1], range(2, spans, 2)
    links.greet([1, *masks[1:], core, *[m * core for m in tops]])
    first.wait()
    across = [links.send(narrows[0], narrow.at[:, pl.ds(m * size, size)], m * core) for m in tops]

    def block(b):
        return rows.at[pl.ds(b * own, own)]

    each = range(chunks)
    over_side = [links.plan(block(2 * i), block(2 * i + 1), 1) for i in each]
    over_inner = [None] + [links.plan(block(0), block(2 * i), masks[i]) for i in each[1:]]
    back_side = [links.plan(to_side.at[i], from_side.at[i], 1) for i in each]
    back_inner = [links.plan(to_inner.at[i - 1], from_inner.at[i - 1], masks[i]) for i in each[1:]]
    over_side[0].start()
    for i in each[1:]:
        over_inner[i].start()
    for copy in late:
        copy.wait()
    beside = [links.plan(narrow.at[:, pl.ds(m * size, size)], narrow.at[:, pl.ds((m + 1) * size, size)], core) for m in tops]

    def narrow_here():
        for copy, onto in zip(across, beside):
            copy.wait_recv()
            onto.start()
        for copy in beside:
            copy.wait_recv()

    def onward(i):
        over_inner[i].wait_recv()
        over_side[i].start()

    def give_on(i):
        back_side[i].wait_recv()
        to_inner[i - 1] = (near[i].astype(F32) + from_side[i].astype(F32)).astype(BF16)
        back_inner[i - 1].start()

    last = chunks - 1

    def ahead(i):
        over_side[i].wait_recv()
        if i == 0:
            for k in (2, 1):
                if k < last:
                    onward(k)
            narrow_here()

    def midway(i):
        if i == min(1, last - 1):
            for k in range(3, chunks):
                onward(k)
        if i == last:
            give_on(1)

    def behind(i):
        if 0 < i < last - 1:
            back_side[i].start()
        if i == last:
            for k in (last, last - 1, 0):
                back_side[k].start()

    def compute(i):
        here = pl.ds(pl.multiple_of(i * pair, 16), pair)
        mine = rows[here]
        given = cot[here]
        start = 0
        while start < units:
            n = min(384, units - start)
            gate = lax.dot_general(mine, wide[start : start + n], (((1,), (1,)), ((), ())), preferred_element_type=F32)
            up = lax.dot_general(
                mine, wide[units + start : units + start + n], (((1,), (1,)), ((), ())), preferred_element_type=F32
            )
            back = lax.dot_general(given, narrow[start : start + n], (((1,), (1,)), ((), ())), preferred_element_type=F32)
            value, slope = gelu_parts(gate)
            hidden[here, start : start + n] = (value * up).astype(BF16)
            act[here, start : start + n] = (back * up * slope).astype(BF16)
            act[here, units + start : units + start + n] = (back * value).astype(BF16)
            start += n
        for k in range(chunks):
            pl.when(i == k)(functools.partial(midway, k))
        step = 512

        @pl.loop(0, width // step)
        def _(k):
            columns = pl.ds(pl.multiple_of(k * step, 128), step)
            total = jnp.dot(act[here], wide[:, columns], preferred_element_type=F32)
            near[i, :, columns] = total[:own].astype(BF16)
            to_side[i, :, columns] = total[own:].astype(BF16)
            total = jnp.dot(hidden[here], narrow[:, columns], preferred_element_type=F32)
            down_near[i, :, columns] = total[:own].astype(BF16)
            down_far[i, :, columns] = total[own:].astype(BF16)

    @pl.loop(0, chunks)
    def _(i):
        for k in range(chunks):
            pl.when(i == k)(functools.partial(ahead, k))
        compute(i)
        for k in range(chunks):
            pl.when(i == k)(functools.partial(behind, k))

    pairs = [(act, act_o), (hidden, hidden_o), (down_near, near_o), (down_far, far_o)]
    for k, source in enumerate((rows, cot)):
        for j in range(spans):
            target = parts_o[k * (1 + spans // 2) + (j // 2 if j % 2 == 0 else spans // 2)]
            if j % 2:
                target = target.at[:, pl.ds(j // 2 * size, size)]
            pairs.append((source.at[:, pl.ds(j * size, size)], target))
    out = []
    for k, (source, target) in enumerate(pairs):
        out.append(pltpu.make_async_copy(source, target, stores.at[k]))
        out[-1].start()
    for k in range(last, 1, -1):
        give_on(k)
    back_side[0].wait_recv()
    for k in range(chunks - 1):
        back_inner[k].wait_recv()
    for j in range(spans):
        columns = slice(j * size, (j + 1) * size)
        total = near[0, :, columns].astype(F32) + from_side[0, :, columns].astype(F32)
        for k in range(chunks - 1):
            total = total + from_inner[k, :, columns].astype(F32)
        grad_o[:, pl.ds(pl.multiple_of(links.flipped(links.span, j) * size, 128), size)] = total
    for copy in out:
        copy.wait()
    links.close()


def feed_forward(sizes, masks, own_rows, cots, wides, narrows):
    own, width = own_rows.shape
    units = narrows[0].shape[0]
    chunks = len(masks)
    total = 2 * chunks * own
    anywhere = pl.BlockSpec(memory_space=pl.ANY)
    copies = 4 * chunks + sizes[0]
    blocks = (chunks, own, width)
    spans = sizes[0]
    features = [(total, width // spans)] * (spans // 2) + [(total, width // 2)]
    shapes = [blocks, blocks, (total, 2 * units), (total, units), *features, *features]
    held = [
        (total, width), (total, width), (2 * units, width), (units, width), (total, 2 * units), (total, units), blocks, blocks,
        blocks, blocks, blocks, (chunks - 1, own, width), (chunks - 1, own, width),
    ]
    return pl.pallas_call(
        functools.partial(feed_kernel, sizes, masks, own),
        in_specs=[anywhere] * (4 + len(wides)),
        out_specs=[pl.BlockSpec(memory_space=pltpu.VMEM)] + [anywhere] * len(shapes),
        out_shape=[jax.ShapeDtypeStruct((own, width), F32)] + [jax.ShapeDtypeStruct(s, BF16) for s in shapes],
        scratch_shapes=[pltpu.VMEM(s, BF16) for s in held]
        + [pltpu.SemaphoreType.DMA((k,)) for k in (copies, copies, 3 + 2 * chunks + len(wides), 4 + 2 * spans)],
        compiler_params=pltpu.CompilerParams(collective_id=2, has_side_effects=True, vmem_limit_bytes=VMEM_LIMIT),
    )(own_rows, cots, *wides, *narrows)


def expanded(v, quarters):
    return spread(v, quarters, 0), spread(roll(v, -1), quarters, 0)


def chunk_inflow(links, line, blocks, quarters, backward, between):
    n, spans = line.shape[0], blocks.shape[0]
    place = links.seq // 2
    copies = [links.send(line.at[0], line.at[k], 2 * k) for k in range(1, n)]
    for copy in copies:
        copy.wait_recv()
    between()
    one, nought = jnp.ones(line.shape[1:], F32), jnp.zeros(line.shape[1:], F32)
    prod, total = one, nought
    all_prod, all_total = one, nought

    def ordered(count):
        return range(count - 1, -1, -1) if backward else range(count)

    def ahead(j, at):
        return at < j if backward else at > j

    for j in ordered(n):
        p, s = expanded(line[links.flipped(place, j)], quarters)
        inside = ahead(j, place)
        total = jnp.where(inside, p * total + s, total)
        prod = jnp.where(inside, p * prod, prod)
        all_total = p * all_total + s
        all_prod = p * all_prod
    q = quarter_of(line.shape[1:], quarters)
    blocks[0] = jnp.where(q == 0, all_prod, all_total)
    copies = [links.send(blocks.at[0], blocks.at[m], m * links.seqs) for m in range(1, spans)]
    for copy in copies:
        copy.wait_recv()
    h = nought
    for j in ordered(spans):
        p, s = expanded(blocks[links.flipped(links.span, j)], quarters)
        h = jnp.where(ahead(j, links.span), p * h + s, h)
    return prod * h + total


def by_head(heads, head_w, body):
    @pl.loop(0, heads)
    def _(h):
        start = pl.multiple_of(h * head_w, 128)
        columns = pl.ds(start, head_w)
        body(lambda ref: ref.at[:, columns], lambda ref: ref.at[pl.ds(start, head_w)])


def front_kernel(
    sizes, steps, quarters, heads, head_w, share, x_own, halo, params_in, rec_proj, out_proj, gate_weight, cot, wide, narrow, *refs
):
    spans, seqs = sizes
    count = spans * seqs
    inner = [2 * k for k in range(1, seqs // 2)]
    n = len(inner) + 1
    core, top = seqs, count // 2
    (normal, xb, y_pre, conv, recur, inject, decay, states, flow, mixed, resid, normal_two, params, chan), refs = refs[:14], refs[14:]
    (proj_x, proj_y, out_half, gates), refs = refs[:4], refs[4:]
    wides, beside_narrow, cots, refs = refs[: spans - 1], refs[spans - 1], refs[spans], refs[spans + 1 :]
    (lead, held_x, held_y, held_o, held_g, every, prod, enter, line, blocks, inflow, to_side, from_side, low,
     sends, recvs, locals_) = refs
    links = Links(sizes, sends, recvs)
    me = links.span * seqs + links.seq
    side, upper = me % 2, me // (count // 2)
    own, width = x_own.shape
    rows = 2 * own
    half = width // 2
    double = 2 * share
    links.greet([1, *inner, *[m * seqs for m in range(1, spans)]])
    kept = [0]

    def local(source, target, only=None):
        copy = pltpu.make_async_copy(source, target, locals_.at[kept[0]])
        kept[0] += 1
        if only is None:
            copy.start()
        else:
            pl.when(only)(copy.start)
        return copy

    z = links.seq // 2
    offsets = [o for s in range(1, n) for o in (-s, s)]
    there = {o: jnp.logical_and(z + o >= 0, z + o < n) for o in offsets}
    beyond = {-1: (links.span, jnp.maximum(links.seq - 2, 0)), 1: (links.span, jnp.minimum(links.seq + 2, seqs - 1))}

    def along(piece):
        passing = {}
        for o in (0, *offsets):
            for way in (-1, 1):
                if o * way <= 0 and abs(o) + 1 < n:
                    both = jnp.logical_and(there[way], there[o]) if o else there[way]
                    passing[o, way] = links.plan(piece(o), piece(o), None, both, beyond[way])
        return passing

    def arrival(passing, o):
        way = 1 if o < 0 else -1
        return passing[o + way, way]

    def begin(passing):
        for way in (-1, 1):
            pl.when(there[way])(passing[0, way].start)

    def take(passing, o):
        arrival(passing, o).wait_recv()
        way = 1 if o < 0 else -1
        if (o, way) in passing:
            pl.when(there[way])(passing[o, way].start)

    def pieces_out(own_out, piece, part, far):
        passing = along(piece)
        over_top = {o: links.plan(piece(o), piece(o), top, there[o]) for o in offsets}
        over_core = {o: links.plan(part(o), part(o), core, there[o]) for o in offsets}
        far_core = {o: links.plan(far(o), far(o), core, there[o]) for o in offsets}
        begin(passing)
        first_core = links.send(own_out, own_out, core)
        first_top = first_far = None
        if far(0) is not None:
            first_top = links.send(piece(0), piece(0), top)
        yield
        for o in offsets:

            @pl.when(there[o])
            def _():
                take(passing, o)
                over_top[o].start()
                over_core[o].start()

            if o == offsets[len(offsets) // 2 - 1]:
                yield
        yield
        if first_top is not None:
            first_top.wait_recv()
            first_far = links.send(far(0), far(0), core)
        for o in offsets:

            @pl.when(there[o])
            def _():
                over_top[o].wait_recv()
                far_core[o].start()

        yield
        first_core.wait_recv()
        if first_far is not None:
            first_far.wait_recv()
        for o in offsets:

            @pl.when(there[o])
            def _():
                over_core[o].wait_recv()
                far_core[o].wait_recv()

    def pieces_direct(whole, piece):
        over_inner = {m: links.send(piece(0), piece(0), m) for m in inner}
        over_core = [links.send(whole, whole, core)]
        over_top = {}
        yield
        for m in inner:
            over_inner[m].wait_recv()
            here = piece(links.flipped(z, m // 2) - z)
            over_top[m] = links.send(here, here, top)
            over_core.append(links.send(here, here, core))
        yield
        for m in inner:
            over_top[m].wait_recv()
            here = piece(links.flipped(z, m // 2) - z, 1 - upper)
            over_core.append(links.send(here, here, core))
        yield
        for copy in over_core:
            copy.wait_recv()

    def columns_part(source, first, target):
        def piece(o, over=0):
            device = (links.other(over) if over else me) + 2 * o
            start = jnp.clip(device // 2 * double, 0, target.shape[0] - double)
            return target.at[pl.ds(pl.multiple_of(start, 16), double)]

        def columns(which):
            return source.at[:, pl.ds(pl.multiple_of(first + which * half, 128), half)]

        row = target.at[pl.ds(pl.multiple_of(me * share, 16), share)]
        mine = local(columns(side), row)
        theirs = links.send(columns(1 - side), row, 1)
        yield
        mine.wait()
        theirs.wait_recv()
        yield from pieces_out(piece(0), piece, piece, lambda o: piece(o, top))

    def rows_part(source, target, direct):
        cols = source.shape[1]
        pairs_half = count // 4

        def rows_at(start, size):
            return target.at[pl.ds(pl.multiple_of(start, 16), size)]

        begin_at = me // 2 % pairs_half * double

        def piece(o, which=None):
            start = jnp.clip(begin_at + o * double, 0, target.shape[0] - double)
            which = upper if which is None else which
            return target.at[pl.ds(pl.multiple_of(start, 16), double), pl.ds(pl.multiple_of(which * (cols // 2), 128), cols // 2)]

        holds = side == upper
        row = rows_at(begin_at + side * share, share)
        mine = local(source, row, holds)
        gift = links.send(source, row, 1, side != upper)
        yield

        @pl.when(holds)
        def _():
            mine.wait()
            gift.wait_recv()

        whole = rows_at(begin_at, double)
        across = links.send(whole, whole, top, holds)
        yield
        pl.when(side != upper)(across.wait_recv)
        if direct:
            yield from pieces_direct(whole, piece)
        else:
            yield from pieces_out(whole, piece, piece, lambda o: piece(o, 1 - upper) if o else None)

    def small_part():
        height = params_in.shape[0]

        def rows_of(device):
            return every.at[pl.ds(pl.multiple_of(device // 2 * 2 * height, 16), 2 * height)]

        row = pl.ds(pl.multiple_of(me * height, 16), height)
        every[row] = params_in[...]
        theirs = links.send(every.at[row], every.at[row], 1)
        yield
        theirs.wait_recv()
        held = [me]
        for masks in (inner, [top], [core]):
            copies = [links.send(rows_of(d), rows_of(d), m) for d in held for m in masks]
            held = held + [links.flipped_index(d, m) for d in held for m in masks]
            yield
            for copy in copies:
                copy.wait_recv()
        params[...] = jnp.zeros_like(params)
        lanes = params_in.shape[1]
        for d in range(count):
            tile = every[d * height : (d + 1) * height]
            base, shift = d * share // lanes * lanes, d * share % lanes
            if shift + share <= lanes:
                params[:, base : base + lanes] += pltpu.roll(tile, shift, 1) if shift else tile
            else:
                turned = pltpu.roll(jnp.concatenate([tile, jnp.zeros_like(tile)], axis=1), shift, 1)
                params[:, base : base + 2 * lanes] += turned
        chan[...] = params[:SUBS, pl.ds(pl.multiple_of(side * half, 128), half)]

    parts = {
        "x": columns_part(rec_proj, 0, proj_x),
        "v": small_part(),
        "g": rows_part(gate_weight, gates, False),
        "y": columns_part(rec_proj, 2 * half, proj_y),
        "o": rows_part(out_proj, out_half, True),
    }

    def advance(order):
        for name in order:
            next(parts[name], None)

    place = pl.ds(pl.multiple_of(side * own, 16), own)
    def cot_at(o, far=0):
        return cots.at[jnp.clip(z + o, 0, n - 1), far]

    cot_inner = [links.plan(cot_at(0), cot_at(0), m) for m in inner]
    cot_side = []
    own_cot = local(cot, cot_at(0))
    advance("xvgoy")
    tokens = links.send(x_own, lead.at[place], 1)
    lead[place] = x_own[...]
    lead[rows:] = halo[...]
    advance("xvgo")
    own_cot.wait()
    own_side = links.send(cot_at(0), cot_at(0, 1), 1)
    advance("xvxgyov")
    advance("ggxgvyyxg")
    loads = [local(proj_x, held_x), local(gates, held_g)]
    tokens.wait_recv()
    few = 16

    @pl.loop(0, lead.shape[0] // few)
    def _(k):
        here = pl.ds(pl.multiple_of(k * few, few), few)
        normal[here] = normed(lead[here].astype(F32), params[SUBS : SUBS + 1]).astype(BF16)

    for copy in loads:
        copy.wait()

    def gate(cols, tall):
        cols(xb)[...] = jnp.dot(normal[...], cols(held_x)[...], preferred_element_type=F32).astype(BF16)
        forward_kernel(
            steps, quarters, cols(xb), cols(chan), tall(held_g), cols(conv), cols(recur), cols(inject), cols(decay),
            cols(states), cols(prod), cols(enter), cols(line.at[0]),
        )

    by_head(heads, head_w, gate)
    inflow[...] = chunk_inflow(links, line, blocks, quarters, False, lambda: [copy.start() for copy in cot_inner])
    advance("o")
    tops = [2 * seqs * k for k in range(1, spans // 2)]
    across = {m: links.send(wide, wides[m // seqs - 1], m) for m in tops}
    beside = [links.send(wide, wides[0], core), links.send(narrow, beside_narrow, core)]
    def onward(k):
        cot_inner[k].wait_recv()
        here = links.flipped(z, inner[k] // 2) - z
        cot_side.append(links.send(cot_at(here), cot_at(here, 1), 1))

    advance("yy")
    loads = [local(proj_y, held_y)]
    loads[0].wait()
    block = steps * SUBS

    def mix(cols, tall):
        cols(y_pre)[...] = jnp.dot(normal[:rows], cols(held_y)[...], preferred_element_type=F32)
        ins, flows, hold, gain_y = cols(inflow), cols(flow), cols(states), cols(y_pre)
        for b in (0, 1):
            entered = cols(enter)[b * SUBS : (b + 1) * SUBS] * ins[...] + cols(enter)[(2 + b) * SUBS : (3 + b) * SUBS]
            flows[b * SUBS : (b + 1) * SUBS] = entered
            flows[(2 + b) * SUBS : (3 + b) * SUBS] = cols(prod)[(b + 1) * block - SUBS : (b + 1) * block]
            here = slice(b * block, (b + 1) * block)
            total = hold[here].reshape(steps, SUBS, head_w) + cols(prod)[here].reshape(steps, SUBS, head_w) * entered[None]
            total = total.reshape(block, head_w)
            hold[here] = total
            cols(mixed)[here] = (total * gelu_parts(gain_y[here])[0]).astype(BF16)

    by_head(heads, head_w, mix)

    onward(0)
    advance("oo")
    load = local(out_half, held_o)
    load.wait()
    step = 512

    @pl.loop(0, width // step)
    def _(k):
        columns = pl.ds(pl.multiple_of(k * step, 128), step)
        total = jnp.dot(mixed[...], held_o[:, columns], preferred_element_type=F32)
        first = side == 0
        resid[:, columns] = x_own[:, columns].astype(F32) + jnp.where(first, total[:own], total[own:])
        to_side[:, columns] = jnp.where(first, total[own:], total[:own]).astype(BF16)

    partial = links.send(to_side, from_side, 1)
    for k in range(1, n - 2):
        onward(k)
    partial.wait_recv()
    size = width // spans

    @pl.loop(0, own // few)
    def _(k):
        here = pl.ds(pl.multiple_of(k * few, few), few)
        total = resid[here] + from_side[here].astype(F32)
        resid[here] = total
        low[here] = normed(total, params[SUBS + 1 : SUBS + 2]).astype(BF16)

    for j in range(spans):
        start = pl.multiple_of(links.flipped(links.span, j) * size, 128)
        normal_two[:, j * size : (j + 1) * size] = low[:, pl.ds(start, size)]

    onward(n - 2)
    for m in tops:
        across[m].wait_recv()
        beside.append(links.send(wides[m // seqs - 1], wides[m // seqs], core))
    for copy in (*beside, own_side, *cot_side):
        copy.wait_recv()
    for part in parts.values():
        for _ in part:
            pass
    links.close()


def front(sizes, steps, quarters, heads, head_w, x_own, halo, params, rec_proj, out_proj, gate_weight, cot, wide, narrow):
    spans, seqs = sizes
    count = spans * seqs
    own, width = x_own.shape
    half, rows, share = width // 2, 2 * own, rec_proj.shape[0]
    n = seqs // 2
    inside, anywhere = pl.BlockSpec(memory_space=pltpu.VMEM), pl.BlockSpec(memory_space=pl.ANY)

    def high(*shape):
        return jax.ShapeDtypeStruct(shape, F32)

    def low(*shape):
        return jax.ShapeDtypeStruct(shape, BF16)

    lead = rows + halo.shape[0]
    near = [
        low(lead, width), low(lead, half), *[high(rows, half)] * 6, high(4 * SUBS, half), low(rows, half), high(own, width),
        low(own, width), high(params.shape[0], width), high(SUBS, half),
    ]
    far = [
        low(width, half), low(width, half), low(half, width), low(half, gate_weight.shape[1]), *[low(*wide.shape)] * (spans - 1),
        low(*narrow.shape), low(n, 2, *cot.shape),
    ]
    end = (SUBS, half)
    copies = 4 * (3 + 10 * n) + 4 * n + 3 + 6 * n + (n - 1) + 2 * spans + 4
    outs = pl.pallas_call(
        functools.partial(front_kernel, sizes, steps, quarters, heads, head_w, share),
        in_specs=[inside] * 7 + [anywhere] * 2,
        out_specs=[inside] * len(near) + [anywhere] * len(far),
        out_shape=[*near, *far],
        scratch_shapes=[
            pltpu.VMEM((lead, width), BF16), pltpu.VMEM((width, half), BF16), pltpu.VMEM((width, half), BF16),
            pltpu.VMEM((half, width), BF16), pltpu.VMEM((half, gate_weight.shape[1]), BF16), pltpu.VMEM((count * params.shape[0], params.shape[1]), F32),
            pltpu.VMEM((rows, half), F32), pltpu.VMEM((4 * SUBS, half), F32), pltpu.VMEM((n, *end), F32),
            pltpu.VMEM((spans, *end), F32), pltpu.VMEM(end, F32), *[pltpu.VMEM((own, width), BF16)] * 3,
            pltpu.SemaphoreType.DMA((copies,)), pltpu.SemaphoreType.DMA((copies,)), pltpu.SemaphoreType.DMA((16,)),
        ],
        compiler_params=pltpu.CompilerParams(collective_id=0, has_side_effects=True, vmem_limit_bytes=VMEM_LIMIT),
    )(x_own, halo, params, rec_proj, out_proj, gate_weight, cot, wide, narrow)
    wides, narrows, cots = outs[18 : 17 + spans], outs[17 + spans], outs[18 + spans]
    return outs[:14], outs[14:18], [wide, *wides], [narrow, narrows], cots


def return_kernel(
    sizes, steps, quarters, heads, inner, branch, out_w, y_pre, states, decay, flow, conv, recur, inject, xb, chan, gate,
    resid, near, far, wide, narrow, branch_o, y_grad, x_grad, gate_o, small, output, wides, narrows, dx, spill, came_back, grad, local, after, enter, carry, line, blocks, inflow, dmix, from_side, to_inner, from_inner, sends, recvs,
):
    spans, seqs = sizes
    tops = [2 * seqs * k for k in range(1, spans // 2)]
    n = len(inner) + 1
    links = Links(sizes, sends, recvs)
    side = links.seq % 2
    own, width = branch.shape
    me, count = links.span * seqs + links.seq, spans * seqs

    def device(index):
        return (index // seqs, index % seqs)

    links.greet([1, *inner, *[m * seqs for m in range(1, spans)]], [device((me + 2) % count)])
    place = pl.ds(pl.multiple_of(side * own, 16), own)
    whole = links.send(branch, branch_o.at[place], 1)
    tall = wide.shape[1] // 2
    across = [links.send(wide.at[k, pl.ds(0, tall)], wides.at[k, pl.ds(0, tall)], m) for k, m in enumerate(tops)]
    branch_o[place] = branch[...]
    whole.wait_recv()
    sums = [*range(1, n), 0]
    over_side = {}

    def side_sum(i):
        over_side[sums[i]] = links.send(far.at[sums[i]], from_side.at[sums[i]], 1)

    over_inner = []

    def inner_sum(i):
        k = sums[i]
        over_side[k].wait_recv()
        if k:
            to_inner[k - 1] = (near[k].astype(F32) + from_side[k].astype(F32)).astype(BF16)
            over_inner.append(links.send(to_inner.at[k - 1], from_inner.at[k - 1], inner[k - 1]))

    side_sum(0)
    head_w = gate.shape[1] // 2

    def first(cols, tall):
        mixed_grad = lax.dot_general(branch_o[...], tall(out_w)[...], (((1,), (1,)), ((), ())), preferred_element_type=F32)
        value, slope = gelu_parts(cols(y_pre)[...])
        cols(grad)[...] = mixed_grad * value
        cols(y_grad)[...] = (mixed_grad * cols(states)[...] * slope).astype(BF16)
        adjoint_kernel(
            steps, quarters, cols(grad), cols(decay), cols(flow), cols(local), cols(after), cols(enter), cols(line.at[0])
        )

    by_head(heads, head_w, first)

    def between():
        inner_sum(0)
        side_sum(1)

    inflow[...] = chunk_inflow(links, line, blocks, quarters, True, between)
    for k, m in enumerate(tops):
        across.append(links.send(wide.at[k, pl.ds(tall, tall)], wides.at[k, pl.ds(tall, tall)], m))
        across.append(links.send(narrow.at[k], narrows.at[k], m))
    inner_sum(1)
    side_sum(2)

    def second(cols, tall):
        came = jnp.concatenate(
            [
                cols(enter)[b * SUBS : (b + 1) * SUBS] * cols(inflow)[...] + cols(enter)[(2 + b) * SUBS : (3 + b) * SUBS]
                for b in (0, 1)
            ],
            axis=0,
        )
        backward_kernel(
            steps, quarters, cols(local), cols(after), cols(states), came, cols(flow), cols(conv), cols(recur),
            cols(inject), cols(decay), cols(xb), cols(chan), tall(gate), cols(dx), cols(spill), tall(gate_o), cols(small),
        )

    by_head(heads, head_w, second)
    edge = (CONV - 1) * SUBS
    slot = links.used
    links.used += 1
    handed = pltpu.make_async_remote_copy(
        spill, came_back, links.sends.at[slot], links.recvs.at[slot], device_id=device(jnp.maximum(me - 2, 0)), device_id_type=MESH
    )
    pl.when(me >= 2)(handed.start)
    links.open.append((handed, me >= 2))
    rows = 2 * own
    x_grad[: rows - 2 * edge] = dx[: rows - 2 * edge].astype(BF16)
    for i in range(2, n):
        inner_sum(i)
        if i + 1 < n:
            side_sum(i + 1)
    pl.when(me + 2 < count)(handed.wait_recv)

    @pl.when(me + 2 >= count)
    def _():
        came_back[...] = jnp.zeros_like(came_back)

    last = quarter_of((SUBS, came_back.shape[1]), quarters) == quarters - 1
    total = [dx[rows - 2 * edge : rows - edge]]
    for k in range(CONV - 1, 0, -1):
        added = roll(came_back[(k - 1) * SUBS : k * SUBS], quarters - 1)
        total.append(dx[rows - k * SUBS : rows - (k - 1) * SUBS] + jnp.where(last, added, 0.0))
    x_grad[rows - 2 * edge :] = jnp.concatenate(total, axis=0).astype(BF16)
    few = 16
    size = width // spans
    for copy in over_inner:
        copy.wait_recv()

    for j in range(spans):
        columns = slice(j * size, (j + 1) * size)
        there = pl.ds(pl.multiple_of(links.flipped(links.span, j) * size, 128), size)
        total = resid[:, there] + near[0, :, columns].astype(F32) + from_side[0, :, columns].astype(F32)
        for k in range(n - 1):
            total = total + from_inner[k, :, columns].astype(F32)
        output[:, there] = total.astype(BF16)

    for copy in across:
        copy.wait_recv()
    links.close()


def returned(sizes, steps, quarters, heads, inner, branch, out_w, y_pre, states, decay, flow, conv, recur, inject, xb, chan, gate,
             resid, near, far, wide, narrow):
    spans, _ = sizes
    own, width = branch.shape
    rows, half = y_pre.shape
    n = len(inner) + 1
    inside, anywhere = pl.BlockSpec(memory_space=pltpu.VMEM), pl.BlockSpec(memory_space=pl.ANY)

    def high(*shape):
        return jax.ShapeDtypeStruct(shape, F32)

    def low(*shape):
        return jax.ShapeDtypeStruct(shape, BF16)

    shapes = [
        low(rows, width), low(rows, half), low(rows, half), high(*gate.shape), high(SUBS, half), low(own, width),
        low(*wide.shape), low(*narrow.shape),
    ]
    end = (SUBS, half)
    copies = 3 * (spans // 2) + 2 * n + 2 * n + spans + 2
    tail = ((CONV - 1) * SUBS, half)
    return pl.pallas_call(
        functools.partial(return_kernel, sizes, steps, quarters, heads, inner),
        in_specs=[inside] * 15 + [anywhere] * 2,
        out_specs=[inside] * 6 + [anywhere] * 2,
        out_shape=shapes,
        scratch_shapes=[
            pltpu.VMEM((rows, half), F32), pltpu.VMEM(tail, F32), pltpu.VMEM(tail, F32), *[pltpu.VMEM((rows, half), F32)] * 3, pltpu.VMEM((4 * SUBS, half), F32), pltpu.VMEM(end, F32),
            pltpu.VMEM((n, *end), F32), pltpu.VMEM((spans, *end), F32), pltpu.VMEM(end, F32), pltpu.VMEM(end, F32),
            pltpu.VMEM((n, own, width), BF16), pltpu.VMEM((n - 1, own, width), BF16), pltpu.VMEM((n - 1, own, width), BF16),
            pltpu.SemaphoreType.DMA((copies,)), pltpu.SemaphoreType.DMA((copies,)),
        ],
        compiler_params=pltpu.CompilerParams(collective_id=4, has_side_effects=True, vmem_limit_bytes=VMEM_LIMIT),
    )(branch, out_w, y_pre, states, decay, flow, conv, recur, inject, xb, chan, gate, resid, near, far, wide, narrow)


def on_device(
    inputs, norm_one, rec_proj, conv_weight, conv_bias, gate_weight, gate_bias, decay_param, out_proj, norm_two,
    mlp_wide, mlp_narrow, cotangent,
):
    spans, seqs = lax.axis_size("span"), lax.axis_size("seq")
    count = spans * seqs
    span, seq = lax.axis_index("span"), lax.axis_index("seq")
    me = span * seqs + seq
    side = me % 2
    pair = me // 2
    pairs = count // 2
    batch, tokens, width = inputs.shape
    half = width // 2
    quarters = SUBS // batch
    steps = tokens // quarters
    own = batch * tokens
    rows = 2 * own
    head_w = gate_weight.shape[1] // 2
    heads = half // head_w
    edge = CONV - 1
    share = width // count
    units = mlp_narrow.shape[1]
    inner = [2 * k for k in range(1, seqs // 2)]
    core = seqs
    xs = [2 * seqs * k for k in range(1, spans // 2)]
    top = count // 2
    upper = me // top
    chunk_masks = [0, *inner[1::-1], *inner[2:]]

    def to_rows(v):
        return v.reshape(batch, quarters, steps, width).transpose(2, 0, 1, 3).reshape(own, width)

    def from_rows(v):
        return v.reshape(steps, batch, quarters, width).transpose(1, 2, 0, 3).reshape(batch, tokens, width)

    def in_order(mine, other, axis):
        return jnp.concatenate([jnp.where(side == 0, mine, other), jnp.where(side == 0, other, mine)], axis=axis)

    def cut(v, index, size, axis):
        return lax.dynamic_slice_in_dim(v, index * size, size, axis)

    direct = share % 16 == 0 and (spans, seqs) == (4, 8)

    def gathered_rows(block, buffer, place):
        pieces = {0: block}
        for m in inner:
            pieces[m] = swap(block, m)
        for m in xs:
            for n in (0, *inner):
                pieces[m ^ n] = swap(pieces[n], m)
        for n in list(pieces):
            pieces[core ^ n] = swap(pieces[n], core)
        for m, piece in pieces.items():
            buffer = lax.dynamic_update_slice_in_dim(buffer, piece, place(me ^ m), 0)
        return buffer

    def columns_half(block):
        mine, theirs = cut(block, side, half, 1), cut(block, 1 - side, half, 1)
        block = in_order(mine, swap(theirs, 1), 0)
        return gathered_rows(block, jnp.zeros((width, half), BF16), lambda d: d // 2 * 2 * share)

    def rows_half(block):
        full = lax.all_gather(block, AXES, axis=0, tiled=True)
        return cut(full, side, half, 0)

    def by_span(v):
        size = width // spans
        return jnp.concatenate([cut(v, span ^ j, size, 1) for j in range(spans)], axis=1)

    def over_sides(partial):
        partial = partial.reshape(2, own, width)
        other = lax.dynamic_index_in_dim(partial, 1 - side, 0, keepdims=False).astype(BF16)
        return lax.dynamic_index_in_dim(partial, side, 0, keepdims=False) + swap(other, 1).astype(F32)

    def exchanged(carry):
        every = lax.all_gather(carry, AXES, axis=0).reshape(pairs, 2, batch, quarters, half)
        every = lax.dynamic_index_in_dim(every, side, 1, keepdims=False)
        return every[:, :, 0], every[:, :, 1]

    def entering(enter, h):
        enter = enter.reshape(2, 2, SUBS, half)
        return enter[0] * jnp.repeat(h, quarters, axis=0)[None] + enter[1]

    def by_steps(v):
        return v.reshape(2, steps, SUBS, half)

    def span_gather(block):
        pieces = {0: block}
        for m in xs:
            pieces[m] = swap(block, m)
        for n in list(pieces):
            pieces[n ^ core] = swap(pieces[n], core)
        return [pieces[m * seqs] for m in range(spans)]

    def token_gather(v):
        blocks = [v] + [swap(v, m) for m in inner]
        return [b for block in blocks for b in (block, swap(block, 1))]

    small = jnp.stack([*conv_weight.T, conv_bias, *gate_bias.T, decay_param, norm_one, norm_two]).astype(F32)
    small = jnp.concatenate([small[:7], jax.nn.softplus(small[7:8]), small[8:]], axis=0)
    wide_own = mlp_wide.transpose(1, 2, 0).reshape(2 * units, width // spans)
    narrow_own = mlp_narrow.T
    grads_own = by_span(to_rows(cotangent))
    c = to_rows(cotangent).astype(F32)

    mine = to_rows(inputs)
    x = mine.astype(F32)
    tail = inputs[:, tokens - edge :]
    halo = lax.ppermute(tail, AXES, [(i, i + 1) for i in range(1, count - 1, 2)]) + lax.ppermute(
        tail, AXES, [(i, i + 2) for i in range(1, count - 2, 2)]
    )
    halo = jnp.zeros((edge, batch, quarters, width), BF16).at[:, :, 0].set(halo[:, ::-1].transpose(1, 0, 2))
    halo = jnp.concatenate([halo.reshape(edge * SUBS, width), jnp.zeros((8, width), BF16)], axis=0)

    if direct:
        packed = jnp.pad(small, ((0, 6), (0, -share % 128)))
        nearby, (proj_x, proj_y, out_half, gates), wides, narrows, cots = front(
            (spans, seqs), steps, quarters, heads, head_w, mine, halo, packed, rec_proj, out_proj, gate_weight, grads_own,
            wide_own, narrow_own,
        )
        normal_one, x_branch, y_pre, conv, recur, inject, decay, states, flow, mixed, resid, normal_two, params, chan = nearby
        gain_one, gain_two = params[SUBS], params[SUBS + 1]
        normal_one = normal_one[:rows]
    else:
        proj_x = columns_half(rec_proj[:, :width])
        proj_y = columns_half(rec_proj[:, width:])
        gates = rows_half(gate_weight)
        out_half = rows_half(out_proj)
        small = lax.all_gather(small, AXES, axis=1, tiled=True)
        gain_one, gain_two = small[SUBS], small[SUBS + 1]
        chan = cut(small[:SUBS], side, half, 1)
        lead = jnp.concatenate([in_order(mine, swap(mine, 1), 0), halo], axis=0)
        normal_one = normed(lead.astype(F32), gain_one).astype(BF16)
        x_branch = nn(normal_one, proj_x, BF16)
        normal_one = normal_one[:rows]
        y_pre = nn(normal_one, proj_y)
        y_branch, gelu_back = jax.vjp(jax.nn.gelu, y_pre)
        kernel = functools.partial(forward_kernel, steps, quarters)
        full = ((rows, half), False)
        ends = ((4 * SUBS, half), False)
        conv, recur, inject, decay, local, prod, enter, carry = by_heads(
            kernel, heads, head_w, [(x_branch, False), (chan, False), (gates, True)],
            [full] * 6 + [ends, ((SUBS, half), False)],
        )
        prods, sums = exchanged(carry)
        h = jnp.zeros((batch, half), F32)
        for j in range(pairs - 1):
            h = jnp.where(j < pair, prods[j] * h + sums[j], h)
        entered = entering(enter, h)
        states = (by_steps(local) + by_steps(prod) * entered[:, None]).reshape(rows, half)
        flow = jnp.concatenate([entered, by_steps(prod)[:, -1]], axis=0).reshape(4 * SUBS, half)
        mixed = (states * y_branch).astype(BF16)
        resid = x + over_sides(nn(mixed, out_half))
        normal_two = by_span(normed(resid, gain_two).astype(BF16))
        wides, narrows = span_gather(wide_own), span_gather(narrow_own)
        cots = token_gather(grads_own)

    def token_scatter(near, far):
        total = None
        for k, m in enumerate((0, *inner)):
            block = near[k].astype(F32) + swap(far[k], 1).astype(F32)
            total = block if m == 0 else total + swap(block.astype(BF16), m).astype(F32)
        return by_span(total)

    size = width // spans

    def by_core(v):
        blocks = [v[:, j * size : (j + 1) * size] for j in range(spans)]
        return [*blocks[::2], jnp.concatenate(blocks[1::2], axis=1)]

    if direct:
        normal_two_grad, near, far, all_act, all_hidden, *features = feed_forward(
            (spans, seqs), chunk_masks, normal_two, cots, wides, narrows
        )
        all_normal, all_grads = features[: 1 + spans // 2], features[1 + spans // 2 :]
    else:
        wide, narrow = jnp.concatenate(wides, axis=1), jnp.concatenate(narrows, axis=1)
        all_normal = jnp.concatenate(token_gather(normal_two), axis=0)
        all_grads = jnp.concatenate(cots, axis=0)

        def activate(values):
            return jax.nn.gelu(values[:, :units]) * values[:, units:]

        value, back = jax.vjp(activate, nt(all_normal, wide))
        all_hidden = value.astype(BF16)
        all_act = back(nt(all_grads, narrow))[0].astype(BF16)

        def sided(v):
            v = v.reshape(len(inner) + 1, 2, own, width)
            return v[:, 0], v[:, 1]

        all_normal, all_grads = by_core(all_normal), by_core(all_grads)
        normal_two_grad = token_scatter(*sided(nn(all_act, wide, BF16)))
        near, far = sided(nn(all_hidden, narrow, BF16))
    def core_sum(left, right):
        recv = swap(tn(left, right[-1], BF16), core).astype(F32)
        total = [tn(left, v) + recv[:, k * size : (k + 1) * size] for k, v in enumerate(right[:-1])]
        return total[0], jnp.stack([v.astype(BF16) for v in total[1:]])

    wide_kept, wide_away = core_sum(all_act, all_normal)
    narrow_kept, narrow_away = core_sum(all_hidden, all_grads)
    resid_part, gain_two_grad = norm_back(resid, gain_two, normal_two_grad)
    resid_grad = c + resid_part
    branch_low = resid_grad.astype(BF16)
    if direct:
        branch_low, y_grad, x_grad, gate_grad, small_grad, output, wide_came, narrow_came = returned(
            (spans, seqs), steps, quarters, heads, chunk_masks[1:], branch_low, out_half, y_pre, states, decay, flow, conv, recur, inject,
            x_branch, chan, gates, resid, near, far, wide_away, narrow_away,
        )
    else:
        output = (resid + token_scatter(near, far)).astype(BF16)
        wide_came = jnp.stack([swap(wide_away[k], m) for k, m in enumerate(xs)])
        narrow_came = jnp.stack([swap(narrow_away[k], m) for k, m in enumerate(xs)])
        branch_low = in_order(branch_low, swap(branch_low, 1), 0)
        mixed_grad = nt(branch_low, out_half)
        y_grad = gelu_back(mixed_grad * states)[0].astype(BF16)
        kernel = functools.partial(adjoint_kernel, steps, quarters)
        local_adj, after, enter, carry = by_heads(
            kernel, heads, head_w, [(mixed_grad * y_branch, False), (decay, False), (flow, False)],
            [full, full, ends, ((SUBS, half), False)],
        )
        prods, sums = exchanged(carry)
        h = jnp.zeros((batch, half), F32)
        for j in range(pairs - 1, 0, -1):
            h = jnp.where(j > pair, prods[j] * h + sums[j], h)
        came = entering(enter, h).reshape(2 * SUBS, half)
        kernel = functools.partial(backward_kernel, steps, quarters)
        dx, spill, gate_grad, small_grad = by_heads(
            kernel, heads, head_w,
            [(v, False) for v in (local_adj, after, states, came, flow, conv, recur, inject, decay, x_branch, chan)]
            + [(gates, True)],
            [full, ((edge * SUBS, half), False), ((half, 2 * head_w), True), ((SUBS, half), False)],
        )
        spill = lax.ppermute(
            spill.reshape(edge, batch, quarters, half)[::-1, :, 0], AXES, [(i, i - 2) for i in range(2, count)]
        )
        spill = jnp.pad(
            spill[:, :, None], ((0, 0), (0, 0), (quarters - 1, 0), (0, 0))
        ).reshape(edge * SUBS, half)
        x_grad = jnp.concatenate([dx[: rows - edge * SUBS], dx[rows - edge * SUBS :] + spill], axis=0).astype(BF16)
    output = from_rows(output)
    wide_owned = wide_kept + jnp.sum(wide_came.astype(F32), axis=0)
    wide_owned = wide_owned.reshape(2, units, size).transpose(2, 0, 1)
    narrow_owned = (narrow_kept + jnp.sum(narrow_came.astype(F32), axis=0)).T
    normal_one_part = nt(y_grad, proj_y) + nt(x_grad, proj_x)

    def blocks_of(v, masks, wrap):
        size = 2 * share
        return [lax.dynamic_slice_in_dim(v, (me ^ m) // 2 % wrap * size, size, 0) for m in masks]

    def to_columns_owner(v_kept, v_given):
        recv = swap(v_given, core)
        n = len(inner) + 1
        total = (v_kept + recv.astype(F32)).reshape(len(xs) + 1, n, 2 * share, v_kept.shape[1])
        near = total[0]
        for k, m in enumerate(xs):
            near = near + swap(total[k + 1].astype(BF16), m).astype(F32)
        out = near[0]
        for k, m in enumerate(inner):
            out = out + swap(near[k + 1].astype(BF16), m).astype(F32)
        out = out.reshape(2, share, out.shape[1])
        other = lax.dynamic_index_in_dim(out, 1 - side, 0, keepdims=False).astype(BF16)
        return lax.dynamic_index_in_dim(out, side, 0, keepdims=False), swap(other, 1).astype(F32)

    def to_rows_owner(v_kept, v_given):
        cols = v_kept.shape[1]
        total = (v_kept + swap(v_given, core).astype(F32)).reshape(len(low_order), 2 * share, cols)
        away = cut(total, 1 - upper, cols // 2, 2).astype(BF16)
        near = cut(total, upper, cols // 2, 2) + swap(away, top).astype(F32)
        out = near[0]
        for k, m in enumerate(low_order[1:]):
            out = out + swap(near[k + 1].astype(BF16), m).astype(F32)
        other = swap(out.astype(BF16), top).astype(F32)
        out = in_order(out, other, 1).reshape(2, share, cols)
        gone = lax.dynamic_index_in_dim(out, 1 - side, 0, keepdims=False).astype(BF16)
        here = lax.dynamic_index_in_dim(out, side, 0, keepdims=False)
        return jnp.where(upper == side, here, swap(gone, 1).astype(F32))

    order = [m ^ n for m in (0, *xs) for n in (0, *inner)]
    low_order = [m ^ n for m in (0, *[v for v in xs if v < top]) for n in (0, *inner)]

    def ordered(v, masks, wrap):
        return [jnp.concatenate(blocks_of(v, [m ^ c for m in masks], wrap), axis=0) for c in (0, core)]

    if direct:
        part = normal_one_part.reshape(2, own, width)
        proj_owned, out_owned, gate_owned, input_grad, sums = scatter_grads(
            (spans, seqs), share, normal_one.T, mixed.T, x_grad, y_grad, branch_low, gate_grad, small_grad, gain_two_grad[None],
            mine, gain_one[None], resid_grad, lax.dynamic_index_in_dim(part, side, 0, keepdims=False),
            lax.dynamic_index_in_dim(part, 1 - side, 0, keepdims=False).astype(BF16),
        )
        gains = cut(sums[:2, :width], me, share, 1).T
        small_owned = cut(sums[:, width:], me % (count // 2), share, 1).T
    else:
        input_part, gain_one_grad = norm_back(x, gain_one, over_sides(normal_one_part))
        input_grad = resid_grad + input_part
        kept_d, given_d = ordered(normal_one.T, order, pairs)
        kept_m, given_m = ordered(mixed.T, low_order, pairs // 2)
        by_row = jnp.concatenate([gate_grad, small_grad.T, jnp.zeros((half, head_w - SUBS), F32)], axis=1)
        kept_g, given_g = ordered(by_row, low_order, pairs // 2)
        gains = jnp.pad(jnp.stack([gain_one_grad, gain_two_grad], axis=1), ((0, 0), (0, 126)))
        kept_n, given_n = ordered(gains, order, pairs)
        proj_owned = jnp.concatenate(
            [in_order(*to_columns_owner(nn(kept_d, g), nn(given_d, g, BF16)), 1) for g in (x_grad, y_grad)], axis=1
        )
        out_owned = to_rows_owner(nn(kept_m, branch_low), nn(given_m, branch_low, BF16))
        rest = to_rows_owner(kept_g, given_g.astype(BF16))
        gate_owned, small_owned = rest[:, : 2 * head_w], rest[:, 2 * head_w : 2 * head_w + SUBS]
        gains = sum(to_columns_owner(kept_n, given_n.astype(BF16)))
    input_grad = from_rows(input_grad)

    return (
        output,
        input_grad,
        gains[:, 0],
        proj_owned,
        small_owned[:, :CONV],
        small_owned[:, 4],
        gate_owned,
        small_owned[:, 5:7],
        small_owned[:, 7] * jax.nn.sigmoid(decay_param.astype(F32)),
        out_owned,
        gains[:, 1],
        wide_owned,
        narrow_owned,
    )


def solution(mesh):
    both = ("span", "seq")
    tokens = P(None, both, None)
    placed = (
        tokens, P(both), P(both, None), P(both, None), P(both), P(both, None), P(both, None), P(both), P(both, None),
        P(both), P("span", None, "seq"), P("span", "seq"), tokens,
    )
    given = (
        tokens, tokens, P(both), P(both, None), P(both, None), P(both), P(both, None), P(both, None), P(both),
        P(both, None), P(both), P("span", None, "seq"), P("span", "seq"),
    )
    return jax.shard_map(on_device, mesh=mesh, in_specs=placed, out_specs=given, check_vma=False)
```

```python
import functools

import jax
import jax.numpy as jnp
from jax import lax
from jax.experimental import pallas as pl
from jax.experimental.pallas import tpu as pltpu
from jax.sharding import PartitionSpec as P

CONV = 4
EPS = 1e-06
AXES = ("span", "seq")
F32 = jnp.float32
BF16 = jnp.bfloat16
SUBS = 8


def swap(value, mask):
    count = lax.axis_size("span") * lax.axis_size("seq")
    return lax.ppermute(value, AXES, [(i, i ^ mask) for i in range(count)])


def dot(a, b, dims, out=F32):
    return lax.dot_general(a, b, ((dims[0], dims[1]), ((), ())), preferred_element_type=F32).astype(out)


def nn(a, b, out=F32):
    return dot(a, b, ((1,), (0,)), out)


def nt(a, b, out=F32):
    return dot(a, b, ((1,), (1,)), out)


def tn(a, b, out=F32):
    return dot(a, b, ((0,), (0,)), out)


def normed(v, gain):
    return v * lax.rsqrt(jnp.mean(v * v, axis=-1, keepdims=True) + EPS) * gain


def norm_back(v, gain, grad):
    scale = lax.rsqrt(jnp.mean(v * v, axis=-1, keepdims=True) + EPS)
    z = v * scale
    e = grad * gain
    return scale * (e - z * jnp.mean(e * z, axis=-1, keepdims=True)), jnp.sum(grad * z, axis=0)


def one_less_exp(u):
    series = 1.0 + u / 7.0
    for n in (6.0, 5.0, 4.0, 3.0, 2.0):
        series = 1.0 + u / n * series
    return jnp.where(u > -0.25, -u * series, 1.0 - jnp.exp(u))


def roll(v, by):
    return pltpu.roll(v, by % SUBS, 0)


def quarter_of(shape, quarters):
    return lax.broadcasted_iota(jnp.int32, shape, 0) % quarters


def spread(v, quarters, at):
    q = quarter_of(v.shape, quarters)
    held = jnp.where(q == at, v, 0.0)
    total = held
    for k in range(1, quarters):
        total = total + roll(held, k if at == 0 else -k)
    return total


def scan_carries(prods, sums, quarters, backward):
    q = quarter_of(prods[0].shape, quarters)
    sign = -1 if backward else 1
    order = (1, 0) if backward else (0, 1)
    place = quarters - 1 - q if backward else q
    whole = None
    enter = [None, None]
    for b in order:
        p, s = prods[b], sums[b]
        d = 1
        while d < quarters:
            pp, ss = roll(p, sign * d), roll(s, sign * d)
            ok = place >= d
            s = jnp.where(ok, p * ss + s, s)
            p = jnp.where(ok, p * pp, p)
            d *= 2
        first = place == 0
        ep = jnp.where(first, 1.0, roll(p, sign))
        es = jnp.where(first, 0.0, roll(s, sign))
        last = 0 if backward else quarters - 1
        tp, ts = spread(p, quarters, last), spread(s, quarters, last)
        if whole is None:
            enter[b] = (ep, es)
            whole = (tp, ts)
        else:
            enter[b] = (ep * whole[0], ep * whole[1] + es)
            whole = (tp * whole[0], tp * whole[1] + ts)
    return enter, whole


def earlier_rows(groups, halo, quarters, steps):
    q = quarter_of(groups[0].shape[1:], quarters)
    edge = CONV - 1
    out = []
    for b in (0, 1):
        ahead = []
        for k in range(edge, 0, -1):
            same = roll(groups[b][steps - k], 1)
            before = halo[k - 1] if b == 0 else roll(groups[0][steps - k], 1 - quarters)
            ahead.append(jnp.where(q == 0, before, same)[None])
        out.append(jnp.concatenate([*ahead, groups[b]], axis=0))
    return out


def forward_kernel(steps, quarters, xb, chan, gate, conv_o, recur_o, inject_o, decay_o, local_o, prod_o, enter_o, carry_o):
    rows = 2 * steps * SUBS
    width = xb.shape[1]
    head = xb[...].astype(F32)
    groups = [head[b * steps * SUBS : (b + 1) * steps * SUBS].reshape(steps, SUBS, width) for b in (0, 1)]
    halo = [head[rows + k * SUBS : rows + (k + 1) * SUBS] for k in range(CONV - 1)]
    edge = CONV - 1
    convs = []
    for ext in earlier_rows(groups, halo, quarters, steps):
        total = jnp.broadcast_to(chan[4:5][None], (steps, SUBS, width))
        for k in range(CONV):
            total = total + chan[k : k + 1][None] * ext[edge - k : edge - k + steps]
        convs.append(total.reshape(steps * SUBS, width))
    conv = jnp.concatenate(convs, axis=0)
    pre = jnp.dot(conv.astype(BF16), gate[...], preferred_element_type=F32)
    recur = jax.nn.sigmoid(pre[:, :width] + chan[5:6])
    inject = jax.nn.sigmoid(pre[:, width:] + chan[6:7])
    log_decay = -8.0 * recur * chan[7:8]
    decay = jnp.exp(log_decay)
    driven = jnp.sqrt(one_less_exp(2.0 * log_decay)) * inject * conv
    conv_o[...] = conv
    recur_o[...] = recur
    inject_o[...] = inject
    decay_o[...] = decay
    prods, sums = [], []
    for b in (0, 1):
        h = p = None
        for t in range(steps):
            at = (b * steps + t) * SUBS
            d, u = decay[at : at + SUBS], driven[at : at + SUBS]
            h = u if h is None else d * h + u
            p = d if p is None else d * p
            local_o[at : at + SUBS] = h
            prod_o[at : at + SUBS] = p
        prods.append(p)
        sums.append(h)
    enter, whole = scan_carries(prods, sums, quarters, False)
    for b in (0, 1):
        enter_o[b * SUBS : (b + 1) * SUBS] = enter[b][0]
        enter_o[(2 + b) * SUBS : (3 + b) * SUBS] = enter[b][1]
    q = quarter_of(whole[0].shape, quarters)
    carry_o[...] = jnp.where(q == 0, whole[0], whole[1])


def adjoint_kernel(steps, quarters, grad, decay, flow, local_o, after_o, enter_o, carry_o):
    prods, sums = [], []
    for b in (0, 1):
        g = r = None
        for t in range(steps - 1, -1, -1):
            at = (b * steps + t) * SUBS
            rows = slice(at, at + SUBS)
            a = grad[rows] if g is None else grad[rows] + g
            r = jnp.ones_like(a) if r is None else r * decay[at + SUBS : at + 2 * SUBS]
            local_o[rows] = a
            after_o[rows] = r
            g = decay[rows] * a
        prods.append(flow[(2 + b) * SUBS : (3 + b) * SUBS])
        sums.append(g)
    enter, whole = scan_carries(prods, sums, quarters, True)
    for b in (0, 1):
        enter_o[b * SUBS : (b + 1) * SUBS] = enter[b][0]
        enter_o[(2 + b) * SUBS : (3 + b) * SUBS] = enter[b][1]
    q = quarter_of(whole[0].shape, quarters)
    carry_o[...] = jnp.where(q == 0, whole[0], whole[1])


def backward_kernel(
    steps, quarters, local, after, states, came, entered, conv_r, recur_r, inject_r, decay_r, xb, chan, gate,
    dx_o, spill_o, gate_o, small_o,
):
    rows = 2 * steps * SUBS
    width = xb.shape[1]
    edge = CONV - 1
    block = steps * SUBS

    def by_step(v):
        return [v[b * block : (b + 1) * block].reshape(steps, SUBS, width) for b in (0, 1)]

    adjoint = jnp.concatenate(
        [
            (l + a * came[b * SUBS : (b + 1) * SUBS][None]).reshape(block, width)
            for b, (l, a) in enumerate(zip(by_step(local[...]), by_step(after[...])))
        ],
        axis=0,
    )
    earlier = jnp.concatenate(
        [
            jnp.concatenate([entered[b * SUBS : (b + 1) * SUBS], states[b * block : (b + 1) * block - SUBS]], axis=0)
            for b in (0, 1)
        ],
        axis=0,
    )
    conv, recur, inject, decay = conv_r[...], recur_r[...], inject_r[...], decay_r[...]
    rate = chan[7:8]
    mult = jnp.sqrt(one_less_exp(-16.0 * recur * rate))
    d_decay = adjoint * earlier
    d_log = d_decay * decay - adjoint * inject * conv * (decay * decay / mult)
    d_inject = adjoint * mult * conv
    d_conv = adjoint * mult * inject
    d_rate = jnp.sum(d_log * (-8.0 * recur), axis=0, keepdims=True)
    d_recur = d_log * (-8.0 * rate) * recur * (1.0 - recur)
    d_inject = d_inject * inject * (1.0 - inject)
    low = jnp.concatenate([d_recur.astype(BF16), d_inject.astype(BF16)], axis=1)
    d_conv = d_conv + lax.dot_general(low, gate[...], (((1,), (1,)), ((), ())), preferred_element_type=F32)
    gate_o[...] = lax.dot_general(conv.astype(BF16), low, (((0,), (0,)), ((), ())), preferred_element_type=F32)
    head = xb[...].astype(F32)
    halo = [head[rows + k * SUBS : rows + (k + 1) * SUBS] for k in range(edge)]
    exts = earlier_rows(by_step(head), halo, quarters, steps)
    groups = by_step(d_conv)
    for k in range(CONV):
        taps = sum(
            jnp.sum(groups[b] * exts[b][edge - k : edge - k + steps], axis=(0, 1), keepdims=True)[0] for b in (0, 1)
        )
        small_o[k : k + 1] = taps
    small_o[4:5] = jnp.sum(d_conv, axis=0, keepdims=True)
    small_o[5:6] = jnp.sum(d_recur, axis=0, keepdims=True)
    small_o[6:7] = jnp.sum(d_inject, axis=0, keepdims=True)
    small_o[7:8] = d_rate
    q = quarter_of((SUBS, width), quarters)
    for b in (0, 1):
        beyond = []
        for j in range(edge):
            same = roll(groups[b][j], -1)
            later = roll(groups[1][j], quarters - 1) if b == 0 else jnp.zeros_like(same)
            beyond.append(jnp.where(q == quarters - 1, later, same)[None])
        ext = jnp.concatenate([groups[b], *beyond], axis=0)
        total = chan[0:1][None] * ext[:steps]
        for k in range(1, CONV):
            total = total + chan[k : k + 1][None] * ext[k : k + steps]
        dx_o[b * block : (b + 1) * block] = total.reshape(block, width)
    for j in range(1, CONV):
        total = jnp.zeros((SUBS, width), F32)
        for k in range(j, CONV):
            total = total + chan[k : k + 1] * groups[0][k - j]
        spill_o[(j - 1) * SUBS : j * SUBS] = total


def by_heads(kernel, heads, head_w, arrays, outs):
    def spec(shape, tall):
        if tall:
            return pl.BlockSpec((head_w, shape[1]), lambda h: (h, 0))
        return pl.BlockSpec((shape[0], head_w), lambda h: (0, h))

    return pl.pallas_call(
        kernel,
        grid=(heads,),
        in_specs=[spec(a.shape, tall) for a, tall in arrays],
        out_specs=[spec(s, tall) for s, tall in outs],
        out_shape=[jax.ShapeDtypeStruct(s, F32) for s, _ in outs],
        compiler_params=pltpu.CompilerParams(vmem_limit_bytes=48 * 1024 * 1024),
    )(*[a for a, _ in arrays])


MESH = pl.DeviceIdType.MESH
VMEM_LIMIT = 60 * 1024 * 1024


class Links:
    def __init__(self, sizes, sends, recvs):
        self.spans, self.seqs = sizes
        self.span, self.seq = lax.axis_index("span"), lax.axis_index("seq")
        self.sends, self.recvs = sends, recvs
        self.used = 0
        self.open = []

    def flipped(self, index, mask):
        bit = 1
        while bit <= mask:
            if mask & bit:
                index = index + (1 - 2 * (index // bit % 2)) * bit
            bit *= 2
        return index

    def flipped_index(self, index, mask):
        return self.flipped(index, mask)

    def peer(self, mask):
        low, high = mask % self.seqs, mask // self.seqs
        return (self.flipped(self.span, high), self.flipped(self.seq, low))

    def other(self, mask):
        span, seq = self.peer(mask)
        return span * self.seqs + seq

    def greet(self, masks, others=()):
        barrier = pltpu.get_barrier_semaphore()
        for device in (*[self.peer(mask) for mask in masks], *others):
            pl.semaphore_signal(barrier, inc=1, device_id=device, device_id_type=MESH)
        pl.semaphore_wait(barrier, len(masks) + len(others))

    def plan(self, source, target, mask, only=None, device=None):
        slot = self.used
        self.used += 1
        device = self.peer(mask) if device is None else device
        copy = pltpu.make_async_remote_copy(
            source, target, self.sends.at[slot], self.recvs.at[slot], device_id=device, device_id_type=MESH
        )
        self.open.append((copy, only))
        return copy

    def send(self, source, target, mask, only=None):
        copy = self.plan(source, target, mask, only)
        if only is None:
            copy.start()
        else:
            pl.when(only)(copy.start)
        return copy

    def sent(self, copy):
        copy.wait_send()
        self.open = [(c, only) for c, only in self.open if c is not copy]

    def close(self):
        for copy, only in self.open:
            if only is None:
                copy.wait_send()
            else:
                pl.when(only)(copy.wait_send)


def in_turn(parts, order):
    for name in order:
        next(parts[name], None)
    for part in parts.values():
        for _ in part:
            pass


def scatter_kernel(
    sizes, share, turned, mixed, grad_x, grad_y, branch, gates, small, gain, x_own, gain_one, keep, part_own, part_other,
    proj_o, out_o, gate_o, input_o, sum_o, sends, recvs, from_part, vector, *bufs,
):
    links = Links(sizes, sends, recvs)
    spans, seqs = sizes
    count = spans * seqs
    me = links.span * seqs + links.seq
    side = me % 2
    upper = me // (count // 2)
    inner = [2 * k for k in range(1, seqs // 2)]
    core, top = seqs, count // 2
    double = 2 * share
    n = len(inner) + 1
    links.greet([1, *inner, core, top])
    whole = links.send(part_other, from_part, 1)

    def part(block, scratch, finish, shared=None):
        to_core, from_core, to_top, from_top, to_inner, from_inner, to_side, from_side = scratch
        if shared is not None:
            for copy in shared:
                links.sent(copy)
        crossing = [] if shared is None else shared
        crossing.clear()
        for i in range(2):
            for j in range(n):
                to_core[i * n + j] = block(1, (1 - i) * n + j).astype(BF16)
            crossing.append(links.send(to_core.at[pl.ds(i * n, n)], from_core.at[pl.ds(i * n, n)], core))
        mine = list(crossing)
        yield
        mine[0].wait_recv()
        over_top = {}
        for j in (*range(1, n), 0):
            to_top[j] = (block(0, n + j) + from_core[j].astype(F32)).astype(BF16)
            over_top[j] = links.send(to_top.at[j], from_top.at[j], top)
        mine[1].wait_recv()
        yield
        over_inner = []
        for j in range(1, n):
            over_top[j].wait_recv()
            to_inner[j - 1] = (block(0, j) + from_core[n + j].astype(F32) + from_top[j].astype(F32)).astype(BF16)
            over_inner.append(links.send(to_inner.at[j - 1], from_inner.at[j - 1], inner[j - 1]))
        over_top[0].wait_recv()
        yield
        total = block(0, 0) + from_core[n].astype(F32) + from_top[0].astype(F32)
        for j in range(1, n):
            over_inner[j - 1].wait_recv()
            total = total + from_inner[j - 1].astype(F32)
        yield from finish(total, to_side, from_side)

    def sided(total):
        low, high = total[:share], total[share:]
        first = side == 0
        return jnp.where(first, low, high), jnp.where(first, high, low)

    def by_columns(first, cols):
        def finish(total, to_side, from_side):
            mine, theirs = sided(total)
            to_side[...] = theirs.astype(BF16)
            copy = links.send(to_side, from_side, 1)
            yield
            copy.wait_recv()
            recv = from_side[...].astype(F32)
            proj_o[:, first : first + cols] = jnp.where(side == 0, mine, recv)
            proj_o[:, first + cols : first + 2 * cols] = jnp.where(side == 0, recv, mine)

        return finish

    def by_rows(target, to_last, from_last):
        cols = target.shape[1] // 2

        def finish(total, to_side, from_side):
            to_side[...] = total.astype(BF16)
            copy = links.send(to_side, from_side, top)
            yield
            copy.wait_recv()
            other = from_side[...].astype(F32)
            first = side == 0
            (low, low_far), (high, high_far) = sided(jnp.where(first, total, other)), sided(jnp.where(first, other, total))
            to_last[:, :cols] = low_far.astype(BF16)
            to_last[:, cols:] = high_far.astype(BF16)
            copy = links.send(to_last, from_last, 1)
            yield
            copy.wait_recv()
            holds = side == upper
            target[:, :cols] = jnp.where(holds, low, from_last[:, :cols].astype(F32))
            target[:, cols:] = jnp.where(holds, high, from_last[:, cols:].astype(F32))

        return finish

    def rows_of(c, j, whole):
        pairs = count // 2 if whole else count // 4
        owner = links.other(c * core + (j // n * top if whole else 0) + (0, *inner)[j % n])
        return pl.ds(pl.multiple_of(owner // 2 % pairs * double, 16), double)

    def columns_of(j, columns):
        return pl.ds(pl.multiple_of((upper if j < n else 1 - upper) * columns, 128), columns)

    def product(lhs, rhs):
        return lambda c, j: jnp.dot(lhs[rows_of(c, j, True)], rhs[...], preferred_element_type=F32)

    def product_half(lhs, rhs, columns):
        return lambda c, j: jnp.dot(lhs[rows_of(c, j, False)], rhs[:, columns_of(j, columns)], preferred_element_type=F32)

    def stored(blocks, columns):
        return lambda c, j: blocks[rows_of(c, j, False), columns_of(j, columns)]

    def sums():
        whole.wait_recv()
        few = 16
        own, width = x_own.shape
        vector[0] = jnp.zeros(vector.shape[1:], F32)
        vector[0, 1:2, :width] = gain[...]
        vector[0, :, width:] = small[...]

        @pl.loop(0, own // few)
        def _(k):
            here = pl.ds(pl.multiple_of(k * few, few), few)
            v = x_own[here].astype(F32)
            scale = lax.rsqrt(jnp.mean(v * v, axis=-1, keepdims=True) + EPS)
            z = v * scale
            d = part_own[here] + from_part[here].astype(F32)
            e = d * gain_one[...]
            input_o[here] = keep[here] + scale * (e - z * jnp.mean(e * z, axis=-1, keepdims=True))
            vector[0, 0:1, :width] += jnp.sum(d * z, axis=0, keepdims=True)

        slot = 1
        for masks in ([core], [top], inner):
            copies = [links.send(vector.at[0], vector.at[slot + k], m) for k, m in enumerate(masks)]
            yield
            for copy in copies:
                copy.wait_recv()
                links.sent(copy)
            total = vector[0]
            for k in range(len(masks)):
                total = total + vector[slot + k]
            vector[0] = total
            slot += len(masks)
        copy = links.send(vector.at[0], vector.at[slot], 1)
        yield
        copy.wait_recv()
        sum_o[:, :width] = vector[0, :, :width] + vector[slot, :, :width]
        sum_o[:, width:] = jnp.where(side == upper, vector[0, :, width:], vector[slot, :, width:])

    half = grad_x.shape[1]
    wide = branch.shape[1] // 2
    thin = gates.shape[1] // 2
    shared = []
    first = bufs[0]
    parts = {
        "y": part(product(turned, grad_y), [first, *bufs[1:8]], by_columns(2 * half, half), shared),
        "o": part(product_half(mixed, branch, wide), [first, *bufs[8:15]], by_rows(out_o, *bufs[15:17]), shared),
        "x": part(product(turned, grad_x), [first, *bufs[17:24]], by_columns(0, half), shared),
        "g": part(stored(gates, thin), bufs[24:32], by_rows(gate_o, *bufs[32:34])),
        "n": sums(),
    }
    in_turn(parts, "yoyxoyxgnoyxgnoygnoxoygnoxgnngg")
    links.close()


def scatter_grads(sizes, share, turned, mixed, grad_x, grad_y, branch, gates, small, gain, x_own, gain_one, keep, part_own, part_other):
    n = sizes[1] // 2
    half, wide, thin = grad_x.shape[1], branch.shape[1], gates.shape[1]
    own, width = x_own.shape
    double = 2 * share

    def scratch(cols, last, core=True):
        side = share if last is None else double
        shapes = [(2 * n, double, cols)] * (2 if core else 1) + [(n, double, cols)] * 2 + [(n - 1, double, cols)] * 2 + [(side, cols)] * 2
        if last is not None:
            shapes += [(share, last)] * 2
        return [pltpu.VMEM(s, BF16) for s in shapes]

    bufs = [*scratch(half, None), *scratch(wide // 2, wide, False), *scratch(half, None, False), *scratch(thin // 2, thin)]
    copies = 4 * (2 + n + (n - 1) + 2) + n + 4
    inside = pl.BlockSpec(memory_space=pltpu.VMEM)
    shapes = [(share, 4 * half), (share, wide), (share, thin), (own, width), (SUBS, width + half)]
    return pl.pallas_call(
        functools.partial(scatter_kernel, sizes, share),
        in_specs=[inside] * 13,
        out_specs=[inside] * 5,
        out_shape=[jax.ShapeDtypeStruct(s, F32) for s in shapes],
        scratch_shapes=[
            pltpu.SemaphoreType.DMA((copies,)), pltpu.SemaphoreType.DMA((copies,)), pltpu.VMEM((own, width), BF16),
            pltpu.VMEM((n + 3, SUBS, width + half), F32), *bufs,
        ],
        compiler_params=pltpu.CompilerParams(collective_id=1, has_side_effects=True, vmem_limit_bytes=VMEM_LIMIT),
    )(turned, mixed, grad_x, grad_y, branch, gates, small, gain, x_own, gain_one, keep, part_own, part_other)


def gelu_parts(v):
    root = 0.7978845608028654
    t = jnp.tanh(root * (v + 0.044715 * (v * v * v)))
    slope = 0.5 * (1.0 + t) + 0.5 * v * (1.0 - t * t) * root * (1.0 + 3.0 * 0.044715 * (v * v))
    return 0.5 * v * (1.0 + t), slope


def feed_kernel(sizes, masks, own, *refs):
    chunks = len(masks)
    spans = sizes[0]
    own_rows, refs = refs[0], refs[1:]
    cots, refs = refs[0], refs[1:]
    wides, refs = refs[:spans], refs[spans:]
    narrows, refs = refs[:2], refs[2:]
    grad_o, near_o, far_o, act_o, hidden_o, refs = *refs[:5], refs[5:]
    (rows_o, cots_o, wide_away, narrow_away, wide_recv, narrow_recv), refs = refs[:6], refs[6:]
    (rows, cot, wide, narrow, act, hidden, near, down_near, down_far, to_side, from_side, to_inner, from_inner,
     sends, recvs, loads, stores) = refs
    units = narrow.shape[0]
    width = narrow.shape[1]
    size = width // spans
    pair = 2 * own
    links = Links(sizes, sends, recvs)

    def load(source, target, slot):
        copy = pltpu.make_async_copy(source, target, loads.at[slot])
        copy.start()
        return copy

    first = load(own_rows, rows.at[pl.ds(0, own)], 0)
    late = [
        load(cots.at[links.flipped(links.seq // 2, masks[b // 2] // 2), b % 2], cot.at[pl.ds(b * own, own)], 1 + b)
        for b in range(2 * chunks)
    ]
    for j in range(spans):
        columns = pl.ds(j * size, size)
        late.append(load(wides[j], wide.at[:, columns], 1 + 2 * chunks + j))
        if j < 2:
            late.append(load(narrows[j], narrow.at[:, columns], 1 + 2 * chunks + spans + j))
    core, tops = sizes[1], range(2, spans, 2)
    links.greet([1, *masks[1:], core, *[m * core for m in tops]])
    first.wait()
    across = [links.send(narrows[0], narrow.at[:, pl.ds(m * size, size)], m * core) for m in tops]

    def block(b):
        return rows.at[pl.ds(b * own, own)]

    each = range(chunks)
    over_side = [links.plan(block(2 * i), block(2 * i + 1), 1) for i in each]
    over_inner = [None] + [links.plan(block(0), block(2 * i), masks[i]) for i in each[1:]]
    back_side = [links.plan(to_side.at[i], from_side.at[i], 1) for i in each]
    back_inner = [links.plan(to_inner.at[i - 1], from_inner.at[i - 1], masks[i]) for i in each[1:]]
    over_side[0].start()
    for i in each[1:]:
        over_inner[i].start()
    for copy in late:
        copy.wait()
    beside = [links.plan(narrow.at[:, pl.ds(m * size, size)], narrow.at[:, pl.ds((m + 1) * size, size)], core) for m in tops]

    def narrow_here():
        for copy, onto in zip(across, beside):
            copy.wait_recv()
            onto.start()
        for copy in beside:
            copy.wait_recv()

    def onward(i):
        over_inner[i].wait_recv()
        over_side[i].start()

    def give_on(i):
        back_side[i].wait_recv()
        to_inner[i - 1] = (near[i].astype(F32) + from_side[i].astype(F32)).astype(BF16)
        back_inner[i - 1].start()

    last = chunks - 1

    def ahead(i):
        over_side[i].wait_recv()
        if i == 0:
            for k in (2, 1):
                if k < last:
                    onward(k)
            narrow_here()

    def midway(i):
        if i == min(1, last - 1):
            for k in range(3, chunks):
                onward(k)
        if i == last:
            give_on(1)

    def behind(i):
        if 0 < i < last - 1:
            back_side[i].start()
        if i == last:
            for k in (last, last - 1, 0):
                back_side[k].start()

    def compute(i):
        here = pl.ds(pl.multiple_of(i * pair, 16), pair)
        mine = rows[here]
        given = cot[here]
        start = 0
        while start < units:
            n = min(384, units - start)
            gate = lax.dot_general(mine, wide[start : start + n], (((1,), (1,)), ((), ())), preferred_element_type=F32)
            up = lax.dot_general(
                mine, wide[units + start : units + start + n], (((1,), (1,)), ((), ())), preferred_element_type=F32
            )
            back = lax.dot_general(given, narrow[start : start + n], (((1,), (1,)), ((), ())), preferred_element_type=F32)
            value, slope = gelu_parts(gate)
            hidden[here, start : start + n] = (value * up).astype(BF16)
            act[here, start : start + n] = (back * up * slope).astype(BF16)
            act[here, units + start : units + start + n] = (back * value).astype(BF16)
            start += n
        for k in range(chunks):
            pl.when(i == k)(functools.partial(midway, k))
        step = 512

        @pl.loop(0, width // step)
        def _(k):
            columns = pl.ds(pl.multiple_of(k * step, 128), step)
            total = jnp.dot(act[here], wide[:, columns], preferred_element_type=F32)
            near[i, :, columns] = total[:own].astype(BF16)
            to_side[i, :, columns] = total[own:].astype(BF16)
            total = jnp.dot(hidden[here], narrow[:, columns], preferred_element_type=F32)
            down_near[i, :, columns] = total[:own].astype(BF16)
            down_far[i, :, columns] = total[own:].astype(BF16)

    @pl.loop(0, chunks)
    def _(i):
        for k in range(chunks):
            pl.when(i == k)(functools.partial(ahead, k))
        compute(i)
        for k in range(chunks):
            pl.when(i == k)(functools.partial(behind, k))

    out = []

    def store(source, target):
        out.append(pltpu.make_async_copy(source, target, stores.at[len(out)]))
        out[-1].start()
        return out[-1]

    own_columns, away_columns = pl.ds(0, size), pl.ds(2 * size, size)
    for source, target in (
        (act, act_o), (hidden, hidden_o), (down_near, near_o), (down_far, far_o), (rows.at[:, own_columns], rows_o),
        (cot.at[:, own_columns], cots_o),
    ):
        store(source, target)
    for copy in beside:
        links.sent(copy)

    def gradient(left, right, start, count, j):
        return lax.dot_general(
            left[:, pl.ds(start, count)], right[:, j * size : (j + 1) * size], (((0,), (0,)), ((), ())), preferred_element_type=F32
        )

    def by_tiles(total, body):
        whole = total // 384

        @pl.loop(0, whole)
        def _(k):
            body(pl.multiple_of(k * 384, 128), 384)

        if total % 384:
            body(whole * 384, total % 384)

    def give_core(left, right, held, landed):
        def tile(start, count):
            for k, j in enumerate(range(1, spans, 2)):
                held[pl.ds(start, count), k * size : (k + 1) * size] = gradient(left, right, start, count, j).astype(BF16)

        by_tiles(left.shape[1], tile)
        return links.send(held.at[:, pl.ds(0, 2 * size)], landed, core)

    def give_top(left, right, held, landed, came, target):
        came.wait_recv()
        store(landed.at[:, pl.ds(size, size)], held.at[:, away_columns]).wait()
        out.pop()

        def tile(start, count):
            here = pl.ds(start, count)
            total = gradient(left, right, start, count, 2) + held[here, 2 * size : 3 * size].astype(F32)
            held[here, 3 * size : 4 * size] = total.astype(BF16)

        by_tiles(left.shape[1], tile)
        store(held.at[:, pl.ds(3 * size, size)], target)

    crossing = give_core(act, rows, wide, wide_recv)
    give_on(last)
    crossing_narrow = give_core(hidden, cot, narrow, narrow_recv)
    for k in range(last - 1, 1, -1):
        give_on(k)
    give_top(act, rows, wide, wide_recv, crossing, wide_away)
    give_top(hidden, cot, narrow, narrow_recv, crossing_narrow, narrow_away)
    back_side[0].wait_recv()
    for k in range(chunks - 1):
        back_inner[k].wait_recv()
    for j in range(spans):
        columns = slice(j * size, (j + 1) * size)
        total = near[0, :, columns].astype(F32) + from_side[0, :, columns].astype(F32)
        for k in range(chunks - 1):
            total = total + from_inner[k, :, columns].astype(F32)
        grad_o[:, pl.ds(pl.multiple_of(links.flipped(links.span, j) * size, 128), size)] = total
    for copy in out:
        copy.wait()
    links.close()


def feed_forward(sizes, masks, own_rows, cots, wides, narrows):
    own, width = own_rows.shape
    units = narrows[0].shape[0]
    chunks = len(masks)
    total = 2 * chunks * own
    anywhere = pl.BlockSpec(memory_space=pl.ANY)
    copies = 4 * chunks + sizes[0] + 2
    blocks = (chunks, own, width)
    spans = sizes[0]
    size = width // spans
    shapes = [
        blocks, blocks, (total, 2 * units), (total, units), (total, size), (total, size), (2 * units, size), (units, size),
        (2 * units, 2 * size), (units, 2 * size),
    ]
    held = [
        (total, width), (total, width), (2 * units, width), (units, width), (total, 2 * units), (total, units), blocks, blocks,
        blocks, blocks, blocks, (chunks - 1, own, width), (chunks - 1, own, width),
    ]
    return pl.pallas_call(
        functools.partial(feed_kernel, sizes, masks, own),
        in_specs=[anywhere] * (4 + len(wides)),
        out_specs=[pl.BlockSpec(memory_space=pltpu.VMEM)] + [anywhere] * len(shapes),
        out_shape=[jax.ShapeDtypeStruct((own, width), F32)] + [jax.ShapeDtypeStruct(s, BF16) for s in shapes],
        scratch_shapes=[pltpu.VMEM(s, BF16) for s in held]
        + [pltpu.SemaphoreType.DMA((k,)) for k in (copies, copies, 3 + 2 * chunks + len(wides), 8)],
        compiler_params=pltpu.CompilerParams(collective_id=2, has_side_effects=True, vmem_limit_bytes=VMEM_LIMIT),
    )(own_rows, cots, *wides, *narrows)


def expanded(v, quarters):
    return spread(v, quarters, 0), spread(roll(v, -1), quarters, 0)


def chunk_inflow(links, line, blocks, quarters, backward, between):
    n, spans = line.shape[0], blocks.shape[0]
    place = links.seq // 2
    copies = [links.send(line.at[0], line.at[k], 2 * k) for k in range(1, n)]
    for copy in copies:
        copy.wait_recv()
    between()
    one, nought = jnp.ones(line.shape[1:], F32), jnp.zeros(line.shape[1:], F32)
    prod, total = one, nought
    all_prod, all_total = one, nought

    def ordered(count):
        return range(count - 1, -1, -1) if backward else range(count)

    def ahead(j, at):
        return at < j if backward else at > j

    for j in ordered(n):
        p, s = expanded(line[links.flipped(place, j)], quarters)
        inside = ahead(j, place)
        total = jnp.where(inside, p * total + s, total)
        prod = jnp.where(inside, p * prod, prod)
        all_total = p * all_total + s
        all_prod = p * all_prod
    q = quarter_of(line.shape[1:], quarters)
    blocks[0] = jnp.where(q == 0, all_prod, all_total)
    copies = [links.send(blocks.at[0], blocks.at[m], m * links.seqs) for m in range(1, spans)]
    for copy in copies:
        copy.wait_recv()
    h = nought
    for j in ordered(spans):
        p, s = expanded(blocks[links.flipped(links.span, j)], quarters)
        h = jnp.where(ahead(j, links.span), p * h + s, h)
    return prod * h + total


def by_head(heads, head_w, body):
    @pl.loop(0, heads)
    def _(h):
        start = pl.multiple_of(h * head_w, 128)
        columns = pl.ds(start, head_w)
        body(lambda ref: ref.at[:, columns], lambda ref: ref.at[pl.ds(start, head_w)])


def front_kernel(
    sizes, steps, quarters, heads, head_w, share, x_own, halo, params_in, rec_proj, out_proj, gate_weight, cot, wide, narrow, *refs
):
    spans, seqs = sizes
    count = spans * seqs
    inner = [2 * k for k in range(1, seqs // 2)]
    n = len(inner) + 1
    core, top = seqs, count // 2
    (normal, xb, y_pre, conv, recur, inject, decay, states, flow, mixed, resid, normal_two, params, chan, turned, mixed_turned), refs = (
        refs[:16], refs[16:]
    )
    (proj_x, proj_y, out_half, gates), refs = refs[:4], refs[4:]
    wides, beside_narrow, cots, refs = refs[: spans - 1], refs[spans - 1], refs[spans], refs[spans + 1 :]
    (lead, held_x, held_y, held_o, held_g, every, prod, enter, line, blocks, inflow, to_side, from_side, low,
     sends, recvs, locals_) = refs
    links = Links(sizes, sends, recvs)
    me = links.span * seqs + links.seq
    side, upper = me % 2, me // (count // 2)
    own, width = x_own.shape
    rows = 2 * own
    half = width // 2
    double = 2 * share
    links.greet([1, *inner, *[m * seqs for m in range(1, spans)]])
    kept = [0]

    def local(source, target, only=None):
        copy = pltpu.make_async_copy(source, target, locals_.at[kept[0]])
        kept[0] += 1
        if only is None:
            copy.start()
        else:
            pl.when(only)(copy.start)
        return copy

    z = links.seq // 2
    offsets = [o for s in range(1, n) for o in (-s, s)]
    there = {o: jnp.logical_and(z + o >= 0, z + o < n) for o in offsets}
    beyond = {-1: (links.span, jnp.maximum(links.seq - 2, 0)), 1: (links.span, jnp.minimum(links.seq + 2, seqs - 1))}

    def along(piece):
        passing = {}
        for o in (0, *offsets):
            for way in (-1, 1):
                if o * way <= 0 and abs(o) + 1 < n:
                    both = jnp.logical_and(there[way], there[o]) if o else there[way]
                    passing[o, way] = links.plan(piece(o), piece(o), None, both, beyond[way])
        return passing

    def arrival(passing, o):
        way = 1 if o < 0 else -1
        return passing[o + way, way]

    def begin(passing):
        for way in (-1, 1):
            pl.when(there[way])(passing[0, way].start)

    def take(passing, o):
        arrival(passing, o).wait_recv()
        way = 1 if o < 0 else -1
        if (o, way) in passing:
            pl.when(there[way])(passing[o, way].start)

    def pieces_out(own_out, piece, part, far):
        passing = along(piece)
        over_top = {o: links.plan(piece(o), piece(o), top, there[o]) for o in offsets}
        over_core = {o: links.plan(part(o), part(o), core, there[o]) for o in offsets}
        far_core = {o: links.plan(far(o), far(o), core, there[o]) for o in offsets}
        begin(passing)
        first_core = links.send(own_out, own_out, core)
        first_top = first_far = None
        if far(0) is not None:
            first_top = links.send(piece(0), piece(0), top)
        yield
        for o in offsets:

            @pl.when(there[o])
            def _():
                take(passing, o)
                over_top[o].start()
                over_core[o].start()

            if o == offsets[len(offsets) // 2 - 1]:
                yield
        yield
        if first_top is not None:
            first_top.wait_recv()
            first_far = links.send(far(0), far(0), core)
        for o in offsets:

            @pl.when(there[o])
            def _():
                over_top[o].wait_recv()
                far_core[o].start()

        yield
        first_core.wait_recv()
        if first_far is not None:
            first_far.wait_recv()
        for o in offsets:

            @pl.when(there[o])
            def _():
                over_core[o].wait_recv()
                far_core[o].wait_recv()

    def pieces_direct(whole, piece):
        over_inner = {m: links.send(piece(0), piece(0), m) for m in inner}
        over_core = [links.send(whole, whole, core)]
        over_top = {}
        yield
        for m in inner:
            over_inner[m].wait_recv()
            here = piece(links.flipped(z, m // 2) - z)
            over_top[m] = links.send(here, here, top)
            over_core.append(links.send(here, here, core))
        yield
        for m in inner:
            over_top[m].wait_recv()
            here = piece(links.flipped(z, m // 2) - z, 1 - upper)
            over_core.append(links.send(here, here, core))
        yield
        for copy in over_core:
            copy.wait_recv()

    def columns_part(source, first, target):
        def piece(o, over=0):
            device = (links.other(over) if over else me) + 2 * o
            start = jnp.clip(device // 2 * double, 0, target.shape[0] - double)
            return target.at[pl.ds(pl.multiple_of(start, 16), double)]

        def columns(which):
            return source.at[:, pl.ds(pl.multiple_of(first + which * half, 128), half)]

        row = target.at[pl.ds(pl.multiple_of(me * share, 16), share)]
        mine = local(columns(side), row)
        theirs = links.send(columns(1 - side), row, 1)
        yield
        mine.wait()
        theirs.wait_recv()
        yield from pieces_out(piece(0), piece, piece, lambda o: piece(o, top))

    def rows_part(source, target, direct):
        cols = source.shape[1]
        pairs_half = count // 4

        def rows_at(start, size):
            return target.at[pl.ds(pl.multiple_of(start, 16), size)]

        begin_at = me // 2 % pairs_half * double

        def piece(o, which=None):
            start = jnp.clip(begin_at + o * double, 0, target.shape[0] - double)
            which = upper if which is None else which
            return target.at[pl.ds(pl.multiple_of(start, 16), double), pl.ds(pl.multiple_of(which * (cols // 2), 128), cols // 2)]

        holds = side == upper
        row = rows_at(begin_at + side * share, share)
        mine = local(source, row, holds)
        gift = links.send(source, row, 1, side != upper)
        yield

        @pl.when(holds)
        def _():
            mine.wait()
            gift.wait_recv()

        whole = rows_at(begin_at, double)
        across = links.send(whole, whole, top, holds)
        yield
        pl.when(side != upper)(across.wait_recv)
        if direct:
            yield from pieces_direct(whole, piece)
        else:
            yield from pieces_out(whole, piece, piece, lambda o: piece(o, 1 - upper) if o else None)

    def small_part():
        height = params_in.shape[0]

        def rows_of(device):
            return every.at[pl.ds(pl.multiple_of(device // 2 * 2 * height, 16), 2 * height)]

        row = pl.ds(pl.multiple_of(me * height, 16), height)
        every[row] = params_in[...]
        theirs = links.send(every.at[row], every.at[row], 1)
        yield
        theirs.wait_recv()
        held = [me]
        for masks in (inner, [top], [core]):
            copies = [links.send(rows_of(d), rows_of(d), m) for d in held for m in masks]
            held = held + [links.flipped_index(d, m) for d in held for m in masks]
            yield
            for copy in copies:
                copy.wait_recv()
        params[...] = jnp.zeros_like(params)
        lanes = params_in.shape[1]
        for d in range(count):
            tile = every[d * height : (d + 1) * height]
            base, shift = d * share // lanes * lanes, d * share % lanes
            if shift + share <= lanes:
                params[:, base : base + lanes] += pltpu.roll(tile, shift, 1) if shift else tile
            else:
                turned = pltpu.roll(jnp.concatenate([tile, jnp.zeros_like(tile)], axis=1), shift, 1)
                params[:, base : base + 2 * lanes] += turned
        chan[...] = params[:SUBS, pl.ds(pl.multiple_of(side * half, 128), half)]

    parts = {
        "x": columns_part(rec_proj, 0, proj_x),
        "v": small_part(),
        "g": rows_part(gate_weight, gates, False),
        "y": columns_part(rec_proj, 2 * half, proj_y),
        "o": rows_part(out_proj, out_half, True),
    }

    def advance(order):
        for name in order:
            next(parts[name], None)

    place = pl.ds(pl.multiple_of(side * own, 16), own)
    def cot_at(o, far=0):
        return cots.at[jnp.clip(z + o, 0, n - 1), far]

    cot_inner = [links.plan(cot_at(0), cot_at(0), m) for m in inner]
    cot_side = []
    own_cot = local(cot, cot_at(0))
    advance("xvgoy")
    tokens = links.send(x_own, lead.at[place], 1)
    lead[place] = x_own[...]
    lead[rows:] = halo[...]
    advance("xvgo")
    own_cot.wait()
    own_side = links.send(cot_at(0), cot_at(0, 1), 1)
    advance("xvxgyov")
    advance("ggxgvyyxg")
    loads = [local(proj_x, held_x), local(gates, held_g)]
    tokens.wait_recv()
    few = 16

    @pl.loop(0, lead.shape[0] // few)
    def _(k):
        here = pl.ds(pl.multiple_of(k * few, few), few)
        normal[here] = normed(lead[here].astype(F32), params[SUBS : SUBS + 1]).astype(BF16)

    for copy in loads:
        copy.wait()

    def gate(cols, tall):
        cols(xb)[...] = jnp.dot(normal[...], cols(held_x)[...], preferred_element_type=F32).astype(BF16)
        forward_kernel(
            steps, quarters, cols(xb), cols(chan), tall(held_g), cols(conv), cols(recur), cols(inject), cols(decay),
            cols(states), cols(prod), cols(enter), cols(line.at[0]),
        )

    by_head(heads, head_w, gate)
    inflow[...] = chunk_inflow(links, line, blocks, quarters, False, lambda: [copy.start() for copy in cot_inner])
    advance("o")
    tops = [2 * seqs * k for k in range(1, spans // 2)]
    across = {m: links.send(wide, wides[m // seqs - 1], m) for m in tops}
    beside = [links.send(wide, wides[0], core), links.send(narrow, beside_narrow, core)]
    def onward(k):
        cot_inner[k].wait_recv()
        here = links.flipped(z, inner[k] // 2) - z
        cot_side.append(links.send(cot_at(here), cot_at(here, 1), 1))

    advance("yy")
    loads = [local(proj_y, held_y)]
    loads[0].wait()
    block = steps * SUBS

    def mix(cols, tall):
        cols(y_pre)[...] = jnp.dot(normal[:rows], cols(held_y)[...], preferred_element_type=F32)
        ins, flows, hold, gain_y = cols(inflow), cols(flow), cols(states), cols(y_pre)
        for b in (0, 1):
            entered = cols(enter)[b * SUBS : (b + 1) * SUBS] * ins[...] + cols(enter)[(2 + b) * SUBS : (3 + b) * SUBS]
            flows[b * SUBS : (b + 1) * SUBS] = entered
            flows[(2 + b) * SUBS : (3 + b) * SUBS] = cols(prod)[(b + 1) * block - SUBS : (b + 1) * block]
            here = slice(b * block, (b + 1) * block)
            total = hold[here].reshape(steps, SUBS, head_w) + cols(prod)[here].reshape(steps, SUBS, head_w) * entered[None]
            total = total.reshape(block, head_w)
            hold[here] = total
            low_part = total * gelu_parts(gain_y[here])[0]
            cols(mixed)[here] = low_part.astype(BF16)
            tall(mixed_turned)[:, here] = low_part.T.astype(BF16)

    by_head(heads, head_w, mix)

    onward(0)
    advance("oo")
    load = local(out_half, held_o)
    load.wait()
    step = 512

    @pl.loop(0, width // step)
    def _(k):
        columns = pl.ds(pl.multiple_of(k * step, 128), step)
        total = jnp.dot(mixed[...], held_o[:, columns], preferred_element_type=F32)
        first = side == 0
        resid[:, columns] = x_own[:, columns].astype(F32) + jnp.where(first, total[:own], total[own:])
        to_side[:, columns] = jnp.where(first, total[own:], total[:own]).astype(BF16)

    partial = links.send(to_side, from_side, 1)
    for k in range(1, n - 2):
        onward(k)

    @pl.loop(0, width // head_w)
    def _(k):
        columns = pl.ds(pl.multiple_of(k * head_w, 128), head_w)
        turned[columns] = normal[:rows, columns].astype(F32).T.astype(BF16)

    partial.wait_recv()
    size = width // spans

    @pl.loop(0, own // few)
    def _(k):
        here = pl.ds(pl.multiple_of(k * few, few), few)
        total = resid[here] + from_side[here].astype(F32)
        resid[here] = total
        low[here] = normed(total, params[SUBS + 1 : SUBS + 2]).astype(BF16)

    for j in range(spans):
        start = pl.multiple_of(links.flipped(links.span, j) * size, 128)
        normal_two[:, j * size : (j + 1) * size] = low[:, pl.ds(start, size)]

    onward(n - 2)
    for m in tops:
        across[m].wait_recv()
        beside.append(links.send(wides[m // seqs - 1], wides[m // seqs], core))
    for copy in (*beside, own_side, *cot_side):
        copy.wait_recv()
    for part in parts.values():
        for _ in part:
            pass
    links.close()


def front(sizes, steps, quarters, heads, head_w, x_own, halo, params, rec_proj, out_proj, gate_weight, cot, wide, narrow):
    spans, seqs = sizes
    count = spans * seqs
    own, width = x_own.shape
    half, rows, share = width // 2, 2 * own, rec_proj.shape[0]
    n = seqs // 2
    inside, anywhere = pl.BlockSpec(memory_space=pltpu.VMEM), pl.BlockSpec(memory_space=pl.ANY)

    def high(*shape):
        return jax.ShapeDtypeStruct(shape, F32)

    def low(*shape):
        return jax.ShapeDtypeStruct(shape, BF16)

    lead = rows + halo.shape[0]
    near = [
        low(lead, width), low(lead, half), *[high(rows, half)] * 6, high(4 * SUBS, half), low(rows, half), high(own, width),
        low(own, width), high(params.shape[0], width), high(SUBS, half),
        low(width, rows), low(half, rows),
    ]
    far = [
        low(width, half), low(width, half), low(half, width), low(half, gate_weight.shape[1]), *[low(*wide.shape)] * (spans - 1),
        low(*narrow.shape), low(n, 2, *cot.shape),
    ]
    end = (SUBS, half)
    copies = 4 * (3 + 10 * n) + 4 * n + 3 + 6 * n + (n - 1) + 2 * spans + 4
    outs = pl.pallas_call(
        functools.partial(front_kernel, sizes, steps, quarters, heads, head_w, share),
        in_specs=[inside] * 7 + [anywhere] * 2,
        out_specs=[inside] * len(near) + [anywhere] * len(far),
        out_shape=[*near, *far],
        scratch_shapes=[
            pltpu.VMEM((lead, width), BF16), pltpu.VMEM((width, half), BF16), pltpu.VMEM((width, half), BF16),
            pltpu.VMEM((half, width), BF16), pltpu.VMEM((half, gate_weight.shape[1]), BF16), pltpu.VMEM((count * params.shape[0], params.shape[1]), F32),
            pltpu.VMEM((rows, half), F32), pltpu.VMEM((4 * SUBS, half), F32), pltpu.VMEM((n, *end), F32),
            pltpu.VMEM((spans, *end), F32), pltpu.VMEM(end, F32), *[pltpu.VMEM((own, width), BF16)] * 3,
            pltpu.SemaphoreType.DMA((copies,)), pltpu.SemaphoreType.DMA((copies,)), pltpu.SemaphoreType.DMA((16,)),
        ],
        compiler_params=pltpu.CompilerParams(collective_id=0, has_side_effects=True, vmem_limit_bytes=VMEM_LIMIT),
    )(x_own, halo, params, rec_proj, out_proj, gate_weight, cot, wide, narrow)
    wides, narrows, cots = outs[20 : 19 + spans], outs[19 + spans], outs[20 + spans]
    return outs[:16], outs[16:20], [wide, *wides], [narrow, narrows], cots


def return_kernel(
    sizes, steps, quarters, heads, inner, branch, out_w, y_pre, states, decay, flow, conv, recur, inject, xb, chan, gate,
    resid, near, far, wide, narrow, branch_o, y_grad, x_grad, gate_o, small, output, wides, narrows, dx, spill, came_back, grad, local, after, enter, carry, line, blocks, inflow, dmix, from_side, to_inner, from_inner, sends, recvs,
):
    spans, seqs = sizes
    tops = [2 * seqs * k for k in range(1, spans // 2)]
    n = len(inner) + 1
    links = Links(sizes, sends, recvs)
    side = links.seq % 2
    own, width = branch.shape
    me, count = links.span * seqs + links.seq, spans * seqs

    def device(index):
        return (index // seqs, index % seqs)

    links.greet([1, *inner, *[m * seqs for m in range(1, spans)]], [device((me + 2) % count)])
    place = pl.ds(pl.multiple_of(side * own, 16), own)
    whole = links.send(branch, branch_o.at[place], 1)
    tall = wide.shape[1] // 2
    across = [links.send(wide.at[k, pl.ds(0, tall)], wides.at[k, pl.ds(0, tall)], m) for k, m in enumerate(tops)]
    branch_o[place] = branch[...]
    whole.wait_recv()
    sums = [*range(1, n), 0]
    over_side = {}

    def side_sum(i):
        over_side[sums[i]] = links.send(far.at[sums[i]], from_side.at[sums[i]], 1)

    over_inner = []

    def inner_sum(i):
        k = sums[i]
        over_side[k].wait_recv()
        if k:
            to_inner[k - 1] = (near[k].astype(F32) + from_side[k].astype(F32)).astype(BF16)
            over_inner.append(links.send(to_inner.at[k - 1], from_inner.at[k - 1], inner[k - 1]))

    side_sum(0)
    head_w = gate.shape[1] // 2

    def first(cols, tall):
        mixed_grad = lax.dot_general(branch_o[...], tall(out_w)[...], (((1,), (1,)), ((), ())), preferred_element_type=F32)
        value, slope = gelu_parts(cols(y_pre)[...])
        cols(grad)[...] = mixed_grad * value
        cols(y_grad)[...] = (mixed_grad * cols(states)[...] * slope).astype(BF16)
        adjoint_kernel(
            steps, quarters, cols(grad), cols(decay), cols(flow), cols(local), cols(after), cols(enter), cols(line.at[0])
        )

    by_head(heads, head_w, first)

    def between():
        inner_sum(0)
        side_sum(1)

    inflow[...] = chunk_inflow(links, line, blocks, quarters, True, between)
    for k, m in enumerate(tops):
        across.append(links.send(wide.at[k, pl.ds(tall, tall)], wides.at[k, pl.ds(tall, tall)], m))
        across.append(links.send(narrow.at[k], narrows.at[k], m))
    inner_sum(1)
    side_sum(2)

    def second(cols, tall):
        came = jnp.concatenate(
            [
                cols(enter)[b * SUBS : (b + 1) * SUBS] * cols(inflow)[...] + cols(enter)[(2 + b) * SUBS : (3 + b) * SUBS]
                for b in (0, 1)
            ],
            axis=0,
        )
        backward_kernel(
            steps, quarters, cols(local), cols(after), cols(states), came, cols(flow), cols(conv), cols(recur),
            cols(inject), cols(decay), cols(xb), cols(chan), tall(gate), cols(dx), cols(spill), tall(gate_o), cols(small),
        )

    by_head(heads, head_w, second)
    edge = (CONV - 1) * SUBS
    slot = links.used
    links.used += 1
    handed = pltpu.make_async_remote_copy(
        spill, came_back, links.sends.at[slot], links.recvs.at[slot], device_id=device(jnp.maximum(me - 2, 0)), device_id_type=MESH
    )
    pl.when(me >= 2)(handed.start)
    links.open.append((handed, me >= 2))
    rows = 2 * own
    x_grad[: rows - 2 * edge] = dx[: rows - 2 * edge].astype(BF16)
    for i in range(2, n):
        inner_sum(i)
        if i + 1 < n:
            side_sum(i + 1)
    pl.when(me + 2 < count)(handed.wait_recv)

    @pl.when(me + 2 >= count)
    def _():
        came_back[...] = jnp.zeros_like(came_back)

    last = quarter_of((SUBS, came_back.shape[1]), quarters) == quarters - 1
    total = [dx[rows - 2 * edge : rows - edge]]
    for k in range(CONV - 1, 0, -1):
        added = roll(came_back[(k - 1) * SUBS : k * SUBS], quarters - 1)
        total.append(dx[rows - k * SUBS : rows - (k - 1) * SUBS] + jnp.where(last, added, 0.0))
    x_grad[rows - 2 * edge :] = jnp.concatenate(total, axis=0).astype(BF16)
    few = 16
    size = width // spans
    for copy in over_inner:
        copy.wait_recv()

    for j in range(spans):
        columns = slice(j * size, (j + 1) * size)
        there = pl.ds(pl.multiple_of(links.flipped(links.span, j) * size, 128), size)
        total = resid[:, there] + near[0, :, columns].astype(F32) + from_side[0, :, columns].astype(F32)
        for k in range(n - 1):
            total = total + from_inner[k, :, columns].astype(F32)
        output[:, there] = total.astype(BF16)

    for copy in across:
        copy.wait_recv()
    links.close()


def returned(sizes, steps, quarters, heads, inner, branch, out_w, y_pre, states, decay, flow, conv, recur, inject, xb, chan, gate,
             resid, near, far, wide, narrow):
    spans, _ = sizes
    own, width = branch.shape
    rows, half = y_pre.shape
    n = len(inner) + 1
    inside, anywhere = pl.BlockSpec(memory_space=pltpu.VMEM), pl.BlockSpec(memory_space=pl.ANY)

    def high(*shape):
        return jax.ShapeDtypeStruct(shape, F32)

    def low(*shape):
        return jax.ShapeDtypeStruct(shape, BF16)

    shapes = [
        low(rows, width), low(rows, half), low(rows, half), high(*gate.shape), high(SUBS, half), low(own, width),
        low(*wide.shape), low(*narrow.shape),
    ]
    end = (SUBS, half)
    copies = 3 * (spans // 2) + 2 * n + 2 * n + spans + 2
    tail = ((CONV - 1) * SUBS, half)
    return pl.pallas_call(
        functools.partial(return_kernel, sizes, steps, quarters, heads, inner),
        in_specs=[inside] * 15 + [anywhere] * 2,
        out_specs=[inside] * 6 + [anywhere] * 2,
        out_shape=shapes,
        scratch_shapes=[
            pltpu.VMEM((rows, half), F32), pltpu.VMEM(tail, F32), pltpu.VMEM(tail, F32), *[pltpu.VMEM((rows, half), F32)] * 3, pltpu.VMEM((4 * SUBS, half), F32), pltpu.VMEM(end, F32),
            pltpu.VMEM((n, *end), F32), pltpu.VMEM((spans, *end), F32), pltpu.VMEM(end, F32), pltpu.VMEM(end, F32),
            pltpu.VMEM((n, own, width), BF16), pltpu.VMEM((n - 1, own, width), BF16), pltpu.VMEM((n - 1, own, width), BF16),
            pltpu.SemaphoreType.DMA((copies,)), pltpu.SemaphoreType.DMA((copies,)),
        ],
        compiler_params=pltpu.CompilerParams(collective_id=4, has_side_effects=True, vmem_limit_bytes=VMEM_LIMIT),
    )(branch, out_w, y_pre, states, decay, flow, conv, recur, inject, xb, chan, gate, resid, near, far, wide, narrow)


def on_device(
    inputs, norm_one, rec_proj, conv_weight, conv_bias, gate_weight, gate_bias, decay_param, out_proj, norm_two,
    mlp_wide, mlp_narrow, cotangent,
):
    spans, seqs = lax.axis_size("span"), lax.axis_size("seq")
    count = spans * seqs
    span, seq = lax.axis_index("span"), lax.axis_index("seq")
    me = span * seqs + seq
    side = me % 2
    pair = me // 2
    pairs = count // 2
    batch, tokens, width = inputs.shape
    half = width // 2
    quarters = SUBS // batch
    steps = tokens // quarters
    own = batch * tokens
    rows = 2 * own
    head_w = gate_weight.shape[1] // 2
    heads = half // head_w
    edge = CONV - 1
    share = width // count
    units = mlp_narrow.shape[1]
    inner = [2 * k for k in range(1, seqs // 2)]
    core = seqs
    xs = [2 * seqs * k for k in range(1, spans // 2)]
    top = count // 2
    upper = me // top
    chunk_masks = [0, *inner[1::-1], *inner[2:]]

    def to_rows(v):
        return v.reshape(batch, quarters, steps, width).transpose(2, 0, 1, 3).reshape(own, width)

    def from_rows(v):
        return v.reshape(steps, batch, quarters, width).transpose(1, 2, 0, 3).reshape(batch, tokens, width)

    def in_order(mine, other, axis):
        return jnp.concatenate([jnp.where(side == 0, mine, other), jnp.where(side == 0, other, mine)], axis=axis)

    def cut(v, index, size, axis):
        return lax.dynamic_slice_in_dim(v, index * size, size, axis)

    direct = share % 16 == 0 and (spans, seqs) == (4, 8)

    def gathered_rows(block, buffer, place):
        pieces = {0: block}
        for m in inner:
            pieces[m] = swap(block, m)
        for m in xs:
            for n in (0, *inner):
                pieces[m ^ n] = swap(pieces[n], m)
        for n in list(pieces):
            pieces[core ^ n] = swap(pieces[n], core)
        for m, piece in pieces.items():
            buffer = lax.dynamic_update_slice_in_dim(buffer, piece, place(me ^ m), 0)
        return buffer

    def columns_half(block):
        mine, theirs = cut(block, side, half, 1), cut(block, 1 - side, half, 1)
        block = in_order(mine, swap(theirs, 1), 0)
        return gathered_rows(block, jnp.zeros((width, half), BF16), lambda d: d // 2 * 2 * share)

    def rows_half(block):
        full = lax.all_gather(block, AXES, axis=0, tiled=True)
        return cut(full, side, half, 0)

    def by_span(v):
        size = width // spans
        return jnp.concatenate([cut(v, span ^ j, size, 1) for j in range(spans)], axis=1)

    def over_sides(partial):
        partial = partial.reshape(2, own, width)
        other = lax.dynamic_index_in_dim(partial, 1 - side, 0, keepdims=False).astype(BF16)
        return lax.dynamic_index_in_dim(partial, side, 0, keepdims=False) + swap(other, 1).astype(F32)

    def exchanged(carry):
        every = lax.all_gather(carry, AXES, axis=0).reshape(pairs, 2, batch, quarters, half)
        every = lax.dynamic_index_in_dim(every, side, 1, keepdims=False)
        return every[:, :, 0], every[:, :, 1]

    def entering(enter, h):
        enter = enter.reshape(2, 2, SUBS, half)
        return enter[0] * jnp.repeat(h, quarters, axis=0)[None] + enter[1]

    def by_steps(v):
        return v.reshape(2, steps, SUBS, half)

    def span_gather(block):
        pieces = {0: block}
        for m in xs:
            pieces[m] = swap(block, m)
        for n in list(pieces):
            pieces[n ^ core] = swap(pieces[n], core)
        return [pieces[m * seqs] for m in range(spans)]

    def token_gather(v):
        blocks = [v] + [swap(v, m) for m in inner]
        return [b for block in blocks for b in (block, swap(block, 1))]

    small = jnp.stack([*conv_weight.T, conv_bias, *gate_bias.T, decay_param, norm_one, norm_two]).astype(F32)
    small = jnp.concatenate([small[:7], jax.nn.softplus(small[7:8]), small[8:]], axis=0)
    wide_own = mlp_wide.transpose(1, 2, 0).reshape(2 * units, width // spans)
    narrow_own = mlp_narrow.T
    grads_own = by_span(to_rows(cotangent))
    c = to_rows(cotangent).astype(F32)

    mine = to_rows(inputs)
    x = mine.astype(F32)
    tail = inputs[:, tokens - edge :]
    halo = lax.ppermute(tail, AXES, [(i, i + 1) for i in range(1, count - 1, 2)]) + lax.ppermute(
        tail, AXES, [(i, i + 2) for i in range(1, count - 2, 2)]
    )
    halo = jnp.zeros((edge, batch, quarters, width), BF16).at[:, :, 0].set(halo[:, ::-1].transpose(1, 0, 2))
    halo = jnp.concatenate([halo.reshape(edge * SUBS, width), jnp.zeros((8, width), BF16)], axis=0)

    if direct:
        packed = jnp.pad(small, ((0, 6), (0, -share % 128)))
        nearby, (proj_x, proj_y, out_half, gates), wides, narrows, cots = front(
            (spans, seqs), steps, quarters, heads, head_w, mine, halo, packed, rec_proj, out_proj, gate_weight, grads_own,
            wide_own, narrow_own,
        )
        normal_one, x_branch, y_pre, conv, recur, inject, decay, states, flow, mixed, resid, normal_two, params, chan, turned, mixed_turned = nearby
        gain_one, gain_two = params[SUBS], params[SUBS + 1]
    else:
        proj_x = columns_half(rec_proj[:, :width])
        proj_y = columns_half(rec_proj[:, width:])
        gates = rows_half(gate_weight)
        out_half = rows_half(out_proj)
        small = lax.all_gather(small, AXES, axis=1, tiled=True)
        gain_one, gain_two = small[SUBS], small[SUBS + 1]
        chan = cut(small[:SUBS], side, half, 1)
        lead = jnp.concatenate([in_order(mine, swap(mine, 1), 0), halo], axis=0)
        normal_one = normed(lead.astype(F32), gain_one).astype(BF16)
        x_branch = nn(normal_one, proj_x, BF16)
        normal_one = normal_one[:rows]
        y_pre = nn(normal_one, proj_y)
        y_branch, gelu_back = jax.vjp(jax.nn.gelu, y_pre)
        kernel = functools.partial(forward_kernel, steps, quarters)
        full = ((rows, half), False)
        ends = ((4 * SUBS, half), False)
        conv, recur, inject, decay, local, prod, enter, carry = by_heads(
            kernel, heads, head_w, [(x_branch, False), (chan, False), (gates, True)],
            [full] * 6 + [ends, ((SUBS, half), False)],
        )
        prods, sums = exchanged(carry)
        h = jnp.zeros((batch, half), F32)
        for j in range(pairs - 1):
            h = jnp.where(j < pair, prods[j] * h + sums[j], h)
        entered = entering(enter, h)
        states = (by_steps(local) + by_steps(prod) * entered[:, None]).reshape(rows, half)
        flow = jnp.concatenate([entered, by_steps(prod)[:, -1]], axis=0).reshape(4 * SUBS, half)
        mixed = (states * y_branch).astype(BF16)
        resid = x + over_sides(nn(mixed, out_half))
        normal_two = by_span(normed(resid, gain_two).astype(BF16))
        wides, narrows = span_gather(wide_own), span_gather(narrow_own)
        cots = token_gather(grads_own)

    def token_scatter(near, far):
        total = None
        for k, m in enumerate((0, *inner)):
            block = near[k].astype(F32) + swap(far[k], 1).astype(F32)
            total = block if m == 0 else total + swap(block.astype(BF16), m).astype(F32)
        return by_span(total)

    size = width // spans

    def by_core(v):
        blocks = [v[:, j * size : (j + 1) * size] for j in range(spans)]
        return [*blocks[::2], jnp.concatenate(blocks[1::2], axis=1)]

    if direct:
        normal_two_grad, near, far, all_act, all_hidden, *features, wide_away, narrow_away, wide_recv, narrow_recv = feed_forward(
            (spans, seqs), chunk_masks, normal_two, cots, wides, narrows
        )
        all_normal, all_grads = [features[0]], [features[1]]
        wide_away, narrow_away, wide_recv, narrow_recv = wide_away[None], narrow_away[None], wide_recv[:, :size], narrow_recv[:, :size]
    else:
        wide, narrow = jnp.concatenate(wides, axis=1), jnp.concatenate(narrows, axis=1)
        all_normal = jnp.concatenate(token_gather(normal_two), axis=0)
        all_grads = jnp.concatenate(cots, axis=0)

        def activate(values):
            return jax.nn.gelu(values[:, :units]) * values[:, units:]

        value, back = jax.vjp(activate, nt(all_normal, wide))
        all_hidden = value.astype(BF16)
        all_act = back(nt(all_grads, narrow))[0].astype(BF16)

        def sided(v):
            v = v.reshape(len(inner) + 1, 2, own, width)
            return v[:, 0], v[:, 1]

        all_normal, all_grads = by_core(all_normal), by_core(all_grads)
        normal_two_grad = token_scatter(*sided(nn(all_act, wide, BF16)))
        near, far = sided(nn(all_hidden, narrow, BF16))
    def core_sum(left, right):
        recv = swap(tn(left, right[-1], BF16), core)
        away = [
            (tn(left, v) + recv[:, (k + 1) * size : (k + 2) * size].astype(F32)).astype(BF16) for k, v in enumerate(right[1:-1])
        ]
        return recv[:, :size], jnp.stack(away)

    def own_sum(left, right, recv, came):
        left, came = lax.optimization_barrier((left, came))
        return tn(left, right[0]) + recv.astype(F32) + jnp.sum(came.astype(F32), axis=0)

    if not direct:
        wide_recv, wide_away = core_sum(all_act, all_normal)
        narrow_recv, narrow_away = core_sum(all_hidden, all_grads)
    resid_part, gain_two_grad = norm_back(resid, gain_two, normal_two_grad)
    resid_grad = c + resid_part
    branch_low = resid_grad.astype(BF16)
    if direct:
        branch_low, y_grad, x_grad, gate_grad, small_grad, output, wide_came, narrow_came = returned(
            (spans, seqs), steps, quarters, heads, chunk_masks[1:], branch_low, out_half, y_pre, states, decay, flow, conv, recur, inject,
            x_branch, chan, gates, resid, near, far, wide_away, narrow_away,
        )
    else:
        output = (resid + token_scatter(near, far)).astype(BF16)
        wide_came = jnp.stack([swap(wide_away[k], m) for k, m in enumerate(xs)])
        narrow_came = jnp.stack([swap(narrow_away[k], m) for k, m in enumerate(xs)])
        branch_low = in_order(branch_low, swap(branch_low, 1), 0)
        mixed_grad = nt(branch_low, out_half)
        y_grad = gelu_back(mixed_grad * states)[0].astype(BF16)
        kernel = functools.partial(adjoint_kernel, steps, quarters)
        local_adj, after, enter, carry = by_heads(
            kernel, heads, head_w, [(mixed_grad * y_branch, False), (decay, False), (flow, False)],
            [full, full, ends, ((SUBS, half), False)],
        )
        prods, sums = exchanged(carry)
        h = jnp.zeros((batch, half), F32)
        for j in range(pairs - 1, 0, -1):
            h = jnp.where(j > pair, prods[j] * h + sums[j], h)
        came = entering(enter, h).reshape(2 * SUBS, half)
        kernel = functools.partial(backward_kernel, steps, quarters)
        dx, spill, gate_grad, small_grad = by_heads(
            kernel, heads, head_w,
            [(v, False) for v in (local_adj, after, states, came, flow, conv, recur, inject, decay, x_branch, chan)]
            + [(gates, True)],
            [full, ((edge * SUBS, half), False), ((half, 2 * head_w), True), ((SUBS, half), False)],
        )
        spill = lax.ppermute(
            spill.reshape(edge, batch, quarters, half)[::-1, :, 0], AXES, [(i, i - 2) for i in range(2, count)]
        )
        spill = jnp.pad(
            spill[:, :, None], ((0, 0), (0, 0), (quarters - 1, 0), (0, 0))
        ).reshape(edge * SUBS, half)
        x_grad = jnp.concatenate([dx[: rows - edge * SUBS], dx[rows - edge * SUBS :] + spill], axis=0).astype(BF16)
    output = from_rows(output)
    wide_owned = own_sum(all_act, all_normal, wide_recv, wide_came)
    wide_owned = wide_owned.reshape(2, units, size).transpose(2, 0, 1)
    narrow_owned = own_sum(all_hidden, all_grads, narrow_recv, narrow_came).T
    normal_one_part = nt(y_grad, proj_y) + nt(x_grad, proj_x)

    def blocks_of(v, masks, wrap):
        size = 2 * share
        return [lax.dynamic_slice_in_dim(v, (me ^ m) // 2 % wrap * size, size, 0) for m in masks]

    def to_columns_owner(v_kept, v_given):
        recv = swap(v_given, core)
        n = len(inner) + 1
        total = (v_kept + recv.astype(F32)).reshape(len(xs) + 1, n, 2 * share, v_kept.shape[1])
        near = total[0]
        for k, m in enumerate(xs):
            near = near + swap(total[k + 1].astype(BF16), m).astype(F32)
        out = near[0]
        for k, m in enumerate(inner):
            out = out + swap(near[k + 1].astype(BF16), m).astype(F32)
        out = out.reshape(2, share, out.shape[1])
        other = lax.dynamic_index_in_dim(out, 1 - side, 0, keepdims=False).astype(BF16)
        return lax.dynamic_index_in_dim(out, side, 0, keepdims=False), swap(other, 1).astype(F32)

    def to_rows_owner(v_kept, v_given):
        cols = v_kept.shape[1]
        total = (v_kept + swap(v_given, core).astype(F32)).reshape(len(low_order), 2 * share, cols)
        away = cut(total, 1 - upper, cols // 2, 2).astype(BF16)
        near = cut(total, upper, cols // 2, 2) + swap(away, top).astype(F32)
        out = near[0]
        for k, m in enumerate(low_order[1:]):
            out = out + swap(near[k + 1].astype(BF16), m).astype(F32)
        other = swap(out.astype(BF16), top).astype(F32)
        out = in_order(out, other, 1).reshape(2, share, cols)
        gone = lax.dynamic_index_in_dim(out, 1 - side, 0, keepdims=False).astype(BF16)
        here = lax.dynamic_index_in_dim(out, side, 0, keepdims=False)
        return jnp.where(upper == side, here, swap(gone, 1).astype(F32))

    order = [m ^ n for m in (0, *xs) for n in (0, *inner)]
    low_order = [m ^ n for m in (0, *[v for v in xs if v < top]) for n in (0, *inner)]

    def ordered(v, masks, wrap):
        return [jnp.concatenate(blocks_of(v, [m ^ c for m in masks], wrap), axis=0) for c in (0, core)]

    if direct:
        part = normal_one_part.reshape(2, own, width)
        proj_owned, out_owned, gate_owned, input_grad, sums = scatter_grads(
            (spans, seqs), share, turned, mixed_turned, x_grad, y_grad, branch_low, gate_grad, small_grad, gain_two_grad[None],
            mine, gain_one[None], resid_grad, lax.dynamic_index_in_dim(part, side, 0, keepdims=False),
            lax.dynamic_index_in_dim(part, 1 - side, 0, keepdims=False).astype(BF16),
        )
        gains = cut(sums[:2, :width], me, share, 1).T
        small_owned = cut(sums[:, width:], me % (count // 2), share, 1).T
    else:
        input_part, gain_one_grad = norm_back(x, gain_one, over_sides(normal_one_part))
        input_grad = resid_grad + input_part
        kept_d, given_d = ordered(normal_one.T, order, pairs)
        kept_m, given_m = ordered(mixed.T, low_order, pairs // 2)
        by_row = jnp.concatenate([gate_grad, small_grad.T, jnp.zeros((half, head_w - SUBS), F32)], axis=1)
        kept_g, given_g = ordered(by_row, low_order, pairs // 2)
        gains = jnp.pad(jnp.stack([gain_one_grad, gain_two_grad], axis=1), ((0, 0), (0, 126)))
        kept_n, given_n = ordered(gains, order, pairs)
        proj_owned = jnp.concatenate(
            [in_order(*to_columns_owner(nn(kept_d, g), nn(given_d, g, BF16)), 1) for g in (x_grad, y_grad)], axis=1
        )
        out_owned = to_rows_owner(nn(kept_m, branch_low), nn(given_m, branch_low, BF16))
        rest = to_rows_owner(kept_g, given_g.astype(BF16))
        gate_owned, small_owned = rest[:, : 2 * head_w], rest[:, 2 * head_w : 2 * head_w + SUBS]
        gains = sum(to_columns_owner(kept_n, given_n.astype(BF16)))
    input_grad = from_rows(input_grad)

    return (
        output,
        input_grad,
        gains[:, 0],
        proj_owned,
        small_owned[:, :CONV],
        small_owned[:, 4],
        gate_owned,
        small_owned[:, 5:7],
        small_owned[:, 7] * jax.nn.sigmoid(decay_param.astype(F32)),
        out_owned,
        gains[:, 1],
        wide_owned,
        narrow_owned,
    )


def solution(mesh):
    both = ("span", "seq")
    tokens = P(None, both, None)
    placed = (
        tokens, P(both), P(both, None), P(both, None), P(both), P(both, None), P(both, None), P(both), P(both, None),
        P(both), P("span", None, "seq"), P("span", "seq"), tokens,
    )
    given = (
        tokens, tokens, P(both), P(both, None), P(both, None), P(both), P(both, None), P(both, None), P(both),
        P(both, None), P(both), P("span", None, "seq"), P("span", "seq"),
    )
    return jax.shard_map(on_device, mesh=mesh, in_specs=placed, out_specs=given, check_vma=False)
```

```python
import functools

import jax
import jax.numpy as jnp
from jax import lax
from jax.experimental import pallas as pl
from jax.experimental.pallas import tpu as pltpu
from jax.sharding import PartitionSpec as P

CONV = 4
EPS = 1e-06
AXES = ("span", "seq")
F32 = jnp.float32
BF16 = jnp.bfloat16
SUBS = 8


def swap(value, mask):
    count = lax.axis_size("span") * lax.axis_size("seq")
    return lax.ppermute(value, AXES, [(i, i ^ mask) for i in range(count)])


def dot(a, b, dims, out=F32):
    return lax.dot_general(a, b, ((dims[0], dims[1]), ((), ())), preferred_element_type=F32).astype(out)


def nn(a, b, out=F32):
    return dot(a, b, ((1,), (0,)), out)


def nt(a, b, out=F32):
    return dot(a, b, ((1,), (1,)), out)


def tn(a, b, out=F32):
    return dot(a, b, ((0,), (0,)), out)


def normed(v, gain):
    return v * lax.rsqrt(jnp.mean(v * v, axis=-1, keepdims=True) + EPS) * gain


def norm_back(v, gain, grad):
    scale = lax.rsqrt(jnp.mean(v * v, axis=-1, keepdims=True) + EPS)
    z = v * scale
    e = grad * gain
    return scale * (e - z * jnp.mean(e * z, axis=-1, keepdims=True)), jnp.sum(grad * z, axis=0)


def one_less_exp(u):
    series = 1.0 + u / 7.0
    for n in (6.0, 5.0, 4.0, 3.0, 2.0):
        series = 1.0 + u / n * series
    return jnp.where(u > -0.25, -u * series, 1.0 - jnp.exp(u))


def roll(v, by):
    return pltpu.roll(v, by % SUBS, 0)


def quarter_of(shape, quarters):
    return lax.broadcasted_iota(jnp.int32, shape, 0) % quarters


def spread(v, quarters, at):
    q = quarter_of(v.shape, quarters)
    held = jnp.where(q == at, v, 0.0)
    total = held
    for k in range(1, quarters):
        total = total + roll(held, k if at == 0 else -k)
    return total


def scan_carries(prods, sums, quarters, backward):
    q = quarter_of(prods[0].shape, quarters)
    sign = -1 if backward else 1
    order = (1, 0) if backward else (0, 1)
    place = quarters - 1 - q if backward else q
    whole = None
    enter = [None, None]
    for b in order:
        p, s = prods[b], sums[b]
        d = 1
        while d < quarters:
            pp, ss = roll(p, sign * d), roll(s, sign * d)
            ok = place >= d
            s = jnp.where(ok, p * ss + s, s)
            p = jnp.where(ok, p * pp, p)
            d *= 2
        first = place == 0
        ep = jnp.where(first, 1.0, roll(p, sign))
        es = jnp.where(first, 0.0, roll(s, sign))
        last = 0 if backward else quarters - 1
        tp, ts = spread(p, quarters, last), spread(s, quarters, last)
        if whole is None:
            enter[b] = (ep, es)
            whole = (tp, ts)
        else:
            enter[b] = (ep * whole[0], ep * whole[1] + es)
            whole = (tp * whole[0], tp * whole[1] + ts)
    return enter, whole


def earlier_rows(groups, halo, quarters, steps):
    q = quarter_of(groups[0].shape[1:], quarters)
    edge = CONV - 1
    out = []
    for b in (0, 1):
        ahead = []
        for k in range(edge, 0, -1):
            same = roll(groups[b][steps - k], 1)
            before = halo[k - 1] if b == 0 else roll(groups[0][steps - k], 1 - quarters)
            ahead.append(jnp.where(q == 0, before, same)[None])
        out.append(jnp.concatenate([*ahead, groups[b]], axis=0))
    return out


def forward_kernel(steps, quarters, xb, chan, gate, conv_o, recur_o, inject_o, decay_o, local_o, prod_o, enter_o, carry_o):
    rows = 2 * steps * SUBS
    width = xb.shape[1]
    head = xb[...].astype(F32)
    groups = [head[b * steps * SUBS : (b + 1) * steps * SUBS].reshape(steps, SUBS, width) for b in (0, 1)]
    halo = [head[rows + k * SUBS : rows + (k + 1) * SUBS] for k in range(CONV - 1)]
    edge = CONV - 1
    convs = []
    for ext in earlier_rows(groups, halo, quarters, steps):
        total = jnp.broadcast_to(chan[4:5][None], (steps, SUBS, width))
        for k in range(CONV):
            total = total + chan[k : k + 1][None] * ext[edge - k : edge - k + steps]
        convs.append(total.reshape(steps * SUBS, width))
    conv = jnp.concatenate(convs, axis=0)
    pre = jnp.dot(conv.astype(BF16), gate[...], preferred_element_type=F32)
    recur = jax.nn.sigmoid(pre[:, :width] + chan[5:6])
    inject = jax.nn.sigmoid(pre[:, width:] + chan[6:7])
    log_decay = -8.0 * recur * chan[7:8]
    decay = jnp.exp(log_decay)
    driven = jnp.sqrt(one_less_exp(2.0 * log_decay)) * inject * conv
    conv_o[...] = conv
    recur_o[...] = recur
    inject_o[...] = inject
    decay_o[...] = decay
    prods, sums = [], []
    for b in (0, 1):
        h = p = None
        for t in range(steps):
            at = (b * steps + t) * SUBS
            d, u = decay[at : at + SUBS], driven[at : at + SUBS]
            h = u if h is None else d * h + u
            p = d if p is None else d * p
            local_o[at : at + SUBS] = h
            prod_o[at : at + SUBS] = p
        prods.append(p)
        sums.append(h)
    enter, whole = scan_carries(prods, sums, quarters, False)
    for b in (0, 1):
        enter_o[b * SUBS : (b + 1) * SUBS] = enter[b][0]
        enter_o[(2 + b) * SUBS : (3 + b) * SUBS] = enter[b][1]
    q = quarter_of(whole[0].shape, quarters)
    carry_o[...] = jnp.where(q == 0, whole[0], whole[1])


def adjoint_kernel(steps, quarters, grad, decay, flow, local_o, after_o, enter_o, carry_o):
    prods, sums = [], []
    for b in (0, 1):
        g = r = None
        for t in range(steps - 1, -1, -1):
            at = (b * steps + t) * SUBS
            rows = slice(at, at + SUBS)
            a = grad[rows] if g is None else grad[rows] + g
            r = jnp.ones_like(a) if r is None else r * decay[at + SUBS : at + 2 * SUBS]
            local_o[rows] = a
            after_o[rows] = r
            g = decay[rows] * a
        prods.append(flow[(2 + b) * SUBS : (3 + b) * SUBS])
        sums.append(g)
    enter, whole = scan_carries(prods, sums, quarters, True)
    for b in (0, 1):
        enter_o[b * SUBS : (b + 1) * SUBS] = enter[b][0]
        enter_o[(2 + b) * SUBS : (3 + b) * SUBS] = enter[b][1]
    q = quarter_of(whole[0].shape, quarters)
    carry_o[...] = jnp.where(q == 0, whole[0], whole[1])


def backward_kernel(
    steps, quarters, local, after, states, came, entered, conv_r, recur_r, inject_r, decay_r, xb, chan, gate,
    dx_o, spill_o, gate_o, small_o,
):
    rows = 2 * steps * SUBS
    width = xb.shape[1]
    edge = CONV - 1
    block = steps * SUBS

    def by_step(v):
        return [v[b * block : (b + 1) * block].reshape(steps, SUBS, width) for b in (0, 1)]

    adjoint = jnp.concatenate(
        [
            (l + a * came[b * SUBS : (b + 1) * SUBS][None]).reshape(block, width)
            for b, (l, a) in enumerate(zip(by_step(local[...]), by_step(after[...])))
        ],
        axis=0,
    )
    earlier = jnp.concatenate(
        [
            jnp.concatenate([entered[b * SUBS : (b + 1) * SUBS], states[b * block : (b + 1) * block - SUBS]], axis=0)
            for b in (0, 1)
        ],
        axis=0,
    )
    conv, recur, inject, decay = conv_r[...], recur_r[...], inject_r[...], decay_r[...]
    rate = chan[7:8]
    mult = jnp.sqrt(one_less_exp(-16.0 * recur * rate))
    d_decay = adjoint * earlier
    d_log = d_decay * decay - adjoint * inject * conv * (decay * decay / mult)
    d_inject = adjoint * mult * conv
    d_conv = adjoint * mult * inject
    d_rate = jnp.sum(d_log * (-8.0 * recur), axis=0, keepdims=True)
    d_recur = d_log * (-8.0 * rate) * recur * (1.0 - recur)
    d_inject = d_inject * inject * (1.0 - inject)
    low = jnp.concatenate([d_recur.astype(BF16), d_inject.astype(BF16)], axis=1)
    d_conv = d_conv + lax.dot_general(low, gate[...], (((1,), (1,)), ((), ())), preferred_element_type=F32)
    gate_o[...] = lax.dot_general(conv.astype(BF16), low, (((0,), (0,)), ((), ())), preferred_element_type=F32)
    head = xb[...].astype(F32)
    halo = [head[rows + k * SUBS : rows + (k + 1) * SUBS] for k in range(edge)]
    exts = earlier_rows(by_step(head), halo, quarters, steps)
    groups = by_step(d_conv)
    for k in range(CONV):
        taps = sum(
            jnp.sum(groups[b] * exts[b][edge - k : edge - k + steps], axis=(0, 1), keepdims=True)[0] for b in (0, 1)
        )
        small_o[k : k + 1] = taps
    small_o[4:5] = jnp.sum(d_conv, axis=0, keepdims=True)
    small_o[5:6] = jnp.sum(d_recur, axis=0, keepdims=True)
    small_o[6:7] = jnp.sum(d_inject, axis=0, keepdims=True)
    small_o[7:8] = d_rate
    q = quarter_of((SUBS, width), quarters)
    for b in (0, 1):
        beyond = []
        for j in range(edge):
            same = roll(groups[b][j], -1)
            later = roll(groups[1][j], quarters - 1) if b == 0 else jnp.zeros_like(same)
            beyond.append(jnp.where(q == quarters - 1, later, same)[None])
        ext = jnp.concatenate([groups[b], *beyond], axis=0)
        total = chan[0:1][None] * ext[:steps]
        for k in range(1, CONV):
            total = total + chan[k : k + 1][None] * ext[k : k + steps]
        dx_o[b * block : (b + 1) * block] = total.reshape(block, width)
    for j in range(1, CONV):
        total = jnp.zeros((SUBS, width), F32)
        for k in range(j, CONV):
            total = total + chan[k : k + 1] * groups[0][k - j]
        spill_o[(j - 1) * SUBS : j * SUBS] = total


def by_heads(kernel, heads, head_w, arrays, outs):
    def spec(shape, tall):
        if tall:
            return pl.BlockSpec((head_w, shape[1]), lambda h: (h, 0))
        return pl.BlockSpec((shape[0], head_w), lambda h: (0, h))

    return pl.pallas_call(
        kernel,
        grid=(heads,),
        in_specs=[spec(a.shape, tall) for a, tall in arrays],
        out_specs=[spec(s, tall) for s, tall in outs],
        out_shape=[jax.ShapeDtypeStruct(s, F32) for s, _ in outs],
        compiler_params=pltpu.CompilerParams(vmem_limit_bytes=48 * 1024 * 1024),
    )(*[a for a, _ in arrays])


MESH = pl.DeviceIdType.MESH
VMEM_LIMIT = 60 * 1024 * 1024


class Links:
    def __init__(self, sizes, sends, recvs):
        self.spans, self.seqs = sizes
        self.span, self.seq = lax.axis_index("span"), lax.axis_index("seq")
        self.sends, self.recvs = sends, recvs
        self.used = 0
        self.open = []

    def flipped(self, index, mask):
        bit = 1
        while bit <= mask:
            if mask & bit:
                index = index + (1 - 2 * (index // bit % 2)) * bit
            bit *= 2
        return index

    def flipped_index(self, index, mask):
        return self.flipped(index, mask)

    def peer(self, mask):
        low, high = mask % self.seqs, mask // self.seqs
        return (self.flipped(self.span, high), self.flipped(self.seq, low))

    def other(self, mask):
        span, seq = self.peer(mask)
        return span * self.seqs + seq

    def greet(self, masks, others=()):
        barrier = pltpu.get_barrier_semaphore()
        for device in (*[self.peer(mask) for mask in masks], *others):
            pl.semaphore_signal(barrier, inc=1, device_id=device, device_id_type=MESH)
        pl.semaphore_wait(barrier, len(masks) + len(others))

    def plan(self, source, target, mask, only=None, device=None):
        slot = self.used
        self.used += 1
        device = self.peer(mask) if device is None else device
        copy = pltpu.make_async_remote_copy(
            source, target, self.sends.at[slot], self.recvs.at[slot], device_id=device, device_id_type=MESH
        )
        self.open.append((copy, only))
        return copy

    def send(self, source, target, mask, only=None):
        copy = self.plan(source, target, mask, only)
        if only is None:
            copy.start()
        else:
            pl.when(only)(copy.start)
        return copy

    def sent(self, copy):
        copy.wait_send()
        self.open = [(c, only) for c, only in self.open if c is not copy]

    def close(self):
        for copy, only in self.open:
            if only is None:
                copy.wait_send()
            else:
                pl.when(only)(copy.wait_send)


def in_turn(parts, order):
    for name in order:
        next(parts[name], None)
    for part in parts.values():
        for _ in part:
            pass


def scatter_kernel(
    sizes, share, turned, mixed, grad_x, grad_y, branch, gates, small, gain, x_own, gain_one, keep, part_own, part_other,
    proj_o, out_o, gate_o, input_o, sum_o, sends, recvs, from_part, vector, *bufs,
):
    links = Links(sizes, sends, recvs)
    spans, seqs = sizes
    count = spans * seqs
    me = links.span * seqs + links.seq
    side = me % 2
    upper = me // (count // 2)
    inner = [2 * k for k in range(1, seqs // 2)]
    core, top = seqs, count // 2
    double = 2 * share
    n = len(inner) + 1
    links.greet([1, *inner, core, top])
    whole = links.send(part_other, from_part, 1)

    def part(block, scratch, finish, shared=None):
        to_core, from_core, to_top, from_top, to_inner, from_inner, to_side, from_side = scratch
        if shared is not None:
            for copy in shared:
                links.sent(copy)
        crossing = [] if shared is None else shared
        crossing.clear()
        for i in range(2):
            for j in range(n):
                to_core[i * n + j] = block(1, (1 - i) * n + j).astype(BF16)
            crossing.append(links.send(to_core.at[pl.ds(i * n, n)], from_core.at[pl.ds(i * n, n)], core))
        mine = list(crossing)
        yield
        mine[0].wait_recv()
        over_top = {}
        for j in (*range(1, n), 0):
            to_top[j] = (block(0, n + j) + from_core[j].astype(F32)).astype(BF16)
            over_top[j] = links.send(to_top.at[j], from_top.at[j], top)
        mine[1].wait_recv()
        yield
        over_inner = []
        for j in range(1, n):
            over_top[j].wait_recv()
            to_inner[j - 1] = (block(0, j) + from_core[n + j].astype(F32) + from_top[j].astype(F32)).astype(BF16)
            over_inner.append(links.send(to_inner.at[j - 1], from_inner.at[j - 1], inner[j - 1]))
        over_top[0].wait_recv()
        yield
        total = block(0, 0) + from_core[n].astype(F32) + from_top[0].astype(F32)
        for j in range(1, n):
            over_inner[j - 1].wait_recv()
            total = total + from_inner[j - 1].astype(F32)
        yield from finish(total, to_side, from_side)

    def sided(total):
        low, high = total[:share], total[share:]
        first = side == 0
        return jnp.where(first, low, high), jnp.where(first, high, low)

    def by_columns(first, cols):
        def finish(total, to_side, from_side):
            mine, theirs = sided(total)
            to_side[...] = theirs.astype(BF16)
            copy = links.send(to_side, from_side, 1)
            yield
            copy.wait_recv()
            recv = from_side[...].astype(F32)
            proj_o[:, first : first + cols] = jnp.where(side == 0, mine, recv)
            proj_o[:, first + cols : first + 2 * cols] = jnp.where(side == 0, recv, mine)

        return finish

    def by_rows(target, to_last, from_last):
        cols = target.shape[1] // 2

        def finish(total, to_side, from_side):
            to_side[...] = total.astype(BF16)
            copy = links.send(to_side, from_side, top)
            yield
            copy.wait_recv()
            other = from_side[...].astype(F32)
            first = side == 0
            (low, low_far), (high, high_far) = sided(jnp.where(first, total, other)), sided(jnp.where(first, other, total))
            to_last[:, :cols] = low_far.astype(BF16)
            to_last[:, cols:] = high_far.astype(BF16)
            copy = links.send(to_last, from_last, 1)
            yield
            copy.wait_recv()
            holds = side == upper
            target[:, :cols] = jnp.where(holds, low, from_last[:, :cols].astype(F32))
            target[:, cols:] = jnp.where(holds, high, from_last[:, cols:].astype(F32))

        return finish

    def rows_of(c, j, whole):
        pairs = count // 2 if whole else count // 4
        owner = links.other(c * core + (j // n * top if whole else 0) + (0, *inner)[j % n])
        return pl.ds(pl.multiple_of(owner // 2 % pairs * double, 16), double)

    def columns_of(j, columns):
        return pl.ds(pl.multiple_of((upper if j < n else 1 - upper) * columns, 128), columns)

    def product(lhs, rhs):
        return lambda c, j: jnp.dot(lhs[rows_of(c, j, True)], rhs[...], preferred_element_type=F32)

    def product_half(lhs, rhs, columns):
        return lambda c, j: jnp.dot(lhs[rows_of(c, j, False)], rhs[:, columns_of(j, columns)], preferred_element_type=F32)

    def stored(blocks, columns):
        return lambda c, j: blocks[rows_of(c, j, False), columns_of(j, columns)]

    def sums():
        whole.wait_recv()
        few = 16
        own, width = x_own.shape
        vector[0] = jnp.zeros(vector.shape[1:], F32)
        vector[0, 1:2, :width] = gain[...]
        vector[0, :, width:] = small[...]

        @pl.loop(0, own // few)
        def _(k):
            here = pl.ds(pl.multiple_of(k * few, few), few)
            v = x_own[here].astype(F32)
            scale = lax.rsqrt(jnp.mean(v * v, axis=-1, keepdims=True) + EPS)
            z = v * scale
            d = part_own[here] + from_part[here].astype(F32)
            e = d * gain_one[...]
            input_o[here] = keep[here] + scale * (e - z * jnp.mean(e * z, axis=-1, keepdims=True))
            vector[0, 0:1, :width] += jnp.sum(d * z, axis=0, keepdims=True)

        slot = 1
        for masks in ([core], [top], inner):
            copies = [links.send(vector.at[0], vector.at[slot + k], m) for k, m in enumerate(masks)]
            yield
            for copy in copies:
                copy.wait_recv()
                links.sent(copy)
            total = vector[0]
            for k in range(len(masks)):
                total = total + vector[slot + k]
            vector[0] = total
            slot += len(masks)
        copy = links.send(vector.at[0], vector.at[slot], 1)
        yield
        copy.wait_recv()
        sum_o[:, :width] = vector[0, :, :width] + vector[slot, :, :width]
        sum_o[:, width:] = jnp.where(side == upper, vector[0, :, width:], vector[slot, :, width:])

    half = grad_x.shape[1]
    wide = branch.shape[1] // 2
    thin = gates.shape[1] // 2
    shared = []
    first = bufs[0]
    parts = {
        "y": part(product(turned, grad_y), [first, *bufs[1:8]], by_columns(2 * half, half), shared),
        "o": part(product_half(mixed, branch, wide), [first, *bufs[8:15]], by_rows(out_o, *bufs[15:17]), shared),
        "x": part(product(turned, grad_x), [first, *bufs[17:24]], by_columns(0, half), shared),
        "g": part(stored(gates, thin), bufs[24:32], by_rows(gate_o, *bufs[32:34])),
        "n": sums(),
    }
    in_turn(parts, "yoyxoyxgnoyxgnoygnoxoygnoxgnngg")
    links.close()


def scatter_grads(sizes, share, turned, mixed, grad_x, grad_y, branch, gates, small, gain, x_own, gain_one, keep, part_own, part_other):
    n = sizes[1] // 2
    half, wide, thin = grad_x.shape[1], branch.shape[1], gates.shape[1]
    own, width = x_own.shape
    double = 2 * share

    def scratch(cols, last, core=True):
        side = share if last is None else double
        shapes = [(2 * n, double, cols)] * (2 if core else 1) + [(n, double, cols)] * 2 + [(n - 1, double, cols)] * 2 + [(side, cols)] * 2
        if last is not None:
            shapes += [(share, last)] * 2
        return [pltpu.VMEM(s, BF16) for s in shapes]

    bufs = [*scratch(half, None), *scratch(wide // 2, wide, False), *scratch(half, None, False), *scratch(thin // 2, thin)]
    copies = 4 * (2 + n + (n - 1) + 2) + n + 4
    inside = pl.BlockSpec(memory_space=pltpu.VMEM)
    shapes = [(share, 4 * half), (share, wide), (share, thin), (own, width), (SUBS, width + half)]
    return pl.pallas_call(
        functools.partial(scatter_kernel, sizes, share),
        in_specs=[inside] * 13,
        out_specs=[inside] * 5,
        out_shape=[jax.ShapeDtypeStruct(s, F32) for s in shapes],
        scratch_shapes=[
            pltpu.SemaphoreType.DMA((copies,)), pltpu.SemaphoreType.DMA((copies,)), pltpu.VMEM((own, width), BF16),
            pltpu.VMEM((n + 3, SUBS, width + half), F32), *bufs,
        ],
        compiler_params=pltpu.CompilerParams(collective_id=1, has_side_effects=True, vmem_limit_bytes=VMEM_LIMIT),
    )(turned, mixed, grad_x, grad_y, branch, gates, small, gain, x_own, gain_one, keep, part_own, part_other)


def gelu_parts(v):
    root = 0.7978845608028654
    t = jnp.tanh(root * (v + 0.044715 * (v * v * v)))
    slope = 0.5 * (1.0 + t) + 0.5 * v * (1.0 - t * t) * root * (1.0 + 3.0 * 0.044715 * (v * v))
    return 0.5 * v * (1.0 + t), slope


def feed_kernel(sizes, masks, own, *refs):
    chunks = len(masks)
    spans = sizes[0]
    own_rows, refs = refs[0], refs[1:]
    cots, refs = refs[0], refs[1:]
    wides, refs = refs[:spans], refs[spans:]
    narrows, refs = refs[:2], refs[2:]
    grad_o, near_o, far_o, act_o, hidden_o, refs = *refs[:5], refs[5:]
    (rows_o, cots_o, wide_away, narrow_away, wide_recv, narrow_recv), refs = refs[:6], refs[6:]
    (rows, cot, wide, narrow, act, hidden, near, down_near, down_far, to_side, from_side, to_inner, from_inner,
     sends, recvs, loads, stores) = refs
    units = narrow.shape[0]
    width = narrow.shape[1]
    size = width // spans
    pair = 2 * own
    links = Links(sizes, sends, recvs)

    def load(source, target, slot):
        copy = pltpu.make_async_copy(source, target, loads.at[slot])
        copy.start()
        return copy

    first = load(own_rows, rows.at[pl.ds(0, own)], 0)
    late = [
        load(cots.at[links.flipped(links.seq // 2, masks[b // 2] // 2), b % 2], cot.at[pl.ds(b * own, own)], 1 + b)
        for b in range(2 * chunks)
    ]
    for j in range(spans):
        columns = pl.ds(j * size, size)
        late.append(load(wides[j], wide.at[:, columns], 1 + 2 * chunks + j))
        if j < 2:
            late.append(load(narrows[j], narrow.at[:, columns], 1 + 2 * chunks + spans + j))
    core, tops = sizes[1], range(2, spans, 2)
    links.greet([1, *masks[1:], core, *[m * core for m in tops]])
    first.wait()
    across = [links.send(narrows[0], narrow.at[:, pl.ds(m * size, size)], m * core) for m in tops]

    def block(b):
        return rows.at[pl.ds(b * own, own)]

    each = range(chunks)
    over_side = [links.plan(block(2 * i), block(2 * i + 1), 1) for i in each]
    over_inner = [None] + [links.plan(block(0), block(2 * i), masks[i]) for i in each[1:]]
    back_side = [links.plan(to_side.at[i], from_side.at[i], 1) for i in each]
    back_inner = [links.plan(to_inner.at[i - 1], from_inner.at[i - 1], masks[i]) for i in each[1:]]
    over_side[0].start()
    for i in each[1:]:
        over_inner[i].start()
    for copy in late:
        copy.wait()
    beside = [links.plan(narrow.at[:, pl.ds(m * size, size)], narrow.at[:, pl.ds((m + 1) * size, size)], core) for m in tops]

    def narrow_here():
        for copy, onto in zip(across, beside):
            copy.wait_recv()
            onto.start()
        for copy in beside:
            copy.wait_recv()

    def onward(i):
        over_inner[i].wait_recv()
        over_side[i].start()

    def give_on(i):
        back_side[i].wait_recv()
        to_inner[i - 1] = (near[i].astype(F32) + from_side[i].astype(F32)).astype(BF16)
        back_inner[i - 1].start()

    last = chunks - 1

    def ahead(i):
        over_side[i].wait_recv()
        if i == 0:
            for k in (2, 1):
                if k < last:
                    onward(k)
            narrow_here()

    def midway(i):
        if i == min(1, last - 1):
            for k in range(3, chunks):
                onward(k)
        if i == last:
            give_on(1)

    def behind(i):
        if 0 < i < last - 1:
            back_side[i].start()
        if i == last:
            for k in (last, last - 1, 0):
                back_side[k].start()

    def compute(i):
        here = pl.ds(pl.multiple_of(i * pair, 16), pair)
        mine = rows[here]
        given = cot[here]
        start = 0
        while start < units:
            n = min(384, units - start)
            gate = lax.dot_general(mine, wide[start : start + n], (((1,), (1,)), ((), ())), preferred_element_type=F32)
            up = lax.dot_general(
                mine, wide[units + start : units + start + n], (((1,), (1,)), ((), ())), preferred_element_type=F32
            )
            back = lax.dot_general(given, narrow[start : start + n], (((1,), (1,)), ((), ())), preferred_element_type=F32)
            value, slope = gelu_parts(gate)
            hidden[here, start : start + n] = (value * up).astype(BF16)
            act[here, start : start + n] = (back * up * slope).astype(BF16)
            act[here, units + start : units + start + n] = (back * value).astype(BF16)
            start += n
        for k in range(chunks):
            pl.when(i == k)(functools.partial(midway, k))
        step = 512

        @pl.loop(0, width // step)
        def _(k):
            columns = pl.ds(pl.multiple_of(k * step, 128), step)
            total = jnp.dot(act[here], wide[:, columns], preferred_element_type=F32)
            near[i, :, columns] = total[:own].astype(BF16)
            to_side[i, :, columns] = total[own:].astype(BF16)
            total = jnp.dot(hidden[here], narrow[:, columns], preferred_element_type=F32)
            down_near[i, :, columns] = total[:own].astype(BF16)
            down_far[i, :, columns] = total[own:].astype(BF16)

    @pl.loop(0, chunks)
    def _(i):
        for k in range(chunks):
            pl.when(i == k)(functools.partial(ahead, k))
        compute(i)
        for k in range(chunks):
            pl.when(i == k)(functools.partial(behind, k))

    out = []

    def store(source, target):
        out.append(pltpu.make_async_copy(source, target, stores.at[len(out)]))
        out[-1].start()
        return out[-1]

    own_columns, away_columns = pl.ds(0, size), pl.ds(2 * size, size)
    for source, target in (
        (act, act_o), (hidden, hidden_o), (down_near, near_o), (down_far, far_o), (rows.at[:, own_columns], rows_o),
        (cot.at[:, own_columns], cots_o),
    ):
        store(source, target)
    for copy in beside:
        links.sent(copy)

    def gradient(left, right, start, count, j):
        return lax.dot_general(
            left[:, pl.ds(start, count)], right[:, j * size : (j + 1) * size], (((0,), (0,)), ((), ())), preferred_element_type=F32
        )

    def by_tiles(total, body):
        whole = total // 384

        @pl.loop(0, whole)
        def _(k):
            body(pl.multiple_of(k * 384, 128), 384)

        if total % 384:
            body(whole * 384, total % 384)

    def give_core(left, right, held, landed):
        def tile(start, count):
            for k, j in enumerate(range(1, spans, 2)):
                held[pl.ds(start, count), k * size : (k + 1) * size] = gradient(left, right, start, count, j).astype(BF16)

        by_tiles(left.shape[1], tile)
        return links.send(held.at[:, pl.ds(0, 2 * size)], landed, core)

    def give_top(left, right, held, landed, came, target):
        came.wait_recv()
        store(landed.at[:, pl.ds(size, size)], held.at[:, away_columns]).wait()
        out.pop()

        def tile(start, count):
            here = pl.ds(start, count)
            total = gradient(left, right, start, count, 2) + held[here, 2 * size : 3 * size].astype(F32)
            held[here, 3 * size : 4 * size] = total.astype(BF16)

        by_tiles(left.shape[1], tile)
        store(held.at[:, pl.ds(3 * size, size)], target)

    crossing = give_core(act, rows, wide, wide_recv)
    give_on(last)
    crossing_narrow = give_core(hidden, cot, narrow, narrow_recv)
    for k in range(last - 1, 1, -1):
        give_on(k)
    give_top(act, rows, wide, wide_recv, crossing, wide_away)
    give_top(hidden, cot, narrow, narrow_recv, crossing_narrow, narrow_away)
    back_side[0].wait_recv()
    for k in range(chunks - 1):
        back_inner[k].wait_recv()
    for j in range(spans):
        columns = slice(j * size, (j + 1) * size)
        total = near[0, :, columns].astype(F32) + from_side[0, :, columns].astype(F32)
        for k in range(chunks - 1):
            total = total + from_inner[k, :, columns].astype(F32)
        grad_o[:, pl.ds(pl.multiple_of(links.flipped(links.span, j) * size, 128), size)] = total
    for copy in out:
        copy.wait()
    links.close()


def feed_forward(sizes, masks, own_rows, cots, wides, narrows):
    own, width = own_rows.shape
    units = narrows[0].shape[0]
    chunks = len(masks)
    total = 2 * chunks * own
    anywhere = pl.BlockSpec(memory_space=pl.ANY)
    copies = 4 * chunks + sizes[0] + 2
    blocks = (chunks, own, width)
    spans = sizes[0]
    size = width // spans
    shapes = [
        blocks, blocks, (total, 2 * units), (total, units), (total, size), (total, size), (2 * units, size), (units, size),
        (2 * units, 2 * size), (units, 2 * size),
    ]
    held = [
        (total, width), (total, width), (2 * units, width), (units, width), (total, 2 * units), (total, units), blocks, blocks,
        blocks, blocks, blocks, (chunks - 1, own, width), (chunks - 1, own, width),
    ]
    return pl.pallas_call(
        functools.partial(feed_kernel, sizes, masks, own),
        in_specs=[anywhere] * (4 + len(wides)),
        out_specs=[pl.BlockSpec(memory_space=pltpu.VMEM)] + [anywhere] * len(shapes),
        out_shape=[jax.ShapeDtypeStruct((own, width), F32)] + [jax.ShapeDtypeStruct(s, BF16) for s in shapes],
        scratch_shapes=[pltpu.VMEM(s, BF16) for s in held]
        + [pltpu.SemaphoreType.DMA((k,)) for k in (copies, copies, 3 + 2 * chunks + len(wides), 8)],
        compiler_params=pltpu.CompilerParams(collective_id=2, has_side_effects=True, vmem_limit_bytes=VMEM_LIMIT),
    )(own_rows, cots, *wides, *narrows)


def expanded(v, quarters):
    return spread(v, quarters, 0), spread(roll(v, -1), quarters, 0)


def chunk_inflow(links, line, blocks, quarters, backward, between):
    n, spans = line.shape[0], blocks.shape[0]
    place = links.seq // 2
    copies = [links.send(line.at[0], line.at[k], 2 * k) for k in range(1, n)]
    for copy in copies:
        copy.wait_recv()
    between()
    one, nought = jnp.ones(line.shape[1:], F32), jnp.zeros(line.shape[1:], F32)
    prod, total = one, nought
    all_prod, all_total = one, nought

    def ordered(count):
        return range(count - 1, -1, -1) if backward else range(count)

    def ahead(j, at):
        return at < j if backward else at > j

    for j in ordered(n):
        p, s = expanded(line[links.flipped(place, j)], quarters)
        inside = ahead(j, place)
        total = jnp.where(inside, p * total + s, total)
        prod = jnp.where(inside, p * prod, prod)
        all_total = p * all_total + s
        all_prod = p * all_prod
    q = quarter_of(line.shape[1:], quarters)
    blocks[0] = jnp.where(q == 0, all_prod, all_total)
    copies = [links.send(blocks.at[0], blocks.at[m], m * links.seqs) for m in range(1, spans)]
    for copy in copies:
        copy.wait_recv()
    h = nought
    for j in ordered(spans):
        p, s = expanded(blocks[links.flipped(links.span, j)], quarters)
        h = jnp.where(ahead(j, links.span), p * h + s, h)
    return prod * h + total


def by_head(heads, head_w, body):
    @pl.loop(0, heads)
    def _(h):
        start = pl.multiple_of(h * head_w, 128)
        columns = pl.ds(start, head_w)
        body(lambda ref: ref.at[:, columns], lambda ref: ref.at[pl.ds(start, head_w)])


def front_kernel(
    sizes, steps, quarters, heads, head_w, share, x_own, halo, params_in, rec_proj, out_proj, gate_weight, cot, wide, narrow, *refs
):
    spans, seqs = sizes
    count = spans * seqs
    inner = [2 * k for k in range(1, seqs // 2)]
    n = len(inner) + 1
    core, top = seqs, count // 2
    (normal, xb, y_pre, conv, recur, inject, decay, states, flow, mixed, resid, normal_two, params, chan, turned, mixed_turned), refs = (
        refs[:16], refs[16:]
    )
    (proj_x, proj_y, out_half, gates), refs = refs[:4], refs[4:]
    wides, beside_narrow, cots, refs = refs[: spans - 1], refs[spans - 1], refs[spans], refs[spans + 1 :]
    (lead, held_x, held_y, held_o, held_g, every, prod, enter, line, blocks, inflow, to_side, from_side, low,
     sends, recvs, locals_) = refs
    links = Links(sizes, sends, recvs)
    me = links.span * seqs + links.seq
    side, upper = me % 2, me // (count // 2)
    own, width = x_own.shape
    rows = 2 * own
    half = width // 2
    double = 2 * share
    links.greet([1, *inner, *[m * seqs for m in range(1, spans)]])
    kept = [0]

    def local(source, target, only=None):
        copy = pltpu.make_async_copy(source, target, locals_.at[kept[0]])
        kept[0] += 1
        if only is None:
            copy.start()
        else:
            pl.when(only)(copy.start)
        return copy

    z = links.seq // 2
    offsets = [o for s in range(1, n) for o in (-s, s)]
    there = {o: jnp.logical_and(z + o >= 0, z + o < n) for o in offsets}
    beyond = {-1: (links.span, jnp.maximum(links.seq - 2, 0)), 1: (links.span, jnp.minimum(links.seq + 2, seqs - 1))}

    def along(piece):
        passing = {}
        for o in (0, *offsets):
            for way in (-1, 1):
                if o * way <= 0 and abs(o) + 1 < n:
                    both = jnp.logical_and(there[way], there[o]) if o else there[way]
                    passing[o, way] = links.plan(piece(o), piece(o), None, both, beyond[way])
        return passing

    def arrival(passing, o):
        way = 1 if o < 0 else -1
        return passing[o + way, way]

    def begin(passing):
        for way in (-1, 1):
            pl.when(there[way])(passing[0, way].start)

    def take(passing, o):
        arrival(passing, o).wait_recv()
        way = 1 if o < 0 else -1
        if (o, way) in passing:
            pl.when(there[way])(passing[o, way].start)

    def pieces_out(own_out, piece, part, far):
        passing = along(piece)
        over_top = {o: links.plan(piece(o), piece(o), top, there[o]) for o in offsets}
        over_core = {o: links.plan(part(o), part(o), core, there[o]) for o in offsets}
        far_core = {o: links.plan(far(o), far(o), core, there[o]) for o in offsets}
        begin(passing)
        first_core = links.send(own_out, own_out, core)
        first_top = first_far = None
        if far(0) is not None:
            first_top = links.send(piece(0), piece(0), top)
        yield
        for o in offsets:

            @pl.when(there[o])
            def _():
                take(passing, o)
                over_top[o].start()
                over_core[o].start()

            if o == offsets[len(offsets) // 2 - 1]:
                yield
        yield
        if first_top is not None:
            first_top.wait_recv()
            first_far = links.send(far(0), far(0), core)
        for o in offsets:

            @pl.when(there[o])
            def _():
                over_top[o].wait_recv()
                far_core[o].start()

        yield
        first_core.wait_recv()
        if first_far is not None:
            first_far.wait_recv()
        for o in offsets:

            @pl.when(there[o])
            def _():
                over_core[o].wait_recv()
                far_core[o].wait_recv()

    def pieces_direct(whole, piece):
        over_inner = {m: links.send(piece(0), piece(0), m) for m in inner}
        over_core = [links.send(whole, whole, core)]
        over_top = {}
        yield
        for m in inner:
            over_inner[m].wait_recv()
            here = piece(links.flipped(z, m // 2) - z)
            over_top[m] = links.send(here, here, top)
            over_core.append(links.send(here, here, core))
        yield
        for m in inner:
            over_top[m].wait_recv()
            here = piece(links.flipped(z, m // 2) - z, 1 - upper)
            over_core.append(links.send(here, here, core))
        yield
        for copy in over_core:
            copy.wait_recv()

    def columns_part(source, first, target):
        def piece(o, over=0):
            device = (links.other(over) if over else me) + 2 * o
            start = jnp.clip(device // 2 * double, 0, target.shape[0] - double)
            return target.at[pl.ds(pl.multiple_of(start, 16), double)]

        def columns(which):
            return source.at[:, pl.ds(pl.multiple_of(first + which * half, 128), half)]

        row = target.at[pl.ds(pl.multiple_of(me * share, 16), share)]
        mine = local(columns(side), row)
        theirs = links.send(columns(1 - side), row, 1)
        yield
        mine.wait()
        theirs.wait_recv()
        yield from pieces_out(piece(0), piece, piece, lambda o: piece(o, top))

    def rows_part(source, target, direct):
        cols = source.shape[1]
        pairs_half = count // 4

        def rows_at(start, size):
            return target.at[pl.ds(pl.multiple_of(start, 16), size)]

        begin_at = me // 2 % pairs_half * double

        def piece(o, which=None):
            start = jnp.clip(begin_at + o * double, 0, target.shape[0] - double)
            which = upper if which is None else which
            return target.at[pl.ds(pl.multiple_of(start, 16), double), pl.ds(pl.multiple_of(which * (cols // 2), 128), cols // 2)]

        holds = side == upper
        row = rows_at(begin_at + side * share, share)
        mine = local(source, row, holds)
        gift = links.send(source, row, 1, side != upper)
        yield

        @pl.when(holds)
        def _():
            mine.wait()
            gift.wait_recv()

        whole = rows_at(begin_at, double)
        across = links.send(whole, whole, top, holds)
        yield
        pl.when(side != upper)(across.wait_recv)
        if direct:
            yield from pieces_direct(whole, piece)
        else:
            yield from pieces_out(whole, piece, piece, lambda o: piece(o, 1 - upper) if o else None)

    def small_part():
        height = params_in.shape[0]

        def rows_of(device):
            return every.at[pl.ds(pl.multiple_of(device // 2 * 2 * height, 16), 2 * height)]

        row = pl.ds(pl.multiple_of(me * height, 16), height)
        every[row] = params_in[...]
        theirs = links.send(every.at[row], every.at[row], 1)
        yield
        theirs.wait_recv()
        held = [me]
        for masks in (inner, [top], [core]):
            copies = [links.send(rows_of(d), rows_of(d), m) for d in held for m in masks]
            held = held + [links.flipped_index(d, m) for d in held for m in masks]
            yield
            for copy in copies:
                copy.wait_recv()
        params[...] = jnp.zeros_like(params)
        lanes = params_in.shape[1]
        for d in range(count):
            tile = every[d * height : (d + 1) * height]
            base, shift = d * share // lanes * lanes, d * share % lanes
            if shift + share <= lanes:
                params[:, base : base + lanes] += pltpu.roll(tile, shift, 1) if shift else tile
            else:
                turned = pltpu.roll(jnp.concatenate([tile, jnp.zeros_like(tile)], axis=1), shift, 1)
                params[:, base : base + 2 * lanes] += turned
        chan[...] = params[:SUBS, pl.ds(pl.multiple_of(side * half, 128), half)]

    parts = {
        "x": columns_part(rec_proj, 0, proj_x),
        "v": small_part(),
        "g": rows_part(gate_weight, gates, False),
        "y": columns_part(rec_proj, 2 * half, proj_y),
        "o": rows_part(out_proj, out_half, True),
    }

    def advance(order):
        for name in order:
            next(parts[name], None)

    place = pl.ds(pl.multiple_of(side * own, 16), own)
    def cot_at(o, far=0):
        return cots.at[jnp.clip(z + o, 0, n - 1), far]

    cot_inner = [links.plan(cot_at(0), cot_at(0), m) for m in inner]
    cot_side = []
    own_cot = local(cot, cot_at(0))
    advance("xvgoy")
    tokens = links.send(x_own, lead.at[place], 1)
    lead[place] = x_own[...]
    lead[rows:] = halo[...]
    advance("xvgo")
    own_cot.wait()
    own_side = links.send(cot_at(0), cot_at(0, 1), 1)
    advance("xvxgyov")
    advance("ggxgvyyxg")
    loads = [local(proj_x, held_x), local(gates, held_g)]
    tokens.wait_recv()
    few = 16

    @pl.loop(0, lead.shape[0] // few)
    def _(k):
        here = pl.ds(pl.multiple_of(k * few, few), few)
        normal[here] = normed(lead[here].astype(F32), params[SUBS : SUBS + 1]).astype(BF16)

    for copy in loads:
        copy.wait()

    def gate(cols, tall):
        cols(xb)[...] = jnp.dot(normal[...], cols(held_x)[...], preferred_element_type=F32).astype(BF16)
        forward_kernel(
            steps, quarters, cols(xb), cols(chan), tall(held_g), cols(conv), cols(recur), cols(inject), cols(decay),
            cols(states), cols(prod), cols(enter), cols(line.at[0]),
        )

    by_head(heads, head_w, gate)
    inflow[...] = chunk_inflow(links, line, blocks, quarters, False, lambda: [copy.start() for copy in cot_inner])
    advance("o")
    tops = [2 * seqs * k for k in range(1, spans // 2)]
    across = {m: links.send(wide, wides[m // seqs - 1], m) for m in tops}
    beside = [links.send(wide, wides[0], core), links.send(narrow, beside_narrow, core)]
    def onward(k):
        cot_inner[k].wait_recv()
        here = links.flipped(z, inner[k] // 2) - z
        cot_side.append(links.send(cot_at(here), cot_at(here, 1), 1))

    advance("yy")
    loads = [local(proj_y, held_y)]
    loads[0].wait()
    block = steps * SUBS

    def mix(cols, tall):
        cols(y_pre)[...] = jnp.dot(normal[:rows], cols(held_y)[...], preferred_element_type=F32)
        ins, flows, hold, gain_y = cols(inflow), cols(flow), cols(states), cols(y_pre)
        for b in (0, 1):
            entered = cols(enter)[b * SUBS : (b + 1) * SUBS] * ins[...] + cols(enter)[(2 + b) * SUBS : (3 + b) * SUBS]
            flows[b * SUBS : (b + 1) * SUBS] = entered
            flows[(2 + b) * SUBS : (3 + b) * SUBS] = cols(prod)[(b + 1) * block - SUBS : (b + 1) * block]
            here = slice(b * block, (b + 1) * block)
            total = hold[here].reshape(steps, SUBS, head_w) + cols(prod)[here].reshape(steps, SUBS, head_w) * entered[None]
            total = total.reshape(block, head_w)
            hold[here] = total
            low_part = total * gelu_parts(gain_y[here])[0]
            cols(mixed)[here] = low_part.astype(BF16)
            tall(mixed_turned)[:, here] = low_part.T.astype(BF16)

    by_head(heads, head_w, mix)

    onward(0)
    advance("oo")
    load = local(out_half, held_o)
    load.wait()
    step = 512

    @pl.loop(0, width // step)
    def _(k):
        columns = pl.ds(pl.multiple_of(k * step, 128), step)
        total = jnp.dot(mixed[...], held_o[:, columns], preferred_element_type=F32)
        first = side == 0
        resid[:, columns] = x_own[:, columns].astype(F32) + jnp.where(first, total[:own], total[own:])
        to_side[:, columns] = jnp.where(first, total[own:], total[:own]).astype(BF16)

    partial = links.send(to_side, from_side, 1)
    for k in range(1, n - 2):
        onward(k)

    @pl.loop(0, width // head_w)
    def _(k):
        columns = pl.ds(pl.multiple_of(k * head_w, 128), head_w)
        turned[columns] = normal[:rows, columns].astype(F32).T.astype(BF16)

    partial.wait_recv()
    size = width // spans

    @pl.loop(0, own // few)
    def _(k):
        here = pl.ds(pl.multiple_of(k * few, few), few)
        total = resid[here] + from_side[here].astype(F32)
        resid[here] = total
        low[here] = normed(total, params[SUBS + 1 : SUBS + 2]).astype(BF16)

    for j in range(spans):
        start = pl.multiple_of(links.flipped(links.span, j) * size, 128)
        normal_two[:, j * size : (j + 1) * size] = low[:, pl.ds(start, size)]

    onward(n - 2)
    for m in tops:
        across[m].wait_recv()
        beside.append(links.send(wides[m // seqs - 1], wides[m // seqs], core))
    for copy in (*beside, own_side, *cot_side):
        copy.wait_recv()
    for part in parts.values():
        for _ in part:
            pass
    links.close()


def front(sizes, steps, quarters, heads, head_w, x_own, halo, params, rec_proj, out_proj, gate_weight, cot, wide, narrow):
    spans, seqs = sizes
    count = spans * seqs
    own, width = x_own.shape
    half, rows, share = width // 2, 2 * own, rec_proj.shape[0]
    n = seqs // 2
    inside, anywhere = pl.BlockSpec(memory_space=pltpu.VMEM), pl.BlockSpec(memory_space=pl.ANY)

    def high(*shape):
        return jax.ShapeDtypeStruct(shape, F32)

    def low(*shape):
        return jax.ShapeDtypeStruct(shape, BF16)

    lead = rows + halo.shape[0]
    near = [
        low(lead, width), low(lead, half), *[high(rows, half)] * 6, high(4 * SUBS, half), low(rows, half), high(own, width),
        low(own, width), high(params.shape[0], width), high(SUBS, half),
        low(width, rows), low(half, rows),
    ]
    far = [
        low(width, half), low(width, half), low(half, width), low(half, gate_weight.shape[1]), *[low(*wide.shape)] * (spans - 1),
        low(*narrow.shape), low(n, 2, *cot.shape),
    ]
    end = (SUBS, half)
    copies = 4 * (3 + 10 * n) + 4 * n + 3 + 6 * n + (n - 1) + 2 * spans + 4
    outs = pl.pallas_call(
        functools.partial(front_kernel, sizes, steps, quarters, heads, head_w, share),
        in_specs=[inside] * 7 + [anywhere] * 2,
        out_specs=[inside] * len(near) + [anywhere] * len(far),
        out_shape=[*near, *far],
        scratch_shapes=[
            pltpu.VMEM((lead, width), BF16), pltpu.VMEM((width, half), BF16), pltpu.VMEM((width, half), BF16),
            pltpu.VMEM((half, width), BF16), pltpu.VMEM((half, gate_weight.shape[1]), BF16), pltpu.VMEM((count * params.shape[0], params.shape[1]), F32),
            pltpu.VMEM((rows, half), F32), pltpu.VMEM((4 * SUBS, half), F32), pltpu.VMEM((n, *end), F32),
            pltpu.VMEM((spans, *end), F32), pltpu.VMEM(end, F32), *[pltpu.VMEM((own, width), BF16)] * 3,
            pltpu.SemaphoreType.DMA((copies,)), pltpu.SemaphoreType.DMA((copies,)), pltpu.SemaphoreType.DMA((16,)),
        ],
        compiler_params=pltpu.CompilerParams(collective_id=0, has_side_effects=True, vmem_limit_bytes=VMEM_LIMIT),
    )(x_own, halo, params, rec_proj, out_proj, gate_weight, cot, wide, narrow)
    wides, narrows, cots = outs[20 : 19 + spans], outs[19 + spans], outs[20 + spans]
    return outs[:16], outs[16:20], [wide, *wides], [narrow, narrows], cots


def return_kernel(
    sizes, steps, quarters, heads, inner, branch, out_w, y_pre, states, decay, flow, conv, recur, inject, xb, chan, gate,
    resid, near, far, wide, narrow, proj_y, branch_o, y_grad, x_grad, gate_o, small, output, part, wides, narrows, held_y, loads, dx, spill, came_back, grad, local, after, enter, carry, line, blocks, inflow, dmix, from_side, to_inner, from_inner, sends, recvs,
):
    spans, seqs = sizes
    tops = [2 * seqs * k for k in range(1, spans // 2)]
    n = len(inner) + 1
    links = Links(sizes, sends, recvs)
    side = links.seq % 2
    own, width = branch.shape
    me, count = links.span * seqs + links.seq, spans * seqs

    def device(index):
        return (index // seqs, index % seqs)

    links.greet([1, *inner, *[m * seqs for m in range(1, spans)]], [device((me + 2) % count)])
    place = pl.ds(pl.multiple_of(side * own, 16), own)
    whole = links.send(branch, branch_o.at[place], 1)
    tall = wide.shape[1] // 2
    across = [links.send(wide.at[k, pl.ds(0, tall)], wides.at[k, pl.ds(0, tall)], m) for k, m in enumerate(tops)]
    branch_o[place] = branch[...]
    load = pltpu.make_async_copy(proj_y, held_y, loads.at[0])
    load.start()
    whole.wait_recv()
    sums = [*range(1, n), 0]
    over_side = {}

    def side_sum(i):
        over_side[sums[i]] = links.send(far.at[sums[i]], from_side.at[sums[i]], 1)

    over_inner = []

    def inner_sum(i):
        k = sums[i]
        over_side[k].wait_recv()
        if k:
            to_inner[k - 1] = (near[k].astype(F32) + from_side[k].astype(F32)).astype(BF16)
            over_inner.append(links.send(to_inner.at[k - 1], from_inner.at[k - 1], inner[k - 1]))

    side_sum(0)
    head_w = gate.shape[1] // 2

    def first(cols, tall):
        mixed_grad = lax.dot_general(branch_o[...], tall(out_w)[...], (((1,), (1,)), ((), ())), preferred_element_type=F32)
        value, slope = gelu_parts(cols(y_pre)[...])
        cols(grad)[...] = mixed_grad * value
        cols(y_grad)[...] = (mixed_grad * cols(states)[...] * slope).astype(BF16)
        adjoint_kernel(
            steps, quarters, cols(grad), cols(decay), cols(flow), cols(local), cols(after), cols(enter), cols(line.at[0])
        )

    by_head(heads, head_w, first)

    def between():
        inner_sum(0)
        side_sum(1)

    inflow[...] = chunk_inflow(links, line, blocks, quarters, True, between)
    for k, m in enumerate(tops):
        across.append(links.send(wide.at[k, pl.ds(tall, tall)], wides.at[k, pl.ds(tall, tall)], m))
        across.append(links.send(narrow.at[k], narrows.at[k], m))
    inner_sum(1)
    side_sum(2)

    def second(cols, tall):
        came = jnp.concatenate(
            [
                cols(enter)[b * SUBS : (b + 1) * SUBS] * cols(inflow)[...] + cols(enter)[(2 + b) * SUBS : (3 + b) * SUBS]
                for b in (0, 1)
            ],
            axis=0,
        )
        backward_kernel(
            steps, quarters, cols(local), cols(after), cols(states), came, cols(flow), cols(conv), cols(recur),
            cols(inject), cols(decay), cols(xb), cols(chan), tall(gate), cols(dx), cols(spill), tall(gate_o), cols(small),
        )

    by_head(heads, head_w, second)
    edge = (CONV - 1) * SUBS
    slot = links.used
    links.used += 1
    handed = pltpu.make_async_remote_copy(
        spill, came_back, links.sends.at[slot], links.recvs.at[slot], device_id=device(jnp.maximum(me - 2, 0)), device_id_type=MESH
    )
    pl.when(me >= 2)(handed.start)
    links.open.append((handed, me >= 2))
    rows = 2 * own
    x_grad[: rows - 2 * edge] = dx[: rows - 2 * edge].astype(BF16)
    load.wait()
    step = 512

    @pl.loop(0, width // step)
    def _(k):
        start = pl.multiple_of(k * step, 128)
        weights = held_y[pl.ds(start, step)]
        part[:, pl.ds(start, step)] = lax.dot_general(
            y_grad[...], weights, (((1,), (1,)), ((), ())), preferred_element_type=F32
        )

    for i in range(2, n):
        inner_sum(i)
        if i + 1 < n:
            side_sum(i + 1)
    pl.when(me + 2 < count)(handed.wait_recv)

    @pl.when(me + 2 >= count)
    def _():
        came_back[...] = jnp.zeros_like(came_back)

    last = quarter_of((SUBS, came_back.shape[1]), quarters) == quarters - 1
    total = [dx[rows - 2 * edge : rows - edge]]
    for k in range(CONV - 1, 0, -1):
        added = roll(came_back[(k - 1) * SUBS : k * SUBS], quarters - 1)
        total.append(dx[rows - k * SUBS : rows - (k - 1) * SUBS] + jnp.where(last, added, 0.0))
    x_grad[rows - 2 * edge :] = jnp.concatenate(total, axis=0).astype(BF16)
    few = 16
    size = width // spans
    for copy in over_inner:
        copy.wait_recv()

    for j in range(spans):
        columns = slice(j * size, (j + 1) * size)
        there = pl.ds(pl.multiple_of(links.flipped(links.span, j) * size, 128), size)
        total = resid[:, there] + near[0, :, columns].astype(F32) + from_side[0, :, columns].astype(F32)
        for k in range(n - 1):
            total = total + from_inner[k, :, columns].astype(F32)
        output[:, there] = total.astype(BF16)

    for copy in across:
        copy.wait_recv()
    links.close()


def returned(sizes, steps, quarters, heads, inner, branch, out_w, y_pre, states, decay, flow, conv, recur, inject, xb, chan, gate,
             resid, near, far, wide, narrow, proj_y):
    spans, _ = sizes
    own, width = branch.shape
    rows, half = y_pre.shape
    n = len(inner) + 1
    inside, anywhere = pl.BlockSpec(memory_space=pltpu.VMEM), pl.BlockSpec(memory_space=pl.ANY)

    def high(*shape):
        return jax.ShapeDtypeStruct(shape, F32)

    def low(*shape):
        return jax.ShapeDtypeStruct(shape, BF16)

    shapes = [
        low(rows, width), low(rows, half), low(rows, half), high(*gate.shape), high(SUBS, half), low(own, width),
        high(rows, width), low(*wide.shape), low(*narrow.shape),
    ]
    end = (SUBS, half)
    copies = 3 * (spans // 2) + 2 * n + 2 * n + spans + 2
    tail = ((CONV - 1) * SUBS, half)
    return pl.pallas_call(
        functools.partial(return_kernel, sizes, steps, quarters, heads, inner),
        in_specs=[inside] * 15 + [anywhere] * 3,
        out_specs=[inside] * 7 + [anywhere] * 2,
        out_shape=shapes,
        scratch_shapes=[
            pltpu.VMEM(proj_y.shape, BF16), pltpu.SemaphoreType.DMA((1,)),
            pltpu.VMEM((rows, half), F32), pltpu.VMEM(tail, F32), pltpu.VMEM(tail, F32), *[pltpu.VMEM((rows, half), F32)] * 3, pltpu.VMEM((4 * SUBS, half), F32), pltpu.VMEM(end, F32),
            pltpu.VMEM((n, *end), F32), pltpu.VMEM((spans, *end), F32), pltpu.VMEM(end, F32), pltpu.VMEM(end, F32),
            pltpu.VMEM((n, own, width), BF16), pltpu.VMEM((n - 1, own, width), BF16), pltpu.VMEM((n - 1, own, width), BF16),
            pltpu.SemaphoreType.DMA((copies,)), pltpu.SemaphoreType.DMA((copies,)),
        ],
        compiler_params=pltpu.CompilerParams(collective_id=4, has_side_effects=True, vmem_limit_bytes=VMEM_LIMIT),
    )(branch, out_w, y_pre, states, decay, flow, conv, recur, inject, xb, chan, gate, resid, near, far, wide, narrow, proj_y)


def on_device(
    inputs, norm_one, rec_proj, conv_weight, conv_bias, gate_weight, gate_bias, decay_param, out_proj, norm_two,
    mlp_wide, mlp_narrow, cotangent,
):
    spans, seqs = lax.axis_size("span"), lax.axis_size("seq")
    count = spans * seqs
    span, seq = lax.axis_index("span"), lax.axis_index("seq")
    me = span * seqs + seq
    side = me % 2
    pair = me // 2
    pairs = count // 2
    batch, tokens, width = inputs.shape
    half = width // 2
    quarters = SUBS // batch
    steps = tokens // quarters
    own = batch * tokens
    rows = 2 * own
    head_w = gate_weight.shape[1] // 2
    heads = half // head_w
    edge = CONV - 1
    share = width // count
    units = mlp_narrow.shape[1]
    inner = [2 * k for k in range(1, seqs // 2)]
    core = seqs
    xs = [2 * seqs * k for k in range(1, spans // 2)]
    top = count // 2
    upper = me // top
    chunk_masks = [0, *inner[1::-1], *inner[2:]]

    def to_rows(v):
        return v.reshape(batch, quarters, steps, width).transpose(2, 0, 1, 3).reshape(own, width)

    def from_rows(v):
        return v.reshape(steps, batch, quarters, width).transpose(1, 2, 0, 3).reshape(batch, tokens, width)

    def in_order(mine, other, axis):
        return jnp.concatenate([jnp.where(side == 0, mine, other), jnp.where(side == 0, other, mine)], axis=axis)

    def cut(v, index, size, axis):
        return lax.dynamic_slice_in_dim(v, index * size, size, axis)

    direct = share % 16 == 0 and (spans, seqs) == (4, 8)

    def gathered_rows(block, buffer, place):
        pieces = {0: block}
        for m in inner:
            pieces[m] = swap(block, m)
        for m in xs:
            for n in (0, *inner):
                pieces[m ^ n] = swap(pieces[n], m)
        for n in list(pieces):
            pieces[core ^ n] = swap(pieces[n], core)
        for m, piece in pieces.items():
            buffer = lax.dynamic_update_slice_in_dim(buffer, piece, place(me ^ m), 0)
        return buffer

    def columns_half(block):
        mine, theirs = cut(block, side, half, 1), cut(block, 1 - side, half, 1)
        block = in_order(mine, swap(theirs, 1), 0)
        return gathered_rows(block, jnp.zeros((width, half), BF16), lambda d: d // 2 * 2 * share)

    def rows_half(block):
        full = lax.all_gather(block, AXES, axis=0, tiled=True)
        return cut(full, side, half, 0)

    def by_span(v):
        size = width // spans
        return jnp.concatenate([cut(v, span ^ j, size, 1) for j in range(spans)], axis=1)

    def over_sides(partial):
        partial = partial.reshape(2, own, width)
        other = lax.dynamic_index_in_dim(partial, 1 - side, 0, keepdims=False).astype(BF16)
        return lax.dynamic_index_in_dim(partial, side, 0, keepdims=False) + swap(other, 1).astype(F32)

    def exchanged(carry):
        every = lax.all_gather(carry, AXES, axis=0).reshape(pairs, 2, batch, quarters, half)
        every = lax.dynamic_index_in_dim(every, side, 1, keepdims=False)
        return every[:, :, 0], every[:, :, 1]

    def entering(enter, h):
        enter = enter.reshape(2, 2, SUBS, half)
        return enter[0] * jnp.repeat(h, quarters, axis=0)[None] + enter[1]

    def by_steps(v):
        return v.reshape(2, steps, SUBS, half)

    def span_gather(block):
        pieces = {0: block}
        for m in xs:
            pieces[m] = swap(block, m)
        for n in list(pieces):
            pieces[n ^ core] = swap(pieces[n], core)
        return [pieces[m * seqs] for m in range(spans)]

    def token_gather(v):
        blocks = [v] + [swap(v, m) for m in inner]
        return [b for block in blocks for b in (block, swap(block, 1))]

    small = jnp.stack([*conv_weight.T, conv_bias, *gate_bias.T, decay_param, norm_one, norm_two]).astype(F32)
    small = jnp.concatenate([small[:7], jax.nn.softplus(small[7:8]), small[8:]], axis=0)
    wide_own = mlp_wide.transpose(1, 2, 0).reshape(2 * units, width // spans)
    narrow_own = mlp_narrow.T
    grads_own = by_span(to_rows(cotangent))
    c = to_rows(cotangent).astype(F32)

    mine = to_rows(inputs)
    x = mine.astype(F32)
    tail = inputs[:, tokens - edge :]
    halo = lax.ppermute(tail, AXES, [(i, i + 1) for i in range(1, count - 1, 2)]) + lax.ppermute(
        tail, AXES, [(i, i + 2) for i in range(1, count - 2, 2)]
    )
    halo = jnp.zeros((edge, batch, quarters, width), BF16).at[:, :, 0].set(halo[:, ::-1].transpose(1, 0, 2))
    halo = jnp.concatenate([halo.reshape(edge * SUBS, width), jnp.zeros((8, width), BF16)], axis=0)

    if direct:
        packed = jnp.pad(small, ((0, 6), (0, -share % 128)))
        nearby, (proj_x, proj_y, out_half, gates), wides, narrows, cots = front(
            (spans, seqs), steps, quarters, heads, head_w, mine, halo, packed, rec_proj, out_proj, gate_weight, grads_own,
            wide_own, narrow_own,
        )
        normal_one, x_branch, y_pre, conv, recur, inject, decay, states, flow, mixed, resid, normal_two, params, chan, turned, mixed_turned = nearby
        gain_one, gain_two = params[SUBS], params[SUBS + 1]
    else:
        proj_x = columns_half(rec_proj[:, :width])
        proj_y = columns_half(rec_proj[:, width:])
        gates = rows_half(gate_weight)
        out_half = rows_half(out_proj)
        small = lax.all_gather(small, AXES, axis=1, tiled=True)
        gain_one, gain_two = small[SUBS], small[SUBS + 1]
        chan = cut(small[:SUBS], side, half, 1)
        lead = jnp.concatenate([in_order(mine, swap(mine, 1), 0), halo], axis=0)
        normal_one = normed(lead.astype(F32), gain_one).astype(BF16)
        x_branch = nn(normal_one, proj_x, BF16)
        normal_one = normal_one[:rows]
        y_pre = nn(normal_one, proj_y)
        y_branch, gelu_back = jax.vjp(jax.nn.gelu, y_pre)
        kernel = functools.partial(forward_kernel, steps, quarters)
        full = ((rows, half), False)
        ends = ((4 * SUBS, half), False)
        conv, recur, inject, decay, local, prod, enter, carry = by_heads(
            kernel, heads, head_w, [(x_branch, False), (chan, False), (gates, True)],
            [full] * 6 + [ends, ((SUBS, half), False)],
        )
        prods, sums = exchanged(carry)
        h = jnp.zeros((batch, half), F32)
        for j in range(pairs - 1):
            h = jnp.where(j < pair, prods[j] * h + sums[j], h)
        entered = entering(enter, h)
        states = (by_steps(local) + by_steps(prod) * entered[:, None]).reshape(rows, half)
        flow = jnp.concatenate([entered, by_steps(prod)[:, -1]], axis=0).reshape(4 * SUBS, half)
        mixed = (states * y_branch).astype(BF16)
        resid = x + over_sides(nn(mixed, out_half))
        normal_two = by_span(normed(resid, gain_two).astype(BF16))
        wides, narrows = span_gather(wide_own), span_gather(narrow_own)
        cots = token_gather(grads_own)

    def token_scatter(near, far):
        total = None
        for k, m in enumerate((0, *inner)):
            block = near[k].astype(F32) + swap(far[k], 1).astype(F32)
            total = block if m == 0 else total + swap(block.astype(BF16), m).astype(F32)
        return by_span(total)

    size = width // spans

    def by_core(v):
        blocks = [v[:, j * size : (j + 1) * size] for j in range(spans)]
        return [*blocks[::2], jnp.concatenate(blocks[1::2], axis=1)]

    if direct:
        normal_two_grad, near, far, all_act, all_hidden, *features, wide_away, narrow_away, wide_recv, narrow_recv = feed_forward(
            (spans, seqs), chunk_masks, normal_two, cots, wides, narrows
        )
        all_normal, all_grads = [features[0]], [features[1]]
        wide_away, narrow_away, wide_recv, narrow_recv = wide_away[None], narrow_away[None], wide_recv[:, :size], narrow_recv[:, :size]
    else:
        wide, narrow = jnp.concatenate(wides, axis=1), jnp.concatenate(narrows, axis=1)
        all_normal = jnp.concatenate(token_gather(normal_two), axis=0)
        all_grads = jnp.concatenate(cots, axis=0)

        def activate(values):
            return jax.nn.gelu(values[:, :units]) * values[:, units:]

        value, back = jax.vjp(activate, nt(all_normal, wide))
        all_hidden = value.astype(BF16)
        all_act = back(nt(all_grads, narrow))[0].astype(BF16)

        def sided(v):
            v = v.reshape(len(inner) + 1, 2, own, width)
            return v[:, 0], v[:, 1]

        all_normal, all_grads = by_core(all_normal), by_core(all_grads)
        normal_two_grad = token_scatter(*sided(nn(all_act, wide, BF16)))
        near, far = sided(nn(all_hidden, narrow, BF16))
    def core_sum(left, right):
        recv = swap(tn(left, right[-1], BF16), core)
        away = [
            (tn(left, v) + recv[:, (k + 1) * size : (k + 2) * size].astype(F32)).astype(BF16) for k, v in enumerate(right[1:-1])
        ]
        return recv[:, :size], jnp.stack(away)

    def own_sum(left, right, recv, came):
        left, came = lax.optimization_barrier((left, came))
        return tn(left, right[0]) + recv.astype(F32) + jnp.sum(came.astype(F32), axis=0)

    if not direct:
        wide_recv, wide_away = core_sum(all_act, all_normal)
        narrow_recv, narrow_away = core_sum(all_hidden, all_grads)
    resid_part, gain_two_grad = norm_back(resid, gain_two, normal_two_grad)
    resid_grad = c + resid_part
    branch_low = resid_grad.astype(BF16)
    if direct:
        branch_low, y_grad, x_grad, gate_grad, small_grad, output, normal_one_part, wide_came, narrow_came = returned(
            (spans, seqs), steps, quarters, heads, chunk_masks[1:], branch_low, out_half, y_pre, states, decay, flow, conv, recur, inject,
            x_branch, chan, gates, resid, near, far, wide_away, narrow_away, proj_y,
        )
    else:
        output = (resid + token_scatter(near, far)).astype(BF16)
        wide_came = jnp.stack([swap(wide_away[k], m) for k, m in enumerate(xs)])
        narrow_came = jnp.stack([swap(narrow_away[k], m) for k, m in enumerate(xs)])
        branch_low = in_order(branch_low, swap(branch_low, 1), 0)
        mixed_grad = nt(branch_low, out_half)
        y_grad = gelu_back(mixed_grad * states)[0].astype(BF16)
        kernel = functools.partial(adjoint_kernel, steps, quarters)
        local_adj, after, enter, carry = by_heads(
            kernel, heads, head_w, [(mixed_grad * y_branch, False), (decay, False), (flow, False)],
            [full, full, ends, ((SUBS, half), False)],
        )
        prods, sums = exchanged(carry)
        h = jnp.zeros((batch, half), F32)
        for j in range(pairs - 1, 0, -1):
            h = jnp.where(j > pair, prods[j] * h + sums[j], h)
        came = entering(enter, h).reshape(2 * SUBS, half)
        kernel = functools.partial(backward_kernel, steps, quarters)
        dx, spill, gate_grad, small_grad = by_heads(
            kernel, heads, head_w,
            [(v, False) for v in (local_adj, after, states, came, flow, conv, recur, inject, decay, x_branch, chan)]
            + [(gates, True)],
            [full, ((edge * SUBS, half), False), ((half, 2 * head_w), True), ((SUBS, half), False)],
        )
        spill = lax.ppermute(
            spill.reshape(edge, batch, quarters, half)[::-1, :, 0], AXES, [(i, i - 2) for i in range(2, count)]
        )
        spill = jnp.pad(
            spill[:, :, None], ((0, 0), (0, 0), (quarters - 1, 0), (0, 0))
        ).reshape(edge * SUBS, half)
        x_grad = jnp.concatenate([dx[: rows - edge * SUBS], dx[rows - edge * SUBS :] + spill], axis=0).astype(BF16)
    output = from_rows(output)
    wide_owned = own_sum(all_act, all_normal, wide_recv, wide_came)
    wide_owned = wide_owned.reshape(2, units, size).transpose(2, 0, 1)
    narrow_owned = own_sum(all_hidden, all_grads, narrow_recv, narrow_came).T
    if not direct:
        normal_one_part = nt(y_grad, proj_y)
    normal_one_part = normal_one_part + nt(x_grad, proj_x)

    def blocks_of(v, masks, wrap):
        size = 2 * share
        return [lax.dynamic_slice_in_dim(v, (me ^ m) // 2 % wrap * size, size, 0) for m in masks]

    def to_columns_owner(v_kept, v_given):
        recv = swap(v_given, core)
        n = len(inner) + 1
        total = (v_kept + recv.astype(F32)).reshape(len(xs) + 1, n, 2 * share, v_kept.shape[1])
        near = total[0]
        for k, m in enumerate(xs):
            near = near + swap(total[k + 1].astype(BF16), m).astype(F32)
        out = near[0]
        for k, m in enumerate(inner):
            out = out + swap(near[k + 1].astype(BF16), m).astype(F32)
        out = out.reshape(2, share, out.shape[1])
        other = lax.dynamic_index_in_dim(out, 1 - side, 0, keepdims=False).astype(BF16)
        return lax.dynamic_index_in_dim(out, side, 0, keepdims=False), swap(other, 1).astype(F32)

    def to_rows_owner(v_kept, v_given):
        cols = v_kept.shape[1]
        total = (v_kept + swap(v_given, core).astype(F32)).reshape(len(low_order), 2 * share, cols)
        away = cut(total, 1 - upper, cols // 2, 2).astype(BF16)
        near = cut(total, upper, cols // 2, 2) + swap(away, top).astype(F32)
        out = near[0]
        for k, m in enumerate(low_order[1:]):
            out = out + swap(near[k + 1].astype(BF16), m).astype(F32)
        other = swap(out.astype(BF16), top).astype(F32)
        out = in_order(out, other, 1).reshape(2, share, cols)
        gone = lax.dynamic_index_in_dim(out, 1 - side, 0, keepdims=False).astype(BF16)
        here = lax.dynamic_index_in_dim(out, side, 0, keepdims=False)
        return jnp.where(upper == side, here, swap(gone, 1).astype(F32))

    order = [m ^ n for m in (0, *xs) for n in (0, *inner)]
    low_order = [m ^ n for m in (0, *[v for v in xs if v < top]) for n in (0, *inner)]

    def ordered(v, masks, wrap):
        return [jnp.concatenate(blocks_of(v, [m ^ c for m in masks], wrap), axis=0) for c in (0, core)]

    if direct:
        part = normal_one_part.reshape(2, own, width)
        proj_owned, out_owned, gate_owned, input_grad, sums = scatter_grads(
            (spans, seqs), share, turned, mixed_turned, x_grad, y_grad, branch_low, gate_grad, small_grad, gain_two_grad[None],
            mine, gain_one[None], resid_grad, lax.dynamic_index_in_dim(part, side, 0, keepdims=False),
            lax.dynamic_index_in_dim(part, 1 - side, 0, keepdims=False).astype(BF16),
        )
        gains = cut(sums[:2, :width], me, share, 1).T
        small_owned = cut(sums[:, width:], me % (count // 2), share, 1).T
    else:
        input_part, gain_one_grad = norm_back(x, gain_one, over_sides(normal_one_part))
        input_grad = resid_grad + input_part
        kept_d, given_d = ordered(normal_one.T, order, pairs)
        kept_m, given_m = ordered(mixed.T, low_order, pairs // 2)
        by_row = jnp.concatenate([gate_grad, small_grad.T, jnp.zeros((half, head_w - SUBS), F32)], axis=1)
        kept_g, given_g = ordered(by_row, low_order, pairs // 2)
        gains = jnp.pad(jnp.stack([gain_one_grad, gain_two_grad], axis=1), ((0, 0), (0, 126)))
        kept_n, given_n = ordered(gains, order, pairs)
        proj_owned = jnp.concatenate(
            [in_order(*to_columns_owner(nn(kept_d, g), nn(given_d, g, BF16)), 1) for g in (x_grad, y_grad)], axis=1
        )
        out_owned = to_rows_owner(nn(kept_m, branch_low), nn(given_m, branch_low, BF16))
        rest = to_rows_owner(kept_g, given_g.astype(BF16))
        gate_owned, small_owned = rest[:, : 2 * head_w], rest[:, 2 * head_w : 2 * head_w + SUBS]
        gains = sum(to_columns_owner(kept_n, given_n.astype(BF16)))
    input_grad = from_rows(input_grad)

    return (
        output,
        input_grad,
        gains[:, 0],
        proj_owned,
        small_owned[:, :CONV],
        small_owned[:, 4],
        gate_owned,
        small_owned[:, 5:7],
        small_owned[:, 7] * jax.nn.sigmoid(decay_param.astype(F32)),
        out_owned,
        gains[:, 1],
        wide_owned,
        narrow_owned,
    )


def solution(mesh):
    both = ("span", "seq")
    tokens = P(None, both, None)
    placed = (
        tokens, P(both), P(both, None), P(both, None), P(both), P(both, None), P(both, None), P(both), P(both, None),
        P(both), P("span", None, "seq"), P("span", "seq"), tokens,
    )
    given = (
        tokens, tokens, P(both), P(both, None), P(both, None), P(both), P(both, None), P(both, None), P(both),
        P(both, None), P(both), P("span", None, "seq"), P("span", "seq"),
    )
    return jax.shard_map(on_device, mesh=mesh, in_specs=placed, out_specs=given, check_vma=False)
```

```python
import functools

import jax
import jax.numpy as jnp
from jax import lax
from jax.experimental import pallas as pl
from jax.experimental.pallas import tpu as pltpu
from jax.sharding import PartitionSpec as P

CONV = 4
EPS = 1e-06
AXES = ("span", "seq")
F32 = jnp.float32
BF16 = jnp.bfloat16
SUBS = 8


def swap(value, mask):
    count = lax.axis_size("span") * lax.axis_size("seq")
    return lax.ppermute(value, AXES, [(i, i ^ mask) for i in range(count)])


def dot(a, b, dims, out=F32):
    return lax.dot_general(a, b, ((dims[0], dims[1]), ((), ())), preferred_element_type=F32).astype(out)


def nn(a, b, out=F32):
    return dot(a, b, ((1,), (0,)), out)


def nt(a, b, out=F32):
    return dot(a, b, ((1,), (1,)), out)


def tn(a, b, out=F32):
    return dot(a, b, ((0,), (0,)), out)


def normed(v, gain):
    return v * lax.rsqrt(jnp.mean(v * v, axis=-1, keepdims=True) + EPS) * gain


def norm_back(v, gain, grad):
    scale = lax.rsqrt(jnp.mean(v * v, axis=-1, keepdims=True) + EPS)
    z = v * scale
    e = grad * gain
    return scale * (e - z * jnp.mean(e * z, axis=-1, keepdims=True)), jnp.sum(grad * z, axis=0)


def one_less_exp(u):
    series = 1.0 + u / 7.0
    for n in (6.0, 5.0, 4.0, 3.0, 2.0):
        series = 1.0 + u / n * series
    return jnp.where(u > -0.25, -u * series, 1.0 - jnp.exp(u))


def roll(v, by):
    return pltpu.roll(v, by % SUBS, 0)


def quarter_of(shape, quarters):
    return lax.broadcasted_iota(jnp.int32, shape, 0) % quarters


def spread(v, quarters, at):
    q = quarter_of(v.shape, quarters)
    held = jnp.where(q == at, v, 0.0)
    total = held
    for k in range(1, quarters):
        total = total + roll(held, k if at == 0 else -k)
    return total


def scan_carries(prods, sums, quarters, backward):
    q = quarter_of(prods[0].shape, quarters)
    sign = -1 if backward else 1
    order = (1, 0) if backward else (0, 1)
    place = quarters - 1 - q if backward else q
    whole = None
    enter = [None, None]
    for b in order:
        p, s = prods[b], sums[b]
        d = 1
        while d < quarters:
            pp, ss = roll(p, sign * d), roll(s, sign * d)
            ok = place >= d
            s = jnp.where(ok, p * ss + s, s)
            p = jnp.where(ok, p * pp, p)
            d *= 2
        first = place == 0
        ep = jnp.where(first, 1.0, roll(p, sign))
        es = jnp.where(first, 0.0, roll(s, sign))
        last = 0 if backward else quarters - 1
        tp, ts = spread(p, quarters, last), spread(s, quarters, last)
        if whole is None:
            enter[b] = (ep, es)
            whole = (tp, ts)
        else:
            enter[b] = (ep * whole[0], ep * whole[1] + es)
            whole = (tp * whole[0], tp * whole[1] + ts)
    return enter, whole


def earlier_rows(groups, halo, quarters, steps):
    q = quarter_of(groups[0].shape[1:], quarters)
    edge = CONV - 1
    out = []
    for b in (0, 1):
        ahead = []
        for k in range(edge, 0, -1):
            same = roll(groups[b][steps - k], 1)
            before = halo[k - 1] if b == 0 else roll(groups[0][steps - k], 1 - quarters)
            ahead.append(jnp.where(q == 0, before, same)[None])
        out.append(jnp.concatenate([*ahead, groups[b]], axis=0))
    return out


def forward_kernel(steps, quarters, xb, chan, gate, conv_o, recur_o, inject_o, decay_o, local_o, prod_o, enter_o, carry_o):
    rows = 2 * steps * SUBS
    width = xb.shape[1]
    head = xb[...].astype(F32)
    groups = [head[b * steps * SUBS : (b + 1) * steps * SUBS].reshape(steps, SUBS, width) for b in (0, 1)]
    halo = [head[rows + k * SUBS : rows + (k + 1) * SUBS] for k in range(CONV - 1)]
    edge = CONV - 1
    convs = []
    for ext in earlier_rows(groups, halo, quarters, steps):
        total = jnp.broadcast_to(chan[4:5][None], (steps, SUBS, width))
        for k in range(CONV):
            total = total + chan[k : k + 1][None] * ext[edge - k : edge - k + steps]
        convs.append(total.reshape(steps * SUBS, width))
    conv = jnp.concatenate(convs, axis=0)
    pre = jnp.dot(conv.astype(BF16), gate[...], preferred_element_type=F32)
    recur = jax.nn.sigmoid(pre[:, :width] + chan[5:6])
    inject = jax.nn.sigmoid(pre[:, width:] + chan[6:7])
    log_decay = -8.0 * recur * chan[7:8]
    decay = jnp.exp(log_decay)
    driven = jnp.sqrt(one_less_exp(2.0 * log_decay)) * inject * conv
    conv_o[...] = conv
    recur_o[...] = recur
    inject_o[...] = inject
    decay_o[...] = decay
    prods, sums = [], []
    for b in (0, 1):
        h = p = None
        for t in range(steps):
            at = (b * steps + t) * SUBS
            d, u = decay[at : at + SUBS], driven[at : at + SUBS]
            h = u if h is None else d * h + u
            p = d if p is None else d * p
            local_o[at : at + SUBS] = h
            prod_o[at : at + SUBS] = p
        prods.append(p)
        sums.append(h)
    enter, whole = scan_carries(prods, sums, quarters, False)
    for b in (0, 1):
        enter_o[b * SUBS : (b + 1) * SUBS] = enter[b][0]
        enter_o[(2 + b) * SUBS : (3 + b) * SUBS] = enter[b][1]
    q = quarter_of(whole[0].shape, quarters)
    carry_o[...] = jnp.where(q == 0, whole[0], whole[1])


def adjoint_kernel(steps, quarters, grad, decay, flow, local_o, after_o, enter_o, carry_o):
    prods, sums = [], []
    for b in (0, 1):
        g = r = None
        for t in range(steps - 1, -1, -1):
            at = (b * steps + t) * SUBS
            rows = slice(at, at + SUBS)
            a = grad[rows] if g is None else grad[rows] + g
            r = jnp.ones_like(a) if r is None else r * decay[at + SUBS : at + 2 * SUBS]
            local_o[rows] = a
            after_o[rows] = r
            g = decay[rows] * a
        prods.append(flow[(2 + b) * SUBS : (3 + b) * SUBS])
        sums.append(g)
    enter, whole = scan_carries(prods, sums, quarters, True)
    for b in (0, 1):
        enter_o[b * SUBS : (b + 1) * SUBS] = enter[b][0]
        enter_o[(2 + b) * SUBS : (3 + b) * SUBS] = enter[b][1]
    q = quarter_of(whole[0].shape, quarters)
    carry_o[...] = jnp.where(q == 0, whole[0], whole[1])


def backward_kernel(
    steps, quarters, local, after, states, came, entered, conv_r, recur_r, inject_r, decay_r, xb, chan, gate,
    dx_o, spill_o, gate_o, small_o,
):
    rows = 2 * steps * SUBS
    width = xb.shape[1]
    edge = CONV - 1
    block = steps * SUBS

    def by_step(v):
        return [v[b * block : (b + 1) * block].reshape(steps, SUBS, width) for b in (0, 1)]

    adjoint = jnp.concatenate(
        [
            (l + a * came[b * SUBS : (b + 1) * SUBS][None]).reshape(block, width)
            for b, (l, a) in enumerate(zip(by_step(local[...]), by_step(after[...])))
        ],
        axis=0,
    )
    earlier = jnp.concatenate(
        [
            jnp.concatenate([entered[b * SUBS : (b + 1) * SUBS], states[b * block : (b + 1) * block - SUBS]], axis=0)
            for b in (0, 1)
        ],
        axis=0,
    )
    conv, recur, inject, decay = conv_r[...], recur_r[...], inject_r[...], decay_r[...]
    rate = chan[7:8]
    mult = jnp.sqrt(one_less_exp(-16.0 * recur * rate))
    d_decay = adjoint * earlier
    d_log = d_decay * decay - adjoint * inject * conv * (decay * decay / mult)
    d_inject = adjoint * mult * conv
    d_conv = adjoint * mult * inject
    d_rate = jnp.sum(d_log * (-8.0 * recur), axis=0, keepdims=True)
    d_recur = d_log * (-8.0 * rate) * recur * (1.0 - recur)
    d_inject = d_inject * inject * (1.0 - inject)
    low = jnp.concatenate([d_recur.astype(BF16), d_inject.astype(BF16)], axis=1)
    d_conv = d_conv + lax.dot_general(low, gate[...], (((1,), (1,)), ((), ())), preferred_element_type=F32)
    gate_o[...] = lax.dot_general(conv.astype(BF16), low, (((0,), (0,)), ((), ())), preferred_element_type=F32)
    head = xb[...].astype(F32)
    halo = [head[rows + k * SUBS : rows + (k + 1) * SUBS] for k in range(edge)]
    exts = earlier_rows(by_step(head), halo, quarters, steps)
    groups = by_step(d_conv)
    for k in range(CONV):
        taps = sum(
            jnp.sum(groups[b] * exts[b][edge - k : edge - k + steps], axis=(0, 1), keepdims=True)[0] for b in (0, 1)
        )
        small_o[k : k + 1] = taps
    small_o[4:5] = jnp.sum(d_conv, axis=0, keepdims=True)
    small_o[5:6] = jnp.sum(d_recur, axis=0, keepdims=True)
    small_o[6:7] = jnp.sum(d_inject, axis=0, keepdims=True)
    small_o[7:8] = d_rate
    q = quarter_of((SUBS, width), quarters)
    for b in (0, 1):
        beyond = []
        for j in range(edge):
            same = roll(groups[b][j], -1)
            later = roll(groups[1][j], quarters - 1) if b == 0 else jnp.zeros_like(same)
            beyond.append(jnp.where(q == quarters - 1, later, same)[None])
        ext = jnp.concatenate([groups[b], *beyond], axis=0)
        total = chan[0:1][None] * ext[:steps]
        for k in range(1, CONV):
            total = total + chan[k : k + 1][None] * ext[k : k + steps]
        dx_o[b * block : (b + 1) * block] = total.reshape(block, width)
    for j in range(1, CONV):
        total = jnp.zeros((SUBS, width), F32)
        for k in range(j, CONV):
            total = total + chan[k : k + 1] * groups[0][k - j]
        spill_o[(j - 1) * SUBS : j * SUBS] = total


def by_heads(kernel, heads, head_w, arrays, outs):
    def spec(shape, tall):
        if tall:
            return pl.BlockSpec((head_w, shape[1]), lambda h: (h, 0))
        return pl.BlockSpec((shape[0], head_w), lambda h: (0, h))

    return pl.pallas_call(
        kernel,
        grid=(heads,),
        in_specs=[spec(a.shape, tall) for a, tall in arrays],
        out_specs=[spec(s, tall) for s, tall in outs],
        out_shape=[jax.ShapeDtypeStruct(s, F32) for s, _ in outs],
        compiler_params=pltpu.CompilerParams(vmem_limit_bytes=48 * 1024 * 1024),
    )(*[a for a, _ in arrays])


MESH = pl.DeviceIdType.MESH
VMEM_LIMIT = 60 * 1024 * 1024


class Links:
    def __init__(self, sizes, sends, recvs):
        self.spans, self.seqs = sizes
        self.span, self.seq = lax.axis_index("span"), lax.axis_index("seq")
        self.sends, self.recvs = sends, recvs
        self.used = 0
        self.open = []

    def flipped(self, index, mask):
        bit = 1
        while bit <= mask:
            if mask & bit:
                index = index + (1 - 2 * (index // bit % 2)) * bit
            bit *= 2
        return index

    def flipped_index(self, index, mask):
        return self.flipped(index, mask)

    def peer(self, mask):
        low, high = mask % self.seqs, mask // self.seqs
        return (self.flipped(self.span, high), self.flipped(self.seq, low))

    def other(self, mask):
        span, seq = self.peer(mask)
        return span * self.seqs + seq

    def greet(self, masks, others=()):
        barrier = pltpu.get_barrier_semaphore()
        for device in (*[self.peer(mask) for mask in masks], *others):
            pl.semaphore_signal(barrier, inc=1, device_id=device, device_id_type=MESH)
        pl.semaphore_wait(barrier, len(masks) + len(others))

    def plan(self, source, target, mask, only=None, device=None):
        slot = self.used
        self.used += 1
        device = self.peer(mask) if device is None else device
        copy = pltpu.make_async_remote_copy(
            source, target, self.sends.at[slot], self.recvs.at[slot], device_id=device, device_id_type=MESH
        )
        self.open.append((copy, only))
        return copy

    def send(self, source, target, mask, only=None):
        copy = self.plan(source, target, mask, only)
        if only is None:
            copy.start()
        else:
            pl.when(only)(copy.start)
        return copy

    def sent(self, copy):
        copy.wait_send()
        self.open = [(c, only) for c, only in self.open if c is not copy]

    def close(self):
        for copy, only in self.open:
            if only is None:
                copy.wait_send()
            else:
                pl.when(only)(copy.wait_send)


def in_turn(parts, order):
    for name in order:
        next(parts[name], None)
    for part in parts.values():
        for _ in part:
            pass


def scatter_kernel(
    sizes, share, turned, mixed, grad_x, grad_y, branch, gates, small, gain, x_own, gain_one, keep, part_own, part_other,
    proj_o, out_o, gate_o, input_o, sum_o, sends, recvs, from_part, vector, *bufs,
):
    links = Links(sizes, sends, recvs)
    spans, seqs = sizes
    count = spans * seqs
    me = links.span * seqs + links.seq
    side = me % 2
    upper = me // (count // 2)
    inner = [2 * k for k in range(1, seqs // 2)]
    core, top = seqs, count // 2
    double = 2 * share
    n = len(inner) + 1
    links.greet([1, *inner, core, top])
    whole = links.send(part_other, from_part, 1)

    def part(block, scratch, finish, shared=None):
        to_core, from_core, to_top, from_top, to_inner, from_inner, to_side, from_side = scratch
        if shared is not None:
            for copy in shared:
                links.sent(copy)
        crossing = [] if shared is None else shared
        crossing.clear()
        for i in range(2):
            for j in range(n):
                to_core[i * n + j] = block(1, (1 - i) * n + j).astype(BF16)
            crossing.append(links.send(to_core.at[pl.ds(i * n, n)], from_core.at[pl.ds(i * n, n)], core))
        mine = list(crossing)
        yield
        mine[0].wait_recv()
        over_top = {}
        for j in (*range(1, n), 0):
            to_top[j] = (block(0, n + j) + from_core[j].astype(F32)).astype(BF16)
            over_top[j] = links.send(to_top.at[j], from_top.at[j], top)
        mine[1].wait_recv()
        yield
        over_inner = []
        for j in range(1, n):
            over_top[j].wait_recv()
            to_inner[j - 1] = (block(0, j) + from_core[n + j].astype(F32) + from_top[j].astype(F32)).astype(BF16)
            over_inner.append(links.send(to_inner.at[j - 1], from_inner.at[j - 1], inner[j - 1]))
        over_top[0].wait_recv()
        yield
        total = block(0, 0) + from_core[n].astype(F32) + from_top[0].astype(F32)
        for j in range(1, n):
            over_inner[j - 1].wait_recv()
            total = total + from_inner[j - 1].astype(F32)
        yield from finish(total, to_side, from_side)

    def sided(total):
        low, high = total[:share], total[share:]
        first = side == 0
        return jnp.where(first, low, high), jnp.where(first, high, low)

    def by_columns(first, cols):
        def finish(total, to_side, from_side):
            mine, theirs = sided(total)
            to_side[...] = theirs.astype(BF16)
            copy = links.send(to_side, from_side, 1)
            yield
            copy.wait_recv()
            recv = from_side[...].astype(F32)
            proj_o[:, first : first + cols] = jnp.where(side == 0, mine, recv)
            proj_o[:, first + cols : first + 2 * cols] = jnp.where(side == 0, recv, mine)

        return finish

    def by_rows(target, to_last, from_last):
        cols = target.shape[1] // 2

        def finish(total, to_side, from_side):
            to_side[...] = total.astype(BF16)
            copy = links.send(to_side, from_side, top)
            yield
            copy.wait_recv()
            other = from_side[...].astype(F32)
            first = side == 0
            (low, low_far), (high, high_far) = sided(jnp.where(first, total, other)), sided(jnp.where(first, other, total))
            to_last[:, :cols] = low_far.astype(BF16)
            to_last[:, cols:] = high_far.astype(BF16)
            copy = links.send(to_last, from_last, 1)
            yield
            copy.wait_recv()
            holds = side == upper
            target[:, :cols] = jnp.where(holds, low, from_last[:, :cols].astype(F32))
            target[:, cols:] = jnp.where(holds, high, from_last[:, cols:].astype(F32))

        return finish

    def rows_of(c, j, whole):
        pairs = count // 2 if whole else count // 4
        owner = links.other(c * core + (j // n * top if whole else 0) + (0, *inner)[j % n])
        return pl.ds(pl.multiple_of(owner // 2 % pairs * double, 16), double)

    def columns_of(j, columns):
        return pl.ds(pl.multiple_of((upper if j < n else 1 - upper) * columns, 128), columns)

    def product(lhs, rhs):
        return lambda c, j: jnp.dot(lhs[rows_of(c, j, True)], rhs[...], preferred_element_type=F32)

    def product_half(lhs, rhs, columns):
        return lambda c, j: jnp.dot(lhs[rows_of(c, j, False)], rhs[:, columns_of(j, columns)], preferred_element_type=F32)

    def stored(blocks, columns):
        return lambda c, j: blocks[rows_of(c, j, False), columns_of(j, columns)]

    def sums():
        whole.wait_recv()
        few = 16
        own, width = x_own.shape
        vector[0] = jnp.zeros(vector.shape[1:], F32)
        vector[0, 1:2, :width] = gain[...]
        vector[0, :, width:] = small[...]

        @pl.loop(0, own // few)
        def _(k):
            here = pl.ds(pl.multiple_of(k * few, few), few)
            v = x_own[here].astype(F32)
            scale = lax.rsqrt(jnp.mean(v * v, axis=-1, keepdims=True) + EPS)
            z = v * scale
            d = part_own[here] + from_part[here].astype(F32)
            e = d * gain_one[...]
            input_o[here] = keep[here] + scale * (e - z * jnp.mean(e * z, axis=-1, keepdims=True))
            vector[0, 0:1, :width] += jnp.sum(d * z, axis=0, keepdims=True)

        slot = 1
        for masks in ([core], [top], inner):
            copies = [links.send(vector.at[0], vector.at[slot + k], m) for k, m in enumerate(masks)]
            yield
            for copy in copies:
                copy.wait_recv()
                links.sent(copy)
            total = vector[0]
            for k in range(len(masks)):
                total = total + vector[slot + k]
            vector[0] = total
            slot += len(masks)
        copy = links.send(vector.at[0], vector.at[slot], 1)
        yield
        copy.wait_recv()
        sum_o[:, :width] = vector[0, :, :width] + vector[slot, :, :width]
        sum_o[:, width:] = jnp.where(side == upper, vector[0, :, width:], vector[slot, :, width:])

    half = grad_x.shape[1]
    wide = branch.shape[1] // 2
    thin = gates.shape[1] // 2
    shared = []
    first = bufs[0]
    parts = {
        "y": part(product(turned, grad_y), [first, *bufs[1:8]], by_columns(2 * half, half), shared),
        "o": part(product_half(mixed, branch, wide), [first, *bufs[8:15]], by_rows(out_o, *bufs[15:17]), shared),
        "x": part(product(turned, grad_x), [first, *bufs[17:24]], by_columns(0, half), shared),
        "g": part(stored(gates, thin), bufs[24:32], by_rows(gate_o, *bufs[32:34])),
        "n": sums(),
    }
    in_turn(parts, "yoyxoyxgnoyxgnoygnoxoygnoxgnngg")
    links.close()


def scatter_grads(sizes, share, turned, mixed, grad_x, grad_y, branch, gates, small, gain, x_own, gain_one, keep, part_own, part_other):
    n = sizes[1] // 2
    half, wide, thin = grad_x.shape[1], branch.shape[1], gates.shape[1]
    own, width = x_own.shape
    double = 2 * share

    def scratch(cols, last, core=True):
        side = share if last is None else double
        shapes = [(2 * n, double, cols)] * (2 if core else 1) + [(n, double, cols)] * 2 + [(n - 1, double, cols)] * 2 + [(side, cols)] * 2
        if last is not None:
            shapes += [(share, last)] * 2
        return [pltpu.VMEM(s, BF16) for s in shapes]

    bufs = [*scratch(half, None), *scratch(wide // 2, wide, False), *scratch(half, None, False), *scratch(thin // 2, thin)]
    copies = 4 * (2 + n + (n - 1) + 2) + n + 4
    inside = pl.BlockSpec(memory_space=pltpu.VMEM)
    shapes = [(share, 4 * half), (share, wide), (share, thin), (own, width), (SUBS, width + half)]
    return pl.pallas_call(
        functools.partial(scatter_kernel, sizes, share),
        in_specs=[inside] * 13,
        out_specs=[inside] * 5,
        out_shape=[jax.ShapeDtypeStruct(s, F32) for s in shapes],
        scratch_shapes=[
            pltpu.SemaphoreType.DMA((copies,)), pltpu.SemaphoreType.DMA((copies,)), pltpu.VMEM((own, width), BF16),
            pltpu.VMEM((n + 3, SUBS, width + half), F32), *bufs,
        ],
        compiler_params=pltpu.CompilerParams(collective_id=1, has_side_effects=True, vmem_limit_bytes=VMEM_LIMIT),
    )(turned, mixed, grad_x, grad_y, branch, gates, small, gain, x_own, gain_one, keep, part_own, part_other)


def gelu_parts(v):
    root = 0.7978845608028654
    t = jnp.tanh(root * (v + 0.044715 * (v * v * v)))
    slope = 0.5 * (1.0 + t) + 0.5 * v * (1.0 - t * t) * root * (1.0 + 3.0 * 0.044715 * (v * v))
    return 0.5 * v * (1.0 + t), slope


def feed_kernel(sizes, masks, own, *refs):
    chunks = len(masks)
    spans = sizes[0]
    own_rows, refs = refs[0], refs[1:]
    cots, refs = refs[0], refs[1:]
    wides, refs = refs[:spans], refs[spans:]
    narrows, refs = refs[:2], refs[2:]
    grad_o, near_o, far_o, act_o, hidden_o, refs = *refs[:5], refs[5:]
    (rows_o, cots_o, wide_away, narrow_away, wide_recv, narrow_recv), refs = refs[:6], refs[6:]
    (rows, cot, wide, narrow, act, hidden, near, down_near, down_far, to_side, from_side, to_inner, from_inner,
     sends, recvs, loads, stores) = refs
    units = narrow.shape[0]
    width = narrow.shape[1]
    size = width // spans
    pair = 2 * own
    links = Links(sizes, sends, recvs)

    def load(source, target, slot):
        copy = pltpu.make_async_copy(source, target, loads.at[slot])
        copy.start()
        return copy

    first = load(own_rows, rows.at[pl.ds(0, own)], 0)
    late = [
        load(cots.at[links.flipped(links.seq // 2, masks[b // 2] // 2), b % 2], cot.at[pl.ds(b * own, own)], 1 + b)
        for b in range(2 * chunks)
    ]
    for j in range(spans):
        columns = pl.ds(j * size, size)
        late.append(load(wides[j], wide.at[:, columns], 1 + 2 * chunks + j))
        if j < 2:
            late.append(load(narrows[j], narrow.at[:, columns], 1 + 2 * chunks + spans + j))
    core, tops = sizes[1], range(2, spans, 2)
    links.greet([1, *masks[1:], core, *[m * core for m in tops]])
    first.wait()
    across = [links.send(narrows[0], narrow.at[:, pl.ds(m * size, size)], m * core) for m in tops]

    def block(b):
        return rows.at[pl.ds(b * own, own)]

    each = range(chunks)
    over_side = [links.plan(block(2 * i), block(2 * i + 1), 1) for i in each]
    over_inner = [None] + [links.plan(block(0), block(2 * i), masks[i]) for i in each[1:]]
    back_side = [links.plan(to_side.at[i], from_side.at[i], 1) for i in each]
    back_inner = [links.plan(to_inner.at[i - 1], from_inner.at[i - 1], masks[i]) for i in each[1:]]
    over_side[0].start()
    for i in each[1:]:
        over_inner[i].start()
    for copy in late:
        copy.wait()
    beside = [links.plan(narrow.at[:, pl.ds(m * size, size)], narrow.at[:, pl.ds((m + 1) * size, size)], core) for m in tops]

    def narrow_here():
        for copy, onto in zip(across, beside):
            copy.wait_recv()
            onto.start()
        for copy in beside:
            copy.wait_recv()

    def onward(i):
        over_inner[i].wait_recv()
        over_side[i].start()

    def give_on(i):
        back_side[i].wait_recv()
        to_inner[i - 1] = (near[i].astype(F32) + from_side[i].astype(F32)).astype(BF16)
        back_inner[i - 1].start()

    last = chunks - 1

    def ahead(i):
        over_side[i].wait_recv()
        if i == 0:
            for k in (2, 1):
                if k < last:
                    onward(k)
            narrow_here()

    def midway(i):
        if i == min(1, last - 1):
            for k in range(3, chunks):
                onward(k)
        if i == last:
            give_on(1)

    def behind(i):
        if 0 < i < last - 1:
            back_side[i].start()
        if i == last:
            for k in (last, last - 1, 0):
                back_side[k].start()

    def compute(i):
        here = pl.ds(pl.multiple_of(i * pair, 16), pair)
        mine = rows[here]
        given = cot[here]
        start = 0
        while start < units:
            n = min(384, units - start)
            gate = lax.dot_general(mine, wide[start : start + n], (((1,), (1,)), ((), ())), preferred_element_type=F32)
            up = lax.dot_general(
                mine, wide[units + start : units + start + n], (((1,), (1,)), ((), ())), preferred_element_type=F32
            )
            back = lax.dot_general(given, narrow[start : start + n], (((1,), (1,)), ((), ())), preferred_element_type=F32)
            value, slope = gelu_parts(gate)
            hidden[here, start : start + n] = (value * up).astype(BF16)
            act[here, start : start + n] = (back * up * slope).astype(BF16)
            act[here, units + start : units + start + n] = (back * value).astype(BF16)
            start += n
        for k in range(chunks):
            pl.when(i == k)(functools.partial(midway, k))
        step = 512

        @pl.loop(0, width // step)
        def _(k):
            columns = pl.ds(pl.multiple_of(k * step, 128), step)
            total = jnp.dot(act[here], wide[:, columns], preferred_element_type=F32)
            near[i, :, columns] = total[:own].astype(BF16)
            to_side[i, :, columns] = total[own:].astype(BF16)
            total = jnp.dot(hidden[here], narrow[:, columns], preferred_element_type=F32)
            down_near[i, :, columns] = total[:own].astype(BF16)
            down_far[i, :, columns] = total[own:].astype(BF16)

    @pl.loop(0, chunks)
    def _(i):
        for k in range(chunks):
            pl.when(i == k)(functools.partial(ahead, k))
        compute(i)
        for k in range(chunks):
            pl.when(i == k)(functools.partial(behind, k))

    out = []

    def store(source, target):
        out.append(pltpu.make_async_copy(source, target, stores.at[len(out)]))
        out[-1].start()
        return out[-1]

    own_columns, away_columns = pl.ds(0, size), pl.ds(2 * size, size)
    for source, target in (
        (act, act_o), (hidden, hidden_o), (down_near, near_o), (down_far, far_o), (rows.at[:, own_columns], rows_o),
        (cot.at[:, own_columns], cots_o),
    ):
        store(source, target)
    for copy in beside:
        links.sent(copy)

    def gradient(left, right, start, count, j):
        return lax.dot_general(
            left[:, pl.ds(start, count)], right[:, j * size : (j + 1) * size], (((0,), (0,)), ((), ())), preferred_element_type=F32
        )

    def by_tiles(total, body):
        whole = total // 384

        @pl.loop(0, whole)
        def _(k):
            body(pl.multiple_of(k * 384, 128), 384)

        if total % 384:
            body(whole * 384, total % 384)

    def give_core(left, right, held, landed):
        def tile(start, count):
            for k, j in enumerate(range(1, spans, 2)):
                held[pl.ds(start, count), k * size : (k + 1) * size] = gradient(left, right, start, count, j).astype(BF16)

        by_tiles(left.shape[1], tile)
        return links.send(held.at[:, pl.ds(0, 2 * size)], landed, core)

    def give_top(left, right, held, landed, came, target):
        came.wait_recv()
        store(landed.at[:, pl.ds(size, size)], held.at[:, away_columns]).wait()
        out.pop()

        def tile(start, count):
            here = pl.ds(start, count)
            total = gradient(left, right, start, count, 2) + held[here, 2 * size : 3 * size].astype(F32)
            held[here, 3 * size : 4 * size] = total.astype(BF16)

        by_tiles(left.shape[1], tile)
        store(held.at[:, pl.ds(3 * size, size)], target)

    crossing = give_core(act, rows, wide, wide_recv)
    give_on(last)
    crossing_narrow = give_core(hidden, cot, narrow, narrow_recv)
    for k in range(last - 1, 1, -1):
        give_on(k)
    give_top(act, rows, wide, wide_recv, crossing, wide_away)
    give_top(hidden, cot, narrow, narrow_recv, crossing_narrow, narrow_away)
    back_side[0].wait_recv()
    for k in range(chunks - 1):
        back_inner[k].wait_recv()
    for j in range(spans):
        columns = slice(j * size, (j + 1) * size)
        total = near[0, :, columns].astype(F32) + from_side[0, :, columns].astype(F32)
        for k in range(chunks - 1):
            total = total + from_inner[k, :, columns].astype(F32)
        grad_o[:, pl.ds(pl.multiple_of(links.flipped(links.span, j) * size, 128), size)] = total
    for copy in out:
        copy.wait()
    links.close()


def feed_forward(sizes, masks, own_rows, cots, wides, narrows):
    own, width = own_rows.shape
    units = narrows[0].shape[0]
    chunks = len(masks)
    total = 2 * chunks * own
    anywhere = pl.BlockSpec(memory_space=pl.ANY)
    copies = 4 * chunks + sizes[0] + 2
    blocks = (chunks, own, width)
    spans = sizes[0]
    size = width // spans
    shapes = [
        blocks, blocks, (total, 2 * units), (total, units), (total, size), (total, size), (2 * units, size), (units, size),
        (2 * units, 2 * size), (units, 2 * size),
    ]
    held = [
        (total, width), (total, width), (2 * units, width), (units, width), (total, 2 * units), (total, units), blocks, blocks,
        blocks, blocks, blocks, (chunks - 1, own, width), (chunks - 1, own, width),
    ]
    return pl.pallas_call(
        functools.partial(feed_kernel, sizes, masks, own),
        in_specs=[anywhere] * (4 + len(wides)),
        out_specs=[pl.BlockSpec(memory_space=pltpu.VMEM)] + [anywhere] * len(shapes),
        out_shape=[jax.ShapeDtypeStruct((own, width), F32)] + [jax.ShapeDtypeStruct(s, BF16) for s in shapes],
        scratch_shapes=[pltpu.VMEM(s, BF16) for s in held]
        + [pltpu.SemaphoreType.DMA((k,)) for k in (copies, copies, 3 + 2 * chunks + len(wides), 8)],
        compiler_params=pltpu.CompilerParams(collective_id=2, has_side_effects=True, vmem_limit_bytes=VMEM_LIMIT),
    )(own_rows, cots, *wides, *narrows)


def expanded(v, quarters):
    return spread(v, quarters, 0), spread(roll(v, -1), quarters, 0)


def chunk_inflow(links, line, blocks, quarters, backward, between):
    n, spans = line.shape[0], blocks.shape[0]
    place = links.seq // 2
    copies = [links.send(line.at[0], line.at[k], 2 * k) for k in range(1, n)]
    for copy in copies:
        copy.wait_recv()
    between()
    one, nought = jnp.ones(line.shape[1:], F32), jnp.zeros(line.shape[1:], F32)
    prod, total = one, nought
    all_prod, all_total = one, nought

    def ordered(count):
        return range(count - 1, -1, -1) if backward else range(count)

    def ahead(j, at):
        return at < j if backward else at > j

    for j in ordered(n):
        p, s = expanded(line[links.flipped(place, j)], quarters)
        inside = ahead(j, place)
        total = jnp.where(inside, p * total + s, total)
        prod = jnp.where(inside, p * prod, prod)
        all_total = p * all_total + s
        all_prod = p * all_prod
    q = quarter_of(line.shape[1:], quarters)
    blocks[0] = jnp.where(q == 0, all_prod, all_total)
    copies = [links.send(blocks.at[0], blocks.at[m], m * links.seqs) for m in range(1, spans)]
    for copy in copies:
        copy.wait_recv()
    h = nought
    for j in ordered(spans):
        p, s = expanded(blocks[links.flipped(links.span, j)], quarters)
        h = jnp.where(ahead(j, links.span), p * h + s, h)
    return prod * h + total


def by_head(heads, head_w, body):
    @pl.loop(0, heads)
    def _(h):
        start = pl.multiple_of(h * head_w, 128)
        columns = pl.ds(start, head_w)
        body(lambda ref: ref.at[:, columns], lambda ref: ref.at[pl.ds(start, head_w)])


def front_kernel(
    sizes, steps, quarters, heads, head_w, share, x_own, halo, params_in, rec_proj, out_proj, gate_weight, cot, wide, narrow, *refs
):
    spans, seqs = sizes
    count = spans * seqs
    inner = [2 * k for k in range(1, seqs // 2)]
    n = len(inner) + 1
    core, top = seqs, count // 2
    (normal, xb, y_pre, conv, recur, inject, decay, states, flow, mixed, resid, normal_two, params, chan, turned, mixed_turned), refs = (
        refs[:16], refs[16:]
    )
    (proj_x, proj_y, out_half, gates), refs = refs[:4], refs[4:]
    wides, beside_narrow, cots, refs = refs[: spans - 1], refs[spans - 1], refs[spans], refs[spans + 1 :]
    (lead, held_x, held_y, held_o, held_g, every, prod, enter, line, blocks, inflow, to_side, from_side, low,
     sends, recvs, locals_) = refs
    links = Links(sizes, sends, recvs)
    me = links.span * seqs + links.seq
    side, upper = me % 2, me // (count // 2)
    own, width = x_own.shape
    rows = 2 * own
    half = width // 2
    double = 2 * share
    links.greet([1, *inner, *[m * seqs for m in range(1, spans)]])
    kept = [0]

    def local(source, target, only=None):
        copy = pltpu.make_async_copy(source, target, locals_.at[kept[0]])
        kept[0] += 1
        if only is None:
            copy.start()
        else:
            pl.when(only)(copy.start)
        return copy

    z = links.seq // 2
    offsets = [o for s in range(1, n) for o in (-s, s)]
    there = {o: jnp.logical_and(z + o >= 0, z + o < n) for o in offsets}
    beyond = {-1: (links.span, jnp.maximum(links.seq - 2, 0)), 1: (links.span, jnp.minimum(links.seq + 2, seqs - 1))}

    def along(piece):
        passing = {}
        for o in (0, *offsets):
            for way in (-1, 1):
                if o * way <= 0 and abs(o) + 1 < n:
                    both = jnp.logical_and(there[way], there[o]) if o else there[way]
                    passing[o, way] = links.plan(piece(o), piece(o), None, both, beyond[way])
        return passing

    def arrival(passing, o):
        way = 1 if o < 0 else -1
        return passing[o + way, way]

    def begin(passing):
        for way in (-1, 1):
            pl.when(there[way])(passing[0, way].start)

    def take(passing, o):
        arrival(passing, o).wait_recv()
        way = 1 if o < 0 else -1
        if (o, way) in passing:
            pl.when(there[way])(passing[o, way].start)

    def pieces_out(own_out, piece, part, far):
        passing = along(piece)
        over_top = {o: links.plan(piece(o), piece(o), top, there[o]) for o in offsets}
        over_core = {o: links.plan(part(o), part(o), core, there[o]) for o in offsets}
        far_core = {o: links.plan(far(o), far(o), core, there[o]) for o in offsets}
        begin(passing)
        first_core = links.send(own_out, own_out, core)
        first_top = first_far = None
        if far(0) is not None:
            first_top = links.send(piece(0), piece(0), top)
        yield
        for o in offsets:

            @pl.when(there[o])
            def _():
                take(passing, o)
                over_top[o].start()
                over_core[o].start()

            if o == offsets[len(offsets) // 2 - 1]:
                yield
        yield
        if first_top is not None:
            first_top.wait_recv()
            first_far = links.send(far(0), far(0), core)
        for o in offsets:

            @pl.when(there[o])
            def _():
                over_top[o].wait_recv()
                far_core[o].start()

        yield
        first_core.wait_recv()
        if first_far is not None:
            first_far.wait_recv()
        for o in offsets:

            @pl.when(there[o])
            def _():
                over_core[o].wait_recv()
                far_core[o].wait_recv()

    def pieces_direct(whole, piece):
        over_inner = {m: links.send(piece(0), piece(0), m) for m in inner}
        over_core = [links.send(whole, whole, core)]
        over_top = {}
        yield
        for m in inner:
            over_inner[m].wait_recv()
            here = piece(links.flipped(z, m // 2) - z)
            over_top[m] = links.send(here, here, top)
            over_core.append(links.send(here, here, core))
        yield
        for m in inner:
            over_top[m].wait_recv()
            here = piece(links.flipped(z, m // 2) - z, 1 - upper)
            over_core.append(links.send(here, here, core))
        yield
        for copy in over_core:
            copy.wait_recv()

    def columns_part(source, first, target):
        def piece(o, over=0):
            device = (links.other(over) if over else me) + 2 * o
            start = jnp.clip(device // 2 * double, 0, target.shape[0] - double)
            return target.at[pl.ds(pl.multiple_of(start, 16), double)]

        def columns(which):
            return source.at[:, pl.ds(pl.multiple_of(first + which * half, 128), half)]

        row = target.at[pl.ds(pl.multiple_of(me * share, 16), share)]
        mine = local(columns(side), row)
        theirs = links.send(columns(1 - side), row, 1)
        yield
        mine.wait()
        theirs.wait_recv()
        yield from pieces_out(piece(0), piece, piece, lambda o: piece(o, top))

    def rows_part(source, target, direct):
        cols = source.shape[1]
        pairs_half = count // 4

        def rows_at(start, size):
            return target.at[pl.ds(pl.multiple_of(start, 16), size)]

        begin_at = me // 2 % pairs_half * double

        def piece(o, which=None):
            start = jnp.clip(begin_at + o * double, 0, target.shape[0] - double)
            which = upper if which is None else which
            return target.at[pl.ds(pl.multiple_of(start, 16), double), pl.ds(pl.multiple_of(which * (cols // 2), 128), cols // 2)]

        holds = side == upper
        row = rows_at(begin_at + side * share, share)
        mine = local(source, row, holds)
        gift = links.send(source, row, 1, side != upper)
        yield

        @pl.when(holds)
        def _():
            mine.wait()
            gift.wait_recv()

        whole = rows_at(begin_at, double)
        across = links.send(whole, whole, top, holds)
        yield
        pl.when(side != upper)(across.wait_recv)
        if direct:
            yield from pieces_direct(whole, piece)
        else:
            yield from pieces_out(whole, piece, piece, lambda o: piece(o, 1 - upper) if o else None)

    def small_part():
        height = params_in.shape[0]

        def rows_of(device):
            return every.at[pl.ds(pl.multiple_of(device // 2 * 2 * height, 16), 2 * height)]

        row = pl.ds(pl.multiple_of(me * height, 16), height)
        every[row] = params_in[...]
        theirs = links.send(every.at[row], every.at[row], 1)
        yield
        theirs.wait_recv()
        held = [me]
        for masks in (inner, [top], [core]):
            copies = [links.send(rows_of(d), rows_of(d), m) for d in held for m in masks]
            held = held + [links.flipped_index(d, m) for d in held for m in masks]
            yield
            for copy in copies:
                copy.wait_recv()
        params[...] = jnp.zeros_like(params)
        lanes = params_in.shape[1]
        for d in range(count):
            tile = every[d * height : (d + 1) * height]
            base, shift = d * share // lanes * lanes, d * share % lanes
            if shift + share <= lanes:
                params[:, base : base + lanes] += pltpu.roll(tile, shift, 1) if shift else tile
            else:
                turned = pltpu.roll(jnp.concatenate([tile, jnp.zeros_like(tile)], axis=1), shift, 1)
                params[:, base : base + 2 * lanes] += turned
        chan[...] = params[:SUBS, pl.ds(pl.multiple_of(side * half, 128), half)]

    parts = {
        "x": columns_part(rec_proj, 0, proj_x),
        "v": small_part(),
        "g": rows_part(gate_weight, gates, False),
        "y": columns_part(rec_proj, 2 * half, proj_y),
        "o": rows_part(out_proj, out_half, True),
    }

    def advance(order):
        for name in order:
            next(parts[name], None)

    place = pl.ds(pl.multiple_of(side * own, 16), own)
    def cot_at(o, far=0):
        return cots.at[jnp.clip(z + o, 0, n - 1), far]

    cot_inner = [links.plan(cot_at(0), cot_at(0), m) for m in inner]
    cot_side = []
    own_cot = local(cot, cot_at(0))
    advance("xvgoy")
    tokens = links.send(x_own, lead.at[place], 1)
    lead[place] = x_own[...]
    lead[rows:] = halo[...]
    advance("xvgo")
    own_cot.wait()
    own_side = links.send(cot_at(0), cot_at(0, 1), 1)
    advance("xvxgyov")
    advance("ggxgvyyxg")
    loads = [local(proj_x, held_x), local(gates, held_g)]
    tokens.wait_recv()
    few = 16

    @pl.loop(0, lead.shape[0] // few)
    def _(k):
        here = pl.ds(pl.multiple_of(k * few, few), few)
        normal[here] = normed(lead[here].astype(F32), params[SUBS : SUBS + 1]).astype(BF16)

    for copy in loads:
        copy.wait()

    def gate(cols, tall):
        cols(xb)[...] = jnp.dot(normal[...], cols(held_x)[...], preferred_element_type=F32).astype(BF16)
        forward_kernel(
            steps, quarters, cols(xb), cols(chan), tall(held_g), cols(conv), cols(recur), cols(inject), cols(decay),
            cols(states), cols(prod), cols(enter), cols(line.at[0]),
        )

    by_head(heads, head_w, gate)
    inflow[...] = chunk_inflow(links, line, blocks, quarters, False, lambda: [copy.start() for copy in cot_inner])
    advance("o")
    tops = [2 * seqs * k for k in range(1, spans // 2)]
    across = {m: links.send(wide, wides[m // seqs - 1], m) for m in tops}
    beside = [links.send(wide, wides[0], core), links.send(narrow, beside_narrow, core)]
    def onward(k):
        cot_inner[k].wait_recv()
        here = links.flipped(z, inner[k] // 2) - z
        cot_side.append(links.send(cot_at(here), cot_at(here, 1), 1))

    advance("yy")
    loads = [local(proj_y, held_y)]
    loads[0].wait()
    block = steps * SUBS

    def mix(cols, tall):
        cols(y_pre)[...] = jnp.dot(normal[:rows], cols(held_y)[...], preferred_element_type=F32)
        ins, flows, hold, gain_y = cols(inflow), cols(flow), cols(states), cols(y_pre)
        for b in (0, 1):
            entered = cols(enter)[b * SUBS : (b + 1) * SUBS] * ins[...] + cols(enter)[(2 + b) * SUBS : (3 + b) * SUBS]
            flows[b * SUBS : (b + 1) * SUBS] = entered
            flows[(2 + b) * SUBS : (3 + b) * SUBS] = cols(prod)[(b + 1) * block - SUBS : (b + 1) * block]
            here = slice(b * block, (b + 1) * block)
            total = hold[here].reshape(steps, SUBS, head_w) + cols(prod)[here].reshape(steps, SUBS, head_w) * entered[None]
            total = total.reshape(block, head_w)
            hold[here] = total
            low_part = total * gelu_parts(gain_y[here])[0]
            cols(mixed)[here] = low_part.astype(BF16)
            tall(mixed_turned)[:, here] = low_part.T.astype(BF16)

    by_head(heads, head_w, mix)

    onward(0)
    advance("oo")
    load = local(out_half, held_o)
    load.wait()
    step = 512

    @pl.loop(0, width // step)
    def _(k):
        columns = pl.ds(pl.multiple_of(k * step, 128), step)
        total = jnp.dot(mixed[...], held_o[:, columns], preferred_element_type=F32)
        first = side == 0
        resid[:, columns] = x_own[:, columns].astype(F32) + jnp.where(first, total[:own], total[own:])
        to_side[:, columns] = jnp.where(first, total[own:], total[:own]).astype(BF16)

    partial = links.send(to_side, from_side, 1)
    for k in range(1, n - 2):
        onward(k)

    @pl.loop(0, width // head_w)
    def _(k):
        columns = pl.ds(pl.multiple_of(k * head_w, 128), head_w)
        turned[columns] = normal[:rows, columns].astype(F32).T.astype(BF16)

    partial.wait_recv()
    size = width // spans

    @pl.loop(0, own // few)
    def _(k):
        here = pl.ds(pl.multiple_of(k * few, few), few)
        total = resid[here] + from_side[here].astype(F32)
        resid[here] = total
        low[here] = normed(total, params[SUBS + 1 : SUBS + 2]).astype(BF16)

    for j in range(spans):
        start = pl.multiple_of(links.flipped(links.span, j) * size, 128)
        normal_two[:, j * size : (j + 1) * size] = low[:, pl.ds(start, size)]

    onward(n - 2)
    for m in tops:
        across[m].wait_recv()
        beside.append(links.send(wides[m // seqs - 1], wides[m // seqs], core))
    for copy in (*beside, own_side, *cot_side):
        copy.wait_recv()
    for part in parts.values():
        for _ in part:
            pass
    links.close()


def front(sizes, steps, quarters, heads, head_w, x_own, halo, params, rec_proj, out_proj, gate_weight, cot, wide, narrow):
    spans, seqs = sizes
    count = spans * seqs
    own, width = x_own.shape
    half, rows, share = width // 2, 2 * own, rec_proj.shape[0]
    n = seqs // 2
    inside, anywhere = pl.BlockSpec(memory_space=pltpu.VMEM), pl.BlockSpec(memory_space=pl.ANY)

    def high(*shape):
        return jax.ShapeDtypeStruct(shape, F32)

    def low(*shape):
        return jax.ShapeDtypeStruct(shape, BF16)

    lead = rows + halo.shape[0]
    near = [
        low(lead, width), low(lead, half), *[high(rows, half)] * 6, high(4 * SUBS, half), low(rows, half), high(own, width),
        low(own, width), high(params.shape[0], width), high(SUBS, half),
        low(width, rows), low(half, rows),
    ]
    far = [
        low(width, half), low(width, half), low(half, width), low(half, gate_weight.shape[1]), *[low(*wide.shape)] * (spans - 1),
        low(*narrow.shape), low(n, 2, *cot.shape),
    ]
    end = (SUBS, half)
    copies = 4 * (3 + 10 * n) + 4 * n + 3 + 6 * n + (n - 1) + 2 * spans + 4
    outs = pl.pallas_call(
        functools.partial(front_kernel, sizes, steps, quarters, heads, head_w, share),
        in_specs=[inside] * 7 + [anywhere] * 2,
        out_specs=[inside] * len(near) + [anywhere] * len(far),
        out_shape=[*near, *far],
        scratch_shapes=[
            pltpu.VMEM((lead, width), BF16), pltpu.VMEM((width, half), BF16), pltpu.VMEM((width, half), BF16),
            pltpu.VMEM((half, width), BF16), pltpu.VMEM((half, gate_weight.shape[1]), BF16), pltpu.VMEM((count * params.shape[0], params.shape[1]), F32),
            pltpu.VMEM((rows, half), F32), pltpu.VMEM((4 * SUBS, half), F32), pltpu.VMEM((n, *end), F32),
            pltpu.VMEM((spans, *end), F32), pltpu.VMEM(end, F32), *[pltpu.VMEM((own, width), BF16)] * 3,
            pltpu.SemaphoreType.DMA((copies,)), pltpu.SemaphoreType.DMA((copies,)), pltpu.SemaphoreType.DMA((16,)),
        ],
        compiler_params=pltpu.CompilerParams(collective_id=0, has_side_effects=True, vmem_limit_bytes=VMEM_LIMIT),
    )(x_own, halo, params, rec_proj, out_proj, gate_weight, cot, wide, narrow)
    wides, narrows, cots = outs[20 : 19 + spans], outs[19 + spans], outs[20 + spans]
    return outs[:16], outs[16:20], [wide, *wides], [narrow, narrows], cots


def return_kernel(
    sizes, steps, quarters, heads, inner, branch, out_w, y_pre, states, decay, flow, conv, recur, inject, xb, chan, gate,
    resid, near, far, wide, narrow, proj_y, proj_x, branch_o, y_grad, x_grad, gate_o, small, output, part_own, part_other, wides, narrows,
    part, held_y, loads, dx, spill, came_back, grad, local, after, enter, carry, line, blocks, inflow, dmix, from_side, to_inner, from_inner, sends, recvs,
):
    spans, seqs = sizes
    tops = [2 * seqs * k for k in range(1, spans // 2)]
    n = len(inner) + 1
    links = Links(sizes, sends, recvs)
    side = links.seq % 2
    own, width = branch.shape
    me, count = links.span * seqs + links.seq, spans * seqs

    def device(index):
        return (index // seqs, index % seqs)

    links.greet([1, *inner, *[m * seqs for m in range(1, spans)]], [device((me + 2) % count)])
    place = pl.ds(pl.multiple_of(side * own, 16), own)
    whole = links.send(branch, branch_o.at[place], 1)
    tall = wide.shape[1] // 2
    across = [links.send(wide.at[k, pl.ds(0, tall)], wides.at[k, pl.ds(0, tall)], m) for k, m in enumerate(tops)]
    branch_o[place] = branch[...]
    load = pltpu.make_async_copy(proj_y, held_y, loads.at[0])
    load.start()
    whole.wait_recv()
    sums = [*range(1, n), 0]
    over_side = {}

    def side_sum(i):
        over_side[sums[i]] = links.send(far.at[sums[i]], from_side.at[sums[i]], 1)

    over_inner = []

    def inner_sum(i):
        k = sums[i]
        over_side[k].wait_recv()
        if k:
            to_inner[k - 1] = (near[k].astype(F32) + from_side[k].astype(F32)).astype(BF16)
            over_inner.append(links.send(to_inner.at[k - 1], from_inner.at[k - 1], inner[k - 1]))

    side_sum(0)
    head_w = gate.shape[1] // 2

    def first(cols, tall):
        mixed_grad = lax.dot_general(branch_o[...], tall(out_w)[...], (((1,), (1,)), ((), ())), preferred_element_type=F32)
        value, slope = gelu_parts(cols(y_pre)[...])
        cols(grad)[...] = mixed_grad * value
        cols(y_grad)[...] = (mixed_grad * cols(states)[...] * slope).astype(BF16)
        adjoint_kernel(
            steps, quarters, cols(grad), cols(decay), cols(flow), cols(local), cols(after), cols(enter), cols(line.at[0])
        )

    by_head(heads, head_w, first)

    def between():
        inner_sum(0)
        side_sum(1)

    inflow[...] = chunk_inflow(links, line, blocks, quarters, True, between)
    for k, m in enumerate(tops):
        across.append(links.send(wide.at[k, pl.ds(tall, tall)], wides.at[k, pl.ds(tall, tall)], m))
        across.append(links.send(narrow.at[k], narrows.at[k], m))
    inner_sum(1)
    side_sum(2)

    def second(cols, tall):
        came = jnp.concatenate(
            [
                cols(enter)[b * SUBS : (b + 1) * SUBS] * cols(inflow)[...] + cols(enter)[(2 + b) * SUBS : (3 + b) * SUBS]
                for b in (0, 1)
            ],
            axis=0,
        )
        backward_kernel(
            steps, quarters, cols(local), cols(after), cols(states), came, cols(flow), cols(conv), cols(recur),
            cols(inject), cols(decay), cols(xb), cols(chan), tall(gate), cols(dx), cols(spill), tall(gate_o), cols(small),
        )

    by_head(heads, head_w, second)
    edge = (CONV - 1) * SUBS
    slot = links.used
    links.used += 1
    handed = pltpu.make_async_remote_copy(
        spill, came_back, links.sends.at[slot], links.recvs.at[slot], device_id=device(jnp.maximum(me - 2, 0)), device_id_type=MESH
    )
    pl.when(me >= 2)(handed.start)
    links.open.append((handed, me >= 2))
    rows = 2 * own
    x_grad[: rows - 2 * edge] = dx[: rows - 2 * edge].astype(BF16)
    load.wait()
    step = 512

    @pl.loop(0, width // step)
    def _(k):
        start = pl.multiple_of(k * step, 128)
        weights = held_y[pl.ds(start, step)]
        part[:, pl.ds(start, step)] = lax.dot_general(
            y_grad[...], weights, (((1,), (1,)), ((), ())), preferred_element_type=F32
        )

    load = pltpu.make_async_copy(proj_x, held_y, loads.at[0])
    load.start()
    for i in range(2, n):
        inner_sum(i)
        if i + 1 < n:
            side_sum(i + 1)
    pl.when(me + 2 < count)(handed.wait_recv)

    @pl.when(me + 2 >= count)
    def _():
        came_back[...] = jnp.zeros_like(came_back)

    last = quarter_of((SUBS, came_back.shape[1]), quarters) == quarters - 1
    total = [dx[rows - 2 * edge : rows - edge]]
    for k in range(CONV - 1, 0, -1):
        added = roll(came_back[(k - 1) * SUBS : k * SUBS], quarters - 1)
        total.append(dx[rows - k * SUBS : rows - (k - 1) * SUBS] + jnp.where(last, added, 0.0))
    x_grad[rows - 2 * edge :] = jnp.concatenate(total, axis=0).astype(BF16)
    few = 16
    size = width // spans
    for copy in over_inner:
        copy.wait_recv()

    for j in range(spans):
        columns = slice(j * size, (j + 1) * size)
        there = pl.ds(pl.multiple_of(links.flipped(links.span, j) * size, 128), size)
        total = resid[:, there] + near[0, :, columns].astype(F32) + from_side[0, :, columns].astype(F32)
        for k in range(n - 1):
            total = total + from_inner[k, :, columns].astype(F32)
        output[:, there] = total.astype(BF16)

    load.wait()

    @pl.loop(0, width // step)
    def _(k):
        start = pl.multiple_of(k * step, 128)
        columns = pl.ds(start, step)
        total = part[:, columns] + lax.dot_general(
            x_grad[...], held_y[columns], (((1,), (1,)), ((), ())), preferred_element_type=F32
        )
        lower = side == 0
        part_own[:, columns] = jnp.where(lower, total[:own], total[own:])
        part_other[:, columns] = jnp.where(lower, total[own:], total[:own]).astype(BF16)

    for copy in across:
        copy.wait_recv()
    links.close()


def returned(sizes, steps, quarters, heads, inner, branch, out_w, y_pre, states, decay, flow, conv, recur, inject, xb, chan, gate,
             resid, near, far, wide, narrow, proj_y, proj_x):
    spans, _ = sizes
    own, width = branch.shape
    rows, half = y_pre.shape
    n = len(inner) + 1
    inside, anywhere = pl.BlockSpec(memory_space=pltpu.VMEM), pl.BlockSpec(memory_space=pl.ANY)

    def high(*shape):
        return jax.ShapeDtypeStruct(shape, F32)

    def low(*shape):
        return jax.ShapeDtypeStruct(shape, BF16)

    shapes = [
        low(rows, width), low(rows, half), low(rows, half), high(*gate.shape), high(SUBS, half), low(own, width),
        high(own, width), low(own, width), low(*wide.shape), low(*narrow.shape),
    ]
    end = (SUBS, half)
    copies = 3 * (spans // 2) + 2 * n + 2 * n + spans + 2
    tail = ((CONV - 1) * SUBS, half)
    return pl.pallas_call(
        functools.partial(return_kernel, sizes, steps, quarters, heads, inner),
        in_specs=[inside] * 15 + [anywhere] * 4,
        out_specs=[inside] * 8 + [anywhere] * 2,
        out_shape=shapes,
        scratch_shapes=[
            pltpu.VMEM((rows, width), F32), pltpu.VMEM(proj_y.shape, BF16), pltpu.SemaphoreType.DMA((1,)),
            pltpu.VMEM((rows, half), F32), pltpu.VMEM(tail, F32), pltpu.VMEM(tail, F32), *[pltpu.VMEM((rows, half), F32)] * 3, pltpu.VMEM((4 * SUBS, half), F32), pltpu.VMEM(end, F32),
            pltpu.VMEM((n, *end), F32), pltpu.VMEM((spans, *end), F32), pltpu.VMEM(end, F32), pltpu.VMEM(end, F32),
            pltpu.VMEM((n, own, width), BF16), pltpu.VMEM((n - 1, own, width), BF16), pltpu.VMEM((n - 1, own, width), BF16),
            pltpu.SemaphoreType.DMA((copies,)), pltpu.SemaphoreType.DMA((copies,)),
        ],
        compiler_params=pltpu.CompilerParams(collective_id=4, has_side_effects=True, vmem_limit_bytes=VMEM_LIMIT),
    )(branch, out_w, y_pre, states, decay, flow, conv, recur, inject, xb, chan, gate, resid, near, far, wide, narrow, proj_y, proj_x)


def on_device(
    inputs, norm_one, rec_proj, conv_weight, conv_bias, gate_weight, gate_bias, decay_param, out_proj, norm_two,
    mlp_wide, mlp_narrow, cotangent,
):
    spans, seqs = lax.axis_size("span"), lax.axis_size("seq")
    count = spans * seqs
    span, seq = lax.axis_index("span"), lax.axis_index("seq")
    me = span * seqs + seq
    side = me % 2
    pair = me // 2
    pairs = count // 2
    batch, tokens, width = inputs.shape
    half = width // 2
    quarters = SUBS // batch
    steps = tokens // quarters
    own = batch * tokens
    rows = 2 * own
    head_w = gate_weight.shape[1] // 2
    heads = half // head_w
    edge = CONV - 1
    share = width // count
    units = mlp_narrow.shape[1]
    inner = [2 * k for k in range(1, seqs // 2)]
    core = seqs
    xs = [2 * seqs * k for k in range(1, spans // 2)]
    top = count // 2
    upper = me // top
    chunk_masks = [0, *inner[1::-1], *inner[2:]]

    def to_rows(v):
        return v.reshape(batch, quarters, steps, width).transpose(2, 0, 1, 3).reshape(own, width)

    def from_rows(v):
        return v.reshape(steps, batch, quarters, width).transpose(1, 2, 0, 3).reshape(batch, tokens, width)

    def in_order(mine, other, axis):
        return jnp.concatenate([jnp.where(side == 0, mine, other), jnp.where(side == 0, other, mine)], axis=axis)

    def cut(v, index, size, axis):
        return lax.dynamic_slice_in_dim(v, index * size, size, axis)

    direct = share % 16 == 0 and (spans, seqs) == (4, 8)

    def gathered_rows(block, buffer, place):
        pieces = {0: block}
        for m in inner:
            pieces[m] = swap(block, m)
        for m in xs:
            for n in (0, *inner):
                pieces[m ^ n] = swap(pieces[n], m)
        for n in list(pieces):
            pieces[core ^ n] = swap(pieces[n], core)
        for m, piece in pieces.items():
            buffer = lax.dynamic_update_slice_in_dim(buffer, piece, place(me ^ m), 0)
        return buffer

    def columns_half(block):
        mine, theirs = cut(block, side, half, 1), cut(block, 1 - side, half, 1)
        block = in_order(mine, swap(theirs, 1), 0)
        return gathered_rows(block, jnp.zeros((width, half), BF16), lambda d: d // 2 * 2 * share)

    def rows_half(block):
        full = lax.all_gather(block, AXES, axis=0, tiled=True)
        return cut(full, side, half, 0)

    def by_span(v):
        size = width // spans
        return jnp.concatenate([cut(v, span ^ j, size, 1) for j in range(spans)], axis=1)

    def over_sides(partial):
        partial = partial.reshape(2, own, width)
        other = lax.dynamic_index_in_dim(partial, 1 - side, 0, keepdims=False).astype(BF16)
        return lax.dynamic_index_in_dim(partial, side, 0, keepdims=False) + swap(other, 1).astype(F32)

    def exchanged(carry):
        every = lax.all_gather(carry, AXES, axis=0).reshape(pairs, 2, batch, quarters, half)
        every = lax.dynamic_index_in_dim(every, side, 1, keepdims=False)
        return every[:, :, 0], every[:, :, 1]

    def entering(enter, h):
        enter = enter.reshape(2, 2, SUBS, half)
        return enter[0] * jnp.repeat(h, quarters, axis=0)[None] + enter[1]

    def by_steps(v):
        return v.reshape(2, steps, SUBS, half)

    def span_gather(block):
        pieces = {0: block}
        for m in xs:
            pieces[m] = swap(block, m)
        for n in list(pieces):
            pieces[n ^ core] = swap(pieces[n], core)
        return [pieces[m * seqs] for m in range(spans)]

    def token_gather(v):
        blocks = [v] + [swap(v, m) for m in inner]
        return [b for block in blocks for b in (block, swap(block, 1))]

    small = jnp.stack([*conv_weight.T, conv_bias, *gate_bias.T, decay_param, norm_one, norm_two]).astype(F32)
    small = jnp.concatenate([small[:7], jax.nn.softplus(small[7:8]), small[8:]], axis=0)
    wide_own = mlp_wide.transpose(1, 2, 0).reshape(2 * units, width // spans)
    narrow_own = mlp_narrow.T
    grads_own = by_span(to_rows(cotangent))
    c = to_rows(cotangent).astype(F32)

    mine = to_rows(inputs)
    x = mine.astype(F32)
    tail = inputs[:, tokens - edge :]
    halo = lax.ppermute(tail, AXES, [(i, i + 1) for i in range(1, count - 1, 2)]) + lax.ppermute(
        tail, AXES, [(i, i + 2) for i in range(1, count - 2, 2)]
    )
    halo = jnp.zeros((edge, batch, quarters, width), BF16).at[:, :, 0].set(halo[:, ::-1].transpose(1, 0, 2))
    halo = jnp.concatenate([halo.reshape(edge * SUBS, width), jnp.zeros((8, width), BF16)], axis=0)

    if direct:
        packed = jnp.pad(small, ((0, 6), (0, -share % 128)))
        nearby, (proj_x, proj_y, out_half, gates), wides, narrows, cots = front(
            (spans, seqs), steps, quarters, heads, head_w, mine, halo, packed, rec_proj, out_proj, gate_weight, grads_own,
            wide_own, narrow_own,
        )
        normal_one, x_branch, y_pre, conv, recur, inject, decay, states, flow, mixed, resid, normal_two, params, chan, turned, mixed_turned = nearby
        gain_one, gain_two = params[SUBS], params[SUBS + 1]
    else:
        proj_x = columns_half(rec_proj[:, :width])
        proj_y = columns_half(rec_proj[:, width:])
        gates = rows_half(gate_weight)
        out_half = rows_half(out_proj)
        small = lax.all_gather(small, AXES, axis=1, tiled=True)
        gain_one, gain_two = small[SUBS], small[SUBS + 1]
        chan = cut(small[:SUBS], side, half, 1)
        lead = jnp.concatenate([in_order(mine, swap(mine, 1), 0), halo], axis=0)
        normal_one = normed(lead.astype(F32), gain_one).astype(BF16)
        x_branch = nn(normal_one, proj_x, BF16)
        normal_one = normal_one[:rows]
        y_pre = nn(normal_one, proj_y)
        y_branch, gelu_back = jax.vjp(jax.nn.gelu, y_pre)
        kernel = functools.partial(forward_kernel, steps, quarters)
        full = ((rows, half), False)
        ends = ((4 * SUBS, half), False)
        conv, recur, inject, decay, local, prod, enter, carry = by_heads(
            kernel, heads, head_w, [(x_branch, False), (chan, False), (gates, True)],
            [full] * 6 + [ends, ((SUBS, half), False)],
        )
        prods, sums = exchanged(carry)
        h = jnp.zeros((batch, half), F32)
        for j in range(pairs - 1):
            h = jnp.where(j < pair, prods[j] * h + sums[j], h)
        entered = entering(enter, h)
        states = (by_steps(local) + by_steps(prod) * entered[:, None]).reshape(rows, half)
        flow = jnp.concatenate([entered, by_steps(prod)[:, -1]], axis=0).reshape(4 * SUBS, half)
        mixed = (states * y_branch).astype(BF16)
        resid = x + over_sides(nn(mixed, out_half))
        normal_two = by_span(normed(resid, gain_two).astype(BF16))
        wides, narrows = span_gather(wide_own), span_gather(narrow_own)
        cots = token_gather(grads_own)

    def token_scatter(near, far):
        total = None
        for k, m in enumerate((0, *inner)):
            block = near[k].astype(F32) + swap(far[k], 1).astype(F32)
            total = block if m == 0 else total + swap(block.astype(BF16), m).astype(F32)
        return by_span(total)

    size = width // spans

    def by_core(v):
        blocks = [v[:, j * size : (j + 1) * size] for j in range(spans)]
        return [*blocks[::2], jnp.concatenate(blocks[1::2], axis=1)]

    if direct:
        normal_two_grad, near, far, all_act, all_hidden, *features, wide_away, narrow_away, wide_recv, narrow_recv = feed_forward(
            (spans, seqs), chunk_masks, normal_two, cots, wides, narrows
        )
        all_normal, all_grads = [features[0]], [features[1]]
        wide_away, narrow_away, wide_recv, narrow_recv = wide_away[None], narrow_away[None], wide_recv[:, :size], narrow_recv[:, :size]
    else:
        wide, narrow = jnp.concatenate(wides, axis=1), jnp.concatenate(narrows, axis=1)
        all_normal = jnp.concatenate(token_gather(normal_two), axis=0)
        all_grads = jnp.concatenate(cots, axis=0)

        def activate(values):
            return jax.nn.gelu(values[:, :units]) * values[:, units:]

        value, back = jax.vjp(activate, nt(all_normal, wide))
        all_hidden = value.astype(BF16)
        all_act = back(nt(all_grads, narrow))[0].astype(BF16)

        def sided(v):
            v = v.reshape(len(inner) + 1, 2, own, width)
            return v[:, 0], v[:, 1]

        all_normal, all_grads = by_core(all_normal), by_core(all_grads)
        normal_two_grad = token_scatter(*sided(nn(all_act, wide, BF16)))
        near, far = sided(nn(all_hidden, narrow, BF16))
    def core_sum(left, right):
        recv = swap(tn(left, right[-1], BF16), core)
        away = [
            (tn(left, v) + recv[:, (k + 1) * size : (k + 2) * size].astype(F32)).astype(BF16) for k, v in enumerate(right[1:-1])
        ]
        return recv[:, :size], jnp.stack(away)

    def own_sum(left, right, recv, came):
        left, came = lax.optimization_barrier((left, came))
        return tn(left, right[0]) + recv.astype(F32) + jnp.sum(came.astype(F32), axis=0)

    if not direct:
        wide_recv, wide_away = core_sum(all_act, all_normal)
        narrow_recv, narrow_away = core_sum(all_hidden, all_grads)
    resid_part, gain_two_grad = norm_back(resid, gain_two, normal_two_grad)
    resid_grad = c + resid_part
    branch_low = resid_grad.astype(BF16)
    if direct:
        branch_low, y_grad, x_grad, gate_grad, small_grad, output, part_own, part_other, wide_came, narrow_came = returned(
            (spans, seqs), steps, quarters, heads, chunk_masks[1:], branch_low, out_half, y_pre, states, decay, flow, conv, recur, inject,
            x_branch, chan, gates, resid, near, far, wide_away, narrow_away, proj_y, proj_x,
        )
    else:
        output = (resid + token_scatter(near, far)).astype(BF16)
        wide_came = jnp.stack([swap(wide_away[k], m) for k, m in enumerate(xs)])
        narrow_came = jnp.stack([swap(narrow_away[k], m) for k, m in enumerate(xs)])
        branch_low = in_order(branch_low, swap(branch_low, 1), 0)
        mixed_grad = nt(branch_low, out_half)
        y_grad = gelu_back(mixed_grad * states)[0].astype(BF16)
        kernel = functools.partial(adjoint_kernel, steps, quarters)
        local_adj, after, enter, carry = by_heads(
            kernel, heads, head_w, [(mixed_grad * y_branch, False), (decay, False), (flow, False)],
            [full, full, ends, ((SUBS, half), False)],
        )
        prods, sums = exchanged(carry)
        h = jnp.zeros((batch, half), F32)
        for j in range(pairs - 1, 0, -1):
            h = jnp.where(j > pair, prods[j] * h + sums[j], h)
        came = entering(enter, h).reshape(2 * SUBS, half)
        kernel = functools.partial(backward_kernel, steps, quarters)
        dx, spill, gate_grad, small_grad = by_heads(
            kernel, heads, head_w,
            [(v, False) for v in (local_adj, after, states, came, flow, conv, recur, inject, decay, x_branch, chan)]
            + [(gates, True)],
            [full, ((edge * SUBS, half), False), ((half, 2 * head_w), True), ((SUBS, half), False)],
        )
        spill = lax.ppermute(
            spill.reshape(edge, batch, quarters, half)[::-1, :, 0], AXES, [(i, i - 2) for i in range(2, count)]
        )
        spill = jnp.pad(
            spill[:, :, None], ((0, 0), (0, 0), (quarters - 1, 0), (0, 0))
        ).reshape(edge * SUBS, half)
        x_grad = jnp.concatenate([dx[: rows - edge * SUBS], dx[rows - edge * SUBS :] + spill], axis=0).astype(BF16)
    output = from_rows(output)
    wide_owned = own_sum(all_act, all_normal, wide_recv, wide_came)
    wide_owned = wide_owned.reshape(2, units, size).transpose(2, 0, 1)
    narrow_owned = own_sum(all_hidden, all_grads, narrow_recv, narrow_came).T
    if not direct:
        normal_one_part = nt(y_grad, proj_y) + nt(x_grad, proj_x)

    def blocks_of(v, masks, wrap):
        size = 2 * share
        return [lax.dynamic_slice_in_dim(v, (me ^ m) // 2 % wrap * size, size, 0) for m in masks]

    def to_columns_owner(v_kept, v_given):
        recv = swap(v_given, core)
        n = len(inner) + 1
        total = (v_kept + recv.astype(F32)).reshape(len(xs) + 1, n, 2 * share, v_kept.shape[1])
        near = total[0]
        for k, m in enumerate(xs):
            near = near + swap(total[k + 1].astype(BF16), m).astype(F32)
        out = near[0]
        for k, m in enumerate(inner):
            out = out + swap(near[k + 1].astype(BF16), m).astype(F32)
        out = out.reshape(2, share, out.shape[1])
        other = lax.dynamic_index_in_dim(out, 1 - side, 0, keepdims=False).astype(BF16)
        return lax.dynamic_index_in_dim(out, side, 0, keepdims=False), swap(other, 1).astype(F32)

    def to_rows_owner(v_kept, v_given):
        cols = v_kept.shape[1]
        total = (v_kept + swap(v_given, core).astype(F32)).reshape(len(low_order), 2 * share, cols)
        away = cut(total, 1 - upper, cols // 2, 2).astype(BF16)
        near = cut(total, upper, cols // 2, 2) + swap(away, top).astype(F32)
        out = near[0]
        for k, m in enumerate(low_order[1:]):
            out = out + swap(near[k + 1].astype(BF16), m).astype(F32)
        other = swap(out.astype(BF16), top).astype(F32)
        out = in_order(out, other, 1).reshape(2, share, cols)
        gone = lax.dynamic_index_in_dim(out, 1 - side, 0, keepdims=False).astype(BF16)
        here = lax.dynamic_index_in_dim(out, side, 0, keepdims=False)
        return jnp.where(upper == side, here, swap(gone, 1).astype(F32))

    order = [m ^ n for m in (0, *xs) for n in (0, *inner)]
    low_order = [m ^ n for m in (0, *[v for v in xs if v < top]) for n in (0, *inner)]

    def ordered(v, masks, wrap):
        return [jnp.concatenate(blocks_of(v, [m ^ c for m in masks], wrap), axis=0) for c in (0, core)]

    if direct:
        proj_owned, out_owned, gate_owned, input_grad, sums = scatter_grads(
            (spans, seqs), share, turned, mixed_turned, x_grad, y_grad, branch_low, gate_grad, small_grad, gain_two_grad[None],
            mine, gain_one[None], resid_grad, part_own, part_other,
        )
        gains = cut(sums[:2, :width], me, share, 1).T
        small_owned = cut(sums[:, width:], me % (count // 2), share, 1).T
    else:
        input_part, gain_one_grad = norm_back(x, gain_one, over_sides(normal_one_part))
        input_grad = resid_grad + input_part
        kept_d, given_d = ordered(normal_one.T, order, pairs)
        kept_m, given_m = ordered(mixed.T, low_order, pairs // 2)
        by_row = jnp.concatenate([gate_grad, small_grad.T, jnp.zeros((half, head_w - SUBS), F32)], axis=1)
        kept_g, given_g = ordered(by_row, low_order, pairs // 2)
        gains = jnp.pad(jnp.stack([gain_one_grad, gain_two_grad], axis=1), ((0, 0), (0, 126)))
        kept_n, given_n = ordered(gains, order, pairs)
        proj_owned = jnp.concatenate(
            [in_order(*to_columns_owner(nn(kept_d, g), nn(given_d, g, BF16)), 1) for g in (x_grad, y_grad)], axis=1
        )
        out_owned = to_rows_owner(nn(kept_m, branch_low), nn(given_m, branch_low, BF16))
        rest = to_rows_owner(kept_g, given_g.astype(BF16))
        gate_owned, small_owned = rest[:, : 2 * head_w], rest[:, 2 * head_w : 2 * head_w + SUBS]
        gains = sum(to_columns_owner(kept_n, given_n.astype(BF16)))
    input_grad = from_rows(input_grad)

    return (
        output,
        input_grad,
        gains[:, 0],
        proj_owned,
        small_owned[:, :CONV],
        small_owned[:, 4],
        gate_owned,
        small_owned[:, 5:7],
        small_owned[:, 7] * jax.nn.sigmoid(decay_param.astype(F32)),
        out_owned,
        gains[:, 1],
        wide_owned,
        narrow_owned,
    )


def solution(mesh):
    both = ("span", "seq")
    tokens = P(None, both, None)
    placed = (
        tokens, P(both), P(both, None), P(both, None), P(both), P(both, None), P(both, None), P(both), P(both, None),
        P(both), P("span", None, "seq"), P("span", "seq"), tokens,
    )
    given = (
        tokens, tokens, P(both), P(both, None), P(both, None), P(both), P(both, None), P(both, None), P(both),
        P(both, None), P(both), P("span", None, "seq"), P("span", "seq"),
    )
    return jax.shard_map(on_device, mesh=mesh, in_specs=placed, out_specs=given, check_vma=False)
```
